128 devices in a mesh: ctx: 32 (over x, z_hi, y), fsdp: 4 (over z_lo, core).
Axes of the slice: x: 4, y: 4, z: 4 (z_hi: 2, z_lo: 2; z = z_hi * 2 + z_lo), core: 2. Of those that a mesh axis runs over, the one named last changes fastest.
Arguments:
- layer_input: bfloat16 [4, 32, 1, 2, 64, 1024], P('fsdp', 'ctx'), may hold values from -6 to 6
- routes: int32 [4, 32, 1, 2, 64, 8], P('fsdp', 'ctx'), may hold values from 0 to 31, all different within a row; in each aligned block of 128 rows (0 to 127, 128 to 255, ..., all dimensions but the last counted through in order) at most 64 rows name the same one
- gates: float32 [4, 32, 1, 2, 64, 8], P('fsdp', 'ctx'), may hold values from 0.1 to 0.3
- cotangent: bfloat16 [4, 32, 1, 2, 64, 1024], P('fsdp', 'ctx'), may hold values from -6 to 6
- norm_attn: float32 [1024], P(('ctx', 'fsdp')), may hold values from 0.5 to 1.5
- query_key_value_weight: float32 [1024, 2048], P(('ctx', 'fsdp')), may hold values from -0.1875 to 0.1875
- output_weight: float32 [1024, 1024], P(('ctx', 'fsdp')), may hold values from -6 to 6
- norm_ffn: float32 [1024], P(('ctx', 'fsdp')), may hold values from 0.5 to 1.5
- exp_gate: float32 [32, 1024, 512], P('ctx', 'fsdp'), may hold values from -0.1875 to 0.1875
- exp_up: float32 [32, 1024, 512], P('ctx', 'fsdp'), may hold values from -0.1875 to 0.1875
- exp_down: float32 [32, 512, 1024], P('ctx', 'fsdp'), may hold values from -0.5 to 0.5
Outputs:
- layer_output: bfloat16 [4, 32, 1, 2, 64, 1024], P('fsdp', 'ctx')
- input_grad: float32 [4, 32, 1, 2, 64, 1024], P('fsdp', 'ctx')
- grad_norm_attn: float32 [1024], P(('ctx', 'fsdp'))
- grad_w_qkv: float32 [1024, 2048], P(('ctx', 'fsdp'))
- grad_w_out: float32 [1024, 1024], P(('ctx', 'fsdp'))
- grad_norm_ffn: float32 [1024], P(('ctx', 'fsdp'))
- grad_exp_gate: float32 [32, 1024, 512], P('ctx', 'fsdp')
- grad_exp_up: float32 [32, 1024, 512], P('ctx', 'fsdp')
- grad_exp_down: float32 [32, 512, 1024], P('ctx', 'fsdp')
The draws below stay inside these ranges and needn't reach their ends.
Inputs may be any that keep to these rules, and one draw needn't show every extreme that they name: `routes`: each token names 8 different experts. In the rows of one device (the entries that share f and c), no expert is named more than 64 times, a bound that some block reaches.
All inputs are finite; a program needn't handle non-finite values.
Results may differ from the reference program's by a relative error of at most 0.024.
Values may be sent and summed in bfloat16 or wider, within the bound.
No kernel may reach another device: no remote copies, remote signals or barrier semaphores. Data moves between devices by JAX's collectives and lax.ppermute only.
A program may use at most 192 MiB of HBM per device.

```python
import math
import jax
import jax.numpy as jnp
import numpy as np
from jax import lax

D = 1024
HEADS = 16
KV_HEADS = 8
HEAD_DIM = 64
FF = 512
TOPK = 8
LENGTH = 4096
SEQ_DEV = 1
EXPERTS = 32
SEQS = 4
BLK = 64
TOK_DEV = 128
CAP = 64
QKVW = 2048
N_CTX = 32
N_FSDP = 4


def block_scale(key, dims, cuts, least, largest):
    def one(dim, blocks):
        draws = jax.random.uniform(jax.random.fold_in(jax.random.fold_in(key, 6), dim), (blocks,), jnp.float32, least / len(cuts), largest / len(cuts))
        return jnp.repeat(jnp.exp(draws), dims[dim] // blocks).reshape((-1,) + (1,) * (len(dims) - dim - 1))

    level = one(*cuts[0])
    for cut in cuts[1:]:
        level = level * one(*cut)
    return level


def routed_block(rng, own, number, rows, amount, top, reach, skew):
    sequence = jax.random.permutation(rng, amount)
    packed, usual = load_shares(amount, rows * top, reach, skew, True), load_shares(amount, rows * top, reach, skew, False)
    places = jnp.arange(amount)

    def named(lengths, rotation):
        used = int((lengths > 0).sum())
        fixed = max(1, used // 4)
        shifted = fixed + (places - fixed + rotation * (used - fixed)) % max(1, amount - fixed)
        return jnp.zeros((amount,), jnp.int32).at[sequence[jnp.where(places < fixed, places, shifted)]].set(jnp.asarray(lengths, jnp.int32))

    lengths = jnp.where(number % 4 == 0, named(packed, number // 4), named(usual, number - number // 4 - 1))
    mixed = jax.random.permutation(jax.random.fold_in(own, 3), amount)
    donor, sink = mixed[0:amount // 2 * 2:2], mixed[1:amount // 2 * 2:2]
    margin = jnp.minimum(lengths[donor] - 1, reach - lengths[sink]) // 2
    margin = jnp.where((donor == sequence[0]) | (sink == sequence[0]) | (lengths[sink] == 0), 0, jnp.maximum(margin, 0))
    shifted = jax.random.randint(jax.random.fold_in(own, 4), (amount // 2,), 0, 1 << 20) % (margin + 1)
    lengths = lengths.at[donor].add(-shifted).at[sink].add(shifted)
    labels = jnp.searchsorted(jnp.cumsum(lengths), jnp.arange(rows * top), side="right").astype(jnp.int32)
    grid = labels.reshape(top, rows).T
    grid = grid[jax.random.permutation(jax.random.fold_in(own, 1), rows)]
    rotation = jax.random.randint(jax.random.fold_in(own, 2), (rows, 1), 0, top)
    return jnp.take_along_axis(grid, (jnp.arange(top)[None, :] + rotation) % top, axis=1)


def load_shares(amount, total, bound, skew, full):
    weights = [(1 << 20) // math.isqrt(grade ** skew) + 1 for grade in range(1, amount + 1)]
    largest = bound if full else min(bound, max(-(-total // amount), total * weights[0] // sum(weights)))
    least = 1 if total - largest >= amount - 1 else 0
    given, surplus = [largest] + [least] * (amount - 1), total - largest - least * (amount - 1)
    while surplus > 0:
        movable = [i for i in range(1, amount) if given[i] < largest] or [i for i in range(1, amount) if given[i] < bound]
        pool, remaining = sum([weights[i] for i in movable]), surplus
        for i in movable:
            extra = min(bound - given[i], max(1, remaining * weights[i] // pool), surplus)
            given[i] = given[i] + extra
            surplus = surplus - extra
    return np.array(given)


def gaussian(key, shape, scale, most, pieces=(), kind=jnp.bfloat16):
    factor_of = block_scale(key, shape, pieces, -0.22, 0.18) if pieces else 1.0
    values = jax.random.normal(key, shape, jnp.float32) * scale * factor_of
    return jnp.minimum(jnp.maximum(values, -most), most).astype(kind)


def setup_inputs(seed: int = 0) -> dict:
    seeds = jax.random.split(jax.random.key(seed), 12)
    layer_input = gaussian(seeds[0], (N_FSDP, N_CTX, SEQ_DEV, 2, BLK, D), 1.0, 6.0, ((0, 4), (1, 32)))
    routes_keys = jax.random.split(jax.random.fold_in(seeds[1], 1), N_FSDP * N_CTX * SEQ_DEV * 2 * BLK // TOK_DEV)
    routes_turns = jax.random.permutation(jax.random.fold_in(seeds[1], 3), N_FSDP * N_CTX * SEQ_DEV * 2 * BLK // TOK_DEV)
    routes = jax.vmap(lambda own, number: routed_block(jax.random.fold_in(seeds[1], 2), own, number, TOK_DEV, EXPERTS, TOPK, CAP, 1))(routes_keys, routes_turns).reshape((N_FSDP, N_CTX, SEQ_DEV, 2, BLK, TOPK))
    gates = jnp.clip(0.1 + 0.20000001043081284 * jax.random.uniform(seeds[2], (N_FSDP, N_CTX, SEQ_DEV, 2, BLK, TOPK), jnp.float32) ** block_scale(seeds[2], (N_FSDP, N_CTX, SEQ_DEV, 2, BLK, TOPK), ((0, 4), (1, 32)), -0.2, 0.2), 0.1, 0.3)
    cotangent = gaussian(seeds[3], (N_FSDP, N_CTX, SEQ_DEV, 2, BLK, D), 1.0, 6.0, ((0, 4), (1, 32)))
    norm_attn = jnp.clip(1.0 + 0.1 * jax.random.normal(seeds[4], (D,), jnp.float32), 0.5, 1.5)
    query_key_value_weight = gaussian(seeds[5], (D, QKVW), D ** -0.5, 0.1875, ((0, 128),), jnp.float32)
    output_weight = gaussian(seeds[6], (D, D), 1.0, 6.0, ((0, 128),), jnp.float32)
    norm_ffn = jnp.clip(1.0 + 0.1 * jax.random.normal(seeds[7], (D,), jnp.float32), 0.5, 1.5)
    exp_gate = gaussian(seeds[8], (EXPERTS, D, FF), D ** -0.5, 0.1875, ((0, 32), (1, 4)), jnp.float32)
    exp_up = gaussian(seeds[9], (EXPERTS, D, FF), D ** -0.5, 0.1875, ((0, 32), (1, 4)), jnp.float32)
    exp_down = gaussian(seeds[10], (EXPERTS, FF, D), (FF // 4) ** -0.5, 0.5, ((0, 32), (1, 4)), jnp.float32)
    return dict(layer_input=layer_input, routes=routes, gates=gates, cotangent=cotangent, norm_attn=norm_attn, query_key_value_weight=query_key_value_weight, output_weight=output_weight, norm_ffn=norm_ffn, exp_gate=exp_gate, exp_up=exp_up, exp_down=exp_down)


EPSILON = 1e-06
ROPE_BASE = 10000.0
MASKED = -1e+30
FULL_PRECISION = lax.Precision.HIGHEST

@jax.custom_vjp
def low(v):
    return lax.optimization_barrier(v.astype(jnp.bfloat16)).astype(jnp.float32)

@jax.custom_vjp
def low_back(v):
    return v

def low_keep(v):
    return (low(v), None)

def low_pass(kept, grad):
    return (grad,)

def back_keep(v):
    return (v, None)

def back_low(kept, grad):
    return (low(grad),)
low.defvjp(low_keep, low_pass)
low_back.defvjp(back_keep, back_low)

def rope_tables(positions, width):
    half = width // 2
    frequency = ROPE_BASE ** (-(jnp.arange(half, dtype=jnp.float32) * 2.0 / width))
    angle = positions[:, None] * frequency[None, :]
    return (jnp.cos(angle), jnp.sin(angle))

def rotate(values, cosine, sine):
    half = values.shape[-1] // 2
    first = values[..., :half]
    second = values[..., half:]
    cosine = cosine[:, None, :]
    sine = sine[:, None, :]
    return jnp.concatenate([first * cosine - second * sine, second * cosine + first * sine], axis=-1)

def to_natural(array):
    moved = jnp.moveaxis(array, 1, 3)
    front = moved[:, :, 0]
    back = jnp.flip(moved[:, :, 1], axis=2)
    joined = jnp.concatenate([front, back], axis=2)
    return joined.reshape((SEQS, LENGTH) + array.shape[5:])

def from_natural(array):
    blocks = array.reshape((N_FSDP, SEQ_DEV, 2 * N_CTX, BLK) + array.shape[2:])
    front = blocks[:, :, :N_CTX]
    back = jnp.flip(blocks[:, :, N_CTX:], axis=2)
    stacked = jnp.stack([front, back], axis=2)
    return jnp.moveaxis(stacked, 3, 1)

def attend_sequence(queries, keys, values):
    length = queries.shape[0]
    block = min(512, length)
    groups = HEADS // KV_HEADS
    key_pos = jnp.arange(length)

    def one_block(start):
        part = lax.dynamic_slice_in_dim(queries, start, block, 0)
        grouped = part.reshape(block, KV_HEADS, groups, HEAD_DIM)
        raw_scores = jnp.einsum('qkgd,tkd->kgqt', grouped, keys, precision=FULL_PRECISION) * HEAD_DIM ** (-0.5)
        scores = low_back(raw_scores)
        query_pos = start + jnp.arange(block)
        causal = key_pos[None, :] <= query_pos[:, None]
        scores = jnp.where(causal[None, None], scores, MASKED)
        weights = low(jax.nn.softmax(scores, axis=-1))
        mixed = jnp.einsum('kgqt,tkd->qkgd', weights, values, precision=FULL_PRECISION)
        return mixed.reshape(block, HEADS * HEAD_DIM)
    starts = (jnp.arange(length // block) * block).astype(jnp.int32)
    return lax.map(jax.checkpoint(one_block), starts).reshape(length, HEADS * HEAD_DIM)

def attend_item(item):
    return attend_sequence(item[0], item[1], item[2])

def expert_term(ident, gate_w, up_w, down_w, hidden, picks, slot_weights):
    total = picks.shape[0]
    most = N_FSDP * N_CTX * CAP
    found = jnp.nonzero(picks == ident, size=most, fill_value=total)[0]
    live = found < total
    safe = jnp.minimum(found, total - 1)
    owner = safe // TOPK
    inputs = low_back(hidden[owner])
    gate_hidden = low_back(jnp.dot(inputs, low(gate_w), precision=FULL_PRECISION))
    up_hidden = low_back(jnp.dot(inputs, low(up_w), precision=FULL_PRECISION))
    activated = low(jax.nn.silu(gate_hidden) * up_hidden)
    result = low(low_back(jnp.dot(activated, low(down_w), precision=FULL_PRECISION)))
    weight = jnp.where(live, slot_weights[safe], 0.0)
    return jnp.zeros_like(hidden).at[owner].add(result * weight[:, None])

def routed(hidden, picks, slot_weights, gate_all, up_all, down_all):

    def step(carry, item):
        term = jax.checkpoint(expert_term)(item[0], item[1], item[2], item[3], hidden, picks, slot_weights)
        return (carry + term, None)
    idents = jnp.arange(gate_all.shape[0]).astype(jnp.int32)
    summed, _ = lax.scan(step, jnp.zeros_like(hidden), (idents, gate_all, up_all, down_all))
    return summed

def layer(layer_inputs, norm_attn, query_key_value_weight, output_weight, norm_ffn, gate_all, up_all, down_all, picks, slot_weights):
    seq_count, length, width = layer_inputs.shape
    kv_width = KV_HEADS * HEAD_DIM
    scale_attn = lax.rsqrt(lax.optimization_barrier(jnp.mean(layer_inputs * layer_inputs, axis=-1, keepdims=True)) + EPSILON)
    attention_hidden = low(layer_inputs * scale_attn * low(norm_attn))
    projected_rows = low_back(jnp.einsum('hmg,gx->hmx', attention_hidden, low(query_key_value_weight), precision=FULL_PRECISION))
    cosine, sine = rope_tables(jnp.arange(length).astype(jnp.float32), HEAD_DIM)
    queries = low(rotate(projected_rows[..., :width].reshape(seq_count, length, HEADS, HEAD_DIM), cosine, sine))
    keys = low(rotate(projected_rows[..., width:width + kv_width].reshape(seq_count, length, KV_HEADS, HEAD_DIM), cosine, sine))
    values = low(projected_rows[..., width + kv_width:].reshape(seq_count, length, KV_HEADS, HEAD_DIM))
    mixed = lax.map(jax.checkpoint(attend_item), (queries, keys, values))
    attention_reduced = low(low_back(mixed))
    middle_output = layer_inputs + low_back(jnp.einsum('hmg,gx->hmx', attention_reduced, low(output_weight), precision=FULL_PRECISION))
    scale_ffn = lax.rsqrt(lax.optimization_barrier(jnp.mean(middle_output * middle_output, axis=-1, keepdims=True)) + EPSILON)
    hidden_ffn = low(middle_output * scale_ffn * low(norm_ffn)).reshape(seq_count * length, width)
    moe = routed(hidden_ffn, picks, slot_weights, gate_all, up_all, down_all)
    return middle_output + moe.reshape(layer_inputs.shape)

def reference(layer_input, routes, gates, cotangent, norm_attn, query_key_value_weight, output_weight, norm_ffn, exp_gate, exp_up, exp_down):
    x_nat = to_natural(layer_input.astype(jnp.float32))
    picks = to_natural(routes).reshape(-1)
    slot_weights = to_natural(gates).reshape(-1)
    grad_nat = to_natural(cotangent.astype(jnp.float32))

    def forward(layer_inputs, gain_attn, weight_qkv, weight_out, gain_ffn, gate_all, up_all, down_all):
        return layer(layer_inputs, gain_attn, weight_qkv, weight_out, gain_ffn, gate_all, up_all, down_all, picks, slot_weights)
    output, pullback = jax.vjp(forward, x_nat, norm_attn, query_key_value_weight, output_weight, norm_ffn, exp_gate, exp_up, exp_down)
    grads = pullback(grad_nat)
    return (from_natural(output).astype(jnp.bfloat16), from_natural(grads[0]), grads[1], grads[2], grads[3], grads[4], grads[5], grads[6], grads[7])
```

```python
import functools

import jax
import jax.numpy as jnp
import numpy as np
from jax import lax
from jax.experimental import pallas as pl
from jax.experimental.pallas import tpu as pltpu
from jax.sharding import Mesh
from jax.sharding import PartitionSpec as P

WIDTH = 1024
EPSILON = 1e-06
ROPE_BASE = 10000.0
MASKED = -1e30
BF = jnp.bfloat16
F32 = jnp.float32
CTX = ("x", "zh", "y")
HEAD_AXES = ("x", "zh")
FSDP = ("zl", "core")
ALL = CTX + FSDP
VMEM_LIMIT = 56 * 1024 * 1024

NT = (((1,), (1,)), ((), ()))
TN = (((0,), (0,)), ((), ()))


def mm(a, b, dims=None):
    if dims is None:
        return jnp.dot(a, b, preferred_element_type=F32)
    return lax.dot_general(a, b, dims, preferred_element_type=F32)


def lane(shape):
    return lax.broadcasted_iota(jnp.int32, shape, len(shape) - 1)


def row(shape):
    return lax.broadcasted_iota(jnp.int32, shape, len(shape) - 2)


def call(kernel, out_shape, cost, **kw):
    flops, bytes_accessed = cost
    return pl.pallas_call(
        kernel,
        out_shape=out_shape,
        compiler_params=pltpu.CompilerParams(vmem_limit_bytes=VMEM_LIMIT),
        cost_estimate=pl.CostEstimate(
            flops=int(flops), bytes_accessed=int(bytes_accessed), transcendentals=0
        ),
        **kw,
    )


def sds(shape, dtype):
    return jax.ShapeDtypeStruct(shape, dtype)


VM = pl.BlockSpec(memory_space=pltpu.VMEM)
SM = pl.BlockSpec(memory_space=pltpu.SMEM)


def slice_matrix():
    table = np.zeros((512, 512), np.float32)
    for k in range(512):
        section, place = k // 128, k % 128
        if section < 2:
            pair, part = section, place // 64
        else:
            pair, part = place // 64, section
        feat = place % 64
        f = (feat % 32) // 8
        column = pair * 64 + part * 16 + (feat // 32) * 8 + feat % 8
        table[k, f * 128 + column] = 1.0
    return table


def head_matrix():
    table = np.zeros((4, 128, 768), np.float32)
    for f in range(4):
        for block in range(2):
            for part in range(4):
                for j in range(16):
                    feat = (j // 8) * 32 + 8 * f + j % 8
                    source = block * 64 + part * 16 + j
                    if part == 2:
                        target = block * 128 + feat
                    elif part == 3:
                        target = block * 128 + 64 + feat
                    else:
                        target = 256 + block * 256 + part * 128 + feat
                    table[f, source, target] = 1.0
    return table


def kernel_route(picks_ref, gates_ref, rank_ref, gate_ref):
    experts = row((32, 128))
    gate = jnp.zeros((32, 128), F32)
    chosen = jnp.zeros((32, 128), F32)
    for k in range(8):
        hit = picks_ref[k : k + 1, :] == experts
        gate = gate + jnp.where(hit, gates_ref[k : k + 1, :], 0.0)
        chosen = chosen + jnp.where(hit, 1.0, 0.0)
    before = jnp.where(row((128, 128)) < lane((128, 128)), 1.0, 0.0).astype(BF)
    rank = mm(chosen.astype(BF), before)
    rank_ref[...] = jnp.where(chosen > 0.5, rank, -1.0)
    gate_ref[...] = gate


def kernel_slices(w_ref, gains_ref, table_ref, out_ref):
    w = w_ref[...].astype(BF).astype(F32)
    parts = []
    for p in range(4):
        parts.append(
            jnp.concatenate(
                [
                    w[:, 256 * p : 256 * p + 256],
                    w[:, 1024 + 128 * p : 1152 + 128 * p],
                    w[:, 1536 + 128 * p : 1664 + 128 * p],
                ],
                axis=1,
            )
        )
    stacked = jnp.concatenate(parts, axis=0).astype(BF)
    cut = mm(stacked, table_ref[...])
    for f in range(4):
        for p in range(4):
            out_ref[f, :, 128 * p : 128 * p + 128] = cut[
                8 * p : 8 * p + 8, 128 * f : 128 * f + 128
            ].astype(BF)
        out_ref[f, :, 512:640] = gains_ref[...].astype(BF)


def kernel_project(x_ref, w_ref, cos_ref, sin_ref, msg_ref, hidden_ref, gains_ref):
    gains = jnp.transpose(w_ref[:, 512:640].astype(F32))
    gains_ref[...] = gains[:8]
    for s in range(4):
        x = x_ref[128 * s : 128 * s + 128, :].astype(F32)
        scale = lax.rsqrt(jnp.mean(x * x, axis=-1, keepdims=True) + EPSILON)
        hidden_ref[128 * s : 128 * s + 128, :] = (x * scale * gains[0:1]).astype(BF)
    proj = mm(hidden_ref[...], w_ref[:, 0:512])
    ahead = pltpu.roll(proj, 512 - 8, 1)
    behind = pltpu.roll(proj, 8, 1)
    partner = jnp.where((lane((512, 512)) // 8) % 2 == 0, ahead, behind)
    cos = jnp.concatenate([cos_ref[...]] * 4, axis=0)
    sin = jnp.concatenate([sin_ref[...]] * 4, axis=0)
    turned = proj * cos + partner * sin
    low = lane((64, 128)) < 64
    for s in range(4):
        for p in range(4):
            front = turned[128 * s : 128 * s + 64, 128 * p : 128 * p + 128]
            back = turned[128 * s + 64 : 128 * s + 128, 128 * p : 128 * p + 128]
            msg_ref[8 * p + s] = jnp.where(low, front, pltpu.roll(back, 64, 1)).astype(BF)
            msg_ref[8 * p + 4 + s] = jnp.where(low, pltpu.roll(front, 64, 1), back).astype(BF)


def kernel_heads(msg_ref, table_ref, kv_ref, q_ref):
    out = jnp.zeros((512, 768), F32)
    for f in range(4):
        out = out + mm(msg_ref[:, f].reshape(512, 128), table_ref[f])
    pairs = out[:, 0:256].astype(BF)
    for half in range(2):
        block = pairs[:, 128 * half : 128 * half + 128]
        for y in range(4):
            kv_ref[y, 512 * half : 512 * half + 512, :] = block
    queries = (out[:, 256:768] * 0.125).astype(BF)
    for half in range(2):
        for head in range(2):
            at = 256 * half + 128 * head
            q_ref[half, :, head] = queries[:, at : at + 128].reshape(8, 64, 128)


def tile_positions(tile, mine):
    front = tile < 4
    i = jnp.where(front, tile, tile - 4)
    q = lane((1, 256))
    k = row((512, 1))
    k = lax.broadcasted_iota(jnp.int32, (512, 1), 0)
    q_front = (8 * i + 4 * (q // 128) + mine) * 64 + q % 64
    q_back = (63 - 8 * i - 4 * (q // 128) - mine) * 64 + q % 64
    k_front = 512 * i + k
    k_back = (59 - 8 * i + 4 * (k // 256) - (k % 256) // 64) * 64 + k % 64
    count = jnp.where(front, i + 1, 8 - i)
    return jnp.where(front, q_front, q_back), jnp.where(front, k_front, k_back), count


def kernel_attend(mine_ref, kv_ref, q_ref, msg_ref, log_ref, out_ref, keys_ref, turned_ref):
    tile = pl.program_id(0)

    @pl.when(tile == 0)
    def _():
        for group in range(16):
            half, place = (0, group) if group < 8 else (1, 15 - group)
            for y in range(4):
                at = 256 * group + 64 * y
                keys_ref[at : at + 64, :] = kv_ref[y, half, place]
        for c in range(8):
            turned_ref[:, 512 * c : 512 * c + 512] = jnp.transpose(
                keys_ref[512 * c : 512 * c + 512, :].astype(F32)
            ).astype(BF)

    q = q_ref[...]
    q_pos, k_pos, count = tile_positions(tile, mine_ref[0])

    def step(c, carry, last):
        peak, total, mixed = carry
        at = pl.multiple_of(c * 512, 512)
        scores = mm(keys_ref[pl.ds(at, 512), :], q, NT)
        if last:
            scores = jnp.where(k_pos <= q_pos, scores, MASKED)
        higher = jnp.maximum(peak, jnp.max(scores, axis=0, keepdims=True))
        weights = jnp.exp(scores - higher)
        fade = jnp.exp(peak - higher)
        total = total * fade + jnp.sum(weights, axis=0, keepdims=True)
        mixed = mixed * fade + mm(turned_ref[64:128, pl.ds(at, 512)], weights.astype(BF))
        return higher, total, mixed

    start = (
        jnp.full((1, 256), MASKED, F32),
        jnp.zeros((1, 256), F32),
        jnp.zeros((64, 256), F32),
    )
    carry = lax.fori_loop(0, count - 1, lambda c, v: step(c, v, False), start)
    peak, total, mixed = step(count - 1, carry, True)
    log_ref[0] = jnp.broadcast_to(peak + jnp.log(total), (8, 256))
    mixed = mixed / total
    out = jnp.transpose(jnp.concatenate([jnp.zeros((64, 256), F32), mixed], axis=0))
    out_ref[...] = out
    low = lane((64, 128)) < 64
    for a in range(2):
        first = out[128 * a : 128 * a + 64]
        second = out[128 * a + 64 : 128 * a + 128]
        msg_ref[a, 0] = jnp.where(low, pltpu.roll(first, 64, 1), second).astype(BF)


def kernel_attend_back(
    mine_ref, keys_ref, turned_ref, q_ref, grad_ref, log_ref, out_ref, dq_ref, dkv_ref, sum_ref
):
    tile = pl.program_id(0)

    @pl.when(tile == 0)
    def _():
        sum_ref[...] = jnp.zeros_like(sum_ref)

    q = q_ref[...]
    low = lane((64, 128)) < 64
    pieces = []
    for a in range(2):
        both = grad_ref[a, 0].astype(F32)
        pieces.append(jnp.where(low, 0.0, pltpu.roll(both, 64, 1)))
        pieces.append(jnp.where(low, 0.0, both))
    grad = jnp.concatenate(pieces, axis=0)
    delta = jnp.sum(jnp.transpose(grad * out_ref[...]), axis=0, keepdims=True)
    grad = grad.astype(BF)
    q_pos, k_pos, count = tile_positions(tile, mine_ref[0])
    log_total = log_ref[0][0:1]

    def step(c, dq, last):
        at = pl.multiple_of(c * 512, 512)
        keys = keys_ref[pl.ds(at, 512), :]
        scores = mm(keys, q, NT)
        if last:
            scores = jnp.where(k_pos <= q_pos, scores, MASKED)
        weights = jnp.exp(scores - log_total)
        slope = (weights * (mm(keys, grad, NT) - delta)).astype(BF)
        sum_ref[pl.ds(at, 512), :] += mm(slope, q) + mm(weights.astype(BF), grad)
        return dq + mm(turned_ref[0:64, pl.ds(at, 512)], slope)

    dq = lax.fori_loop(0, count - 1, lambda c, v: step(c, v, False), jnp.zeros((64, 256), F32))
    dq = step(count - 1, dq, True)
    dq_ref[...] = jnp.transpose(jnp.concatenate([dq * 0.125, jnp.zeros((64, 256), F32)], axis=0))

    @pl.when(tile == 7)
    def _():
        for group in range(16):
            half, place = (0, group) if group < 8 else (1, 15 - group)
            for y in range(4):
                at = 256 * group + 64 * y
                dkv_ref[y, half, place] = sum_ref[at : at + 64, :].astype(BF)


def kernel_middle(
    o_ref, w_ref, x_ref, gains_ref, rank_ref, slots_ref, mid_ref, rows_ref, hidden_ref
):
    @pl.when(pl.program_id(0) == 0)
    def _():
        for g in range(8):
            rows_ref[:, 128 * g : 128 * g + 128] = o_ref[g].reshape(128, 128)
        mid = x_ref[...].astype(F32) + mm(rows_ref[...], w_ref[...])
        mid_ref[...] = mid
        scale = lax.rsqrt(jnp.mean(mid * mid, axis=-1, keepdims=True) + EPSILON)
        hidden_ref[...] = (mid * scale * gains_ref[1:2]).astype(BF)

    slot = lax.broadcasted_iota(jnp.int32, (64, 128), 0).astype(F32)
    for j in range(4):
        rank = rank_ref[pl.ds(4 * pl.program_id(0) + j, 1), :]
        pick = jnp.where(slot == rank, 1.0, 0.0).astype(BF)
        slots_ref[j] = mm(pick, hidden_ref[...]).astype(BF)


def kernel_experts(
    h_ref, dy_ref, gate_ref, w_ref, ys_ref, dxs_ref, grad_ref, gu_ref, v_ref, rank_ref, ggu_ref, gv_ref
):
    step = pl.program_id(0)

    @pl.when(step == 0)
    def _():
        for f in range(4):
            gu_ref[256 * f : 256 * f + 256, :] = w_ref[f, 0:256, :]
            v_ref[128 * f : 128 * f + 128, :] = w_ref[f, 256:384, :]
        before = jnp.where(row((128, 128)) < lane((128, 128)), 1.0, 0.0).astype(BF)
        chosen = gate_ref[...] > 0.0
        rank = mm(jnp.where(chosen, 1.0, 0.0).astype(BF), before)
        rank_ref[...] = jnp.where(chosen, rank, -1.0)
        ggu_ref[...] = jnp.zeros_like(ggu_ref)
        gv_ref[...] = jnp.zeros_like(gv_ref)

    slot = lax.broadcasted_iota(jnp.int32, (64, 128), 0).astype(F32)
    grads = []
    for j in range(4):
        source = 4 * step + j
        pick = slot == rank_ref[pl.ds(source, 1), :]
        weight = jnp.sum(
            jnp.where(pick, gate_ref[pl.ds(source, 1), :], 0.0), axis=1, keepdims=True
        )
        rows = mm(jnp.where(pick, 1.0, 0.0).astype(BF), dy_ref[j])
        grads.append((rows * weight).astype(BF))
    dys = jnp.concatenate(grads, axis=0)
    h = h_ref[...].reshape(256, WIDTH)
    both = mm(h, gu_ref[...])
    gate_h, up_h = both[:, :512], both[:, 512:]
    sig = jax.nn.sigmoid(gate_h)
    swished = gate_h * sig
    act = (swished * up_h).astype(BF)
    ys_ref[...] = mm(act, v_ref[...]).astype(BF).reshape(4, 64, WIDTH)
    dact = mm(dys, v_ref[...], NT)
    dgate = (dact * up_h * sig * (1.0 + gate_h * (1.0 - sig))).astype(BF)
    dup = (dact * swished).astype(BF)
    dboth = jnp.concatenate([dgate, dup], axis=1)
    dxs_ref[...] = mm(dboth, gu_ref[...], NT).astype(BF).reshape(4, 64, WIDTH)
    ggu_ref[...] += mm(h, dboth, TN)
    gv_ref[...] += mm(act, dys, TN)

    @pl.when(step == 7)
    def _():
        for f in range(4):
            grad_ref[f, 0:256, :] = ggu_ref[256 * f : 256 * f + 256, :].astype(BF)
            grad_ref[f, 256:384, :] = gv_ref[128 * f : 128 * f + 128, :].astype(BF)


def kernel_middle_back(
    dxs_ref, rank_ref, mid_ref, cot_ref, gains_ref, w_ref, dmid_ref, low_ref, msg_ref, ggain_ref, sum_ref
):
    step = pl.program_id(0)

    @pl.when(step == 0)
    def _():
        sum_ref[...] = jnp.zeros_like(sum_ref)

    slot = lax.broadcasted_iota(jnp.int32, (64, 128), 0).astype(F32)
    picks = []
    for j in range(4):
        picks.append(jnp.where(slot == rank_ref[pl.ds(4 * step + j, 1), :], 1.0, 0.0))
    picks = jnp.concatenate(picks, axis=0).astype(BF)
    sum_ref[...] += mm(picks, dxs_ref[...].reshape(256, WIDTH), TN)

    @pl.when(step == 7)
    def _():
        mid = mid_ref[...]
        scale = lax.rsqrt(jnp.mean(mid * mid, axis=-1, keepdims=True) + EPSILON)
        dh = sum_ref[...]
        ggain_ref[...] = jnp.broadcast_to(
            jnp.sum(dh * (mid * scale), axis=0, keepdims=True), (8, WIDTH)
        )
        dn = dh * gains_ref[1:2]
        dmid = (
            cot_ref[...].astype(F32)
            + scale * dn
            - mid * (scale * scale * scale) * jnp.mean(dn * mid, axis=-1, keepdims=True)
        )
        dmid_ref[...] = dmid
        low = dmid.astype(BF)
        low_ref[...] = low
        grad = mm(low, w_ref[...], NT).astype(BF)
        for g in range(8):
            msg_ref[g] = grad[:, 128 * g : 128 * g + 128].reshape(2, 64, 128)


def kernel_slices_back(dkv_ref, dq_ref, cos_ref, sin_ref, table_ref, msg_ref):
    def unrotate(w, cos, sin):
        partner = jnp.where(
            lane(w.shape) % 64 < 32, pltpu.roll(w, 96, 1), pltpu.roll(w, 32, 1)
        )
        return (w * cos - partner * sin).astype(BF)

    cos, sin = cos_ref[...], sin_ref[...]
    dkv = dkv_ref[0].astype(F32)
    for y in range(1, 4):
        dkv = dkv + dkv_ref[y].astype(F32)
    dkv = unrotate(dkv, cos, sin)
    parts = [dkv[0:512], dkv[512:1024]]
    for half in range(2):
        table_cos = cos[512 * half : 512 * half + 512]
        table_sin = sin[512 * half : 512 * half + 512]
        for head in range(2):
            parts.append(
                unrotate(dq_ref[half, :, head].reshape(512, 128), table_cos, table_sin)
            )
    whole = jnp.concatenate(parts, axis=1)
    for f in range(4):
        msg_ref[:, f] = mm(whole, table_ref[f], NT).astype(BF).reshape(8, 64, 128)


def kernel_project_back(
    msg_ref, x_ref, hidden_ref, w_ref, gains_ref, ggain_ref, o_ref, da_ref, grads_ref, dh_ref, d_ref
):
    low = lane((64, 128)) < 64
    for s in range(4):
        for p in range(4):
            even = msg_ref[8 * p + s].astype(F32)
            odd = msg_ref[8 * p + 4 + s].astype(F32)
            d_ref[128 * s : 128 * s + 64, 128 * p : 128 * p + 128] = jnp.where(
                low, even, pltpu.roll(odd, 64, 1)
            ).astype(BF)
            d_ref[128 * s + 64 : 128 * s + 128, 128 * p : 128 * p + 128] = jnp.where(
                low, pltpu.roll(even, 64, 1), odd
            ).astype(BF)
    grads_ref[:, 0:512] = mm(hidden_ref[...], d_ref[...], TN).astype(BF)
    total = jnp.zeros((1, WIDTH), F32)
    for s in range(4):
        part = mm(d_ref[128 * s : 128 * s + 128, :], w_ref[:, 0:512], NT)
        dh_ref[128 * s : 128 * s + 128, :] = part.astype(BF)
        x = x_ref[128 * s : 128 * s + 128, :].astype(F32)
        scale = lax.rsqrt(jnp.mean(x * x, axis=-1, keepdims=True) + EPSILON)
        total = total + jnp.sum(part * (x * scale), axis=0, keepdims=True)
    which = lax.broadcasted_iota(jnp.int32, (128, WIDTH), 0)
    both = jnp.where(which == 0, total, jnp.where(which == 1, ggain_ref[0:1], 0.0))
    grads_ref[:, 512:640] = jnp.transpose(both).astype(BF)
    for g in range(8):
        part = jnp.zeros((128, 256), F32)
        for s in range(4):
            part = part + mm(
                o_ref[s, g].reshape(128, 128), da_ref[128 * s : 128 * s + 128, :], TN
            )
        grads_ref[128 * g : 128 * g + 128, 640:896] = part.astype(BF)


def kernel_total(parts_ref, table_ref, qkv_ref, out_ref, gains_ref, sum_ref):
    step = pl.program_id(0)

    @pl.when(step == 0)
    def _():
        sum_ref[...] = jnp.zeros_like(sum_ref)

    sum_ref[...] += jnp.sum(parts_ref[...].astype(F32), axis=0)

    @pl.when(step == 3)
    def _():
        rows = []
        for p in range(4):
            rows.append(
                jnp.concatenate(
                    [sum_ref[f, :, 128 * p : 128 * p + 128] for f in range(4)], axis=1
                )
            )
        rest = jnp.concatenate(rows, axis=0)
        whole = jnp.zeros((32, 512), F32)
        for _ in range(3):
            part = rest.astype(BF)
            rest = rest - part.astype(F32)
            whole = whole + mm(part, table_ref[...], NT)
        for p in range(4):
            piece = whole[8 * p : 8 * p + 8]
            qkv_ref[:, 256 * p : 256 * p + 256] = piece[:, 0:256]
            qkv_ref[:, 1024 + 128 * p : 1152 + 128 * p] = piece[:, 256:384]
            qkv_ref[:, 1536 + 128 * p : 1664 + 128 * p] = piece[:, 384:512]
        for f in range(4):
            out_ref[:, 256 * f : 256 * f + 256] = sum_ref[f, :, 640:896]
        gains_ref[...] = (
            sum_ref[0, :, 512:640]
            + sum_ref[1, :, 512:640]
            + sum_ref[2, :, 512:640]
            + sum_ref[3, :, 512:640]
        )


def kernel_input_grad(dh_ref, x_ref, dmid_ref, gains_ref, out_ref):
    x = x_ref[...].astype(F32)
    scale = lax.rsqrt(jnp.mean(x * x, axis=-1, keepdims=True) + EPSILON)
    dn = dh_ref[...].astype(F32) * gains_ref[0:1]
    out_ref[...] = (
        dmid_ref[...]
        + scale * dn
        - x * (scale * scale * scale) * jnp.mean(dn * x, axis=-1, keepdims=True)
    )


def kernel_output(ys_ref, rank_ref, gate_ref, mid_ref, out_ref, sum_ref):
    step = pl.program_id(0)

    @pl.when(step == 0)
    def _():
        sum_ref[...] = mid_ref[...]

    slot = lax.broadcasted_iota(jnp.int32, (64, 128), 0).astype(F32)
    picks = []
    for j in range(4):
        hit = slot == rank_ref[pl.ds(4 * step + j, 1), :]
        picks.append(jnp.where(hit, gate_ref[pl.ds(4 * step + j, 1), :], 0.0))
    picks = jnp.concatenate(picks, axis=0)
    high = picks.astype(BF)
    rest = (picks - high.astype(F32)).astype(BF)
    ys = ys_ref[...].reshape(256, WIDTH)
    sum_ref[...] += mm(high, ys, TN) + mm(rest, ys, TN)

    @pl.when(step == 7)
    def _():
        out_ref[...] = sum_ref[...].astype(BF)


def angles(positions, features):
    frequency = ROPE_BASE ** (-(features.astype(F32) * 2.0 / 64))
    return positions.astype(F32)[:, None] * frequency[None, :]


def whole(shape):
    return pl.BlockSpec(shape, lambda t: (0,) * len(shape))


def exchange(value, axes):
    return lax.all_to_all(value, axes, split_axis=0, concat_axis=0, tiled=True)


def gather(value, axes):
    return lax.all_gather(value, axes, axis=0, tiled=True)


def on_device(
    layer_input,
    routes,
    gates,
    cotangent,
    norm_attn,
    query_key_value_weight,
    output_weight,
    norm_ffn,
    exp_gate,
    exp_up,
    exp_down,
):
    head_index = lax.axis_index(HEAD_AXES)
    mine = lax.axis_index("y")
    ctx_index = lax.axis_index(CTX)
    part_index = lax.axis_index(FSDP)
    x = layer_input.reshape(128, WIDTH)
    cot = cotangent.reshape(128, WIDTH)
    slice_table = jnp.asarray(slice_matrix(), BF)
    head_table = jnp.asarray(head_matrix(), BF)

    x_all = gather(x, FSDP)
    rank, gate = call(
        kernel_route,
        (sds((32, 128), F32), sds((32, 128), F32)),
        (1e6, 1e5),
        in_specs=[VM, VM],
        out_specs=(VM, VM),
    )(routes.reshape(128, 8).T, gates.reshape(128, 8).T)
    which = lax.broadcasted_iota(jnp.int32, (8, 128), 1)
    gain_rows = jnp.where(
        which == 0, norm_attn[:, None], jnp.where(which == 1, norm_ffn[:, None], 0.0)
    )
    slices = call(
        kernel_slices,
        sds((4, 8, 640), BF),
        (2e7, 1e6),
        in_specs=[VM, VM, VM],
        out_specs=VM,
    )(query_key_value_weight, gain_rows, slice_table)
    slices = jnp.broadcast_to(slices[None], (32, 4, 8, 640)).reshape(128, 8, 640)
    w_slice = exchange(slices, ALL).reshape(WIDTH, 640)
    out_copies = jnp.broadcast_to(output_weight.astype(BF)[None], (128, 8, WIDTH))
    w_out = exchange(out_copies, ALL).reshape(WIDTH, WIDTH)
    cot_all = gather(cot, CTX)
    gate_all = gather(gate, CTX).reshape(32, 32, 128)
    expert_weights = jnp.concatenate(
        [
            jnp.concatenate([exp_gate[0], exp_up[0]], axis=1),
            exp_down[0],
        ],
        axis=0,
    ).astype(BF)
    expert_all = gather(expert_weights, FSDP).reshape(4, 384, WIDTH)

    offset = jnp.arange(64, dtype=jnp.int32)
    token_pos = jnp.concatenate([ctx_index * 64 + offset, (63 - ctx_index) * 64 + offset])
    column = jnp.arange(512, dtype=jnp.int32)
    angle = angles(token_pos, 8 * part_index + column % 8)
    is_value = (column // 16) % 4 == 3
    sign = jnp.where((column // 8) % 2 == 0, -1.0, 1.0)
    cos_slice = jnp.where(is_value, 1.0, jnp.cos(angle))
    sin_slice = jnp.where(is_value, 0.0, jnp.sin(angle) * sign)
    msg, hidden, gains = call(
        kernel_project,
        (sds((32, 64, 128), BF), sds((512, WIDTH), BF), sds((8, WIDTH), F32)),
        (6e8, 4e6),
        in_specs=[VM] * 4,
        out_specs=(VM, VM, VM),
    )(x_all, w_slice, cos_slice, sin_slice)
    msg = exchange(msg, HEAD_AXES + FSDP)

    kv_copies, queries = call(
        kernel_heads,
        (sds((4, 1024, 128), BF), sds((2, 8, 2, 64, 128), BF)),
        (4e8, 3e6),
        in_specs=[VM, VM],
        out_specs=(VM, VM),
    )(msg.reshape(8, 4, 64, 128), head_table)
    queries = queries.reshape(2048, 128)
    kv = exchange(kv_copies, ("y",)).reshape(4, 2, 8, 64, 128)
    mine_ref = mine.astype(jnp.int32).reshape(1)
    msg_spec = pl.BlockSpec((2, 1, 64, 128), lambda t: (t % 4, t // 4, 0, 0))
    row_spec = pl.BlockSpec((256, 128), lambda t: (t, 0))
    log_spec = pl.BlockSpec((1, 8, 256), lambda t: (t, 0, 0))
    o_msg, log_total, o_rows, keys, turned = call(
        kernel_attend,
        (
            sds((8, 2, 64, 128), BF),
            sds((8, 8, 256), F32),
            sds((2048, 128), F32),
            sds((4096, 128), BF),
            sds((128, 4096), BF),
        ),
        (1e10, 5e6),
        grid=(8,),
        in_specs=[SM, whole((4, 2, 8, 64, 128)), row_spec],
        out_specs=(msg_spec, log_spec, row_spec, whole((4096, 128)), whole((128, 4096))),
    )(mine_ref, kv, queries)
    o_heads = exchange(o_msg, HEAD_AXES)
    o_all = gather(o_heads, FSDP).reshape(4, 8, 2, 64, 128)

    slots, mid = call(
        kernel_middle,
        (sds((32, 64, WIDTH), BF), sds((128, WIDTH), F32)),
        (9e8, 8e6),
        grid=(8,),
        in_specs=[
            whole((8, 2, 64, 128)),
            whole((WIDTH, WIDTH)),
            whole((128, WIDTH)),
            whole((8, WIDTH)),
            whole((32, 128)),
        ],
        out_specs=(
            pl.BlockSpec((4, 64, WIDTH), lambda t: (t, 0, 0)),
            whole((128, WIDTH)),
        ),
        scratch_shapes=[pltpu.VMEM((128, WIDTH), BF), pltpu.VMEM((128, WIDTH), BF)],
    )(o_heads, w_out, x, gains, rank)
    slots = exchange(slots, CTX)
    gate_mine = lax.dynamic_index_in_dim(gate_all, ctx_index, axis=1, keepdims=False)
    slot_spec = pl.BlockSpec((4, 64, WIDTH), lambda t: (t, 0, 0))
    ys, dxs, expert_grads = call(
        kernel_experts,
        (sds((32, 64, WIDTH), BF), sds((32, 64, WIDTH), BF), sds((4, 384, WIDTH), BF)),
        (2e10, 3e7),
        grid=(8,),
        in_specs=[
            slot_spec,
            pl.BlockSpec((4, 128, WIDTH), lambda t: (t, 0, 0)),
            whole((32, 128)),
            whole((4, 384, WIDTH)),
        ],
        out_specs=(slot_spec, slot_spec, whole((4, 384, WIDTH))),
        scratch_shapes=[
            pltpu.VMEM((WIDTH, WIDTH), BF),
            pltpu.VMEM((512, WIDTH), BF),
            pltpu.VMEM((32, 128), F32),
            pltpu.VMEM((WIDTH, WIDTH), F32),
            pltpu.VMEM((512, WIDTH), F32),
        ],
    )(slots, cot_all.reshape(32, 128, WIDTH), gate_mine, expert_all)
    dxs = exchange(dxs, CTX)
    expert_own = lax.psum_scatter(
        expert_grads.reshape(4 * 384, WIDTH), FSDP, scatter_dimension=0, tiled=True
    ).astype(F32)

    dmid, dmid_low, grad_msg, gain_ffn_part = call(
        kernel_middle_back,
        (
            sds((128, WIDTH), F32),
            sds((128, WIDTH), BF),
            sds((8, 2, 64, 128), BF),
            sds((8, WIDTH), F32),
        ),
        (9e8, 8e6),
        grid=(8,),
        in_specs=[
            slot_spec,
            whole((32, 128)),
            whole((128, WIDTH)),
            whole((128, WIDTH)),
            whole((8, WIDTH)),
            whole((WIDTH, WIDTH)),
        ],
        out_specs=(
            whole((128, WIDTH)),
            whole((128, WIDTH)),
            whole((8, 2, 64, 128)),
            whole((8, WIDTH)),
        ),
        scratch_shapes=[pltpu.VMEM((128, WIDTH), F32)],
    )(dxs, rank, mid, cot, gains, w_out)
    grad_heads = exchange(grad_msg, HEAD_AXES)
    da_all = gather(dmid_low, FSDP)

    ys, grad_heads = lax.optimization_barrier((ys, grad_heads))
    ys = exchange(ys, CTX)
    layer_output = call(
        kernel_output,
        sds((128, WIDTH), BF),
        (1e9, 5e6),
        grid=(8,),
        in_specs=[slot_spec, whole((32, 128)), whole((32, 128)), whole((128, WIDTH))],
        out_specs=whole((128, WIDTH)),
        scratch_shapes=[pltpu.VMEM((128, WIDTH), F32)],
    )(ys, rank, gate, mid)

    dq, dkv = call(
        kernel_attend_back,
        (sds((2048, 128), F32), sds((4, 2, 8, 64, 128), BF)),
        (2e10, 7e6),
        grid=(8,),
        in_specs=[
            SM,
            whole((4096, 128)),
            whole((128, 4096)),
            row_spec,
            msg_spec,
            log_spec,
            row_spec,
        ],
        out_specs=(row_spec, whole((4, 2, 8, 64, 128))),
        scratch_shapes=[pltpu.VMEM((4096, 128), F32)],
    )(mine_ref, keys, turned, queries, grad_heads, log_total, o_rows)
    dkv = exchange(dkv.reshape(4, 1024, 128), ("y",))

    block = 4 * jnp.arange(8, dtype=jnp.int32)[:, None] + mine
    quarter_pos = jnp.concatenate(
        [
            (block * 64 + offset[None, :]).reshape(-1),
            ((63 - block) * 64 + offset[None, :]).reshape(-1),
        ]
    )
    column = jnp.arange(128, dtype=jnp.int32)
    angle = angles(quarter_pos, column % 32)
    sign = jnp.where(column % 64 < 32, -1.0, 1.0)
    cos_heads = jnp.where(column >= 64, 1.0, jnp.cos(angle))
    sin_heads = jnp.where(column >= 64, 0.0, jnp.sin(angle) * sign)
    back = call(
        kernel_slices_back,
        sds((8, 4, 64, 128), BF),
        (4e8, 5e6),
        in_specs=[VM] * 5,
        out_specs=VM,
    )(dkv, dq.reshape(2, 8, 2, 64, 128), cos_heads, sin_heads, head_table)
    back = exchange(back.reshape(32, 64, 128), HEAD_AXES + FSDP)

    da_part = lax.dynamic_slice_in_dim(da_all, part_index * 256, 256, axis=1)
    grads, dh = call(
        kernel_project_back,
        (sds((WIDTH, 896), BF), sds((512, WIDTH), BF)),
        (1.5e9, 8e6),
        in_specs=[VM] * 8,
        out_specs=(VM, VM),
        scratch_shapes=[pltpu.VMEM((512, 512), BF)],
    )(back, x_all, hidden, w_slice, gains, gain_ffn_part, o_all, da_part)
    dh = lax.psum_scatter(dh, FSDP, scatter_dimension=0, tiled=True)
    grads = exchange(grads.reshape(128, 8, 896), ALL)
    grad_qkv, grad_out, grad_gains = call(
        kernel_total,
        (sds((8, 2048), F32), sds((8, WIDTH), F32), sds((8, 128), F32)),
        (1e8, 4e6),
        grid=(4,),
        in_specs=[pl.BlockSpec((8, 4, 8, 896), lambda t: (t, 0, 0, 0)), whole((512, 512))],
        out_specs=(whole((8, 2048)), whole((8, WIDTH)), whole((8, 128))),
        scratch_shapes=[pltpu.VMEM((4, 8, 896), F32)],
    )(grads.reshape(32, 4, 8, 896), slice_table)
    input_grad = call(
        kernel_input_grad,
        sds((128, WIDTH), F32),
        (1e6, 2e6),
        in_specs=[VM] * 4,
        out_specs=VM,
    )(dh, x, dmid, gains)
    return (
        layer_output.reshape(layer_input.shape),
        input_grad.reshape(layer_input.shape),
        grad_gains[:, 0],
        grad_qkv,
        grad_out,
        grad_gains[:, 1],
        expert_own[0:256, 0:512][None],
        expert_own[0:256, 512:1024][None],
        expert_own[256:384][None],
    )


def solution(mesh):
    parts = Mesh(mesh.devices.reshape(4, 2, 4, 2, 2), ALL)
    tokens = P(FSDP, CTX, None, None, None, None)
    experts = P(CTX, FSDP, None)
    in_specs = (
        tokens,
        tokens,
        tokens,
        tokens,
        P(ALL),
        P(ALL, None),
        P(ALL, None),
        P(ALL),
        experts,
        experts,
        experts,
    )
    out_specs = (
        tokens,
        tokens,
        P(ALL),
        P(ALL, None),
        P(ALL, None),
        P(ALL),
        experts,
        experts,
        experts,
    )
    return jax.shard_map(
        on_device, mesh=parts, in_specs=in_specs, out_specs=out_specs, check_vma=False
    )
```

```python
import functools

import jax
import jax.numpy as jnp
import numpy as np
from jax import lax
from jax.experimental import pallas as pl
from jax.experimental.pallas import tpu as pltpu
from jax.sharding import Mesh
from jax.sharding import PartitionSpec as P

WIDTH = 1024
EPSILON = 1e-06
ROPE_BASE = 10000.0
MASKED = -1e30
BF = jnp.bfloat16
F32 = jnp.float32
CTX = ("x", "zh", "y")
HEAD_AXES = ("x", "zh")
FSDP = ("zl", "core")
ALL = CTX + FSDP
VMEM_LIMIT = 56 * 1024 * 1024

NT = (((1,), (1,)), ((), ()))
TN = (((0,), (0,)), ((), ()))


def mm(a, b, dims=None):
    if dims is None:
        return jnp.dot(a, b, preferred_element_type=F32)
    return lax.dot_general(a, b, dims, preferred_element_type=F32)


def lane(shape):
    return lax.broadcasted_iota(jnp.int32, shape, len(shape) - 1)


def row(shape):
    return lax.broadcasted_iota(jnp.int32, shape, len(shape) - 2)


def call(kernel, out_shape, cost, **kw):
    flops, bytes_accessed = cost
    return pl.pallas_call(
        kernel,
        out_shape=out_shape,
        compiler_params=pltpu.CompilerParams(vmem_limit_bytes=VMEM_LIMIT),
        cost_estimate=pl.CostEstimate(
            flops=int(flops), bytes_accessed=int(bytes_accessed), transcendentals=0
        ),
        **kw,
    )


def sds(shape, dtype):
    return jax.ShapeDtypeStruct(shape, dtype)


VM = pl.BlockSpec(memory_space=pltpu.VMEM)
SM = pl.BlockSpec(memory_space=pltpu.SMEM)


def slice_matrix():
    table = np.zeros((512, 512), np.float32)
    for k in range(512):
        section, place = k // 128, k % 128
        if section < 2:
            pair, part = section, place // 64
        else:
            pair, part = place // 64, section
        feat = place % 64
        f = (feat % 32) // 8
        column = pair * 64 + part * 16 + (feat // 32) * 8 + feat % 8
        table[k, f * 128 + column] = 1.0
    return table


def head_matrix():
    table = np.zeros((4, 128, 768), np.float32)
    for f in range(4):
        for block in range(2):
            for part in range(4):
                for j in range(16):
                    feat = (j // 8) * 32 + 8 * f + j % 8
                    source = block * 64 + part * 16 + j
                    if part == 2:
                        target = block * 128 + feat
                    elif part == 3:
                        target = block * 128 + 64 + feat
                    else:
                        target = 256 + block * 256 + part * 128 + feat
                    table[f, source, target] = 1.0
    return table


def place(part_ref, r, size):
    return pl.ds(pl.multiple_of(lax.bitwise_xor(part_ref[0], r) * size, size), size)


def kernel_route(picks_ref, gates_ref, rank_ref, gate_ref):
    experts = row((32, 128))
    gate = jnp.zeros((32, 128), F32)
    chosen = jnp.zeros((32, 128), F32)
    for k in range(8):
        hit = picks_ref[k : k + 1, :] == experts
        gate = gate + jnp.where(hit, gates_ref[k : k + 1, :], 0.0)
        chosen = chosen + jnp.where(hit, 1.0, 0.0)
    before = jnp.where(row((128, 128)) < lane((128, 128)), 1.0, 0.0).astype(BF)
    rank = mm(chosen.astype(BF), before)
    rank_ref[...] = jnp.where(chosen > 0.5, rank, -1.0)
    gate_ref[...] = gate


def kernel_slices(w_ref, gains_ref, table_ref, gate_ref, out_weight_ref, out_ref):
    w = w_ref[...].astype(BF).astype(F32)
    parts = []
    for p in range(4):
        parts.append(
            jnp.concatenate(
                [
                    w[:, 256 * p : 256 * p + 256],
                    w[:, 1024 + 128 * p : 1152 + 128 * p],
                    w[:, 1536 + 128 * p : 1664 + 128 * p],
                ],
                axis=1,
            )
        )
    stacked = jnp.concatenate(parts, axis=0).astype(BF)
    cut = mm(stacked, table_ref[...])
    columns = []
    for f in range(4):
        columns.append(
            jnp.concatenate(
                [cut[8 * p : 8 * p + 8, 128 * f : 128 * f + 128] for p in range(4)], axis=1
            ).astype(BF)
        )
    gains = gains_ref[...]
    left = lane((8, 128)) < 64
    sub = row((8, 128))
    for c in range(32):
        gate = gate_ref[c : c + 1, :]
        high = gate.astype(BF).astype(F32)
        middle = (gate - high).astype(BF).astype(F32)
        rest = gate - high - middle
        parts = jnp.where(
            sub < 2, high, jnp.where(sub < 4, middle, jnp.where(sub < 6, rest, 0.0))
        )
        parts = jnp.where(sub % 2 == 0, pltpu.roll(parts, 64, 1), parts)
        last = jnp.where(left, gains, parts).astype(BF)
        for f in range(4):
            out_ref[c, f, :, 0:512] = columns[f]
            out_ref[c, f, :, 512:640] = last
            out_ref[c, f, :, 640:896] = out_weight_ref[:, 256 * f : 256 * f + 256].astype(BF)


def kernel_picks(rank_ref, gate_ref, pick_ref, turned_ref, high_ref, rest_ref):
    slot = lax.broadcasted_iota(jnp.int32, (64, 128), 0).astype(F32)
    for p in range(16):
        picks, weights = [], []
        for e in (2 * p, 2 * p + 1):
            hit = slot == rank_ref[e : e + 1, :]
            picks.append(jnp.where(hit, 1.0, 0.0))
            weights.append(jnp.where(hit, gate_ref[e : e + 1, :], 0.0))
        picks = jnp.concatenate(picks, axis=0)
        weights = jnp.transpose(jnp.concatenate(weights, axis=0))
        at = slice(128 * p, 128 * p + 128)
        pick_ref[at, :] = picks.astype(BF)
        turned_ref[:, at] = jnp.transpose(picks).astype(BF)
        high = weights.astype(BF)
        high_ref[:, at] = high
        rest_ref[:, at] = (weights - high.astype(F32)).astype(BF)


def kernel_project(
    part_ref, x0_ref, x1_ref, x2_ref, x3_ref, w_ref, cos_ref, sin_ref, msg_ref, hidden_ref, gains_ref
):
    gains = jnp.transpose(w_ref[:, 512:640].astype(F32))
    gains_ref[...] = gains[:8]
    for r, x_ref in enumerate((x0_ref, x1_ref, x2_ref, x3_ref)):
        x = x_ref[...].astype(F32)
        scale = lax.rsqrt(jnp.mean(x * x, axis=-1, keepdims=True) + EPSILON)
        hidden_ref[place(part_ref, r, 128), :] = (x * scale * gains[0:1]).astype(BF)
    proj = mm(hidden_ref[...], w_ref[:, 0:512])
    ahead = pltpu.roll(proj, 512 - 8, 1)
    behind = pltpu.roll(proj, 8, 1)
    partner = jnp.where((lane((512, 512)) // 8) % 2 == 0, ahead, behind)
    cos = jnp.concatenate([cos_ref[...]] * 4, axis=0)
    sin = jnp.concatenate([sin_ref[...]] * 4, axis=0)
    turned = proj * cos + partner * sin
    low = lane((64, 128)) < 64
    for s in range(4):
        for p in range(4):
            front = turned[128 * s : 128 * s + 64, 128 * p : 128 * p + 128]
            back = turned[128 * s + 64 : 128 * s + 128, 128 * p : 128 * p + 128]
            msg_ref[8 * p + s] = jnp.where(low, front, pltpu.roll(back, 64, 1)).astype(BF)
            msg_ref[8 * p + 4 + s] = jnp.where(low, pltpu.roll(front, 64, 1), back).astype(BF)


def kernel_heads(msg_ref, table_ref, kv_ref, q_ref):
    out = jnp.zeros((512, 768), F32)
    for f in range(4):
        out = out + mm(msg_ref[:, f].reshape(512, 128), table_ref[f])
    pairs = out[:, 0:256].astype(BF)
    for half in range(2):
        block = pairs[:, 128 * half : 128 * half + 128]
        for y in range(4):
            kv_ref[y, 512 * half : 512 * half + 512, :] = block
    queries = (out[:, 256:768] * 0.125).astype(BF)
    for half in range(2):
        for head in range(2):
            at = 256 * half + 128 * head
            q_ref[half, :, head] = queries[:, at : at + 128].reshape(8, 64, 128)


def tile_positions(tile, mine):
    front = tile < 4
    i = jnp.where(front, tile, tile - 4)
    q = lane((1, 256))
    k = row((512, 1))
    k = lax.broadcasted_iota(jnp.int32, (512, 1), 0)
    q_front = (8 * i + 4 * (q // 128) + mine) * 64 + q % 64
    q_back = (63 - 8 * i - 4 * (q // 128) - mine) * 64 + q % 64
    k_front = 512 * i + k
    k_back = (59 - 8 * i + 4 * (k // 256) - (k % 256) // 64) * 64 + k % 64
    count = jnp.where(front, i + 1, 8 - i)
    return jnp.where(front, q_front, q_back), jnp.where(front, k_front, k_back), count


def kernel_attend(mine_ref, kv_ref, q_ref, msg_ref, log_ref, out_ref, keys_ref, turned_ref):
    tile = pl.program_id(0)

    @pl.when(tile == 0)
    def _():
        for group in range(16):
            half, place = (0, group) if group < 8 else (1, 15 - group)
            for y in range(4):
                at = 256 * group + 64 * y
                keys_ref[at : at + 64, :] = kv_ref[y, half, place]
        for c in range(8):
            turned_ref[:, 512 * c : 512 * c + 512] = jnp.transpose(
                keys_ref[512 * c : 512 * c + 512, :].astype(F32)
            ).astype(BF)

    q = q_ref[...]
    q_pos, k_pos, count = tile_positions(tile, mine_ref[0])

    def step(c, carry, last):
        peak, total, mixed = carry
        at = pl.multiple_of(c * 512, 512)
        scores = mm(keys_ref[pl.ds(at, 512), :], q, NT)
        if last:
            scores = jnp.where(k_pos <= q_pos, scores, MASKED)
        higher = jnp.maximum(peak, jnp.max(scores, axis=0, keepdims=True))
        weights = jnp.exp(scores - higher)
        fade = jnp.exp(peak - higher)
        total = total * fade + jnp.sum(weights, axis=0, keepdims=True)
        mixed = mixed * fade + mm(turned_ref[64:128, pl.ds(at, 512)], weights.astype(BF))
        return higher, total, mixed

    start = (
        jnp.full((1, 256), MASKED, F32),
        jnp.zeros((1, 256), F32),
        jnp.zeros((64, 256), F32),
    )
    carry = lax.fori_loop(0, count - 1, lambda c, v: step(c, v, False), start)
    peak, total, mixed = step(count - 1, carry, True)
    log_ref[0] = jnp.broadcast_to(peak + jnp.log(total), (8, 256))
    mixed = mixed / total
    out = jnp.transpose(jnp.concatenate([jnp.zeros((64, 256), F32), mixed], axis=0))
    out_ref[...] = out
    low = lane((64, 128)) < 64
    for a in range(2):
        first = out[128 * a : 128 * a + 64]
        second = out[128 * a + 64 : 128 * a + 128]
        msg_ref[a, 0] = jnp.where(low, pltpu.roll(first, 64, 1), second).astype(BF)


def kernel_attend_back(
    mine_ref, keys_ref, turned_ref, q_ref, grad_ref, log_ref, out_ref, dq_ref, dkv_ref, sum_ref
):
    tile = pl.program_id(0)

    @pl.when(tile == 0)
    def _():
        sum_ref[...] = jnp.zeros_like(sum_ref)

    q = q_ref[...]
    low = lane((64, 128)) < 64
    pieces = []
    for a in range(2):
        both = grad_ref[a, 0].astype(F32)
        pieces.append(jnp.where(low, 0.0, pltpu.roll(both, 64, 1)))
        pieces.append(jnp.where(low, 0.0, both))
    grad = jnp.concatenate(pieces, axis=0)
    delta = jnp.sum(jnp.transpose(grad * out_ref[...]), axis=0, keepdims=True)
    grad = grad.astype(BF)
    q_pos, k_pos, count = tile_positions(tile, mine_ref[0])
    log_total = log_ref[0][0:1]

    def step(c, dq, last):
        at = pl.multiple_of(c * 512, 512)
        keys = keys_ref[pl.ds(at, 512), :]
        scores = mm(keys, q, NT)
        if last:
            scores = jnp.where(k_pos <= q_pos, scores, MASKED)
        weights = jnp.exp(scores - log_total)
        slope = (weights * (mm(keys, grad, NT) - delta)).astype(BF)
        sum_ref[pl.ds(at, 512), :] += mm(slope, q) + mm(weights.astype(BF), grad)
        return dq + mm(turned_ref[0:64, pl.ds(at, 512)], slope)

    dq = lax.fori_loop(0, count - 1, lambda c, v: step(c, v, False), jnp.zeros((64, 256), F32))
    dq = step(count - 1, dq, True)
    dq_ref[...] = jnp.transpose(jnp.concatenate([dq * 0.125, jnp.zeros((64, 256), F32)], axis=0))

    @pl.when(tile == 7)
    def _():
        for group in range(16):
            half, place = (0, group) if group < 8 else (1, 15 - group)
            for y in range(4):
                at = 256 * group + 64 * y
                dkv_ref[y, half, place] = sum_ref[at : at + 64, :].astype(BF)


def kernel_middle(
    part_ref,
    o_ref,
    u0_ref,
    u1_ref,
    u2_ref,
    u3_ref,
    l0_ref,
    l1_ref,
    l2_ref,
    l3_ref,
    x_ref,
    gains_ref,
    pick_ref,
    slots_ref,
    mid_ref,
    rows_ref,
    hidden_ref,
):
    @pl.when(pl.program_id(0) == 0)
    def _():
        for g in range(8):
            rows_ref[:, 128 * g : 128 * g + 128] = o_ref[g].reshape(128, 128)
        uppers = (u0_ref, u1_ref, u2_ref, u3_ref)
        lowers = (l0_ref, l1_ref, l2_ref, l3_ref)
        for r in range(4):
            at = place(part_ref, r, 256)
            mid_ref[:, at] = (
                x_ref[:, at].astype(F32)
                + mm(rows_ref[:, 0:512], uppers[r][...])
                + mm(rows_ref[:, 512:1024], lowers[r][...])
            )
        mid = mid_ref[...]
        scale = lax.rsqrt(jnp.mean(mid * mid, axis=-1, keepdims=True) + EPSILON)
        hidden_ref[...] = (mid * scale * gains_ref[1:2]).astype(BF)

    slots_ref[...] = mm(pick_ref[...], hidden_ref[...]).astype(BF).reshape(4, 64, WIDTH)


def kernel_experts_ready(
    part_ref,
    dy_ref,
    parts_ref,
    v0_ref,
    v1_ref,
    v2_ref,
    v3_ref,
    w0_ref,
    w1_ref,
    w2_ref,
    w3_ref,
    dys_ref,
    dact_ref,
    v_ref,
    gu_ref,
    rank_ref,
    gate_ref,
):
    step = pl.program_id(0)

    @pl.when(step == 0)
    def _():
        for r, w_ref in enumerate((v0_ref, v1_ref, v2_ref, v3_ref)):
            v_ref[place(part_ref, r, 128), :] = w_ref[...]
        for r, w_ref in enumerate((w0_ref, w1_ref, w2_ref, w3_ref)):
            gu_ref[place(part_ref, r, 256), :] = w_ref[...]
        before = jnp.where(row((128, 128)) < lane((128, 128)), 1.0, 0.0).astype(BF)
        parts = [parts_ref[:, k, :].astype(F32) for k in range(6)]
        even = parts[0] + parts[2] + parts[4]
        odd = parts[1] + parts[3] + parts[5]
        gate_ref[...] = jnp.where(lane((32, 128)) < 64, pltpu.roll(even, 64, 1), odd)
        chosen = gate_ref[...] > 0.0
        rank = mm(jnp.where(chosen, 1.0, 0.0).astype(BF), before)
        rank_ref[...] = jnp.where(chosen, rank, -1.0)

    slot = lax.broadcasted_iota(jnp.int32, (64, 128), 0).astype(F32)
    grads = []
    for j in range(4):
        source = 4 * step + j
        pick = slot == rank_ref[pl.ds(source, 1), :]
        weight = jnp.sum(
            jnp.where(pick, gate_ref[pl.ds(source, 1), :], 0.0), axis=1, keepdims=True
        )
        rows = mm(jnp.where(pick, 1.0, 0.0).astype(BF), dy_ref[j])
        grads.append((rows * weight).astype(BF))
    dys = jnp.concatenate(grads, axis=0)
    dys_ref[...] = dys.reshape(4, 64, WIDTH)
    dact_ref[...] = mm(dys, v_ref[...], NT)


def kernel_experts(h_ref, gu_ref, dact_ref, act_ref, dboth_ref, dxs_ref):
    both = mm(h_ref[...].reshape(256, WIDTH), gu_ref[...])
    gate_h, up_h = both[:, :512], both[:, 512:]
    sig = jax.nn.sigmoid(gate_h)
    swished = gate_h * sig
    act_ref[...] = (swished * up_h).astype(BF)
    dact = dact_ref[...]
    dgate = (dact * up_h * sig * (1.0 + gate_h * (1.0 - sig))).astype(BF)
    dup = (dact * swished).astype(BF)
    dboth = jnp.concatenate([dgate, dup], axis=1)
    dboth_ref[...] = dboth
    dxs_ref[...] = mm(dboth, gu_ref[...], NT).astype(BF).reshape(4, 64, WIDTH)


def kernel_experts_after(
    h_ref, act_ref, dys_ref, dboth_ref, v_ref, ys_ref, grad_ref, ggu_ref, gv_ref
):
    step = pl.program_id(0)

    @pl.when(step == 0)
    def _():
        ggu_ref[...] = jnp.zeros_like(ggu_ref)
        gv_ref[...] = jnp.zeros_like(gv_ref)

    act = act_ref[...]
    ys_ref[...] = mm(act, v_ref[...]).astype(BF).reshape(4, 64, WIDTH)
    ggu_ref[...] += mm(h_ref[...].reshape(256, WIDTH), dboth_ref[...], TN)
    gv_ref[...] += mm(act, dys_ref[...].reshape(256, WIDTH), TN)

    @pl.when(step == 7)
    def _():
        for f in range(4):
            grad_ref[f, 0:256, :] = ggu_ref[256 * f : 256 * f + 256, :].astype(BF)
            grad_ref[f, 256:384, :] = gv_ref[128 * f : 128 * f + 128, :].astype(BF)


def kernel_middle_back(
    part_ref,
    dxs_ref,
    pick_ref,
    mid_ref,
    cot_ref,
    gains_ref,
    u0_ref,
    u1_ref,
    u2_ref,
    u3_ref,
    l0_ref,
    l1_ref,
    l2_ref,
    l3_ref,
    dmid_ref,
    parts_ref,
    msg_ref,
    ggain_ref,
    sum_ref,
    low_ref,
):
    step = pl.program_id(0)
    part = mm(pick_ref[...], dxs_ref[...].reshape(512, WIDTH))

    @pl.when(step == 0)
    def _():
        sum_ref[...] = part

    @pl.when(step > 0)
    def _():
        sum_ref[...] += part

    @pl.when(step == 3)
    def _():
        mid = mid_ref[...]
        scale = lax.rsqrt(jnp.mean(mid * mid, axis=-1, keepdims=True) + EPSILON)
        dh = sum_ref[...]
        ggain_ref[...] = jnp.broadcast_to(
            jnp.sum(dh * (mid * scale), axis=0, keepdims=True), (8, WIDTH)
        )
        dn = dh * gains_ref[1:2]
        dmid = (
            cot_ref[...].astype(F32)
            + scale * dn
            - mid * (scale * scale * scale) * jnp.mean(dn * mid, axis=-1, keepdims=True)
        )
        dmid_ref[...] = dmid
        low_ref[...] = dmid.astype(BF)
        uppers = (u0_ref, u1_ref, u2_ref, u3_ref)
        lowers = (l0_ref, l1_ref, l2_ref, l3_ref)
        for r in range(4):
            parts_ref[r] = low_ref[:, place(part_ref, r, 256)]
        for h, w_refs in enumerate((uppers, lowers)):
            grad = mm(parts_ref[0], w_refs[0][...], NT)
            for r in range(1, 4):
                grad = grad + mm(parts_ref[r], w_refs[r][...], NT)
            grad = grad.astype(BF)
            for g in range(4):
                msg_ref[4 * h + g] = grad[:, 128 * g : 128 * g + 128].reshape(2, 64, 128)


def kernel_out_weight(
    o0_ref, o1_ref, o2_ref, o3_ref, da0_ref, da1_ref, da2_ref, da3_ref, gain_ref, grad_ref
):
    which = lax.broadcasted_iota(jnp.int32, (128, WIDTH), 0)
    grad_ref[:, 0:128] = jnp.transpose(jnp.where(which == 1, gain_ref[0:1], 0.0)).astype(BF)
    pairs = ((o0_ref, da0_ref), (o1_ref, da1_ref), (o2_ref, da2_ref), (o3_ref, da3_ref))
    for g in range(8):
        part = jnp.zeros((128, 256), F32)
        for o_ref, da_ref in pairs:
            part = part + mm(o_ref[g].reshape(128, 128), da_ref[...], TN)
        grad_ref[128 * g : 128 * g + 128, 128:384] = part.astype(BF)


def kernel_slices_back(dkv_ref, dq_ref, cos_ref, sin_ref, table_ref, msg_ref):
    def unrotate(w, cos, sin):
        partner = jnp.where(
            lane(w.shape) % 64 < 32, pltpu.roll(w, 96, 1), pltpu.roll(w, 32, 1)
        )
        return (w * cos - partner * sin).astype(BF)

    parts = []
    for half in range(2):
        at = slice(512 * half, 512 * half + 512)
        parts.append(unrotate(dkv_ref[at, :].astype(F32), cos_ref[at, :], sin_ref[at, :]))
    for half in range(2):
        at = slice(512 * half, 512 * half + 512)
        for head in range(2):
            parts.append(
                unrotate(dq_ref[half, :, head].reshape(512, 128), cos_ref[at, :], sin_ref[at, :])
            )
    whole = jnp.concatenate(parts, axis=1)
    for f in range(4):
        msg_ref[:, f] = mm(whole, table_ref[f], NT).astype(BF).reshape(8, 64, 128)


def kernel_hidden_grad(part_ref, d_ref, w_ref, h0_ref, h1_ref, h2_ref, h3_ref):
    for r, h_ref in enumerate((h0_ref, h1_ref, h2_ref, h3_ref)):
        h_ref[...] = mm(d_ref[place(part_ref, r, 128), :], w_ref[:, 0:512], NT).astype(BF)


def kernel_grads(msg_ref, hidden_ref, w_ref, rest_ref, grads_ref, d_ref):
    low = lane((64, 128)) < 64
    for s in range(4):
        for p in range(4):
            even = msg_ref[8 * p + s].astype(F32)
            odd = msg_ref[8 * p + 4 + s].astype(F32)
            d_ref[128 * s : 128 * s + 64, 128 * p : 128 * p + 128] = jnp.where(
                low, even, pltpu.roll(odd, 64, 1)
            ).astype(BF)
            d_ref[128 * s + 64 : 128 * s + 128, 128 * p : 128 * p + 128] = jnp.where(
                low, pltpu.roll(even, 64, 1), odd
            ).astype(BF)
    total = mm(hidden_ref[...], d_ref[...], TN)
    grads_ref[:, 0:512] = total.astype(BF)
    gain = jnp.sum(total * w_ref[:, 0:512].astype(F32), axis=1, keepdims=True)
    gain = gain / w_ref[:, 512:640].astype(F32)[:, 0:1]
    rest = rest_ref[:, 0:128]
    grads_ref[:, 512:640] = jnp.where(lane((WIDTH, 128)) == 0, gain.astype(BF), rest)
    grads_ref[:, 640:896] = rest_ref[:, 128:384]


def kernel_input_grad(d0_ref, d1_ref, d2_ref, d3_ref, x_ref, dmid_ref, gains_ref, out_ref):
    dh = d0_ref[...].astype(F32)
    for d_ref in (d1_ref, d2_ref, d3_ref):
        dh = dh + d_ref[...].astype(F32)
    x = x_ref[...].astype(F32)
    scale = lax.rsqrt(jnp.mean(x * x, axis=-1, keepdims=True) + EPSILON)
    dn = dh * gains_ref[0:1]
    out_ref[...] = (
        dmid_ref[...]
        + scale * dn
        - x * (scale * scale * scale) * jnp.mean(dn * x, axis=-1, keepdims=True)
    )


def kernel_total(parts_ref, table_ref, qkv_ref, out_ref, gains_ref, sum_ref):
    step = pl.program_id(0)

    @pl.when(step == 0)
    def _():
        sum_ref[...] = jnp.zeros_like(sum_ref)

    sum_ref[...] += jnp.sum(parts_ref[...].astype(F32), axis=0)

    @pl.when(step == 3)
    def _():
        rows = []
        for p in range(4):
            rows.append(
                jnp.concatenate(
                    [sum_ref[f, :, 128 * p : 128 * p + 128] for f in range(4)], axis=1
                )
            )
        rest = jnp.concatenate(rows, axis=0)
        whole = jnp.zeros((32, 512), F32)
        for _ in range(3):
            part = rest.astype(BF)
            rest = rest - part.astype(F32)
            whole = whole + mm(part, table_ref[...], NT)
        for p in range(4):
            piece = whole[8 * p : 8 * p + 8]
            qkv_ref[:, 256 * p : 256 * p + 256] = piece[:, 0:256]
            qkv_ref[:, 1024 + 128 * p : 1152 + 128 * p] = piece[:, 256:384]
            qkv_ref[:, 1536 + 128 * p : 1664 + 128 * p] = piece[:, 384:512]
        for f in range(4):
            out_ref[:, 256 * f : 256 * f + 256] = sum_ref[f, :, 640:896]
        gains_ref[...] = (
            sum_ref[0, :, 512:640]
            + sum_ref[1, :, 512:640]
            + sum_ref[2, :, 512:640]
            + sum_ref[3, :, 512:640]
        )


def kernel_output(ys_ref, high_ref, rest_ref, mid_ref, out_ref, sum_ref):
    step = pl.program_id(0)

    @pl.when(step == 0)
    def _():
        sum_ref[...] = mid_ref[...]

    ys = ys_ref[...].reshape(512, WIDTH)
    sum_ref[...] += mm(high_ref[...], ys) + mm(rest_ref[...], ys)

    @pl.when(step == 3)
    def _():
        out_ref[...] = sum_ref[...].astype(BF)


def angles(positions, features):
    frequency = ROPE_BASE ** (-(features.astype(F32) * 2.0 / 64))
    return positions.astype(F32)[:, None] * frequency[None, :]


def whole(shape):
    return pl.BlockSpec(shape, lambda t: (0,) * len(shape))


def exchange(value, axes):
    return lax.all_to_all(value, axes, split_axis=0, concat_axis=0, tiled=True)


def gather(value, axes):
    return lax.all_gather(value, axes, axis=0, tiled=True)


def after(value, marker):
    return lax.optimization_barrier((value, marker))[0]


def swap(value, axis):
    return lax.ppermute(value, axis, [(0, 1), (1, 0)])


def neighbours(value):
    return value, swap(value, "core"), swap(value, "zl")


def cross(parts):
    here = [parts[0]]
    for r in range(1, 4):
        here.append(lax.ppermute(parts[r], FSDP, [(f, f ^ r) for f in range(4)]))
    return here


def on_device(
    layer_input,
    routes,
    gates,
    cotangent,
    norm_attn,
    query_key_value_weight,
    output_weight,
    norm_ffn,
    exp_gate,
    exp_up,
    exp_down,
):
    mine = lax.axis_index("y")
    ctx_index = lax.axis_index(CTX)
    part_index = lax.axis_index(FSDP)
    mine_ref = mine.astype(jnp.int32).reshape(1)
    part_ref = part_index.astype(jnp.int32).reshape(1)
    x = layer_input.reshape(128, WIDTH)
    cot = cotangent.reshape(128, WIDTH)
    slice_table = jnp.asarray(slice_matrix(), BF)
    head_table = jnp.asarray(head_matrix(), BF)

    cot_all = gather(cot, CTX)
    x_all = neighbours(x)
    rank, gate = call(
        kernel_route,
        (sds((32, 128), F32), sds((32, 128), F32)),
        (1e6, 1e5),
        in_specs=[VM, VM],
        out_specs=(VM, VM),
    )(routes.reshape(128, 8).T, gates.reshape(128, 8).T)
    which = lax.broadcasted_iota(jnp.int32, (8, 128), 1)
    gain_rows = jnp.where(
        which == 0, norm_attn[:, None], jnp.where(which == 1, norm_ffn[:, None], 0.0)
    )
    slices = call(
        kernel_slices,
        sds((32, 4, 8, 896), BF),
        (2e7, 3e6),
        in_specs=[VM] * 5,
        out_specs=VM,
    )(query_key_value_weight, gain_rows, slice_table, gate, output_weight)
    slices, rank, gate, x_all = lax.optimization_barrier((slices, rank, gate, x_all))
    x_all = x_all + (swap(x_all[2], "core"),)
    w_slice = exchange(slices.reshape(128, 8, 896), ALL)
    gate_parts = lax.dynamic_slice(
        w_slice.reshape(32, 4, 8, 896), (0, part_index, 0, 512), (32, 1, 8, 128)
    ).reshape(32, 8, 128)
    w_slice = w_slice.reshape(WIDTH, 896)
    picks, picks_turned, picks_high, picks_rest = call(
        kernel_picks,
        (sds((2048, 128), BF),) + (sds((128, 2048), BF),) * 3,
        (2e9, 4e6),
        in_specs=[VM, VM],
        out_specs=(VM,) * 4,
    )(rank, gate)

    offset = jnp.arange(64, dtype=jnp.int32)
    token_pos = jnp.concatenate([ctx_index * 64 + offset, (63 - ctx_index) * 64 + offset])
    column = jnp.arange(512, dtype=jnp.int32)
    angle = angles(token_pos, 8 * part_index + column % 8)
    is_value = (column // 16) % 4 == 3
    sign = jnp.where((column // 8) % 2 == 0, -1.0, 1.0)
    cos_slice = jnp.where(is_value, 1.0, jnp.cos(angle))
    sin_slice = jnp.where(is_value, 0.0, jnp.sin(angle) * sign)
    msg, hidden, gains = call(
        kernel_project,
        (sds((32, 64, 128), BF), sds((512, WIDTH), BF), sds((8, WIDTH), F32)),
        (6e8, 4e6),
        in_specs=[SM] + [VM] * 7,
        out_specs=(VM, VM, VM),
    )(part_ref, *x_all, w_slice, cos_slice, sin_slice)
    out_upper = neighbours(w_slice[0:512, 640:896])
    msg = exchange(msg, HEAD_AXES + FSDP)

    kv_copies, queries = call(
        kernel_heads,
        (sds((4, 1024, 128), BF), sds((2, 8, 2, 64, 128), BF)),
        (4e8, 3e6),
        in_specs=[VM, VM],
        out_specs=(VM, VM),
    )(msg.reshape(8, 4, 64, 128), head_table)
    queries = queries.reshape(2048, 128)
    kv_copies, out_upper = lax.optimization_barrier((kv_copies, out_upper))
    out_lower = neighbours(after(w_slice[512:1024, 640:896], msg))
    kv = exchange(kv_copies, ("y",)).reshape(4, 2, 8, 64, 128)
    block = 4 * jnp.arange(8, dtype=jnp.int32)[:, None] + mine
    quarter_pos = jnp.concatenate(
        [
            (block * 64 + offset[None, :]).reshape(-1),
            ((63 - block) * 64 + offset[None, :]).reshape(-1),
        ]
    )
    column = jnp.arange(128, dtype=jnp.int32)
    angle = angles(quarter_pos, column % 32)
    sign = jnp.where(column % 64 < 32, -1.0, 1.0)
    cos_heads = jnp.where(column >= 64, 1.0, jnp.cos(angle))
    sin_heads = jnp.where(column >= 64, 0.0, jnp.sin(angle) * sign)
    kv, out_lower, cos_heads, sin_heads = lax.optimization_barrier(
        (kv, out_lower, cos_heads, sin_heads)
    )
    downs = neighbours(after(exp_down[0].astype(BF), kv))
    gate_ups = jnp.concatenate([exp_gate[0], exp_up[0]], axis=1).astype(BF)
    gate_ups = neighbours(after(gate_ups, kv))
    out_upper = out_upper + (swap(after(out_upper[2], kv), "core"),)
    out_lower = out_lower + (swap(out_lower[2], "core"),)
    w_out = (*out_upper, *out_lower)
    msg_spec = pl.BlockSpec((2, 1, 64, 128), lambda t: (t % 4, t // 4, 0, 0))
    row_spec = pl.BlockSpec((256, 128), lambda t: (t, 0))
    log_spec = pl.BlockSpec((1, 8, 256), lambda t: (t, 0, 0))
    o_msg, log_total, o_rows, keys, turned = call(
        kernel_attend,
        (
            sds((8, 2, 64, 128), BF),
            sds((8, 8, 256), F32),
            sds((2048, 128), F32),
            sds((4096, 128), BF),
            sds((128, 4096), BF),
        ),
        (1e10, 5e6),
        grid=(8,),
        in_specs=[SM, whole((4, 2, 8, 64, 128)), row_spec],
        out_specs=(msg_spec, log_spec, row_spec, whole((4096, 128)), whole((128, 4096))),
    )(mine_ref, kv, queries)
    o_msg, w_out, downs, gate_ups = lax.optimization_barrier((o_msg, w_out, downs, gate_ups))
    downs = downs + (swap(downs[2], "core"),)
    gate_ups = gate_ups + (swap(gate_ups[2], "core"),)
    o_heads = exchange(o_msg, HEAD_AXES)

    slot_spec = pl.BlockSpec((4, 64, WIDTH), lambda t: (t, 0, 0))
    out_specs = [whole((512, 256))] * 8
    slots, mid = call(
        kernel_middle,
        (sds((32, 64, WIDTH), BF), sds((128, WIDTH), F32)),
        (9e8, 8e6),
        grid=(8,),
        in_specs=[SM, whole((8, 2, 64, 128))]
        + out_specs
        + [
            whole((128, WIDTH)),
            whole((8, WIDTH)),
            pl.BlockSpec((256, 128), lambda t: (t, 0)),
        ],
        out_specs=(slot_spec, whole((128, WIDTH))),
        scratch_shapes=[pltpu.VMEM((128, WIDTH), BF), pltpu.VMEM((128, WIDTH), BF)],
    )(part_ref, o_heads, *w_out, x, gains, picks)
    cot_all = after(cot_all, mid)
    slots, downs, gate_ups = lax.optimization_barrier((slots, downs, gate_ups))
    o_all = neighbours(after(o_heads, mid))
    slots = exchange(slots, CTX)
    dys, dact, down, gate_up = call(
        kernel_experts_ready,
        (
            sds((32, 64, WIDTH), BF),
            sds((2048, 512), F32),
            sds((512, WIDTH), BF),
            sds((WIDTH, WIDTH), BF),
        ),
        (6e9, 2e7),
        grid=(8,),
        in_specs=[
            SM,
            pl.BlockSpec((4, 128, WIDTH), lambda t: (t, 0, 0)),
            whole((32, 8, 128)),
        ]
        + [whole((128, WIDTH))] * 4
        + [whole((256, WIDTH))] * 4,
        out_specs=(
            slot_spec,
            pl.BlockSpec((256, 512), lambda t: (t, 0)),
            whole((512, WIDTH)),
            whole((WIDTH, WIDTH)),
        ),
        scratch_shapes=[pltpu.VMEM((32, 128), F32), pltpu.VMEM((32, 128), F32)],
    )(part_ref, cot_all.reshape(32, 128, WIDTH), gate_parts, *downs, *gate_ups)
    act_spec = pl.BlockSpec((256, 512), lambda t: (t, 0))
    both_spec = pl.BlockSpec((256, WIDTH), lambda t: (t, 0))
    act, dboth, dxs = call(
        kernel_experts,
        (sds((2048, 512), BF), sds((2048, WIDTH), BF), sds((32, 64, WIDTH), BF)),
        (9e9, 2e7),
        grid=(8,),
        in_specs=[slot_spec, whole((WIDTH, WIDTH)), act_spec],
        out_specs=(act_spec, both_spec, slot_spec),
    )(slots, gate_up, dact)
    ys, expert_grads = call(
        kernel_experts_after,
        (sds((32, 64, WIDTH), BF), sds((4, 384, WIDTH), BF)),
        (9e9, 2e7),
        grid=(8,),
        in_specs=[slot_spec, act_spec, slot_spec, both_spec, whole((512, WIDTH))],
        out_specs=(slot_spec, whole((4, 384, WIDTH))),
        scratch_shapes=[pltpu.VMEM((WIDTH, WIDTH), F32), pltpu.VMEM((512, WIDTH), F32)],
    )(slots, act, dys, dboth, down)
    dxs, o_all = lax.optimization_barrier((dxs, o_all))
    o_all = o_all + (swap(o_all[2], "core"),)
    dxs = exchange(dxs, CTX)
    dxs, ys, expert_grads, o_all = lax.optimization_barrier((dxs, ys, expert_grads, o_all))

    dmid, da_parts, grad_msg, gain_ffn_part = call(
        kernel_middle_back,
        (
            sds((128, WIDTH), F32),
            sds((4, 128, 256), BF),
            sds((8, 2, 64, 128), BF),
            sds((8, WIDTH), F32),
        ),
        (9e8, 8e6),
        grid=(4,),
        in_specs=[
            SM,
            pl.BlockSpec((8, 64, WIDTH), lambda t: (t, 0, 0)),
            pl.BlockSpec((128, 512), lambda t: (0, t)),
            whole((128, WIDTH)),
            whole((128, WIDTH)),
            whole((8, WIDTH)),
        ]
        + out_specs,
        out_specs=(
            whole((128, WIDTH)),
            whole((4, 128, 256)),
            whole((8, 2, 64, 128)),
            whole((8, WIDTH)),
        ),
        scratch_shapes=[pltpu.VMEM((128, WIDTH), F32), pltpu.VMEM((128, WIDTH), BF)],
    )(part_ref, dxs, picks_turned, mid, cot, gains, *w_out)
    grad_heads = exchange(grad_msg, HEAD_AXES)
    ys, grad_heads = lax.optimization_barrier((ys, grad_heads))
    ys = exchange(ys, CTX)
    dq, dkv = call(
        kernel_attend_back,
        (sds((2048, 128), F32), sds((4, 2, 8, 64, 128), BF)),
        (2e10, 7e6),
        grid=(8,),
        in_specs=[
            SM,
            whole((4096, 128)),
            whole((128, 4096)),
            row_spec,
            msg_spec,
            log_spec,
            row_spec,
        ],
        out_specs=(row_spec, whole((4, 2, 8, 64, 128))),
        scratch_shapes=[pltpu.VMEM((4096, 128), F32)],
    )(mine_ref, keys, turned, queries, grad_heads, log_total, o_rows)
    da_here = cross(da_parts)
    dkv = lax.psum_scatter(
        dkv.reshape(4096, 128), ("y",), scatter_dimension=0, tiled=True
    )
    dkv, ys, da_here = lax.optimization_barrier((dkv, ys, da_here))
    expert_own = lax.psum_scatter(
        after(expert_grads, dkv).reshape(4 * 384, WIDTH), FSDP, scatter_dimension=0, tiled=True
    ).astype(F32)
    rest_part = call(
        kernel_out_weight,
        sds((WIDTH, 384), BF),
        (3e8, 2e6),
        in_specs=[VM] * 9,
        out_specs=VM,
    )(*o_all, *da_here, gain_ffn_part)
    layer_output = call(
        kernel_output,
        sds((128, WIDTH), BF),
        (1e9, 5e6),
        grid=(4,),
        in_specs=[
            pl.BlockSpec((8, 64, WIDTH), lambda t: (t, 0, 0)),
            pl.BlockSpec((128, 512), lambda t: (0, t)),
            pl.BlockSpec((128, 512), lambda t: (0, t)),
            whole((128, WIDTH)),
        ],
        out_specs=whole((128, WIDTH)),
        scratch_shapes=[pltpu.VMEM((128, WIDTH), F32)],
    )(ys, picks_high, picks_rest, mid)

    back = call(
        kernel_slices_back,
        sds((8, 4, 64, 128), BF),
        (4e8, 5e6),
        in_specs=[VM] * 5,
        out_specs=VM,
    )(dkv, dq.reshape(2, 8, 2, 64, 128), cos_heads, sin_heads, head_table)
    back = exchange(back.reshape(32, 64, 128), HEAD_AXES + FSDP)

    grads, d_all = call(
        kernel_grads,
        (sds((WIDTH, 896), BF), sds((512, 512), BF)),
        (6e8, 5e6),
        in_specs=[VM] * 4,
        out_specs=(VM, VM),
    )(back, hidden, w_slice, rest_part)
    dh_parts = call(
        kernel_hidden_grad,
        (sds((128, WIDTH), BF),) * 4,
        (6e8, 5e6),
        in_specs=[SM, VM, VM],
        out_specs=(VM,) * 4,
    )(part_ref, d_all, w_slice)
    dh_here = cross(dh_parts)
    input_grad = call(
        kernel_input_grad,
        sds((128, WIDTH), F32),
        (1e6, 2e6),
        in_specs=[VM] * 7,
        out_specs=VM,
    )(*dh_here, x, dmid, gains)
    grads = exchange(grads.reshape(128, 8, 896), ALL)
    grad_qkv, grad_out, grad_gains = call(
        kernel_total,
        (sds((8, 2048), F32), sds((8, WIDTH), F32), sds((8, 128), F32)),
        (1e8, 4e6),
        grid=(4,),
        in_specs=[pl.BlockSpec((8, 4, 8, 896), lambda t: (t, 0, 0, 0)), whole((512, 512))],
        out_specs=(whole((8, 2048)), whole((8, WIDTH)), whole((8, 128))),
        scratch_shapes=[pltpu.VMEM((4, 8, 896), F32)],
    )(grads.reshape(32, 4, 8, 896), slice_table)
    return (
        layer_output.reshape(layer_input.shape),
        input_grad.reshape(layer_input.shape),
        grad_gains[:, 0],
        grad_qkv,
        grad_out,
        grad_gains[:, 1],
        expert_own[0:256, 0:512][None],
        expert_own[0:256, 512:1024][None],
        expert_own[256:384][None],
    )


def solution(mesh):
    parts = Mesh(mesh.devices.reshape(4, 2, 4, 2, 2), ALL)
    tokens = P(FSDP, CTX, None, None, None, None)
    experts = P(CTX, FSDP, None)
    in_specs = (
        tokens,
        tokens,
        tokens,
        tokens,
        P(ALL),
        P(ALL, None),
        P(ALL, None),
        P(ALL),
        experts,
        experts,
        experts,
    )
    out_specs = (
        tokens,
        tokens,
        P(ALL),
        P(ALL, None),
        P(ALL, None),
        P(ALL),
        experts,
        experts,
        experts,
    )
    return jax.shard_map(
        on_device, mesh=parts, in_specs=in_specs, out_specs=out_specs, check_vma=False
    )
```

```python
import functools

import jax
import jax.numpy as jnp
import numpy as np
from jax import lax
from jax.experimental import pallas as pl
from jax.experimental.pallas import tpu as pltpu
from jax.sharding import Mesh
from jax.sharding import PartitionSpec as P

WIDTH = 1024
EPSILON = 1e-06
ROPE_BASE = 10000.0
MASKED = -1e30
BF = jnp.bfloat16
F32 = jnp.float32
CTX = ("x", "zh", "y")
HEAD_AXES = ("x", "zh")
FSDP = ("zl", "core")
ALL = CTX + FSDP
VMEM_LIMIT = 56 * 1024 * 1024

NT = (((1,), (1,)), ((), ()))
TN = (((0,), (0,)), ((), ()))


def mm(a, b, dims=None):
    if dims is None:
        return jnp.dot(a, b, preferred_element_type=F32)
    return lax.dot_general(a, b, dims, preferred_element_type=F32)


def lane(shape):
    return lax.broadcasted_iota(jnp.int32, shape, len(shape) - 1)


def row(shape):
    return lax.broadcasted_iota(jnp.int32, shape, len(shape) - 2)


def call(kernel, out_shape, cost, **kw):
    flops, bytes_accessed = cost
    return pl.pallas_call(
        kernel,
        out_shape=out_shape,
        compiler_params=pltpu.CompilerParams(vmem_limit_bytes=VMEM_LIMIT),
        cost_estimate=pl.CostEstimate(
            flops=int(flops), bytes_accessed=int(bytes_accessed), transcendentals=0
        ),
        **kw,
    )


def sds(shape, dtype):
    return jax.ShapeDtypeStruct(shape, dtype)


VM = pl.BlockSpec(memory_space=pltpu.VMEM)
SM = pl.BlockSpec(memory_space=pltpu.SMEM)


def slice_matrix():
    table = np.zeros((512, 512), np.float32)
    for k in range(512):
        section, place = k // 128, k % 128
        if section < 2:
            pair, part = section, place // 64
        else:
            pair, part = place // 64, section
        feat = place % 64
        f = (feat % 32) // 8
        column = pair * 64 + part * 16 + (feat // 32) * 8 + feat % 8
        table[k, f * 128 + column] = 1.0
    return table


def head_matrix():
    table = np.zeros((4, 128, 768), np.float32)
    for f in range(4):
        for block in range(2):
            for part in range(4):
                for j in range(16):
                    feat = (j // 8) * 32 + 8 * f + j % 8
                    source = block * 64 + part * 16 + j
                    if part == 2:
                        target = block * 128 + feat
                    elif part == 3:
                        target = block * 128 + 64 + feat
                    else:
                        target = 256 + block * 256 + part * 128 + feat
                    table[f, source, target] = 1.0
    return table


def place(part_ref, r, size):
    return pl.ds(pl.multiple_of(lax.bitwise_xor(part_ref[0], r) * size, size), size)


def kernel_route(picks_ref, gates_ref, rank_ref, gate_ref):
    experts = row((32, 128))
    gate = jnp.zeros((32, 128), F32)
    chosen = jnp.zeros((32, 128), F32)
    for k in range(8):
        hit = picks_ref[k : k + 1, :] == experts
        gate = gate + jnp.where(hit, gates_ref[k : k + 1, :], 0.0)
        chosen = chosen + jnp.where(hit, 1.0, 0.0)
    before = jnp.where(row((128, 128)) < lane((128, 128)), 1.0, 0.0).astype(BF)
    rank = mm(chosen.astype(BF), before)
    rank_ref[...] = jnp.where(chosen > 0.5, rank, -1.0)
    gate_ref[...] = gate


def kernel_slices(w_ref, gains_ref, table_ref, gate_ref, out_weight_ref, out_ref):
    w = w_ref[...].astype(BF).astype(F32)
    parts = []
    for p in range(4):
        parts.append(
            jnp.concatenate(
                [
                    w[:, 256 * p : 256 * p + 256],
                    w[:, 1024 + 128 * p : 1152 + 128 * p],
                    w[:, 1536 + 128 * p : 1664 + 128 * p],
                ],
                axis=1,
            )
        )
    stacked = jnp.concatenate(parts, axis=0).astype(BF)
    cut = mm(stacked, table_ref[...])
    columns = []
    for f in range(4):
        columns.append(
            jnp.concatenate(
                [cut[8 * p : 8 * p + 8, 128 * f : 128 * f + 128] for p in range(4)], axis=1
            ).astype(BF)
        )
    gains = gains_ref[...]
    left = lane((8, 128)) < 64
    sub = row((8, 128))
    for c in range(32):
        gate = gate_ref[c : c + 1, :]
        high = gate.astype(BF).astype(F32)
        middle = (gate - high).astype(BF).astype(F32)
        rest = gate - high - middle
        parts = jnp.where(
            sub < 2, high, jnp.where(sub < 4, middle, jnp.where(sub < 6, rest, 0.0))
        )
        parts = jnp.where(sub % 2 == 0, pltpu.roll(parts, 64, 1), parts)
        last = jnp.where(left, gains, parts).astype(BF)
        for f in range(4):
            out_ref[c, f, :, 0:512] = columns[f]
            out_ref[c, f, :, 512:640] = last
            out_ref[c, f, :, 640:896] = out_weight_ref[:, 256 * f : 256 * f + 256].astype(BF)


def kernel_picks(rank_ref, gate_ref, pick_ref, turned_ref, high_ref, rest_ref):
    slot = lax.broadcasted_iota(jnp.int32, (64, 128), 0).astype(F32)
    for p in range(16):
        picks, weights = [], []
        for e in (2 * p, 2 * p + 1):
            hit = slot == rank_ref[e : e + 1, :]
            picks.append(jnp.where(hit, 1.0, 0.0))
            weights.append(jnp.where(hit, gate_ref[e : e + 1, :], 0.0))
        picks = jnp.concatenate(picks, axis=0)
        weights = jnp.transpose(jnp.concatenate(weights, axis=0))
        at = slice(128 * p, 128 * p + 128)
        pick_ref[at, :] = picks.astype(BF)
        turned_ref[:, at] = jnp.transpose(picks).astype(BF)
        high = weights.astype(BF)
        high_ref[:, at] = high
        rest_ref[:, at] = (weights - high.astype(F32)).astype(BF)


def kernel_project(
    part_ref, x0_ref, x1_ref, x2_ref, x3_ref, w_ref, cos_ref, sin_ref, msg_ref, hidden_ref, gains_ref
):
    gains = jnp.transpose(w_ref[:, 512:640].astype(F32))
    gains_ref[...] = gains[:8]
    for r, x_ref in enumerate((x0_ref, x1_ref, x2_ref, x3_ref)):
        x = x_ref[...].astype(F32)
        scale = lax.rsqrt(jnp.mean(x * x, axis=-1, keepdims=True) + EPSILON)
        hidden_ref[place(part_ref, r, 128), :] = (x * scale * gains[0:1]).astype(BF)
    proj = mm(hidden_ref[...], w_ref[:, 0:512])
    ahead = pltpu.roll(proj, 512 - 8, 1)
    behind = pltpu.roll(proj, 8, 1)
    partner = jnp.where((lane((512, 512)) // 8) % 2 == 0, ahead, behind)
    cos = jnp.concatenate([cos_ref[...]] * 4, axis=0)
    sin = jnp.concatenate([sin_ref[...]] * 4, axis=0)
    turned = proj * cos + partner * sin
    low = lane((64, 128)) < 64
    for s in range(4):
        for p in range(4):
            front = turned[128 * s : 128 * s + 64, 128 * p : 128 * p + 128]
            back = turned[128 * s + 64 : 128 * s + 128, 128 * p : 128 * p + 128]
            msg_ref[8 * p + s] = jnp.where(low, front, pltpu.roll(back, 64, 1)).astype(BF)
            msg_ref[8 * p + 4 + s] = jnp.where(low, pltpu.roll(front, 64, 1), back).astype(BF)


def kernel_heads(msg_ref, table_ref, kv_ref, q_ref):
    out = jnp.zeros((512, 768), F32)
    for f in range(4):
        out = out + mm(msg_ref[:, f].reshape(512, 128), table_ref[f])
    pairs = out[:, 0:256].astype(BF)
    for half in range(2):
        block = pairs[:, 128 * half : 128 * half + 128]
        for y in range(4):
            kv_ref[y, 512 * half : 512 * half + 512, :] = block
    queries = (out[:, 256:768] * 0.125).astype(BF)
    for half in range(2):
        for head in range(2):
            at = 256 * half + 128 * head
            q_ref[half, :, head] = queries[:, at : at + 128].reshape(8, 64, 128)


CHUNKS = (1, 2, 3, 4, 8, 7, 6, 5)


def tile_positions(tile, mine):
    front = tile < 4
    i = jnp.where(front, tile, tile - 4)
    q = lane((1, 256))
    k = lax.broadcasted_iota(jnp.int32, (512, 1), 0)
    q_front = (8 * i + 4 * (q // 128) + mine) * 64 + q % 64
    q_back = (63 - 8 * i - 4 * (q // 128) - mine) * 64 + q % 64
    k_front = 512 * i + k
    k_back = (59 - 8 * i + 4 * (k // 256) - (k % 256) // 64) * 64 + k % 64
    return jnp.where(front, q_front, q_back), jnp.where(front, k_front, k_back)


def kernel_attend(mine_ref, kv_ref, q_ref, msg_ref, log_ref, out_ref, keys_ref, turned_ref):
    tile = pl.program_id(0)

    @pl.when(tile == 0)
    def _():
        for group in range(16):
            half, place = (0, group) if group < 8 else (1, 15 - group)
            for y in range(4):
                at = 256 * group + 64 * y
                keys_ref[at : at + 64, :] = kv_ref[y, half, place]
        for c in range(8):
            turned_ref[:, 512 * c : 512 * c + 512] = jnp.transpose(
                keys_ref[512 * c : 512 * c + 512, :].astype(F32)
            ).astype(BF)

    q = q_ref[...]
    q_pos, k_pos = tile_positions(tile, mine_ref[0])

    def run(count):
        peak = jnp.full((1, 256), MASKED, F32)
        total = jnp.zeros((1, 256), F32)
        mixed = jnp.zeros((64, 256), F32)
        later = mm(keys_ref[0:512, :], q, NT)
        for c in range(count):
            scores = later
            if c + 1 < count:
                later = mm(keys_ref[512 * c + 512 : 512 * c + 1024, :], q, NT)
            else:
                scores = jnp.where(k_pos <= q_pos, scores, MASKED)
            higher = jnp.maximum(peak, jnp.max(scores, axis=0, keepdims=True))
            weights = jnp.exp(scores - higher)
            fade = jnp.exp(peak - higher)
            total = total * fade + jnp.sum(weights, axis=0, keepdims=True)
            mixed = mixed * fade + mm(
                turned_ref[64:128, 512 * c : 512 * c + 512], weights.astype(BF)
            )
            peak = higher
        log_ref[0] = jnp.broadcast_to(peak + jnp.log(total), (8, 256))
        mixed = mixed / total
        out = jnp.transpose(jnp.concatenate([jnp.zeros((64, 256), F32), mixed], axis=0))
        out_ref[...] = out
        low = lane((64, 128)) < 64
        for a in range(2):
            first = out[128 * a : 128 * a + 64]
            second = out[128 * a + 64 : 128 * a + 128]
            msg_ref[a, 0] = jnp.where(low, pltpu.roll(first, 64, 1), second).astype(BF)

    for t, count in enumerate(CHUNKS):
        pl.when(tile == t)(functools.partial(run, count))


def kernel_attend_back(
    mine_ref, keys_ref, turned_ref, q_ref, grad_ref, log_ref, out_ref, dq_ref, dkv_ref, sum_ref
):
    tile = pl.program_id(0)

    @pl.when(tile == 0)
    def _():
        sum_ref[...] = jnp.zeros_like(sum_ref)

    q = q_ref[...]
    low = lane((64, 128)) < 64
    pieces = []
    for a in range(2):
        both = grad_ref[a, 0].astype(F32)
        pieces.append(jnp.where(low, 0.0, pltpu.roll(both, 64, 1)))
        pieces.append(jnp.where(low, 0.0, both))
    grad = jnp.concatenate(pieces, axis=0)
    delta = jnp.sum(jnp.transpose(grad * out_ref[...]), axis=0, keepdims=True)
    grad = grad.astype(BF)
    q_pos, k_pos = tile_positions(tile, mine_ref[0])
    log_total = log_ref[0][0:1]

    def step(c, dq, last):
        at = 512 * c
        keys = keys_ref[pl.ds(at, 512), :]
        scores = mm(keys, q, NT)
        if last:
            scores = jnp.where(k_pos <= q_pos, scores, MASKED)
        weights = jnp.exp(scores - log_total)
        slope = (weights * (mm(keys, grad, NT) - delta)).astype(BF)
        sum_ref[pl.ds(at, 512), :] += mm(slope, q) + mm(weights.astype(BF), grad)
        return dq + mm(turned_ref[0:64, pl.ds(at, 512)], slope)

    def run(count):
        dq = jnp.zeros((64, 256), F32)
        for c in range(count):
            dq = step(c, dq, c == count - 1)
        dq = jnp.concatenate([dq * 0.125, jnp.zeros((64, 256), F32)], axis=0)
        dq_ref[...] = jnp.transpose(dq)

    for t, count in enumerate(CHUNKS):
        pl.when(tile == t)(functools.partial(run, count))

    @pl.when(tile == 7)
    def _():
        for group in range(16):
            half, place = (0, group) if group < 8 else (1, 15 - group)
            for y in range(4):
                at = 256 * group + 64 * y
                dkv_ref[y, half, place] = sum_ref[at : at + 64, :].astype(BF)


def kernel_middle(
    part_ref,
    o_ref,
    u0_ref,
    u1_ref,
    u2_ref,
    u3_ref,
    l0_ref,
    l1_ref,
    l2_ref,
    l3_ref,
    x_ref,
    gains_ref,
    pick_ref,
    slots_ref,
    mid_ref,
    rows_ref,
    hidden_ref,
):
    @pl.when(pl.program_id(0) == 0)
    def _():
        for g in range(8):
            rows_ref[:, 128 * g : 128 * g + 128] = o_ref[g].reshape(128, 128)
        uppers = (u0_ref, u1_ref, u2_ref, u3_ref)
        lowers = (l0_ref, l1_ref, l2_ref, l3_ref)
        for r in range(4):
            at = place(part_ref, r, 256)
            mid_ref[:, at] = (
                x_ref[:, at].astype(F32)
                + mm(rows_ref[:, 0:512], uppers[r][...])
                + mm(rows_ref[:, 512:1024], lowers[r][...])
            )
        mid = mid_ref[...]
        scale = lax.rsqrt(jnp.mean(mid * mid, axis=-1, keepdims=True) + EPSILON)
        hidden_ref[...] = (mid * scale * gains_ref[1:2]).astype(BF)

    for c in range(4):
        at = slice(256 * c, 256 * c + 256)
        rows = mm(pick_ref[...], hidden_ref[:, at]).astype(BF)
        slots_ref[:, :, at] = rows.reshape(16, 64, 256)


def kernel_experts_ready(
    part_ref,
    dy_ref,
    parts_ref,
    w0_ref,
    w1_ref,
    w2_ref,
    w3_ref,
    dys_ref,
    dact_ref,
    v_ref,
    gu_ref,
    rank_ref,
    gate_ref,
):
    step = pl.program_id(0)

    @pl.when(step == 0)
    def _():
        for r, w_ref in enumerate((w0_ref, w1_ref, w2_ref, w3_ref)):
            gu_ref[place(part_ref, r, 256), :] = w_ref[0:256, :]
            v_ref[place(part_ref, r, 128), :] = w_ref[256:384, :]
        before = jnp.where(row((128, 128)) < lane((128, 128)), 1.0, 0.0).astype(BF)
        parts = [parts_ref[:, k, :].astype(F32) for k in range(6)]
        even = parts[0] + parts[2] + parts[4]
        odd = parts[1] + parts[3] + parts[5]
        gate_ref[...] = jnp.where(lane((32, 128)) < 64, pltpu.roll(even, 64, 1), odd)
        chosen = gate_ref[...] > 0.0
        rank = mm(jnp.where(chosen, 1.0, 0.0).astype(BF), before)
        rank_ref[...] = jnp.where(chosen, rank, -1.0)

    slot = lax.broadcasted_iota(jnp.int32, (64, 128), 0).astype(F32)
    grads = []
    for j in range(4):
        source = 4 * step + j
        pick = slot == rank_ref[pl.ds(source, 1), :]
        weight = jnp.sum(
            jnp.where(pick, gate_ref[pl.ds(source, 1), :], 0.0), axis=1, keepdims=True
        )
        rows = mm(jnp.where(pick, 1.0, 0.0).astype(BF), dy_ref[0, j, 0])
        grads.append((rows * weight).astype(BF))
    dys = jnp.concatenate(grads, axis=0)
    dys_ref[...] = dys.reshape(4, 64, WIDTH)
    dact_ref[...] = mm(dys, v_ref[...], NT)


def kernel_experts(h_ref, gu_ref, dact_ref, act_ref, dboth_ref, dxs_ref):
    both = mm(h_ref[...].reshape(512, WIDTH), gu_ref[...])
    gate_h, up_h = both[:, :512], both[:, 512:]
    sig = jax.nn.sigmoid(gate_h)
    swished = gate_h * sig
    act_ref[...] = (swished * up_h).astype(BF)
    dact = dact_ref[...]
    dgate = (dact * up_h * sig * (1.0 + gate_h * (1.0 - sig))).astype(BF)
    dup = (dact * swished).astype(BF)
    dboth = jnp.concatenate([dgate, dup], axis=1)
    dboth_ref[...] = dboth
    dxs_ref[...] = mm(dboth, gu_ref[...], NT).astype(BF).reshape(8, 64, WIDTH)


def kernel_experts_after(
    h_ref, act_ref, dys_ref, dboth_ref, v_ref, ys_ref, grad_ref, ggu_ref, gv_ref
):
    step = pl.program_id(0)

    @pl.when(step == 0)
    def _():
        ggu_ref[...] = jnp.zeros_like(ggu_ref)
        gv_ref[...] = jnp.zeros_like(gv_ref)

    act = act_ref[...]
    ys_ref[...] = mm(act, v_ref[...]).astype(BF).reshape(4, 64, WIDTH)
    ggu_ref[...] += mm(h_ref[...].reshape(256, WIDTH), dboth_ref[...], TN)
    gv_ref[...] += mm(act, dys_ref[...].reshape(256, WIDTH), TN)

    @pl.when(step == 7)
    def _():
        for f in range(4):
            grad_ref[f, 0:256, :] = ggu_ref[256 * f : 256 * f + 256, :].astype(BF)
            grad_ref[f, 256:384, :] = gv_ref[128 * f : 128 * f + 128, :].astype(BF)


def kernel_middle_back(
    part_ref,
    dxs_ref,
    pick_ref,
    mid_ref,
    cot_ref,
    gains_ref,
    u0_ref,
    u1_ref,
    u2_ref,
    u3_ref,
    l0_ref,
    l1_ref,
    l2_ref,
    l3_ref,
    dmid_ref,
    parts_ref,
    msg_ref,
    ggain_ref,
    sum_ref,
    low_ref,
):
    step = pl.program_id(0)
    part = mm(pick_ref[...], dxs_ref[...].reshape(1024, WIDTH))

    @pl.when(step == 0)
    def _():
        sum_ref[...] = part

    @pl.when(step > 0)
    def _():
        sum_ref[...] += part

    @pl.when(step == 1)
    def _():
        mid = mid_ref[...]
        scale = lax.rsqrt(jnp.mean(mid * mid, axis=-1, keepdims=True) + EPSILON)
        dh = sum_ref[...]
        ggain_ref[...] = jnp.broadcast_to(
            jnp.sum(dh * (mid * scale), axis=0, keepdims=True), (8, WIDTH)
        )
        dn = dh * gains_ref[1:2]
        dmid = (
            cot_ref[...].astype(F32)
            + scale * dn
            - mid * (scale * scale * scale) * jnp.mean(dn * mid, axis=-1, keepdims=True)
        )
        dmid_ref[...] = dmid
        low_ref[...] = dmid.astype(BF)
        uppers = (u0_ref, u1_ref, u2_ref, u3_ref)
        lowers = (l0_ref, l1_ref, l2_ref, l3_ref)
        for r in range(4):
            parts_ref[r] = low_ref[:, place(part_ref, r, 256)]
        for h, w_refs in enumerate((uppers, lowers)):
            grad = mm(parts_ref[0], w_refs[0][...], NT)
            for r in range(1, 4):
                grad = grad + mm(parts_ref[r], w_refs[r][...], NT)
            grad = grad.astype(BF)
            for g in range(4):
                msg_ref[4 * h + g] = grad[:, 128 * g : 128 * g + 128].reshape(2, 64, 128)


def kernel_out_weight(
    o0_ref, o1_ref, o2_ref, o3_ref, da0_ref, da1_ref, da2_ref, da3_ref, gain_ref, grad_ref
):
    which = lax.broadcasted_iota(jnp.int32, (128, WIDTH), 0)
    grad_ref[:, 0:128] = jnp.transpose(jnp.where(which == 1, gain_ref[0:1], 0.0)).astype(BF)
    pairs = ((o0_ref, da0_ref), (o1_ref, da1_ref), (o2_ref, da2_ref), (o3_ref, da3_ref))
    for g in range(8):
        part = jnp.zeros((128, 256), F32)
        for o_ref, da_ref in pairs:
            part = part + mm(o_ref[g].reshape(128, 128), da_ref[...], TN)
        grad_ref[128 * g : 128 * g + 128, 128:384] = part.astype(BF)


def kernel_slices_back(dkv_ref, dq_ref, cos_ref, sin_ref, table_ref, msg_ref):
    def unrotate(w, cos, sin):
        partner = jnp.where(
            lane(w.shape) % 64 < 32, pltpu.roll(w, 96, 1), pltpu.roll(w, 32, 1)
        )
        return (w * cos - partner * sin).astype(BF)

    parts = []
    for half in range(2):
        at = slice(512 * half, 512 * half + 512)
        parts.append(unrotate(dkv_ref[at, :].astype(F32), cos_ref[at, :], sin_ref[at, :]))
    for half in range(2):
        at = slice(512 * half, 512 * half + 512)
        for head in range(2):
            parts.append(
                unrotate(dq_ref[half, :, head].reshape(512, 128), cos_ref[at, :], sin_ref[at, :])
            )
    whole = jnp.concatenate(parts, axis=1)
    for f in range(4):
        msg_ref[:, f] = mm(whole, table_ref[f], NT).astype(BF).reshape(8, 64, 128)


def kernel_hidden_grad(part_ref, d_ref, w_ref, h0_ref, h1_ref, h2_ref, h3_ref):
    for r, h_ref in enumerate((h0_ref, h1_ref, h2_ref, h3_ref)):
        h_ref[...] = mm(d_ref[place(part_ref, r, 128), :], w_ref[:, 0:512], NT).astype(BF)


def kernel_grads(msg_ref, hidden_ref, w_ref, rest_ref, grads_ref, d_ref):
    low = lane((64, 128)) < 64
    for s in range(4):
        for p in range(4):
            even = msg_ref[8 * p + s].astype(F32)
            odd = msg_ref[8 * p + 4 + s].astype(F32)
            d_ref[128 * s : 128 * s + 64, 128 * p : 128 * p + 128] = jnp.where(
                low, even, pltpu.roll(odd, 64, 1)
            ).astype(BF)
            d_ref[128 * s + 64 : 128 * s + 128, 128 * p : 128 * p + 128] = jnp.where(
                low, pltpu.roll(even, 64, 1), odd
            ).astype(BF)
    total = mm(hidden_ref[...], d_ref[...], TN)
    grads_ref[:, 0:512] = total.astype(BF)
    gain = jnp.sum(total * w_ref[:, 0:512].astype(F32), axis=1, keepdims=True)
    gain = gain / w_ref[:, 512:640].astype(F32)[:, 0:1]
    rest = rest_ref[:, 0:128]
    grads_ref[:, 512:640] = jnp.where(lane((WIDTH, 128)) == 0, gain.astype(BF), rest)
    grads_ref[:, 640:896] = rest_ref[:, 128:384]


def kernel_input_grad(d0_ref, d1_ref, d2_ref, d3_ref, x_ref, dmid_ref, gains_ref, out_ref):
    dh = d0_ref[...].astype(F32)
    for d_ref in (d1_ref, d2_ref, d3_ref):
        dh = dh + d_ref[...].astype(F32)
    x = x_ref[...].astype(F32)
    scale = lax.rsqrt(jnp.mean(x * x, axis=-1, keepdims=True) + EPSILON)
    dn = dh * gains_ref[0:1]
    out_ref[...] = (
        dmid_ref[...]
        + scale * dn
        - x * (scale * scale * scale) * jnp.mean(dn * x, axis=-1, keepdims=True)
    )


def kernel_total(parts_ref, table_ref, qkv_ref, out_ref, gains_ref, sum_ref):
    total = parts_ref[0].astype(F32)
    for c in range(1, 32):
        total = total + parts_ref[c].astype(F32)
    sum_ref[...] = total
    rows = []
    for p in range(4):
        rows.append(
            jnp.concatenate([sum_ref[f, :, 128 * p : 128 * p + 128] for f in range(4)], axis=1)
        )
    rest = jnp.concatenate(rows, axis=0)
    parts = []
    for _ in range(3):
        part = rest.astype(BF)
        rest = rest - part.astype(F32)
        parts.append(part)
    whole = mm(jnp.concatenate(parts, axis=0), table_ref[...], NT)
    whole = whole[0:32] + whole[32:64] + whole[64:96]
    for p in range(4):
        piece = whole[8 * p : 8 * p + 8]
        qkv_ref[:, 256 * p : 256 * p + 256] = piece[:, 0:256]
        qkv_ref[:, 1024 + 128 * p : 1152 + 128 * p] = piece[:, 256:384]
        qkv_ref[:, 1536 + 128 * p : 1664 + 128 * p] = piece[:, 384:512]
    for f in range(4):
        out_ref[:, 256 * f : 256 * f + 256] = sum_ref[f, :, 640:896]
    gains_ref[...] = (
        sum_ref[0, :, 512:640]
        + sum_ref[1, :, 512:640]
        + sum_ref[2, :, 512:640]
        + sum_ref[3, :, 512:640]
    )


def kernel_output(ys_ref, high_ref, rest_ref, mid_ref, out_ref, sum_ref):
    step = pl.program_id(0)

    @pl.when(step == 0)
    def _():
        sum_ref[...] = mid_ref[...]

    ys = ys_ref[...].reshape(512, WIDTH)
    sum_ref[...] += mm(high_ref[...], ys) + mm(rest_ref[...], ys)

    @pl.when(step == 3)
    def _():
        out_ref[...] = sum_ref[...].astype(BF)


def angles(positions, features):
    frequency = ROPE_BASE ** (-(features.astype(F32) * 2.0 / 64))
    return positions.astype(F32)[:, None] * frequency[None, :]


def whole(shape):
    return pl.BlockSpec(shape, lambda t: (0,) * len(shape))


def exchange(value, axes):
    return lax.all_to_all(value, axes, split_axis=0, concat_axis=0, tiled=True)


def gather(value, axes):
    return lax.all_gather(value, axes, axis=0, tiled=True)


def after(value, marker):
    return lax.optimization_barrier((value, marker))[0]


def swap(value, axis):
    return lax.ppermute(value, axis, [(0, 1), (1, 0)])


def neighbours(value):
    return value, swap(value, "core"), swap(value, "zl")


def cross(parts):
    here = [parts[0]]
    for r in range(1, 4):
        here.append(lax.ppermute(parts[r], FSDP, [(f, f ^ r) for f in range(4)]))
    return here


def on_device(
    layer_input,
    routes,
    gates,
    cotangent,
    norm_attn,
    query_key_value_weight,
    output_weight,
    norm_ffn,
    exp_gate,
    exp_up,
    exp_down,
):
    mine = lax.axis_index("y")
    ctx_index = lax.axis_index(CTX)
    part_index = lax.axis_index(FSDP)
    mine_ref = mine.astype(jnp.int32).reshape(1)
    part_ref = part_index.astype(jnp.int32).reshape(1)
    x = layer_input.reshape(128, WIDTH)
    cot = cotangent.reshape(128, WIDTH)
    slice_table = jnp.asarray(slice_matrix(), BF)
    head_table = jnp.asarray(head_matrix(), BF)

    x_all = neighbours(x)
    rank, gate = call(
        kernel_route,
        (sds((32, 128), F32), sds((32, 128), F32)),
        (1e6, 1e5),
        in_specs=[VM, VM],
        out_specs=(VM, VM),
    )(routes.reshape(128, 8).T, gates.reshape(128, 8).T)
    which = lax.broadcasted_iota(jnp.int32, (8, 128), 1)
    gain_rows = jnp.where(
        which == 0, norm_attn[:, None], jnp.where(which == 1, norm_ffn[:, None], 0.0)
    )
    slices = call(
        kernel_slices,
        sds((32, 4, 8, 896), BF),
        (2e7, 3e6),
        in_specs=[VM] * 5,
        out_specs=VM,
    )(query_key_value_weight, gain_rows, slice_table, gate, output_weight)
    slices, rank, gate, x_all = lax.optimization_barrier((slices, rank, gate, x_all))
    x_all = x_all + (swap(x_all[2], "core"),)
    offset = jnp.arange(64, dtype=jnp.int32)
    token_pos = jnp.concatenate([ctx_index * 64 + offset, (63 - ctx_index) * 64 + offset])
    column = jnp.arange(512, dtype=jnp.int32)
    angle = angles(token_pos, 8 * part_index + column % 8)
    is_value = (column // 16) % 4 == 3
    sign = jnp.where((column // 8) % 2 == 0, -1.0, 1.0)
    cos_slice = jnp.where(is_value, 1.0, jnp.cos(angle))
    sin_slice = jnp.where(is_value, 0.0, jnp.sin(angle) * sign)
    w_slice = exchange(slices.reshape(128, 8, 896), ALL)
    w_slice, cos_slice, sin_slice = lax.optimization_barrier((w_slice, cos_slice, sin_slice))
    gate_parts = lax.dynamic_slice(
        w_slice.reshape(32, 4, 8, 896), (0, part_index, 0, 512), (32, 1, 8, 128)
    ).reshape(32, 8, 128)
    w_slice = w_slice.reshape(WIDTH, 896)
    picks, picks_turned, picks_high, picks_rest = call(
        kernel_picks,
        (sds((2048, 128), BF),) + (sds((128, 2048), BF),) * 3,
        (2e9, 4e6),
        in_specs=[VM, VM],
        out_specs=(VM,) * 4,
    )(rank, gate)

    msg, hidden, gains = call(
        kernel_project,
        (sds((32, 64, 128), BF), sds((512, WIDTH), BF), sds((8, WIDTH), F32)),
        (6e8, 4e6),
        in_specs=[SM] + [VM] * 7,
        out_specs=(VM, VM, VM),
    )(part_ref, *x_all, w_slice, cos_slice, sin_slice)
    across = swap(after(cot, w_slice), "zh")
    first = lax.axis_index("zh") == 0
    cot_pair = jnp.concatenate(
        [jnp.where(first, cot, across), jnp.where(first, across, cot)], axis=0
    )
    cot_all = gather(after(cot_pair, msg), ("x", "y")).reshape(4, 4, 2, 128, WIDTH)
    out_upper = neighbours(w_slice[0:512, 640:896])
    msg = exchange(msg, HEAD_AXES + FSDP)

    kv_copies, queries = call(
        kernel_heads,
        (sds((4, 1024, 128), BF), sds((2, 8, 2, 64, 128), BF)),
        (4e8, 3e6),
        in_specs=[VM, VM],
        out_specs=(VM, VM),
    )(msg.reshape(8, 4, 64, 128), head_table)
    queries = queries.reshape(2048, 128)
    kv_copies, out_upper = lax.optimization_barrier((kv_copies, out_upper))
    out_lower = neighbours(after(w_slice[512:1024, 640:896], msg))
    kv = exchange(kv_copies, ("y",)).reshape(4, 2, 8, 64, 128)
    expert_weights = jnp.concatenate(
        [jnp.concatenate([exp_gate[0], exp_up[0]], axis=1), exp_down[0]], axis=0
    ).astype(BF)
    block = 4 * jnp.arange(8, dtype=jnp.int32)[:, None] + mine
    quarter_pos = jnp.concatenate(
        [
            (block * 64 + offset[None, :]).reshape(-1),
            ((63 - block) * 64 + offset[None, :]).reshape(-1),
        ]
    )
    column = jnp.arange(128, dtype=jnp.int32)
    angle = angles(quarter_pos, column % 32)
    sign = jnp.where(column % 64 < 32, -1.0, 1.0)
    cos_heads = jnp.where(column >= 64, 1.0, jnp.cos(angle))
    sin_heads = jnp.where(column >= 64, 0.0, jnp.sin(angle) * sign)
    kv, out_lower, cos_heads, sin_heads = lax.optimization_barrier(
        (kv, out_lower, cos_heads, sin_heads)
    )
    experts_all = neighbours(after(expert_weights, msg))
    out_upper = out_upper + (swap(after(out_upper[2], kv), "core"),)
    out_lower = out_lower + (swap(out_lower[2], "core"),)
    w_out = (*out_upper, *out_lower)
    msg_spec = pl.BlockSpec((2, 1, 64, 128), lambda t: (t % 4, t // 4, 0, 0))
    row_spec = pl.BlockSpec((256, 128), lambda t: (t, 0))
    log_spec = pl.BlockSpec((1, 8, 256), lambda t: (t, 0, 0))
    o_msg, log_total, o_rows, keys, turned = call(
        kernel_attend,
        (
            sds((8, 2, 64, 128), BF),
            sds((8, 8, 256), F32),
            sds((2048, 128), F32),
            sds((4096, 128), BF),
            sds((128, 4096), BF),
        ),
        (1e10, 5e6),
        grid=(8,),
        in_specs=[SM, whole((4, 2, 8, 64, 128)), row_spec],
        out_specs=(msg_spec, log_spec, row_spec, whole((4096, 128)), whole((128, 4096))),
    )(mine_ref, kv, queries)
    o_msg, w_out, experts_all = lax.optimization_barrier((o_msg, w_out, experts_all))
    experts_all = experts_all + (swap(experts_all[2], "core"),)
    o_heads = exchange(o_msg, HEAD_AXES)

    slot_spec = pl.BlockSpec((4, 64, WIDTH), lambda t: (t, 0, 0))
    out_specs = [whole((512, 256))] * 8
    slots, mid = call(
        kernel_middle,
        (sds((32, 64, WIDTH), BF), sds((128, WIDTH), F32)),
        (9e8, 8e6),
        grid=(2,),
        in_specs=[SM, whole((8, 2, 64, 128))]
        + out_specs
        + [
            whole((128, WIDTH)),
            whole((8, WIDTH)),
            pl.BlockSpec((1024, 128), lambda t: (t, 0)),
        ],
        out_specs=(pl.BlockSpec((16, 64, WIDTH), lambda t: (t, 0, 0)), whole((128, WIDTH))),
        scratch_shapes=[pltpu.VMEM((128, WIDTH), BF), pltpu.VMEM((128, WIDTH), BF)],
    )(part_ref, o_heads, *w_out, x, gains, picks)
    cot_all = after(cot_all, mid)
    slots, experts_all = lax.optimization_barrier((slots, experts_all))
    o_all = neighbours(after(o_heads, mid))
    slots = exchange(slots, CTX)
    dys, dact, down, gate_up = call(
        kernel_experts_ready,
        (
            sds((32, 64, WIDTH), BF),
            sds((2048, 512), F32),
            sds((512, WIDTH), BF),
            sds((WIDTH, WIDTH), BF),
        ),
        (6e9, 2e7),
        grid=(8,),
        in_specs=[
            SM,
            pl.BlockSpec((1, 4, 1, 128, WIDTH), lambda t: (t // 2, 0, t % 2, 0, 0)),
            whole((32, 8, 128)),
        ]
        + [whole((384, WIDTH))] * 4,
        out_specs=(
            slot_spec,
            pl.BlockSpec((256, 512), lambda t: (t, 0)),
            whole((512, WIDTH)),
            whole((WIDTH, WIDTH)),
        ),
        scratch_shapes=[pltpu.VMEM((32, 128), F32), pltpu.VMEM((32, 128), F32)],
    )(part_ref, cot_all, gate_parts, *experts_all)
    act_spec = pl.BlockSpec((256, 512), lambda t: (t, 0))
    both_spec = pl.BlockSpec((256, WIDTH), lambda t: (t, 0))
    act, dboth, dxs = call(
        kernel_experts,
        (sds((2048, 512), BF), sds((2048, WIDTH), BF), sds((32, 64, WIDTH), BF)),
        (9e9, 2e7),
        grid=(4,),
        in_specs=[
            pl.BlockSpec((8, 64, WIDTH), lambda t: (t, 0, 0)),
            whole((WIDTH, WIDTH)),
            pl.BlockSpec((512, 512), lambda t: (t, 0)),
        ],
        out_specs=(
            pl.BlockSpec((512, 512), lambda t: (t, 0)),
            pl.BlockSpec((512, WIDTH), lambda t: (t, 0)),
            pl.BlockSpec((8, 64, WIDTH), lambda t: (t, 0, 0)),
        ),
    )(slots, gate_up, dact)
    ys, expert_grads = call(
        kernel_experts_after,
        (sds((32, 64, WIDTH), BF), sds((4, 384, WIDTH), BF)),
        (9e9, 2e7),
        grid=(8,),
        in_specs=[slot_spec, act_spec, slot_spec, both_spec, whole((512, WIDTH))],
        out_specs=(slot_spec, whole((4, 384, WIDTH))),
        scratch_shapes=[pltpu.VMEM((WIDTH, WIDTH), F32), pltpu.VMEM((512, WIDTH), F32)],
    )(slots, act, dys, dboth, down)
    dxs, o_all = lax.optimization_barrier((dxs, o_all))
    o_all = o_all + (swap(o_all[2], "core"),)
    dxs = exchange(dxs, CTX)
    dxs, ys, expert_grads, o_all = lax.optimization_barrier((dxs, ys, expert_grads, o_all))

    dmid, da_parts, grad_msg, gain_ffn_part = call(
        kernel_middle_back,
        (
            sds((128, WIDTH), F32),
            sds((4, 128, 256), BF),
            sds((8, 2, 64, 128), BF),
            sds((8, WIDTH), F32),
        ),
        (9e8, 8e6),
        grid=(2,),
        in_specs=[
            SM,
            pl.BlockSpec((16, 64, WIDTH), lambda t: (t, 0, 0)),
            pl.BlockSpec((128, 1024), lambda t: (0, t)),
            whole((128, WIDTH)),
            whole((128, WIDTH)),
            whole((8, WIDTH)),
        ]
        + out_specs,
        out_specs=(
            whole((128, WIDTH)),
            whole((4, 128, 256)),
            whole((8, 2, 64, 128)),
            whole((8, WIDTH)),
        ),
        scratch_shapes=[pltpu.VMEM((128, WIDTH), F32), pltpu.VMEM((128, WIDTH), BF)],
    )(part_ref, dxs, picks_turned, mid, cot, gains, *w_out)
    grad_heads = exchange(grad_msg, HEAD_AXES)
    ys, grad_heads = lax.optimization_barrier((ys, grad_heads))
    ys = exchange(ys, CTX)
    dq, dkv = call(
        kernel_attend_back,
        (sds((2048, 128), F32), sds((4, 2, 8, 64, 128), BF)),
        (2e10, 7e6),
        grid=(8,),
        in_specs=[
            SM,
            whole((4096, 128)),
            whole((128, 4096)),
            row_spec,
            msg_spec,
            log_spec,
            row_spec,
        ],
        out_specs=(row_spec, whole((4, 2, 8, 64, 128))),
        scratch_shapes=[pltpu.VMEM((4096, 128), F32)],
    )(mine_ref, keys, turned, queries, grad_heads, log_total, o_rows)
    da_here = cross(da_parts)
    dkv = lax.psum_scatter(
        dkv.reshape(4096, 128), ("y",), scatter_dimension=0, tiled=True
    )
    dkv, ys, da_here = lax.optimization_barrier((dkv, ys, da_here))
    expert_own = lax.psum_scatter(
        after(expert_grads, dkv).reshape(4 * 384, WIDTH), FSDP, scatter_dimension=0, tiled=True
    ).astype(F32)
    rest_part = call(
        kernel_out_weight,
        sds((WIDTH, 384), BF),
        (3e8, 2e6),
        in_specs=[VM] * 9,
        out_specs=VM,
    )(*o_all, *da_here, gain_ffn_part)
    layer_output = call(
        kernel_output,
        sds((128, WIDTH), BF),
        (1e9, 5e6),
        grid=(4,),
        in_specs=[
            pl.BlockSpec((8, 64, WIDTH), lambda t: (t, 0, 0)),
            pl.BlockSpec((128, 512), lambda t: (0, t)),
            pl.BlockSpec((128, 512), lambda t: (0, t)),
            whole((128, WIDTH)),
        ],
        out_specs=whole((128, WIDTH)),
        scratch_shapes=[pltpu.VMEM((128, WIDTH), F32)],
    )(ys, picks_high, picks_rest, mid)

    back = call(
        kernel_slices_back,
        sds((8, 4, 64, 128), BF),
        (4e8, 5e6),
        in_specs=[VM] * 5,
        out_specs=VM,
    )(dkv, dq.reshape(2, 8, 2, 64, 128), cos_heads, sin_heads, head_table)
    back = exchange(back.reshape(32, 64, 128), HEAD_AXES + FSDP)

    grads, d_all = call(
        kernel_grads,
        (sds((WIDTH, 896), BF), sds((512, 512), BF)),
        (6e8, 5e6),
        in_specs=[VM] * 4,
        out_specs=(VM, VM),
    )(back, hidden, w_slice, rest_part)
    dh_parts = call(
        kernel_hidden_grad,
        (sds((128, WIDTH), BF),) * 4,
        (6e8, 5e6),
        in_specs=[SM, VM, VM],
        out_specs=(VM,) * 4,
    )(part_ref, d_all, w_slice)
    grads = exchange(grads.reshape(128, 8, 896), ALL)
    grad_qkv, grad_out, grad_gains = call(
        kernel_total,
        (sds((8, 2048), F32), sds((8, WIDTH), F32), sds((8, 128), F32)),
        (1e8, 4e6),
        in_specs=[VM, VM],
        out_specs=(VM, VM, VM),
        scratch_shapes=[pltpu.VMEM((4, 8, 896), F32)],
    )(grads.reshape(32, 4, 8, 896), slice_table)
    dh_here = cross(dh_parts)
    input_grad = call(
        kernel_input_grad,
        sds((128, WIDTH), F32),
        (1e6, 2e6),
        in_specs=[VM] * 7,
        out_specs=VM,
    )(*after(dh_here, grad_qkv), x, dmid, gains)
    return (
        layer_output.reshape(layer_input.shape),
        input_grad.reshape(layer_input.shape),
        grad_gains[:, 0],
        grad_qkv,
        grad_out,
        grad_gains[:, 1],
        expert_own[0:256, 0:512][None],
        expert_own[0:256, 512:1024][None],
        expert_own[256:384][None],
    )


def solution(mesh):
    parts = Mesh(mesh.devices.reshape(4, 2, 4, 2, 2), ALL)
    tokens = P(FSDP, CTX, None, None, None, None)
    experts = P(CTX, FSDP, None)
    in_specs = (
        tokens,
        tokens,
        tokens,
        tokens,
        P(ALL),
        P(ALL, None),
        P(ALL, None),
        P(ALL),
        experts,
        experts,
        experts,
    )
    out_specs = (
        tokens,
        tokens,
        P(ALL),
        P(ALL, None),
        P(ALL, None),
        P(ALL),
        experts,
        experts,
        experts,
    )
    return jax.shard_map(
        on_device, mesh=parts, in_specs=in_specs, out_specs=out_specs, check_vma=False
    )
```

```python
import functools

import jax
import jax.numpy as jnp
import numpy as np
from jax import lax
from jax.experimental import pallas as pl
from jax.experimental.pallas import tpu as pltpu
from jax.sharding import Mesh
from jax.sharding import PartitionSpec as P

WIDTH = 1024
EPSILON = 1e-06
ROPE_BASE = 10000.0
MASKED = -1e30
BF = jnp.bfloat16
F32 = jnp.float32
CTX = ("x", "zh", "y")
HEAD_AXES = ("x", "zh")
FSDP = ("zl", "core")
ALL = CTX + FSDP
VMEM_LIMIT = 56 * 1024 * 1024

NT = (((1,), (1,)), ((), ()))
TN = (((0,), (0,)), ((), ()))


def mm(a, b, dims=None):
    if dims is None:
        return jnp.dot(a, b, preferred_element_type=F32)
    return lax.dot_general(a, b, dims, preferred_element_type=F32)


def lane(shape):
    return lax.broadcasted_iota(jnp.int32, shape, len(shape) - 1)


def row(shape):
    return lax.broadcasted_iota(jnp.int32, shape, len(shape) - 2)


def call(kernel, out_shape, cost, **kw):
    flops, bytes_accessed = cost
    return pl.pallas_call(
        kernel,
        out_shape=out_shape,
        compiler_params=pltpu.CompilerParams(vmem_limit_bytes=VMEM_LIMIT),
        cost_estimate=pl.CostEstimate(
            flops=int(flops), bytes_accessed=int(bytes_accessed), transcendentals=0
        ),
        **kw,
    )


def sds(shape, dtype):
    return jax.ShapeDtypeStruct(shape, dtype)


VM = pl.BlockSpec(memory_space=pltpu.VMEM)
SM = pl.BlockSpec(memory_space=pltpu.SMEM)


def slice_matrix():
    table = np.zeros((512, 512), np.float32)
    for k in range(512):
        section, place = k // 128, k % 128
        if section < 2:
            pair, part = section, place // 64
        else:
            pair, part = place // 64, section
        feat = place % 64
        f = (feat % 32) // 8
        column = pair * 64 + part * 16 + (feat // 32) * 8 + feat % 8
        table[k, f * 128 + column] = 1.0
    return table


def head_matrix():
    table = np.zeros((4, 128, 768), np.float32)
    for f in range(4):
        for block in range(2):
            for part in range(4):
                for j in range(16):
                    feat = (j // 8) * 32 + 8 * f + j % 8
                    source = block * 64 + part * 16 + j
                    if part == 2:
                        target = block * 128 + feat
                    elif part == 3:
                        target = block * 128 + 64 + feat
                    else:
                        target = 256 + block * 256 + part * 128 + feat
                    table[f, source, target] = 1.0
    return table


def place(part_ref, r, size):
    return pl.ds(pl.multiple_of(lax.bitwise_xor(part_ref[0], r) * size, size), size)


def kernel_route(picks_ref, gates_ref, rank_ref, gate_ref):
    experts = row((32, 128))
    gate = jnp.zeros((32, 128), F32)
    chosen = jnp.zeros((32, 128), F32)
    for k in range(8):
        hit = picks_ref[k : k + 1, :] == experts
        gate = gate + jnp.where(hit, gates_ref[k : k + 1, :], 0.0)
        chosen = chosen + jnp.where(hit, 1.0, 0.0)
    before = jnp.where(row((128, 128)) < lane((128, 128)), 1.0, 0.0).astype(BF)
    rank = mm(chosen.astype(BF), before)
    rank_ref[...] = jnp.where(chosen > 0.5, rank, -1.0)
    gate_ref[...] = gate


def kernel_slices(w_ref, gains_ref, table_ref, gate_ref, out_weight_ref, out_ref):
    w = w_ref[...].astype(BF).astype(F32)
    parts = []
    for p in range(4):
        parts.append(
            jnp.concatenate(
                [
                    w[:, 256 * p : 256 * p + 256],
                    w[:, 1024 + 128 * p : 1152 + 128 * p],
                    w[:, 1536 + 128 * p : 1664 + 128 * p],
                ],
                axis=1,
            )
        )
    stacked = jnp.concatenate(parts, axis=0).astype(BF)
    cut = mm(stacked, table_ref[...])
    columns = []
    for f in range(4):
        columns.append(
            jnp.concatenate(
                [cut[8 * p : 8 * p + 8, 128 * f : 128 * f + 128] for p in range(4)], axis=1
            ).astype(BF)
        )
    gains = gains_ref[...]
    left = lane((8, 128)) < 64
    sub = row((8, 128))
    for c in range(32):
        gate = gate_ref[c : c + 1, :]
        high = gate.astype(BF).astype(F32)
        middle = (gate - high).astype(BF).astype(F32)
        rest = gate - high - middle
        parts = jnp.where(
            sub < 2, high, jnp.where(sub < 4, middle, jnp.where(sub < 6, rest, 0.0))
        )
        parts = jnp.where(sub % 2 == 0, pltpu.roll(parts, 64, 1), parts)
        last = jnp.where(left, gains, parts).astype(BF)
        for f in range(4):
            out_ref[c, f, :, 0:512] = columns[f]
            out_ref[c, f, :, 512:640] = last
            out_ref[c, f, :, 640:896] = out_weight_ref[:, 256 * f : 256 * f + 256].astype(BF)


def kernel_picks(rank_ref, gate_ref, pick_ref, turned_ref, high_ref, rest_ref):
    slot = lax.broadcasted_iota(jnp.int32, (64, 128), 0).astype(F32)
    for p in range(16):
        picks, weights = [], []
        for e in (2 * p, 2 * p + 1):
            hit = slot == rank_ref[e : e + 1, :]
            picks.append(jnp.where(hit, 1.0, 0.0))
            weights.append(jnp.where(hit, gate_ref[e : e + 1, :], 0.0))
        picks = jnp.concatenate(picks, axis=0)
        weights = jnp.transpose(jnp.concatenate(weights, axis=0))
        at = slice(128 * p, 128 * p + 128)
        pick_ref[at, :] = picks.astype(BF)
        turned_ref[:, at] = jnp.transpose(picks).astype(BF)
        high = weights.astype(BF)
        high_ref[:, at] = high
        rest_ref[:, at] = (weights - high.astype(F32)).astype(BF)


def kernel_project(
    part_ref, x0_ref, x1_ref, x2_ref, x3_ref, w_ref, cos_ref, sin_ref, msg_ref, hidden_ref, gains_ref
):
    gains = jnp.transpose(w_ref[:, 512:640].astype(F32))
    gains_ref[...] = gains[:8]
    for r, x_ref in enumerate((x0_ref, x1_ref, x2_ref, x3_ref)):
        x = x_ref[...].astype(F32)
        scale = lax.rsqrt(jnp.mean(x * x, axis=-1, keepdims=True) + EPSILON)
        hidden_ref[place(part_ref, r, 128), :] = (x * scale * gains[0:1]).astype(BF)
    proj = mm(hidden_ref[...], w_ref[:, 0:512])
    ahead = pltpu.roll(proj, 512 - 8, 1)
    behind = pltpu.roll(proj, 8, 1)
    partner = jnp.where((lane((512, 512)) // 8) % 2 == 0, ahead, behind)
    cos = jnp.concatenate([cos_ref[...]] * 4, axis=0)
    sin = jnp.concatenate([sin_ref[...]] * 4, axis=0)
    turned = proj * cos + partner * sin
    low = lane((64, 128)) < 64
    for s in range(4):
        for p in range(4):
            front = turned[128 * s : 128 * s + 64, 128 * p : 128 * p + 128]
            back = turned[128 * s + 64 : 128 * s + 128, 128 * p : 128 * p + 128]
            msg_ref[8 * p + s] = jnp.where(low, front, pltpu.roll(back, 64, 1)).astype(BF)
            msg_ref[8 * p + 4 + s] = jnp.where(low, pltpu.roll(front, 64, 1), back).astype(BF)


def kernel_heads(msg_ref, table_ref, kv_ref, q_ref):
    out = jnp.zeros((512, 768), F32)
    for f in range(4):
        out = out + mm(msg_ref[:, f].reshape(512, 128), table_ref[f])
    pairs = out[:, 0:256].astype(BF)
    for half in range(2):
        block = pairs[:, 128 * half : 128 * half + 128]
        for y in range(4):
            kv_ref[y, 512 * half : 512 * half + 512, :] = block
    queries = (out[:, 256:768] * 0.125).astype(BF)
    for half in range(2):
        for head in range(2):
            at = 256 * half + 128 * head
            q_ref[half, :, head] = queries[:, at : at + 128].reshape(8, 64, 128)


CHUNKS = (1, 2, 3, 4, 8, 7, 6, 5)


def tile_positions(tile, mine):
    front = tile < 4
    i = jnp.where(front, tile, tile - 4)
    q = lane((1, 256))
    k = lax.broadcasted_iota(jnp.int32, (512, 1), 0)
    q_front = (8 * i + 4 * (q // 128) + mine) * 64 + q % 64
    q_back = (63 - 8 * i - 4 * (q // 128) - mine) * 64 + q % 64
    k_front = 512 * i + k
    k_back = (59 - 8 * i + 4 * (k // 256) - (k % 256) // 64) * 64 + k % 64
    return jnp.where(front, q_front, q_back), jnp.where(front, k_front, k_back)


def kernel_attend(mine_ref, kv_ref, q_ref, msg_ref, log_ref, out_ref, keys_ref, turned_ref):
    tile = pl.program_id(0)

    @pl.when(tile == 0)
    def _():
        for group in range(16):
            half, place = (0, group) if group < 8 else (1, 15 - group)
            for y in range(4):
                at = 256 * group + 64 * y
                keys_ref[at : at + 64, :] = kv_ref[y, half, place]
        for c in range(8):
            turned_ref[:, 512 * c : 512 * c + 512] = jnp.transpose(
                keys_ref[512 * c : 512 * c + 512, :].astype(F32)
            ).astype(BF)

    q = q_ref[...]
    q_pos, k_pos = tile_positions(tile, mine_ref[0])

    def run(count):
        peak = jnp.full((1, 256), MASKED, F32)
        total = jnp.zeros((1, 256), F32)
        mixed = jnp.zeros((64, 256), F32)
        later = mm(keys_ref[0:512, :], q, NT)
        for c in range(count):
            scores = later
            if c + 1 < count:
                later = mm(keys_ref[512 * c + 512 : 512 * c + 1024, :], q, NT)
            else:
                scores = jnp.where(k_pos <= q_pos, scores, MASKED)
            higher = jnp.maximum(peak, jnp.max(scores, axis=0, keepdims=True))
            weights = jnp.exp(scores - higher)
            fade = jnp.exp(peak - higher)
            total = total * fade + jnp.sum(weights, axis=0, keepdims=True)
            mixed = mixed * fade + mm(
                turned_ref[64:128, 512 * c : 512 * c + 512], weights.astype(BF)
            )
            peak = higher
        log_ref[0] = jnp.broadcast_to(peak + jnp.log(total), (8, 256))
        mixed = mixed / total
        out = jnp.transpose(jnp.concatenate([jnp.zeros((64, 256), F32), mixed], axis=0))
        out_ref[...] = out
        low = lane((64, 128)) < 64
        for a in range(2):
            first = out[128 * a : 128 * a + 64]
            second = out[128 * a + 64 : 128 * a + 128]
            msg_ref[a, 0] = jnp.where(low, pltpu.roll(first, 64, 1), second).astype(BF)

    for t, count in enumerate(CHUNKS):
        pl.when(tile == t)(functools.partial(run, count))


def kernel_attend_back(
    mine_ref, keys_ref, turned_ref, q_ref, grad_ref, log_ref, out_ref, dq_ref, d0_ref, d1_ref, d2_ref, d3_ref, sum_ref
):
    tile = pl.program_id(0)

    @pl.when(tile == 0)
    def _():
        sum_ref[...] = jnp.zeros_like(sum_ref)

    q = q_ref[...]
    low = lane((64, 128)) < 64
    pieces = []
    for a in range(2):
        both = grad_ref[a, 0].astype(F32)
        pieces.append(jnp.where(low, 0.0, pltpu.roll(both, 64, 1)))
        pieces.append(jnp.where(low, 0.0, both))
    grad = jnp.concatenate(pieces, axis=0)
    delta = jnp.sum(jnp.transpose(grad * out_ref[...]), axis=0, keepdims=True)
    grad = grad.astype(BF)
    q_pos, k_pos = tile_positions(tile, mine_ref[0])
    log_total = log_ref[0][0:1]

    def step(c, dq, last):
        at = 512 * c
        keys = keys_ref[pl.ds(at, 512), :]
        scores = mm(keys, q, NT)
        if last:
            scores = jnp.where(k_pos <= q_pos, scores, MASKED)
        weights = jnp.exp(scores - log_total)
        slope = (weights * (mm(keys, grad, NT) - delta)).astype(BF)
        sum_ref[pl.ds(at, 512), :] += mm(slope, q) + mm(weights.astype(BF), grad)
        return dq + mm(turned_ref[0:64, pl.ds(at, 512)], slope)

    def run(count):
        dq = jnp.zeros((64, 256), F32)
        for c in range(count):
            dq = step(c, dq, c == count - 1)
        dq = jnp.concatenate([dq * 0.125, jnp.zeros((64, 256), F32)], axis=0)
        dq_ref[...] = jnp.transpose(dq)

    for t, count in enumerate(CHUNKS):
        pl.when(tile == t)(functools.partial(run, count))

    @pl.when(tile == 7)
    def _():
        for group in range(16):
            half, place = (0, group) if group < 8 else (1, 15 - group)
            for r, dkv_ref in enumerate((d0_ref, d1_ref, d2_ref, d3_ref)):
                at = 256 * group + 64 * lax.bitwise_xor(mine_ref[0], r)
                part = sum_ref[pl.ds(pl.multiple_of(at, 64), 64), :]
                dkv_ref[half, place] = part.astype(BF)


def kernel_middle(
    part_ref,
    o_ref,
    u0_ref,
    u1_ref,
    u2_ref,
    u3_ref,
    l0_ref,
    l1_ref,
    l2_ref,
    l3_ref,
    x_ref,
    gains_ref,
    pick_ref,
    slots_ref,
    mid_ref,
    rows_ref,
    hidden_ref,
):
    @pl.when(pl.program_id(0) == 0)
    def _():
        for g in range(8):
            rows_ref[:, 128 * g : 128 * g + 128] = o_ref[g].reshape(128, 128)
        uppers = (u0_ref, u1_ref, u2_ref, u3_ref)
        lowers = (l0_ref, l1_ref, l2_ref, l3_ref)
        for r in range(4):
            at = place(part_ref, r, 256)
            mid_ref[:, at] = (
                x_ref[:, at].astype(F32)
                + mm(rows_ref[:, 0:512], uppers[r][...])
                + mm(rows_ref[:, 512:1024], lowers[r][...])
            )
        mid = mid_ref[...]
        scale = lax.rsqrt(jnp.mean(mid * mid, axis=-1, keepdims=True) + EPSILON)
        hidden_ref[...] = (mid * scale * gains_ref[1:2]).astype(BF)

    for c in range(4):
        at = slice(256 * c, 256 * c + 256)
        rows = mm(pick_ref[...], hidden_ref[:, at]).astype(BF)
        slots_ref[:, :, at] = rows.reshape(16, 64, 256)


def kernel_experts_ready(
    part_ref,
    dy_ref,
    parts_ref,
    w0_ref,
    w1_ref,
    w2_ref,
    w3_ref,
    dys_ref,
    dact_ref,
    v_ref,
    gu_ref,
    rank_ref,
    gate_ref,
):
    step = pl.program_id(0)

    @pl.when(step == 0)
    def _():
        for r, w_ref in enumerate((w0_ref, w1_ref, w2_ref, w3_ref)):
            gu_ref[place(part_ref, r, 256), :] = w_ref[0:256, :]
            v_ref[place(part_ref, r, 128), :] = w_ref[256:384, :]
        before = jnp.where(row((128, 128)) < lane((128, 128)), 1.0, 0.0).astype(BF)
        parts = [parts_ref[:, k, :].astype(F32) for k in range(6)]
        even = parts[0] + parts[2] + parts[4]
        odd = parts[1] + parts[3] + parts[5]
        gate_ref[...] = jnp.where(lane((32, 128)) < 64, pltpu.roll(even, 64, 1), odd)
        chosen = gate_ref[...] > 0.0
        rank = mm(jnp.where(chosen, 1.0, 0.0).astype(BF), before)
        rank_ref[...] = jnp.where(chosen, rank, -1.0)

    slot = lax.broadcasted_iota(jnp.int32, (64, 128), 0).astype(F32)
    grads = []
    for j in range(4):
        source = 4 * step + j
        pick = slot == rank_ref[pl.ds(source, 1), :]
        weight = jnp.sum(
            jnp.where(pick, gate_ref[pl.ds(source, 1), :], 0.0), axis=1, keepdims=True
        )
        rows = mm(jnp.where(pick, 1.0, 0.0).astype(BF), dy_ref[0, j, 0])
        grads.append((rows * weight).astype(BF))
    dys = jnp.concatenate(grads, axis=0)
    dys_ref[...] = dys.reshape(4, 64, WIDTH)
    dact_ref[...] = mm(dys, v_ref[...], NT)


def kernel_experts(h_ref, gu_ref, dact_ref, act_ref, dboth_ref, dxs_ref):
    both = mm(h_ref[...].reshape(512, WIDTH), gu_ref[...])
    gate_h, up_h = both[:, :512], both[:, 512:]
    sig = jax.nn.sigmoid(gate_h)
    swished = gate_h * sig
    act_ref[...] = (swished * up_h).astype(BF)
    dact = dact_ref[...]
    dgate = (dact * up_h * sig * (1.0 + gate_h * (1.0 - sig))).astype(BF)
    dup = (dact * swished).astype(BF)
    dboth = jnp.concatenate([dgate, dup], axis=1)
    dboth_ref[...] = dboth
    dxs_ref[...] = mm(dboth, gu_ref[...], NT).astype(BF).reshape(8, 64, WIDTH)


def kernel_experts_after(
    h_ref, act_ref, dys_ref, dboth_ref, v_ref, ys_ref, grad_ref, ggu_ref, gv_ref
):
    step = pl.program_id(0)

    @pl.when(step == 0)
    def _():
        ggu_ref[...] = jnp.zeros_like(ggu_ref)
        gv_ref[...] = jnp.zeros_like(gv_ref)

    act = act_ref[...]
    ys_ref[...] = mm(act, v_ref[...]).astype(BF).reshape(4, 64, WIDTH)
    ggu_ref[...] += mm(h_ref[...].reshape(256, WIDTH), dboth_ref[...], TN)
    gv_ref[...] += mm(act, dys_ref[...].reshape(256, WIDTH), TN)

    @pl.when(step == 7)
    def _():
        for f in range(4):
            grad_ref[f, 0:256, :] = ggu_ref[256 * f : 256 * f + 256, :].astype(BF)
            grad_ref[f, 256:384, :] = gv_ref[128 * f : 128 * f + 128, :].astype(BF)


def kernel_middle_back(
    part_ref,
    dxs_ref,
    pick_ref,
    mid_ref,
    cot_ref,
    gains_ref,
    u0_ref,
    u1_ref,
    u2_ref,
    u3_ref,
    l0_ref,
    l1_ref,
    l2_ref,
    l3_ref,
    dmid_ref,
    parts_ref,
    msg_ref,
    ggain_ref,
    sum_ref,
    low_ref,
):
    step = pl.program_id(0)
    part = mm(pick_ref[...], dxs_ref[...].reshape(1024, WIDTH))

    @pl.when(step == 0)
    def _():
        sum_ref[...] = part

    @pl.when(step > 0)
    def _():
        sum_ref[...] += part

    @pl.when(step == 1)
    def _():
        mid = mid_ref[...]
        scale = lax.rsqrt(jnp.mean(mid * mid, axis=-1, keepdims=True) + EPSILON)
        dh = sum_ref[...]
        ggain_ref[...] = jnp.broadcast_to(
            jnp.sum(dh * (mid * scale), axis=0, keepdims=True), (8, WIDTH)
        )
        dn = dh * gains_ref[1:2]
        dmid = (
            cot_ref[...].astype(F32)
            + scale * dn
            - mid * (scale * scale * scale) * jnp.mean(dn * mid, axis=-1, keepdims=True)
        )
        dmid_ref[...] = dmid
        low_ref[...] = dmid.astype(BF)
        uppers = (u0_ref, u1_ref, u2_ref, u3_ref)
        lowers = (l0_ref, l1_ref, l2_ref, l3_ref)
        for r in range(4):
            parts_ref[r] = low_ref[:, place(part_ref, r, 256)]
        for h, w_refs in enumerate((uppers, lowers)):
            grad = mm(parts_ref[0], w_refs[0][...], NT)
            for r in range(1, 4):
                grad = grad + mm(parts_ref[r], w_refs[r][...], NT)
            grad = grad.astype(BF)
            for g in range(4):
                msg_ref[4 * h + g] = grad[:, 128 * g : 128 * g + 128].reshape(2, 64, 128)


def kernel_out_weight(
    o0_ref, o1_ref, o2_ref, o3_ref, da0_ref, da1_ref, da2_ref, da3_ref, gain_ref, grad_ref
):
    which = lax.broadcasted_iota(jnp.int32, (128, WIDTH), 0)
    grad_ref[:, 0:128] = jnp.transpose(jnp.where(which == 1, gain_ref[0:1], 0.0)).astype(BF)
    pairs = ((o0_ref, da0_ref), (o1_ref, da1_ref), (o2_ref, da2_ref), (o3_ref, da3_ref))
    for g in range(8):
        part = jnp.zeros((128, 256), F32)
        for o_ref, da_ref in pairs:
            part = part + mm(o_ref[g].reshape(128, 128), da_ref[...], TN)
        grad_ref[128 * g : 128 * g + 128, 128:384] = part.astype(BF)


def kernel_slices_back(
    d0_ref, d1_ref, d2_ref, d3_ref, dq_ref, cos_ref, sin_ref, table_ref, msg_ref
):
    def unrotate(w, cos, sin):
        partner = jnp.where(
            lane(w.shape) % 64 < 32, pltpu.roll(w, 96, 1), pltpu.roll(w, 32, 1)
        )
        return (w * cos - partner * sin).astype(BF)

    parts = []
    for half in range(2):
        at = slice(512 * half, 512 * half + 512)
        dkv = d0_ref[half].reshape(512, 128).astype(F32)
        for d_ref in (d1_ref, d2_ref, d3_ref):
            dkv = dkv + d_ref[half].reshape(512, 128).astype(F32)
        parts.append(unrotate(dkv, cos_ref[at, :], sin_ref[at, :]))
    for half in range(2):
        at = slice(512 * half, 512 * half + 512)
        for head in range(2):
            parts.append(
                unrotate(dq_ref[half, :, head].reshape(512, 128), cos_ref[at, :], sin_ref[at, :])
            )
    whole = jnp.concatenate(parts, axis=1)
    for f in range(4):
        msg_ref[:, f] = mm(whole, table_ref[f], NT).astype(BF).reshape(8, 64, 128)


def kernel_hidden_grad(part_ref, d_ref, w_ref, h0_ref, h1_ref, h2_ref, h3_ref):
    for r, h_ref in enumerate((h0_ref, h1_ref, h2_ref, h3_ref)):
        h_ref[...] = mm(d_ref[place(part_ref, r, 128), :], w_ref[:, 0:512], NT).astype(BF)


def kernel_grads(msg_ref, hidden_ref, w_ref, rest_ref, grads_ref, d_ref):
    low = lane((64, 128)) < 64
    for s in range(4):
        for p in range(4):
            even = msg_ref[8 * p + s].astype(F32)
            odd = msg_ref[8 * p + 4 + s].astype(F32)
            d_ref[128 * s : 128 * s + 64, 128 * p : 128 * p + 128] = jnp.where(
                low, even, pltpu.roll(odd, 64, 1)
            ).astype(BF)
            d_ref[128 * s + 64 : 128 * s + 128, 128 * p : 128 * p + 128] = jnp.where(
                low, pltpu.roll(even, 64, 1), odd
            ).astype(BF)
    total = mm(hidden_ref[...], d_ref[...], TN)
    grads_ref[:, 0:512] = total.astype(BF)
    gain = jnp.sum(total * w_ref[:, 0:512].astype(F32), axis=1, keepdims=True)
    gain = gain / w_ref[:, 512:640].astype(F32)[:, 0:1]
    rest = rest_ref[:, 0:128]
    grads_ref[:, 512:640] = jnp.where(lane((WIDTH, 128)) == 0, gain.astype(BF), rest)
    grads_ref[:, 640:896] = rest_ref[:, 128:384]


def kernel_input_grad(d0_ref, d1_ref, d2_ref, d3_ref, x_ref, dmid_ref, gains_ref, out_ref):
    dh = d0_ref[...].astype(F32)
    for d_ref in (d1_ref, d2_ref, d3_ref):
        dh = dh + d_ref[...].astype(F32)
    x = x_ref[...].astype(F32)
    scale = lax.rsqrt(jnp.mean(x * x, axis=-1, keepdims=True) + EPSILON)
    dn = dh * gains_ref[0:1]
    out_ref[...] = (
        dmid_ref[...]
        + scale * dn
        - x * (scale * scale * scale) * jnp.mean(dn * x, axis=-1, keepdims=True)
    )


def kernel_total(parts_ref, table_ref, qkv_ref, out_ref, gains_ref, sum_ref):
    total = parts_ref[0].astype(F32)
    for c in range(1, 32):
        total = total + parts_ref[c].astype(F32)
    sum_ref[...] = total
    rows = []
    for p in range(4):
        rows.append(
            jnp.concatenate([sum_ref[f, :, 128 * p : 128 * p + 128] for f in range(4)], axis=1)
        )
    rest = jnp.concatenate(rows, axis=0)
    parts = []
    for _ in range(3):
        part = rest.astype(BF)
        rest = rest - part.astype(F32)
        parts.append(part)
    whole = mm(jnp.concatenate(parts, axis=0), table_ref[...], NT)
    whole = whole[0:32] + whole[32:64] + whole[64:96]
    for p in range(4):
        piece = whole[8 * p : 8 * p + 8]
        qkv_ref[:, 256 * p : 256 * p + 256] = piece[:, 0:256]
        qkv_ref[:, 1024 + 128 * p : 1152 + 128 * p] = piece[:, 256:384]
        qkv_ref[:, 1536 + 128 * p : 1664 + 128 * p] = piece[:, 384:512]
    for f in range(4):
        out_ref[:, 256 * f : 256 * f + 256] = sum_ref[f, :, 640:896]
    gains_ref[...] = (
        sum_ref[0, :, 512:640]
        + sum_ref[1, :, 512:640]
        + sum_ref[2, :, 512:640]
        + sum_ref[3, :, 512:640]
    )


def kernel_output(ys_ref, high_ref, rest_ref, mid_ref, out_ref, sum_ref):
    step = pl.program_id(0)

    @pl.when(step == 0)
    def _():
        sum_ref[...] = mid_ref[...]

    ys = ys_ref[...].reshape(512, WIDTH)
    sum_ref[...] += mm(high_ref[...], ys) + mm(rest_ref[...], ys)

    @pl.when(step == 3)
    def _():
        out_ref[...] = sum_ref[...].astype(BF)


def angles(positions, features):
    frequency = ROPE_BASE ** (-(features.astype(F32) * 2.0 / 64))
    return positions.astype(F32)[:, None] * frequency[None, :]


def whole(shape):
    return pl.BlockSpec(shape, lambda t: (0,) * len(shape))


def exchange(value, axes):
    return lax.all_to_all(value, axes, split_axis=0, concat_axis=0, tiled=True)


def gather(value, axes):
    return lax.all_gather(value, axes, axis=0, tiled=True)


def after(value, marker):
    return lax.optimization_barrier((value, marker))[0]


def swap(value, axis):
    return lax.ppermute(value, axis, [(0, 1), (1, 0)])


def neighbours(value):
    return value, swap(value, "core"), swap(value, "zl")


def cross(parts, axes=FSDP):
    here = [parts[0]]
    for r in range(1, 4):
        here.append(lax.ppermute(parts[r], axes, [(i, i ^ r) for i in range(4)]))
    return here


def on_device(
    layer_input,
    routes,
    gates,
    cotangent,
    norm_attn,
    query_key_value_weight,
    output_weight,
    norm_ffn,
    exp_gate,
    exp_up,
    exp_down,
):
    mine = lax.axis_index("y")
    ctx_index = lax.axis_index(CTX)
    part_index = lax.axis_index(FSDP)
    mine_ref = mine.astype(jnp.int32).reshape(1)
    part_ref = part_index.astype(jnp.int32).reshape(1)
    x = layer_input.reshape(128, WIDTH)
    cot = cotangent.reshape(128, WIDTH)
    slice_table = jnp.asarray(slice_matrix(), BF)
    head_table = jnp.asarray(head_matrix(), BF)

    x_all = neighbours(x)
    rank, gate = call(
        kernel_route,
        (sds((32, 128), F32), sds((32, 128), F32)),
        (1e6, 1e5),
        in_specs=[VM, VM],
        out_specs=(VM, VM),
    )(routes.reshape(128, 8).T, gates.reshape(128, 8).T)
    which = lax.broadcasted_iota(jnp.int32, (8, 128), 1)
    gain_rows = jnp.where(
        which == 0, norm_attn[:, None], jnp.where(which == 1, norm_ffn[:, None], 0.0)
    )
    slices = call(
        kernel_slices,
        sds((32, 4, 8, 896), BF),
        (2e7, 3e6),
        in_specs=[VM] * 5,
        out_specs=VM,
    )(query_key_value_weight, gain_rows, slice_table, gate, output_weight)
    slices, rank, gate, x_all = lax.optimization_barrier((slices, rank, gate, x_all))
    x_all = x_all + (swap(x_all[2], "core"),)
    offset = jnp.arange(64, dtype=jnp.int32)
    token_pos = jnp.concatenate([ctx_index * 64 + offset, (63 - ctx_index) * 64 + offset])
    column = jnp.arange(512, dtype=jnp.int32)
    angle = angles(token_pos, 8 * part_index + column % 8)
    is_value = (column // 16) % 4 == 3
    sign = jnp.where((column // 8) % 2 == 0, -1.0, 1.0)
    cos_slice = jnp.where(is_value, 1.0, jnp.cos(angle))
    sin_slice = jnp.where(is_value, 0.0, jnp.sin(angle) * sign)
    w_slice = exchange(slices.reshape(128, 8, 896), ALL)
    w_slice, cos_slice, sin_slice = lax.optimization_barrier((w_slice, cos_slice, sin_slice))
    gate_parts = lax.dynamic_slice(
        w_slice.reshape(32, 4, 8, 896), (0, part_index, 0, 512), (32, 1, 8, 128)
    ).reshape(32, 8, 128)
    w_slice = w_slice.reshape(WIDTH, 896)
    picks, picks_turned, picks_high, picks_rest = call(
        kernel_picks,
        (sds((2048, 128), BF),) + (sds((128, 2048), BF),) * 3,
        (2e9, 4e6),
        in_specs=[VM, VM],
        out_specs=(VM,) * 4,
    )(rank, gate)

    msg, hidden, gains = call(
        kernel_project,
        (sds((32, 64, 128), BF), sds((512, WIDTH), BF), sds((8, WIDTH), F32)),
        (6e8, 4e6),
        in_specs=[SM] + [VM] * 7,
        out_specs=(VM, VM, VM),
    )(part_ref, *x_all, w_slice, cos_slice, sin_slice)
    across = swap(after(cot, w_slice), "zh")
    first = lax.axis_index("zh") == 0
    cot_pair = jnp.concatenate(
        [jnp.where(first, cot, across), jnp.where(first, across, cot)], axis=0
    )
    out_upper = neighbours(w_slice[0:512, 640:896])
    msg = exchange(msg, HEAD_AXES + FSDP)

    kv_copies, queries = call(
        kernel_heads,
        (sds((4, 1024, 128), BF), sds((2, 8, 2, 64, 128), BF)),
        (4e8, 3e6),
        in_specs=[VM, VM],
        out_specs=(VM, VM),
    )(msg.reshape(8, 4, 64, 128), head_table)
    queries = queries.reshape(2048, 128)
    kv_copies, out_upper = lax.optimization_barrier((kv_copies, out_upper))
    out_lower = neighbours(after(w_slice[512:1024, 640:896], msg))
    kv = exchange(kv_copies, ("y",)).reshape(4, 2, 8, 64, 128)
    expert_weights = jnp.concatenate(
        [jnp.concatenate([exp_gate[0], exp_up[0]], axis=1), exp_down[0]], axis=0
    ).astype(BF)
    block = 4 * jnp.arange(8, dtype=jnp.int32)[:, None] + mine
    quarter_pos = jnp.concatenate(
        [
            (block * 64 + offset[None, :]).reshape(-1),
            ((63 - block) * 64 + offset[None, :]).reshape(-1),
        ]
    )
    column = jnp.arange(128, dtype=jnp.int32)
    angle = angles(quarter_pos, column % 32)
    sign = jnp.where(column % 64 < 32, -1.0, 1.0)
    cos_heads = jnp.where(column >= 64, 1.0, jnp.cos(angle))
    sin_heads = jnp.where(column >= 64, 0.0, jnp.sin(angle) * sign)
    kv, out_lower, cos_heads, sin_heads = lax.optimization_barrier(
        (kv, out_lower, cos_heads, sin_heads)
    )
    experts_all = neighbours(after(expert_weights, msg))
    cot_all = gather(after(cot_pair, kv_copies), ("x", "y")).reshape(4, 4, 2, 128, WIDTH)
    out_upper = out_upper + (swap(after(out_upper[2], kv), "core"),)
    out_lower = out_lower + (swap(out_lower[2], "core"),)
    w_out = (*out_upper, *out_lower)
    msg_spec = pl.BlockSpec((2, 1, 64, 128), lambda t: (t % 4, t // 4, 0, 0))
    row_spec = pl.BlockSpec((256, 128), lambda t: (t, 0))
    log_spec = pl.BlockSpec((1, 8, 256), lambda t: (t, 0, 0))
    o_msg, log_total, o_rows, keys, turned = call(
        kernel_attend,
        (
            sds((8, 2, 64, 128), BF),
            sds((8, 8, 256), F32),
            sds((2048, 128), F32),
            sds((4096, 128), BF),
            sds((128, 4096), BF),
        ),
        (1e10, 5e6),
        grid=(8,),
        in_specs=[SM, whole((4, 2, 8, 64, 128)), row_spec],
        out_specs=(msg_spec, log_spec, row_spec, whole((4096, 128)), whole((128, 4096))),
    )(mine_ref, kv, queries)
    o_msg, w_out, experts_all = lax.optimization_barrier((o_msg, w_out, experts_all))
    experts_all = experts_all + (swap(experts_all[2], "core"),)
    o_heads = exchange(o_msg, HEAD_AXES)

    slot_spec = pl.BlockSpec((4, 64, WIDTH), lambda t: (t, 0, 0))
    out_specs = [whole((512, 256))] * 8
    slots, mid = call(
        kernel_middle,
        (sds((32, 64, WIDTH), BF), sds((128, WIDTH), F32)),
        (9e8, 8e6),
        grid=(2,),
        in_specs=[SM, whole((8, 2, 64, 128))]
        + out_specs
        + [
            whole((128, WIDTH)),
            whole((8, WIDTH)),
            pl.BlockSpec((1024, 128), lambda t: (t, 0)),
        ],
        out_specs=(pl.BlockSpec((16, 64, WIDTH), lambda t: (t, 0, 0)), whole((128, WIDTH))),
        scratch_shapes=[pltpu.VMEM((128, WIDTH), BF), pltpu.VMEM((128, WIDTH), BF)],
    )(part_ref, o_heads, *w_out, x, gains, picks)
    cot_all = after(cot_all, mid)
    slots, experts_all = lax.optimization_barrier((slots, experts_all))
    o_all = neighbours(after(o_heads, mid))
    slots = exchange(slots, CTX)
    dys, dact, down, gate_up = call(
        kernel_experts_ready,
        (
            sds((32, 64, WIDTH), BF),
            sds((2048, 512), F32),
            sds((512, WIDTH), BF),
            sds((WIDTH, WIDTH), BF),
        ),
        (6e9, 2e7),
        grid=(8,),
        in_specs=[
            SM,
            pl.BlockSpec((1, 4, 1, 128, WIDTH), lambda t: (t // 2, 0, t % 2, 0, 0)),
            whole((32, 8, 128)),
        ]
        + [whole((384, WIDTH))] * 4,
        out_specs=(
            slot_spec,
            pl.BlockSpec((256, 512), lambda t: (t, 0)),
            whole((512, WIDTH)),
            whole((WIDTH, WIDTH)),
        ),
        scratch_shapes=[pltpu.VMEM((32, 128), F32), pltpu.VMEM((32, 128), F32)],
    )(part_ref, cot_all, gate_parts, *experts_all)
    act_spec = pl.BlockSpec((256, 512), lambda t: (t, 0))
    both_spec = pl.BlockSpec((256, WIDTH), lambda t: (t, 0))
    act, dboth, dxs = call(
        kernel_experts,
        (sds((2048, 512), BF), sds((2048, WIDTH), BF), sds((32, 64, WIDTH), BF)),
        (9e9, 2e7),
        grid=(4,),
        in_specs=[
            pl.BlockSpec((8, 64, WIDTH), lambda t: (t, 0, 0)),
            whole((WIDTH, WIDTH)),
            pl.BlockSpec((512, 512), lambda t: (t, 0)),
        ],
        out_specs=(
            pl.BlockSpec((512, 512), lambda t: (t, 0)),
            pl.BlockSpec((512, WIDTH), lambda t: (t, 0)),
            pl.BlockSpec((8, 64, WIDTH), lambda t: (t, 0, 0)),
        ),
    )(slots, gate_up, dact)
    ys, expert_grads = call(
        kernel_experts_after,
        (sds((32, 64, WIDTH), BF), sds((4, 384, WIDTH), BF)),
        (9e9, 2e7),
        grid=(8,),
        in_specs=[slot_spec, act_spec, slot_spec, both_spec, whole((512, WIDTH))],
        out_specs=(slot_spec, whole((4, 384, WIDTH))),
        scratch_shapes=[pltpu.VMEM((WIDTH, WIDTH), F32), pltpu.VMEM((512, WIDTH), F32)],
    )(slots, act, dys, dboth, down)
    dxs, o_all = lax.optimization_barrier((dxs, o_all))
    o_all = o_all + (swap(o_all[2], "core"),)
    dxs = exchange(dxs, CTX)
    expert_own = lax.psum_scatter(
        expert_grads.reshape(4 * 384, WIDTH), FSDP, scatter_dimension=0, tiled=True
    ).astype(F32)
    dxs, ys, o_all = lax.optimization_barrier((dxs, ys, o_all))

    dmid, da_parts, grad_msg, gain_ffn_part = call(
        kernel_middle_back,
        (
            sds((128, WIDTH), F32),
            sds((4, 128, 256), BF),
            sds((8, 2, 64, 128), BF),
            sds((8, WIDTH), F32),
        ),
        (9e8, 8e6),
        grid=(2,),
        in_specs=[
            SM,
            pl.BlockSpec((16, 64, WIDTH), lambda t: (t, 0, 0)),
            pl.BlockSpec((128, 1024), lambda t: (0, t)),
            whole((128, WIDTH)),
            whole((128, WIDTH)),
            whole((8, WIDTH)),
        ]
        + out_specs,
        out_specs=(
            whole((128, WIDTH)),
            whole((4, 128, 256)),
            whole((8, 2, 64, 128)),
            whole((8, WIDTH)),
        ),
        scratch_shapes=[pltpu.VMEM((128, WIDTH), F32), pltpu.VMEM((128, WIDTH), BF)],
    )(part_ref, dxs, picks_turned, mid, cot, gains, *w_out)
    grad_heads = exchange(grad_msg, HEAD_AXES)
    ys, grad_heads = lax.optimization_barrier((ys, grad_heads))
    ys = exchange(ys, CTX)
    dq, *dkv = call(
        kernel_attend_back,
        (sds((2048, 128), F32),) + (sds((2, 8, 64, 128), BF),) * 4,
        (2e10, 7e6),
        grid=(8,),
        in_specs=[
            SM,
            whole((4096, 128)),
            whole((128, 4096)),
            row_spec,
            msg_spec,
            log_spec,
            row_spec,
        ],
        out_specs=(row_spec,) + (whole((2, 8, 64, 128)),) * 4,
        scratch_shapes=[pltpu.VMEM((4096, 128), F32)],
    )(mine_ref, keys, turned, queries, grad_heads, log_total, o_rows)
    da_here = cross(da_parts)
    dkv = cross(dkv, ("y",))
    dkv, ys, da_here = lax.optimization_barrier((dkv, ys, da_here))
    rest_part = call(
        kernel_out_weight,
        sds((WIDTH, 384), BF),
        (3e8, 2e6),
        in_specs=[VM] * 9,
        out_specs=VM,
    )(*o_all, *da_here, gain_ffn_part)
    layer_output = call(
        kernel_output,
        sds((128, WIDTH), BF),
        (1e9, 5e6),
        grid=(4,),
        in_specs=[
            pl.BlockSpec((8, 64, WIDTH), lambda t: (t, 0, 0)),
            pl.BlockSpec((128, 512), lambda t: (0, t)),
            pl.BlockSpec((128, 512), lambda t: (0, t)),
            whole((128, WIDTH)),
        ],
        out_specs=whole((128, WIDTH)),
        scratch_shapes=[pltpu.VMEM((128, WIDTH), F32)],
    )(ys, picks_high, picks_rest, mid)

    back = call(
        kernel_slices_back,
        sds((8, 4, 64, 128), BF),
        (4e8, 5e6),
        in_specs=[VM] * 8,
        out_specs=VM,
    )(*dkv, dq.reshape(2, 8, 2, 64, 128), cos_heads, sin_heads, head_table)
    back = exchange(back.reshape(32, 64, 128), HEAD_AXES + FSDP)

    grads, d_all = call(
        kernel_grads,
        (sds((WIDTH, 896), BF), sds((512, 512), BF)),
        (6e8, 5e6),
        in_specs=[VM] * 4,
        out_specs=(VM, VM),
    )(back, hidden, w_slice, rest_part)
    dh_parts = call(
        kernel_hidden_grad,
        (sds((128, WIDTH), BF),) * 4,
        (6e8, 5e6),
        in_specs=[SM, VM, VM],
        out_specs=(VM,) * 4,
    )(part_ref, d_all, w_slice)
    grads = exchange(grads.reshape(128, 8, 896), ALL)
    grad_qkv, grad_out, grad_gains = call(
        kernel_total,
        (sds((8, 2048), F32), sds((8, WIDTH), F32), sds((8, 128), F32)),
        (1e8, 4e6),
        in_specs=[VM, VM],
        out_specs=(VM, VM, VM),
        scratch_shapes=[pltpu.VMEM((4, 8, 896), F32)],
    )(grads.reshape(32, 4, 8, 896), slice_table)
    dh_here = cross(dh_parts)
    input_grad = call(
        kernel_input_grad,
        sds((128, WIDTH), F32),
        (1e6, 2e6),
        in_specs=[VM] * 7,
        out_specs=VM,
    )(*after(dh_here, grad_qkv), x, dmid, gains)
    return (
        layer_output.reshape(layer_input.shape),
        input_grad.reshape(layer_input.shape),
        grad_gains[:, 0],
        grad_qkv,
        grad_out,
        grad_gains[:, 1],
        expert_own[0:256, 0:512][None],
        expert_own[0:256, 512:1024][None],
        expert_own[256:384][None],
    )


def solution(mesh):
    parts = Mesh(mesh.devices.reshape(4, 2, 4, 2, 2), ALL)
    tokens = P(FSDP, CTX, None, None, None, None)
    experts = P(CTX, FSDP, None)
    in_specs = (
        tokens,
        tokens,
        tokens,
        tokens,
        P(ALL),
        P(ALL, None),
        P(ALL, None),
        P(ALL),
        experts,
        experts,
        experts,
    )
    out_specs = (
        tokens,
        tokens,
        P(ALL),
        P(ALL, None),
        P(ALL, None),
        P(ALL),
        experts,
        experts,
        experts,
    )
    return jax.shard_map(
        on_device, mesh=parts, in_specs=in_specs, out_specs=out_specs, check_vma=False
    )
```

```python
import functools

import jax
import jax.numpy as jnp
import numpy as np
from jax import lax
from jax.experimental import pallas as pl
from jax.experimental.pallas import tpu as pltpu
from jax.sharding import Mesh
from jax.sharding import PartitionSpec as P

WIDTH = 1024
EPSILON = 1e-06
ROPE_BASE = 10000.0
MASKED = -1e30
BF = jnp.bfloat16
F32 = jnp.float32
CTX = ("x", "zh", "y")
HEAD_AXES = ("x", "zh")
FSDP = ("zl", "core")
ALL = CTX + FSDP
VMEM_LIMIT = 56 * 1024 * 1024

NT = (((1,), (1,)), ((), ()))
TN = (((0,), (0,)), ((), ()))


def mm(a, b, dims=None):
    if dims is None:
        return jnp.dot(a, b, preferred_element_type=F32)
    return lax.dot_general(a, b, dims, preferred_element_type=F32)


def lane(shape):
    return lax.broadcasted_iota(jnp.int32, shape, len(shape) - 1)


def row(shape):
    return lax.broadcasted_iota(jnp.int32, shape, len(shape) - 2)


def call(kernel, out_shape, cost, **kw):
    flops, bytes_accessed = cost
    return pl.pallas_call(
        kernel,
        out_shape=out_shape,
        compiler_params=pltpu.CompilerParams(vmem_limit_bytes=VMEM_LIMIT),
        cost_estimate=pl.CostEstimate(
            flops=int(flops), bytes_accessed=int(bytes_accessed), transcendentals=0
        ),
        **kw,
    )


def sds(shape, dtype):
    return jax.ShapeDtypeStruct(shape, dtype)


VM = pl.BlockSpec(memory_space=pltpu.VMEM)
SM = pl.BlockSpec(memory_space=pltpu.SMEM)


def slice_matrix():
    table = np.zeros((512, 512), np.float32)
    for k in range(512):
        section, place = k // 128, k % 128
        if section < 2:
            pair, part = section, place // 64
        else:
            pair, part = place // 64, section
        feat = place % 64
        f = (feat % 32) // 8
        column = pair * 64 + part * 16 + (feat // 32) * 8 + feat % 8
        table[k, f * 128 + column] = 1.0
    return table


def head_matrix():
    table = np.zeros((4, 128, 768), np.float32)
    for f in range(4):
        for block in range(2):
            for part in range(4):
                for j in range(16):
                    feat = (j // 8) * 32 + 8 * f + j % 8
                    source = block * 64 + part * 16 + j
                    if part == 2:
                        target = block * 128 + feat
                    elif part == 3:
                        target = block * 128 + 64 + feat
                    else:
                        target = 256 + block * 256 + part * 128 + feat
                    table[f, source, target] = 1.0
    return table


def place(part_ref, r, size):
    return pl.ds(pl.multiple_of(lax.bitwise_xor(part_ref[0], r) * size, size), size)


def kernel_route(picks_ref, gates_ref, rank_ref, gate_ref):
    experts = row((32, 128))
    gate = jnp.zeros((32, 128), F32)
    chosen = jnp.zeros((32, 128), F32)
    for k in range(8):
        hit = picks_ref[k : k + 1, :] == experts
        gate = gate + jnp.where(hit, gates_ref[k : k + 1, :], 0.0)
        chosen = chosen + jnp.where(hit, 1.0, 0.0)
    before = jnp.where(row((128, 128)) < lane((128, 128)), 1.0, 0.0).astype(BF)
    rank = mm(chosen.astype(BF), before)
    rank_ref[...] = jnp.where(chosen > 0.5, rank, -1.0)
    gate_ref[...] = gate


def kernel_slices(w_ref, gains_ref, table_ref, gate_ref, out_weight_ref, out_ref):
    w = w_ref[...].astype(BF).astype(F32)
    parts = []
    for p in range(4):
        parts.append(
            jnp.concatenate(
                [
                    w[:, 256 * p : 256 * p + 256],
                    w[:, 1024 + 128 * p : 1152 + 128 * p],
                    w[:, 1536 + 128 * p : 1664 + 128 * p],
                ],
                axis=1,
            )
        )
    stacked = jnp.concatenate(parts, axis=0).astype(BF)
    cut = mm(stacked, table_ref[...])
    columns = []
    for f in range(4):
        columns.append(
            jnp.concatenate(
                [cut[8 * p : 8 * p + 8, 128 * f : 128 * f + 128] for p in range(4)], axis=1
            ).astype(BF)
        )
    gains = gains_ref[...]
    left = lane((8, 128)) < 64
    sub = row((8, 128))
    for c in range(32):
        gate = gate_ref[c : c + 1, :]
        high = gate.astype(BF).astype(F32)
        middle = (gate - high).astype(BF).astype(F32)
        rest = gate - high - middle
        parts = jnp.where(
            sub < 2, high, jnp.where(sub < 4, middle, jnp.where(sub < 6, rest, 0.0))
        )
        parts = jnp.where(sub % 2 == 0, pltpu.roll(parts, 64, 1), parts)
        last = jnp.where(left, gains, parts).astype(BF)
        for f in range(4):
            out_ref[c, f, :, 0:512] = columns[f]
            out_ref[c, f, :, 512:640] = last
            out_ref[c, f, :, 640:896] = out_weight_ref[:, 256 * f : 256 * f + 256].astype(BF)


def kernel_picks(rank_ref, gate_ref, pick_ref, turned_ref, high_ref, rest_ref):
    slot = lax.broadcasted_iota(jnp.int32, (64, 128), 0).astype(F32)
    for p in range(16):
        picks, weights = [], []
        for e in (2 * p, 2 * p + 1):
            hit = slot == rank_ref[e : e + 1, :]
            picks.append(jnp.where(hit, 1.0, 0.0))
            weights.append(jnp.where(hit, gate_ref[e : e + 1, :], 0.0))
        picks = jnp.concatenate(picks, axis=0)
        weights = jnp.transpose(jnp.concatenate(weights, axis=0))
        at = slice(128 * p, 128 * p + 128)
        pick_ref[at, :] = picks.astype(BF)
        turned_ref[:, at] = jnp.transpose(picks).astype(BF)
        high = weights.astype(BF)
        high_ref[:, at] = high
        rest_ref[:, at] = (weights - high.astype(F32)).astype(BF)


def kernel_project(
    part_ref, x0_ref, x1_ref, x2_ref, x3_ref, w_ref, cos_ref, sin_ref, msg_ref, hidden_ref, gains_ref
):
    gains = jnp.transpose(w_ref[:, 512:640].astype(F32))
    gains_ref[...] = gains[:8]
    for r, x_ref in enumerate((x0_ref, x1_ref, x2_ref, x3_ref)):
        x = x_ref[...].astype(F32)
        scale = lax.rsqrt(jnp.mean(x * x, axis=-1, keepdims=True) + EPSILON)
        hidden_ref[place(part_ref, r, 128), :] = (x * scale * gains[0:1]).astype(BF)
    proj = mm(hidden_ref[...], w_ref[:, 0:512])
    ahead = pltpu.roll(proj, 512 - 8, 1)
    behind = pltpu.roll(proj, 8, 1)
    partner = jnp.where((lane((512, 512)) // 8) % 2 == 0, ahead, behind)
    cos = jnp.concatenate([cos_ref[...]] * 4, axis=0)
    sin = jnp.concatenate([sin_ref[...]] * 4, axis=0)
    turned = proj * cos + partner * sin
    low = lane((64, 128)) < 64
    for s in range(4):
        for p in range(4):
            front = turned[128 * s : 128 * s + 64, 128 * p : 128 * p + 128]
            back = turned[128 * s + 64 : 128 * s + 128, 128 * p : 128 * p + 128]
            msg_ref[8 * p + s] = jnp.where(low, front, pltpu.roll(back, 64, 1)).astype(BF)
            msg_ref[8 * p + 4 + s] = jnp.where(low, pltpu.roll(front, 64, 1), back).astype(BF)


def kernel_heads(msg_ref, table_ref, kv_ref, q_ref):
    out = jnp.zeros((512, 768), F32)
    for f in range(4):
        out = out + mm(msg_ref[:, f].reshape(512, 128), table_ref[f])
    pairs = out[:, 0:256].astype(BF)
    for half in range(2):
        block = pairs[:, 128 * half : 128 * half + 128]
        for y in range(4):
            kv_ref[y, 512 * half : 512 * half + 512, :] = block
    queries = (out[:, 256:768] * 0.125).astype(BF)
    for half in range(2):
        for head in range(2):
            at = 256 * half + 128 * head
            q_ref[half, :, head] = queries[:, at : at + 128].reshape(8, 64, 128)


CHUNKS = (1, 2, 3, 4, 8, 7, 6, 5)


def tile_positions(tile, mine):
    front = tile < 4
    i = jnp.where(front, tile, tile - 4)
    q = lane((1, 256))
    k = lax.broadcasted_iota(jnp.int32, (512, 1), 0)
    q_front = (8 * i + 4 * (q // 128) + mine) * 64 + q % 64
    q_back = (63 - 8 * i - 4 * (q // 128) - mine) * 64 + q % 64
    k_front = 512 * i + k
    k_back = (59 - 8 * i + 4 * (k // 256) - (k % 256) // 64) * 64 + k % 64
    return jnp.where(front, q_front, q_back), jnp.where(front, k_front, k_back)


def kernel_attend(mine_ref, kv_ref, q_ref, msg_ref, log_ref, out_ref, keys_ref, turned_ref):
    tile = pl.program_id(0)

    @pl.when(tile == 0)
    def _():
        for group in range(16):
            half, place = (0, group) if group < 8 else (1, 15 - group)
            for y in range(4):
                at = 256 * group + 64 * y
                keys_ref[at : at + 64, :] = kv_ref[y, half, place]
        for c in range(8):
            turned_ref[:, 512 * c : 512 * c + 512] = jnp.transpose(
                keys_ref[512 * c : 512 * c + 512, :].astype(F32)
            ).astype(BF)

    q = q_ref[...]
    q_pos, k_pos = tile_positions(tile, mine_ref[0])

    def run(count):
        peak = jnp.full((1, 256), MASKED, F32)
        total = jnp.zeros((1, 256), F32)
        mixed = jnp.zeros((64, 256), F32)
        later = mm(keys_ref[0:512, :], q, NT)
        for c in range(count):
            scores = later
            if c + 1 < count:
                later = mm(keys_ref[512 * c + 512 : 512 * c + 1024, :], q, NT)
            else:
                scores = jnp.where(k_pos <= q_pos, scores, MASKED)
            higher = jnp.maximum(peak, jnp.max(scores, axis=0, keepdims=True))
            weights = jnp.exp(scores - higher)
            fade = jnp.exp(peak - higher)
            total = total * fade + jnp.sum(weights, axis=0, keepdims=True)
            mixed = mixed * fade + mm(
                turned_ref[64:128, 512 * c : 512 * c + 512], weights.astype(BF)
            )
            peak = higher
        log_ref[0] = jnp.broadcast_to(peak + jnp.log(total), (8, 256))
        mixed = mixed / total
        out = jnp.transpose(jnp.concatenate([jnp.zeros((64, 256), F32), mixed], axis=0))
        out_ref[...] = out
        low = lane((64, 128)) < 64
        for a in range(2):
            first = out[128 * a : 128 * a + 64]
            second = out[128 * a + 64 : 128 * a + 128]
            msg_ref[a, 0] = jnp.where(low, pltpu.roll(first, 64, 1), second).astype(BF)

    for t, count in enumerate(CHUNKS):
        pl.when(tile == t)(functools.partial(run, count))


def kernel_attend_back(
    mine_ref, keys_ref, turned_ref, q_ref, grad_ref, log_ref, out_ref, dq_ref, d0_ref, d1_ref, d2_ref, d3_ref, sum_ref
):
    tile = pl.program_id(0)

    @pl.when(tile == 0)
    def _():
        sum_ref[...] = jnp.zeros_like(sum_ref)

    q = q_ref[...]
    low = lane((64, 128)) < 64
    pieces = []
    for a in range(2):
        both = grad_ref[a, 0].astype(F32)
        pieces.append(jnp.where(low, 0.0, pltpu.roll(both, 64, 1)))
        pieces.append(jnp.where(low, 0.0, both))
    grad = jnp.concatenate(pieces, axis=0)
    delta = jnp.sum(jnp.transpose(grad * out_ref[...]), axis=0, keepdims=True)
    grad = grad.astype(BF)
    q_pos, k_pos = tile_positions(tile, mine_ref[0])
    log_total = log_ref[0][0:1]

    def step(c, dq, last):
        at = pl.ds(pl.multiple_of(c * 512, 512), 512)
        keys = keys_ref[at, :]
        scores = mm(keys, q, NT)
        if last:
            scores = jnp.where(k_pos <= q_pos, scores, MASKED)
        weights = jnp.exp(scores - log_total)
        slope = (weights * (mm(keys, grad, NT) - delta)).astype(BF)
        sum_ref[at, :] += mm(slope, q) + mm(weights.astype(BF), grad)
        return dq + mm(turned_ref[0:64, at], slope)

    count = jnp.where(tile < 4, tile + 1, 12 - tile)
    dq = lax.fori_loop(0, count - 1, lambda c, v: step(c, v, False), jnp.zeros((64, 256), F32))
    dq = step(count - 1, dq, True)
    dq_ref[...] = jnp.transpose(jnp.concatenate([dq * 0.125, jnp.zeros((64, 256), F32)], axis=0))

    @pl.when(tile == 7)
    def _():
        for group in range(16):
            half, place = (0, group) if group < 8 else (1, 15 - group)
            for r, dkv_ref in enumerate((d0_ref, d1_ref, d2_ref, d3_ref)):
                at = 256 * group + 64 * lax.bitwise_xor(mine_ref[0], r)
                part = sum_ref[pl.ds(pl.multiple_of(at, 64), 64), :]
                dkv_ref[half, place] = part.astype(BF)


def kernel_middle(
    part_ref,
    o_ref,
    u0_ref,
    u1_ref,
    u2_ref,
    u3_ref,
    l0_ref,
    l1_ref,
    l2_ref,
    l3_ref,
    x_ref,
    gains_ref,
    pick_ref,
    slots_ref,
    mid_ref,
    rows_ref,
    hidden_ref,
):
    @pl.when(pl.program_id(0) == 0)
    def _():
        for g in range(8):
            rows_ref[:, 128 * g : 128 * g + 128] = o_ref[g].reshape(128, 128)
        uppers = (u0_ref, u1_ref, u2_ref, u3_ref)
        lowers = (l0_ref, l1_ref, l2_ref, l3_ref)
        for r in range(4):
            at = place(part_ref, r, 256)
            mid_ref[:, at] = (
                x_ref[:, at].astype(F32)
                + mm(rows_ref[:, 0:512], uppers[r][...])
                + mm(rows_ref[:, 512:1024], lowers[r][...])
            )
        mid = mid_ref[...]
        scale = lax.rsqrt(jnp.mean(mid * mid, axis=-1, keepdims=True) + EPSILON)
        hidden_ref[...] = (mid * scale * gains_ref[1:2]).astype(BF)

    for c in range(4):
        at = slice(256 * c, 256 * c + 256)
        rows = mm(pick_ref[...], hidden_ref[:, at]).astype(BF)
        slots_ref[:, :, at] = rows.reshape(16, 64, 256)


def kernel_experts_ready(
    part_ref,
    dy_ref,
    parts_ref,
    w0_ref,
    w1_ref,
    w2_ref,
    w3_ref,
    dys_ref,
    dact_ref,
    v_ref,
    gu_ref,
    rank_ref,
    gate_ref,
):
    step = pl.program_id(0)

    @pl.when(step == 0)
    def _():
        for r, w_ref in enumerate((w0_ref, w1_ref, w2_ref, w3_ref)):
            gu_ref[place(part_ref, r, 256), :] = w_ref[0:256, :]
            v_ref[place(part_ref, r, 128), :] = w_ref[256:384, :]
        before = jnp.where(row((128, 128)) < lane((128, 128)), 1.0, 0.0).astype(BF)
        parts = [parts_ref[:, k, :].astype(F32) for k in range(6)]
        even = parts[0] + parts[2] + parts[4]
        odd = parts[1] + parts[3] + parts[5]
        gate_ref[...] = jnp.where(lane((32, 128)) < 64, pltpu.roll(even, 64, 1), odd)
        chosen = gate_ref[...] > 0.0
        rank = mm(jnp.where(chosen, 1.0, 0.0).astype(BF), before)
        rank_ref[...] = jnp.where(chosen, rank, -1.0)

    slot = lax.broadcasted_iota(jnp.int32, (64, 128), 0).astype(F32)
    grads = []
    for j in range(4):
        source = 4 * step + j
        pick = slot == rank_ref[pl.ds(source, 1), :]
        weight = jnp.sum(
            jnp.where(pick, gate_ref[pl.ds(source, 1), :], 0.0), axis=1, keepdims=True
        )
        rows = mm(jnp.where(pick, 1.0, 0.0).astype(BF), dy_ref[0, j, 0])
        grads.append((rows * weight).astype(BF))
    dys = jnp.concatenate(grads, axis=0)
    dys_ref[...] = dys.reshape(4, 64, WIDTH)
    dact_ref[...] = mm(dys, v_ref[...], NT)


def kernel_experts(h_ref, gu_ref, dact_ref, act_ref, dboth_ref, dxs_ref):
    both = mm(h_ref[...].reshape(512, WIDTH), gu_ref[...])
    gate_h, up_h = both[:, :512], both[:, 512:]
    sig = jax.nn.sigmoid(gate_h)
    swished = gate_h * sig
    act_ref[...] = (swished * up_h).astype(BF)
    dact = dact_ref[...]
    dgate = (dact * up_h * sig * (1.0 + gate_h * (1.0 - sig))).astype(BF)
    dup = (dact * swished).astype(BF)
    dboth = jnp.concatenate([dgate, dup], axis=1)
    dboth_ref[...] = dboth
    dxs_ref[...] = mm(dboth, gu_ref[...], NT).astype(BF).reshape(8, 64, WIDTH)


def kernel_experts_after(
    h_ref, act_ref, dys_ref, dboth_ref, v_ref, ys_ref, grad_ref, ggu_ref, gv_ref
):
    step = pl.program_id(0)

    @pl.when(step == 0)
    def _():
        ggu_ref[...] = jnp.zeros_like(ggu_ref)
        gv_ref[...] = jnp.zeros_like(gv_ref)

    act = act_ref[...]
    ys_ref[...] = mm(act, v_ref[...]).astype(BF).reshape(4, 64, WIDTH)
    ggu_ref[...] += mm(h_ref[...].reshape(256, WIDTH), dboth_ref[...], TN)
    gv_ref[...] += mm(act, dys_ref[...].reshape(256, WIDTH), TN)

    @pl.when(step == 7)
    def _():
        for f in range(4):
            grad_ref[f, 0:256, :] = ggu_ref[256 * f : 256 * f + 256, :].astype(BF)
            grad_ref[f, 256:384, :] = gv_ref[128 * f : 128 * f + 128, :].astype(BF)


def kernel_middle_back(
    part_ref,
    dxs_ref,
    pick_ref,
    mid_ref,
    cot_ref,
    gains_ref,
    u0_ref,
    u1_ref,
    u2_ref,
    u3_ref,
    l0_ref,
    l1_ref,
    l2_ref,
    l3_ref,
    dmid_ref,
    parts_ref,
    msg_ref,
    ggain_ref,
    sum_ref,
    low_ref,
):
    step = pl.program_id(0)
    part = mm(pick_ref[...], dxs_ref[...].reshape(1024, WIDTH))

    @pl.when(step == 0)
    def _():
        sum_ref[...] = part

    @pl.when(step > 0)
    def _():
        sum_ref[...] += part

    @pl.when(step == 1)
    def _():
        mid = mid_ref[...]
        scale = lax.rsqrt(jnp.mean(mid * mid, axis=-1, keepdims=True) + EPSILON)
        dh = sum_ref[...]
        ggain_ref[...] = jnp.broadcast_to(
            jnp.sum(dh * (mid * scale), axis=0, keepdims=True), (8, WIDTH)
        )
        dn = dh * gains_ref[1:2]
        dmid = (
            cot_ref[...].astype(F32)
            + scale * dn
            - mid * (scale * scale * scale) * jnp.mean(dn * mid, axis=-1, keepdims=True)
        )
        dmid_ref[...] = dmid
        low_ref[...] = dmid.astype(BF)
        uppers = (u0_ref, u1_ref, u2_ref, u3_ref)
        lowers = (l0_ref, l1_ref, l2_ref, l3_ref)
        for r in range(4):
            parts_ref[r] = low_ref[:, place(part_ref, r, 256)]
        for h, w_refs in enumerate((uppers, lowers)):
            grad = mm(parts_ref[0], w_refs[0][...], NT)
            for r in range(1, 4):
                grad = grad + mm(parts_ref[r], w_refs[r][...], NT)
            grad = grad.astype(BF)
            for g in range(4):
                msg_ref[4 * h + g] = grad[:, 128 * g : 128 * g + 128].reshape(2, 64, 128)


def kernel_out_weight(
    o0_ref, o1_ref, o2_ref, o3_ref, da0_ref, da1_ref, da2_ref, da3_ref, gain_ref, grad_ref
):
    which = lax.broadcasted_iota(jnp.int32, (128, WIDTH), 0)
    grad_ref[:, 0:128] = jnp.transpose(jnp.where(which == 1, gain_ref[0:1], 0.0)).astype(BF)
    pairs = ((o0_ref, da0_ref), (o1_ref, da1_ref), (o2_ref, da2_ref), (o3_ref, da3_ref))
    for g in range(8):
        part = jnp.zeros((128, 256), F32)
        for o_ref, da_ref in pairs:
            part = part + mm(o_ref[g].reshape(128, 128), da_ref[...], TN)
        grad_ref[128 * g : 128 * g + 128, 128:384] = part.astype(BF)


def kernel_slices_back(
    d0_ref, d1_ref, d2_ref, d3_ref, dq_ref, cos_ref, sin_ref, table_ref, msg_ref
):
    def unrotate(w, cos, sin):
        partner = jnp.where(
            lane(w.shape) % 64 < 32, pltpu.roll(w, 96, 1), pltpu.roll(w, 32, 1)
        )
        return (w * cos - partner * sin).astype(BF)

    parts = []
    for half in range(2):
        at = slice(512 * half, 512 * half + 512)
        dkv = d0_ref[half].reshape(512, 128).astype(F32)
        for d_ref in (d1_ref, d2_ref, d3_ref):
            dkv = dkv + d_ref[half].reshape(512, 128).astype(F32)
        parts.append(unrotate(dkv, cos_ref[at, :], sin_ref[at, :]))
    for half in range(2):
        at = slice(512 * half, 512 * half + 512)
        for head in range(2):
            parts.append(
                unrotate(dq_ref[half, :, head].reshape(512, 128), cos_ref[at, :], sin_ref[at, :])
            )
    whole = jnp.concatenate(parts, axis=1)
    for f in range(4):
        msg_ref[:, f] = mm(whole, table_ref[f], NT).astype(BF).reshape(8, 64, 128)


def kernel_hidden_grad(part_ref, d_ref, w_ref, h0_ref, h1_ref, h2_ref, h3_ref):
    for r, h_ref in enumerate((h0_ref, h1_ref, h2_ref, h3_ref)):
        h_ref[...] = mm(d_ref[place(part_ref, r, 128), :], w_ref[:, 0:512], NT).astype(BF)


def kernel_grads(msg_ref, hidden_ref, w_ref, rest_ref, grads_ref, d_ref):
    low = lane((64, 128)) < 64
    for s in range(4):
        for p in range(4):
            even = msg_ref[8 * p + s].astype(F32)
            odd = msg_ref[8 * p + 4 + s].astype(F32)
            d_ref[128 * s : 128 * s + 64, 128 * p : 128 * p + 128] = jnp.where(
                low, even, pltpu.roll(odd, 64, 1)
            ).astype(BF)
            d_ref[128 * s + 64 : 128 * s + 128, 128 * p : 128 * p + 128] = jnp.where(
                low, pltpu.roll(even, 64, 1), odd
            ).astype(BF)
    total = mm(hidden_ref[...], d_ref[...], TN)
    grads_ref[:, 0:512] = total.astype(BF)
    gain = jnp.sum(total * w_ref[:, 0:512].astype(F32), axis=1, keepdims=True)
    gain = gain / w_ref[:, 512:640].astype(F32)[:, 0:1]
    rest = rest_ref[:, 0:128]
    grads_ref[:, 512:640] = jnp.where(lane((WIDTH, 128)) == 0, gain.astype(BF), rest)
    grads_ref[:, 640:896] = rest_ref[:, 128:384]


def kernel_input_grad(d0_ref, d1_ref, d2_ref, d3_ref, x_ref, dmid_ref, gains_ref, out_ref):
    dh = d0_ref[...].astype(F32)
    for d_ref in (d1_ref, d2_ref, d3_ref):
        dh = dh + d_ref[...].astype(F32)
    x = x_ref[...].astype(F32)
    scale = lax.rsqrt(jnp.mean(x * x, axis=-1, keepdims=True) + EPSILON)
    dn = dh * gains_ref[0:1]
    out_ref[...] = (
        dmid_ref[...]
        + scale * dn
        - x * (scale * scale * scale) * jnp.mean(dn * x, axis=-1, keepdims=True)
    )


def kernel_total(parts_ref, table_ref, qkv_ref, out_ref, gains_ref, sum_ref):
    total = parts_ref[0].astype(F32)
    for c in range(1, 32):
        total = total + parts_ref[c].astype(F32)
    sum_ref[...] = total
    rows = []
    for p in range(4):
        rows.append(
            jnp.concatenate([sum_ref[f, :, 128 * p : 128 * p + 128] for f in range(4)], axis=1)
        )
    rest = jnp.concatenate(rows, axis=0)
    parts = []
    for _ in range(3):
        part = rest.astype(BF)
        rest = rest - part.astype(F32)
        parts.append(part)
    whole = mm(jnp.concatenate(parts, axis=0), table_ref[...], NT)
    whole = whole[0:32] + whole[32:64] + whole[64:96]
    for p in range(4):
        piece = whole[8 * p : 8 * p + 8]
        qkv_ref[:, 256 * p : 256 * p + 256] = piece[:, 0:256]
        qkv_ref[:, 1024 + 128 * p : 1152 + 128 * p] = piece[:, 256:384]
        qkv_ref[:, 1536 + 128 * p : 1664 + 128 * p] = piece[:, 384:512]
    for f in range(4):
        out_ref[:, 256 * f : 256 * f + 256] = sum_ref[f, :, 640:896]
    gains_ref[...] = (
        sum_ref[0, :, 512:640]
        + sum_ref[1, :, 512:640]
        + sum_ref[2, :, 512:640]
        + sum_ref[3, :, 512:640]
    )


def kernel_output(ys_ref, high_ref, rest_ref, mid_ref, out_ref, sum_ref):
    step = pl.program_id(0)

    @pl.when(step == 0)
    def _():
        sum_ref[...] = mid_ref[...]

    ys = ys_ref[...].reshape(512, WIDTH)
    sum_ref[...] += mm(high_ref[...], ys) + mm(rest_ref[...], ys)

    @pl.when(step == 3)
    def _():
        out_ref[...] = sum_ref[...].astype(BF)


def angles(positions, features):
    frequency = ROPE_BASE ** (-(features.astype(F32) * 2.0 / 64))
    return positions.astype(F32)[:, None] * frequency[None, :]


def whole(shape):
    return pl.BlockSpec(shape, lambda t: (0,) * len(shape))


def exchange(value, axes):
    return lax.all_to_all(value, axes, split_axis=0, concat_axis=0, tiled=True)


def gather(value, axes):
    return lax.all_gather(value, axes, axis=0, tiled=True)


def after(value, marker):
    return lax.optimization_barrier((value, marker))[0]


def swap(value, axis):
    return lax.ppermute(value, axis, [(0, 1), (1, 0)])


def neighbours(value):
    return value, swap(value, "core"), swap(value, "zl")


def cross(parts, axes=FSDP):
    here = [parts[0]]
    for r in range(1, 4):
        here.append(lax.ppermute(parts[r], axes, [(i, i ^ r) for i in range(4)]))
    return here


def on_device(
    layer_input,
    routes,
    gates,
    cotangent,
    norm_attn,
    query_key_value_weight,
    output_weight,
    norm_ffn,
    exp_gate,
    exp_up,
    exp_down,
):
    mine = lax.axis_index("y")
    ctx_index = lax.axis_index(CTX)
    part_index = lax.axis_index(FSDP)
    mine_ref = mine.astype(jnp.int32).reshape(1)
    part_ref = part_index.astype(jnp.int32).reshape(1)
    x = layer_input.reshape(128, WIDTH)
    cot = cotangent.reshape(128, WIDTH)
    slice_table = jnp.asarray(slice_matrix(), BF)
    head_table = jnp.asarray(head_matrix(), BF)

    x_all = neighbours(x)
    rank, gate = call(
        kernel_route,
        (sds((32, 128), F32), sds((32, 128), F32)),
        (1e6, 1e5),
        in_specs=[VM, VM],
        out_specs=(VM, VM),
    )(routes.reshape(128, 8).T, gates.reshape(128, 8).T)
    which = lax.broadcasted_iota(jnp.int32, (8, 128), 1)
    gain_rows = jnp.where(
        which == 0, norm_attn[:, None], jnp.where(which == 1, norm_ffn[:, None], 0.0)
    )
    slices = call(
        kernel_slices,
        sds((32, 4, 8, 896), BF),
        (2e7, 3e6),
        in_specs=[VM] * 5,
        out_specs=VM,
    )(query_key_value_weight, gain_rows, slice_table, gate, output_weight)
    slices, rank, gate, x_all = lax.optimization_barrier((slices, rank, gate, x_all))
    x_all = x_all + (swap(x_all[2], "core"),)
    offset = jnp.arange(64, dtype=jnp.int32)
    token_pos = jnp.concatenate([ctx_index * 64 + offset, (63 - ctx_index) * 64 + offset])
    column = jnp.arange(512, dtype=jnp.int32)
    angle = angles(token_pos, 8 * part_index + column % 8)
    is_value = (column // 16) % 4 == 3
    sign = jnp.where((column // 8) % 2 == 0, -1.0, 1.0)
    cos_slice = jnp.where(is_value, 1.0, jnp.cos(angle))
    sin_slice = jnp.where(is_value, 0.0, jnp.sin(angle) * sign)
    w_slice = exchange(slices.reshape(128, 8, 896), ALL)
    w_slice, cos_slice, sin_slice = lax.optimization_barrier((w_slice, cos_slice, sin_slice))
    gate_parts = lax.dynamic_slice(
        w_slice.reshape(32, 4, 8, 896), (0, part_index, 0, 512), (32, 1, 8, 128)
    ).reshape(32, 8, 128)
    w_slice = w_slice.reshape(WIDTH, 896)
    picks, picks_turned, picks_high, picks_rest = call(
        kernel_picks,
        (sds((2048, 128), BF),) + (sds((128, 2048), BF),) * 3,
        (2e9, 4e6),
        in_specs=[VM, VM],
        out_specs=(VM,) * 4,
    )(rank, gate)

    msg, hidden, gains = call(
        kernel_project,
        (sds((32, 64, 128), BF), sds((512, WIDTH), BF), sds((8, WIDTH), F32)),
        (6e8, 4e6),
        in_specs=[SM] + [VM] * 7,
        out_specs=(VM, VM, VM),
    )(part_ref, *x_all, w_slice, cos_slice, sin_slice)
    across = swap(after(cot, w_slice), "zh")
    first = lax.axis_index("zh") == 0
    cot_pair = jnp.concatenate(
        [jnp.where(first, cot, across), jnp.where(first, across, cot)], axis=0
    )
    out_upper = neighbours(w_slice[0:512, 640:896])
    msg = exchange(msg, HEAD_AXES + FSDP)

    kv_copies, queries = call(
        kernel_heads,
        (sds((4, 1024, 128), BF), sds((2, 8, 2, 64, 128), BF)),
        (4e8, 3e6),
        in_specs=[VM, VM],
        out_specs=(VM, VM),
    )(msg.reshape(8, 4, 64, 128), head_table)
    queries = queries.reshape(2048, 128)
    kv_copies, out_upper = lax.optimization_barrier((kv_copies, out_upper))
    out_lower = neighbours(after(w_slice[512:1024, 640:896], msg))
    kv = exchange(kv_copies, ("y",)).reshape(4, 2, 8, 64, 128)
    expert_weights = jnp.concatenate(
        [jnp.concatenate([exp_gate[0], exp_up[0]], axis=1), exp_down[0]], axis=0
    ).astype(BF)
    block = 4 * jnp.arange(8, dtype=jnp.int32)[:, None] + mine
    quarter_pos = jnp.concatenate(
        [
            (block * 64 + offset[None, :]).reshape(-1),
            ((63 - block) * 64 + offset[None, :]).reshape(-1),
        ]
    )
    column = jnp.arange(128, dtype=jnp.int32)
    angle = angles(quarter_pos, column % 32)
    sign = jnp.where(column % 64 < 32, -1.0, 1.0)
    cos_heads = jnp.where(column >= 64, 1.0, jnp.cos(angle))
    sin_heads = jnp.where(column >= 64, 0.0, jnp.sin(angle) * sign)
    kv, out_lower, cos_heads, sin_heads = lax.optimization_barrier(
        (kv, out_lower, cos_heads, sin_heads)
    )
    experts_all = neighbours(after(expert_weights, msg))
    cot_all = gather(after(cot_pair, kv_copies), ("x", "y")).reshape(4, 4, 2, 128, WIDTH)
    out_upper = out_upper + (swap(after(out_upper[2], kv), "core"),)
    out_lower = out_lower + (swap(out_lower[2], "core"),)
    w_out = (*out_upper, *out_lower)
    msg_spec = pl.BlockSpec((2, 1, 64, 128), lambda t: (t % 4, t // 4, 0, 0))
    row_spec = pl.BlockSpec((256, 128), lambda t: (t, 0))
    log_spec = pl.BlockSpec((1, 8, 256), lambda t: (t, 0, 0))
    o_msg, log_total, o_rows, keys, turned = call(
        kernel_attend,
        (
            sds((8, 2, 64, 128), BF),
            sds((8, 8, 256), F32),
            sds((2048, 128), F32),
            sds((4096, 128), BF),
            sds((128, 4096), BF),
        ),
        (1e10, 5e6),
        grid=(8,),
        in_specs=[SM, whole((4, 2, 8, 64, 128)), row_spec],
        out_specs=(msg_spec, log_spec, row_spec, whole((4096, 128)), whole((128, 4096))),
    )(mine_ref, kv, queries)
    o_msg, w_out, experts_all = lax.optimization_barrier((o_msg, w_out, experts_all))
    experts_all = experts_all + (swap(experts_all[2], "core"),)
    o_heads = exchange(o_msg, HEAD_AXES)

    slot_spec = pl.BlockSpec((4, 64, WIDTH), lambda t: (t, 0, 0))
    out_specs = [whole((512, 256))] * 8
    slots, mid = call(
        kernel_middle,
        (sds((32, 64, WIDTH), BF), sds((128, WIDTH), F32)),
        (9e8, 8e6),
        grid=(2,),
        in_specs=[SM, whole((8, 2, 64, 128))]
        + out_specs
        + [
            whole((128, WIDTH)),
            whole((8, WIDTH)),
            pl.BlockSpec((1024, 128), lambda t: (t, 0)),
        ],
        out_specs=(pl.BlockSpec((16, 64, WIDTH), lambda t: (t, 0, 0)), whole((128, WIDTH))),
        scratch_shapes=[pltpu.VMEM((128, WIDTH), BF), pltpu.VMEM((128, WIDTH), BF)],
    )(part_ref, o_heads, *w_out, x, gains, picks)
    cot_all = after(cot_all, mid)
    slots, experts_all = lax.optimization_barrier((slots, experts_all))
    o_all = neighbours(after(o_heads, mid))
    slots = exchange(slots, CTX)
    dys, dact, down, gate_up = call(
        kernel_experts_ready,
        (
            sds((32, 64, WIDTH), BF),
            sds((2048, 512), F32),
            sds((512, WIDTH), BF),
            sds((WIDTH, WIDTH), BF),
        ),
        (6e9, 2e7),
        grid=(8,),
        in_specs=[
            SM,
            pl.BlockSpec((1, 4, 1, 128, WIDTH), lambda t: (t // 2, 0, t % 2, 0, 0)),
            whole((32, 8, 128)),
        ]
        + [whole((384, WIDTH))] * 4,
        out_specs=(
            slot_spec,
            pl.BlockSpec((256, 512), lambda t: (t, 0)),
            whole((512, WIDTH)),
            whole((WIDTH, WIDTH)),
        ),
        scratch_shapes=[pltpu.VMEM((32, 128), F32), pltpu.VMEM((32, 128), F32)],
    )(part_ref, cot_all, gate_parts, *experts_all)
    act_spec = pl.BlockSpec((256, 512), lambda t: (t, 0))
    both_spec = pl.BlockSpec((256, WIDTH), lambda t: (t, 0))
    act, dboth, dxs = call(
        kernel_experts,
        (sds((2048, 512), BF), sds((2048, WIDTH), BF), sds((32, 64, WIDTH), BF)),
        (9e9, 2e7),
        grid=(4,),
        in_specs=[
            pl.BlockSpec((8, 64, WIDTH), lambda t: (t, 0, 0)),
            whole((WIDTH, WIDTH)),
            pl.BlockSpec((512, 512), lambda t: (t, 0)),
        ],
        out_specs=(
            pl.BlockSpec((512, 512), lambda t: (t, 0)),
            pl.BlockSpec((512, WIDTH), lambda t: (t, 0)),
            pl.BlockSpec((8, 64, WIDTH), lambda t: (t, 0, 0)),
        ),
    )(slots, gate_up, dact)
    ys, expert_grads = call(
        kernel_experts_after,
        (sds((32, 64, WIDTH), BF), sds((4, 384, WIDTH), BF)),
        (9e9, 2e7),
        grid=(8,),
        in_specs=[slot_spec, act_spec, slot_spec, both_spec, whole((512, WIDTH))],
        out_specs=(slot_spec, whole((4, 384, WIDTH))),
        scratch_shapes=[pltpu.VMEM((WIDTH, WIDTH), F32), pltpu.VMEM((512, WIDTH), F32)],
    )(slots, act, dys, dboth, down)
    dxs, o_all = lax.optimization_barrier((dxs, o_all))
    o_all = o_all + (swap(o_all[2], "core"),)
    dxs = exchange(dxs, CTX)
    expert_own = lax.psum_scatter(
        expert_grads.reshape(4 * 384, WIDTH), FSDP, scatter_dimension=0, tiled=True
    ).astype(F32)
    dxs, ys, o_all = lax.optimization_barrier((dxs, ys, o_all))

    dmid, da_parts, grad_msg, gain_ffn_part = call(
        kernel_middle_back,
        (
            sds((128, WIDTH), F32),
            sds((4, 128, 256), BF),
            sds((8, 2, 64, 128), BF),
            sds((8, WIDTH), F32),
        ),
        (9e8, 8e6),
        grid=(2,),
        in_specs=[
            SM,
            pl.BlockSpec((16, 64, WIDTH), lambda t: (t, 0, 0)),
            pl.BlockSpec((128, 1024), lambda t: (0, t)),
            whole((128, WIDTH)),
            whole((128, WIDTH)),
            whole((8, WIDTH)),
        ]
        + out_specs,
        out_specs=(
            whole((128, WIDTH)),
            whole((4, 128, 256)),
            whole((8, 2, 64, 128)),
            whole((8, WIDTH)),
        ),
        scratch_shapes=[pltpu.VMEM((128, WIDTH), F32), pltpu.VMEM((128, WIDTH), BF)],
    )(part_ref, dxs, picks_turned, mid, cot, gains, *w_out)
    grad_heads = exchange(grad_msg, HEAD_AXES)
    ys, grad_heads = lax.optimization_barrier((ys, grad_heads))
    ys = exchange(ys, CTX)
    dq, *dkv = call(
        kernel_attend_back,
        (sds((2048, 128), F32),) + (sds((2, 8, 64, 128), BF),) * 4,
        (2e10, 7e6),
        grid=(8,),
        in_specs=[
            SM,
            whole((4096, 128)),
            whole((128, 4096)),
            row_spec,
            msg_spec,
            log_spec,
            row_spec,
        ],
        out_specs=(row_spec,) + (whole((2, 8, 64, 128)),) * 4,
        scratch_shapes=[pltpu.VMEM((4096, 128), F32)],
    )(mine_ref, keys, turned, queries, grad_heads, log_total, o_rows)
    da_here = cross(da_parts)
    dkv = cross(dkv, ("y",))
    dkv, ys, da_here = lax.optimization_barrier((dkv, ys, da_here))
    rest_part = call(
        kernel_out_weight,
        sds((WIDTH, 384), BF),
        (3e8, 2e6),
        in_specs=[VM] * 9,
        out_specs=VM,
    )(*o_all, *da_here, gain_ffn_part)
    layer_output = call(
        kernel_output,
        sds((128, WIDTH), BF),
        (1e9, 5e6),
        grid=(4,),
        in_specs=[
            pl.BlockSpec((8, 64, WIDTH), lambda t: (t, 0, 0)),
            pl.BlockSpec((128, 512), lambda t: (0, t)),
            pl.BlockSpec((128, 512), lambda t: (0, t)),
            whole((128, WIDTH)),
        ],
        out_specs=whole((128, WIDTH)),
        scratch_shapes=[pltpu.VMEM((128, WIDTH), F32)],
    )(ys, picks_high, picks_rest, mid)

    back = call(
        kernel_slices_back,
        sds((8, 4, 64, 128), BF),
        (4e8, 5e6),
        in_specs=[VM] * 8,
        out_specs=VM,
    )(*dkv, dq.reshape(2, 8, 2, 64, 128), cos_heads, sin_heads, head_table)
    back = exchange(back.reshape(32, 64, 128), HEAD_AXES + FSDP)

    grads, d_all = call(
        kernel_grads,
        (sds((WIDTH, 896), BF), sds((512, 512), BF)),
        (6e8, 5e6),
        in_specs=[VM] * 4,
        out_specs=(VM, VM),
    )(back, hidden, w_slice, rest_part)
    dh_parts = call(
        kernel_hidden_grad,
        (sds((128, WIDTH), BF),) * 4,
        (6e8, 5e6),
        in_specs=[SM, VM, VM],
        out_specs=(VM,) * 4,
    )(part_ref, d_all, w_slice)
    grads = exchange(grads.reshape(128, 8, 896), ALL)
    grad_qkv, grad_out, grad_gains = call(
        kernel_total,
        (sds((8, 2048), F32), sds((8, WIDTH), F32), sds((8, 128), F32)),
        (1e8, 4e6),
        in_specs=[VM, VM],
        out_specs=(VM, VM, VM),
        scratch_shapes=[pltpu.VMEM((4, 8, 896), F32)],
    )(grads.reshape(32, 4, 8, 896), slice_table)
    dh_here = cross(dh_parts)
    input_grad = call(
        kernel_input_grad,
        sds((128, WIDTH), F32),
        (1e6, 2e6),
        in_specs=[VM] * 7,
        out_specs=VM,
    )(*after(dh_here, grad_qkv), x, dmid, gains)
    return (
        layer_output.reshape(layer_input.shape),
        input_grad.reshape(layer_input.shape),
        grad_gains[:, 0],
        grad_qkv,
        grad_out,
        grad_gains[:, 1],
        expert_own[0:256, 0:512][None],
        expert_own[0:256, 512:1024][None],
        expert_own[256:384][None],
    )


def solution(mesh):
    parts = Mesh(mesh.devices.reshape(4, 2, 4, 2, 2), ALL)
    tokens = P(FSDP, CTX, None, None, None, None)
    experts = P(CTX, FSDP, None)
    in_specs = (
        tokens,
        tokens,
        tokens,
        tokens,
        P(ALL),
        P(ALL, None),
        P(ALL, None),
        P(ALL),
        experts,
        experts,
        experts,
    )
    out_specs = (
        tokens,
        tokens,
        P(ALL),
        P(ALL, None),
        P(ALL, None),
        P(ALL),
        experts,
        experts,
        experts,
    )
    return jax.shard_map(
        on_device, mesh=parts, in_specs=in_specs, out_specs=out_specs, check_vma=False
    )
```

```python
import functools

import jax
import jax.numpy as jnp
import numpy as np
from jax import lax
from jax.experimental import pallas as pl
from jax.experimental.pallas import tpu as pltpu
from jax.sharding import Mesh
from jax.sharding import PartitionSpec as P

WIDTH = 1024
EPSILON = 1e-06
ROPE_BASE = 10000.0
MASKED = -1e30
BF = jnp.bfloat16
F32 = jnp.float32
CTX = ("x", "zh", "y")
HEAD_AXES = ("x", "zh")
FSDP = ("zl", "core")
ALL = CTX + FSDP
VMEM_LIMIT = 56 * 1024 * 1024

NT = (((1,), (1,)), ((), ()))
TN = (((0,), (0,)), ((), ()))


def mm(a, b, dims=None):
    if dims is None:
        return jnp.dot(a, b, preferred_element_type=F32)
    return lax.dot_general(a, b, dims, preferred_element_type=F32)


def lane(shape):
    return lax.broadcasted_iota(jnp.int32, shape, len(shape) - 1)


def row(shape):
    return lax.broadcasted_iota(jnp.int32, shape, len(shape) - 2)


def call(kernel, out_shape, cost, **kw):
    flops, bytes_accessed = cost
    return pl.pallas_call(
        kernel,
        out_shape=out_shape,
        compiler_params=pltpu.CompilerParams(vmem_limit_bytes=VMEM_LIMIT),
        cost_estimate=pl.CostEstimate(
            flops=int(flops), bytes_accessed=int(bytes_accessed), transcendentals=0
        ),
        **kw,
    )


def sds(shape, dtype):
    return jax.ShapeDtypeStruct(shape, dtype)


VM = pl.BlockSpec(memory_space=pltpu.VMEM)
SM = pl.BlockSpec(memory_space=pltpu.SMEM)


def slice_matrix():
    table = np.zeros((512, 512), np.float32)
    for k in range(512):
        section, place = k // 128, k % 128
        if section < 2:
            pair, part = section, place // 64
        else:
            pair, part = place // 64, section
        feat = place % 64
        f = (feat % 32) // 8
        column = pair * 64 + part * 16 + (feat // 32) * 8 + feat % 8
        table[k, f * 128 + column] = 1.0
    return table


def head_matrix():
    table = np.zeros((4, 128, 768), np.float32)
    for f in range(4):
        for block in range(2):
            for part in range(4):
                for j in range(16):
                    feat = (j // 8) * 32 + 8 * f + j % 8
                    source = block * 64 + part * 16 + j
                    if part == 2:
                        target = block * 128 + feat
                    elif part == 3:
                        target = block * 128 + 64 + feat
                    else:
                        target = 256 + block * 256 + part * 128 + feat
                    table[f, source, target] = 1.0
    return table


def place(part_ref, r, size):
    return pl.ds(pl.multiple_of(lax.bitwise_xor(part_ref[0], r) * size, size), size)


def kernel_route(picks_ref, gates_ref, rank_ref, gate_ref):
    experts = row((32, 128))
    gate = jnp.zeros((32, 128), F32)
    chosen = jnp.zeros((32, 128), F32)
    for k in range(8):
        hit = picks_ref[k : k + 1, :] == experts
        gate = gate + jnp.where(hit, gates_ref[k : k + 1, :], 0.0)
        chosen = chosen + jnp.where(hit, 1.0, 0.0)
    before = jnp.where(row((128, 128)) < lane((128, 128)), 1.0, 0.0).astype(BF)
    rank = mm(chosen.astype(BF), before)
    rank_ref[...] = jnp.where(chosen > 0.5, rank, -1.0)
    gate_ref[...] = gate


def kernel_slices(w_ref, gains_ref, table_ref, gate_ref, out_weight_ref, out_ref):
    w = w_ref[...].astype(BF).astype(F32)
    parts = []
    for p in range(4):
        parts.append(
            jnp.concatenate(
                [
                    w[:, 256 * p : 256 * p + 256],
                    w[:, 1024 + 128 * p : 1152 + 128 * p],
                    w[:, 1536 + 128 * p : 1664 + 128 * p],
                ],
                axis=1,
            )
        )
    stacked = jnp.concatenate(parts, axis=0).astype(BF)
    cut = mm(stacked, table_ref[...])
    columns = []
    for f in range(4):
        columns.append(
            jnp.concatenate(
                [cut[8 * p : 8 * p + 8, 128 * f : 128 * f + 128] for p in range(4)], axis=1
            ).astype(BF)
        )
    gains = gains_ref[...]
    left = lane((8, 128)) < 64
    sub = row((8, 128))
    for c in range(32):
        gate = gate_ref[c : c + 1, :]
        high = gate.astype(BF).astype(F32)
        middle = (gate - high).astype(BF).astype(F32)
        rest = gate - high - middle
        parts = jnp.where(
            sub < 2, high, jnp.where(sub < 4, middle, jnp.where(sub < 6, rest, 0.0))
        )
        parts = jnp.where(sub % 2 == 0, pltpu.roll(parts, 64, 1), parts)
        last = jnp.where(left, gains, parts).astype(BF)
        for f in range(4):
            out_ref[c, f, :, 0:512] = columns[f]
            out_ref[c, f, :, 512:640] = last
            out_ref[c, f, :, 640:896] = out_weight_ref[:, 256 * f : 256 * f + 256].astype(BF)


def kernel_picks(rank_ref, gate_ref, pick_ref, turned_ref, high_ref, rest_ref):
    slot = lax.broadcasted_iota(jnp.int32, (64, 128), 0).astype(F32)

    @pl.loop(0, 16)
    def _(p):
        picks, weights = [], []
        for e in (2 * p, 2 * p + 1):
            hit = slot == rank_ref[pl.ds(e, 1), :]
            picks.append(jnp.where(hit, 1.0, 0.0))
            weights.append(jnp.where(hit, gate_ref[pl.ds(e, 1), :], 0.0))
        picks = jnp.concatenate(picks, axis=0)
        weights = jnp.transpose(jnp.concatenate(weights, axis=0))
        at = pl.ds(pl.multiple_of(128 * p, 128), 128)
        pick_ref[at, :] = picks.astype(BF)
        turned_ref[:, at] = jnp.transpose(picks).astype(BF)
        high = weights.astype(BF)
        high_ref[:, at] = high
        rest_ref[:, at] = (weights - high.astype(F32)).astype(BF)


def kernel_project(
    part_ref, x0_ref, x1_ref, x2_ref, x3_ref, w_ref, cos_ref, sin_ref, msg_ref, hidden_ref, gains_ref
):
    gains = jnp.transpose(w_ref[:, 512:640].astype(F32))
    gains_ref[...] = gains[:8]
    for r, x_ref in enumerate((x0_ref, x1_ref, x2_ref, x3_ref)):
        x = x_ref[...].astype(F32)
        scale = lax.rsqrt(jnp.mean(x * x, axis=-1, keepdims=True) + EPSILON)
        hidden_ref[place(part_ref, r, 128), :] = (x * scale * gains[0:1]).astype(BF)
    proj = mm(hidden_ref[...], w_ref[:, 0:512])
    ahead = pltpu.roll(proj, 512 - 8, 1)
    behind = pltpu.roll(proj, 8, 1)
    partner = jnp.where((lane((512, 512)) // 8) % 2 == 0, ahead, behind)
    cos = jnp.concatenate([cos_ref[...]] * 4, axis=0)
    sin = jnp.concatenate([sin_ref[...]] * 4, axis=0)
    turned = proj * cos + partner * sin
    low = lane((64, 128)) < 64
    for s in range(4):
        for p in range(4):
            front = turned[128 * s : 128 * s + 64, 128 * p : 128 * p + 128]
            back = turned[128 * s + 64 : 128 * s + 128, 128 * p : 128 * p + 128]
            msg_ref[8 * p + s] = jnp.where(low, front, pltpu.roll(back, 64, 1)).astype(BF)
            msg_ref[8 * p + 4 + s] = jnp.where(low, pltpu.roll(front, 64, 1), back).astype(BF)


def kernel_heads(msg_ref, table_ref, kv_ref, q_ref):
    out = jnp.zeros((512, 768), F32)
    for f in range(4):
        out = out + mm(msg_ref[:, f].reshape(512, 128), table_ref[f])
    pairs = out[:, 0:256].astype(BF)
    for half in range(2):
        block = pairs[:, 128 * half : 128 * half + 128]
        for y in range(4):
            kv_ref[y, 512 * half : 512 * half + 512, :] = block
    queries = (out[:, 256:768] * 0.125).astype(BF)
    for half in range(2):
        for head in range(2):
            at = 256 * half + 128 * head
            q_ref[half, :, head] = queries[:, at : at + 128].reshape(8, 64, 128)


def tile_positions(tile, mine):
    front = tile < 4
    i = jnp.where(front, tile, tile - 4)
    q = lane((1, 256))
    k = lax.broadcasted_iota(jnp.int32, (512, 1), 0)
    q_front = (8 * i + 4 * (q // 128) + mine) * 64 + q % 64
    q_back = (63 - 8 * i - 4 * (q // 128) - mine) * 64 + q % 64
    k_front = 512 * i + k
    k_back = (59 - 8 * i + 4 * (k // 256) - (k % 256) // 64) * 64 + k % 64
    return jnp.where(front, q_front, q_back), jnp.where(front, k_front, k_back)


def kernel_attend(
    mine_ref,
    kv_ref,
    q_ref,
    msg_ref,
    log_ref,
    out_ref,
    keys_ref,
    turned_ref,
    peak_ref,
    total_ref,
    mixed_ref,
):
    tile = pl.program_id(0)

    @pl.when(tile == 0)
    def _():
        for group in range(16):
            half, place = (0, group) if group < 8 else (1, 15 - group)
            for y in range(4):
                at = 256 * group + 64 * y
                keys_ref[at : at + 64, :] = kv_ref[y, half, place]
        for c in range(8):
            turned_ref[:, 512 * c : 512 * c + 512] = jnp.transpose(
                keys_ref[512 * c : 512 * c + 512, :].astype(F32)
            ).astype(BF)

    q = q_ref[...]
    q_pos, k_pos = tile_positions(tile, mine_ref[0])

    def run(first, count, last):
        def keys(c):
            return pl.ds(pl.multiple_of(first + 512 * c, 512), 512)

        peak = peak_ref[0:1]
        total = total_ref[0:1]
        mixed = mixed_ref[...]
        later = mm(keys_ref[keys(0), :], q, NT)
        for c in range(count):
            scores = later
            if c + 1 < count:
                later = mm(keys_ref[keys(c + 1), :], q, NT)
            elif last:
                scores = jnp.where(k_pos <= q_pos, scores, MASKED)
            higher = jnp.maximum(peak, jnp.max(scores, axis=0, keepdims=True))
            weights = jnp.exp(scores - higher)
            fade = jnp.exp(peak - higher)
            total = total * fade + jnp.sum(weights, axis=0, keepdims=True)
            mixed = mixed * fade + mm(turned_ref[64:128, keys(c)], weights.astype(BF))
            peak = higher
        peak_ref[...] = jnp.broadcast_to(peak, (8, 256))
        total_ref[...] = jnp.broadcast_to(total, (8, 256))
        mixed_ref[...] = mixed

    peak_ref[...] = jnp.full((8, 256), MASKED, F32)
    total_ref[...] = jnp.zeros((8, 256), F32)
    mixed_ref[...] = jnp.zeros((64, 256), F32)

    @pl.when(tile >= 4)
    def _():
        run(0, 4, False)

    first = jnp.where(tile >= 4, 2048, 0)
    rest = jnp.where(tile >= 4, 8 - tile, tile + 1)
    for count in range(1, 5):
        pl.when(rest == count)(functools.partial(run, first, count, True))

    total = total_ref[0:1]
    log_ref[0] = jnp.broadcast_to(peak_ref[0:1] + jnp.log(total), (8, 256))
    mixed = mixed_ref[...] / total
    out = jnp.transpose(jnp.concatenate([jnp.zeros((64, 256), F32), mixed], axis=0))
    out_ref[...] = out
    low = lane((64, 128)) < 64
    for a in range(2):
        one = out[128 * a : 128 * a + 64]
        two = out[128 * a + 64 : 128 * a + 128]
        msg_ref[a, 0] = jnp.where(low, pltpu.roll(one, 64, 1), two).astype(BF)


def kernel_attend_back(
    mine_ref, keys_ref, turned_ref, q_ref, grad_ref, log_ref, out_ref, dq_ref, d0_ref, d1_ref, d2_ref, d3_ref, sum_ref
):
    tile = pl.program_id(0)

    @pl.when(tile == 0)
    def _():
        sum_ref[...] = jnp.zeros_like(sum_ref)

    q = q_ref[...]
    low = lane((64, 128)) < 64
    pieces = []
    for a in range(2):
        both = grad_ref[a, 0].astype(F32)
        pieces.append(jnp.where(low, 0.0, pltpu.roll(both, 64, 1)))
        pieces.append(jnp.where(low, 0.0, both))
    grad = jnp.concatenate(pieces, axis=0)
    delta = jnp.sum(jnp.transpose(grad * out_ref[...]), axis=0, keepdims=True)
    grad = grad.astype(BF)
    q_pos, k_pos = tile_positions(tile, mine_ref[0])
    log_total = log_ref[0][0:1]

    def step(c, dq, last):
        at = pl.ds(pl.multiple_of(c * 512, 512), 512)
        keys = keys_ref[at, :]
        scores = mm(keys, q, NT)
        if last:
            scores = jnp.where(k_pos <= q_pos, scores, MASKED)
        weights = jnp.exp(scores - log_total)
        slope = (weights * (mm(keys, grad, NT) - delta)).astype(BF)
        sum_ref[at, :] += mm(slope, q) + mm(weights.astype(BF), grad)
        return dq + mm(turned_ref[0:64, at], slope)

    count = jnp.where(tile < 4, tile + 1, 12 - tile)
    dq = lax.fori_loop(0, count - 1, lambda c, v: step(c, v, False), jnp.zeros((64, 256), F32))
    dq = step(count - 1, dq, True)
    dq_ref[...] = jnp.transpose(jnp.concatenate([dq * 0.125, jnp.zeros((64, 256), F32)], axis=0))

    @pl.when(tile == 7)
    def _():
        for group in range(16):
            half, place = (0, group) if group < 8 else (1, 15 - group)
            for r, dkv_ref in enumerate((d0_ref, d1_ref, d2_ref, d3_ref)):
                at = 256 * group + 64 * lax.bitwise_xor(mine_ref[0], r)
                part = sum_ref[pl.ds(pl.multiple_of(at, 64), 64), :]
                dkv_ref[half, place] = part.astype(BF)


def kernel_middle(
    part_ref,
    o_ref,
    u0_ref,
    u1_ref,
    u2_ref,
    u3_ref,
    l0_ref,
    l1_ref,
    l2_ref,
    l3_ref,
    x_ref,
    gains_ref,
    pick_ref,
    slots_ref,
    mid_ref,
    rows_ref,
    hidden_ref,
):
    @pl.when(pl.program_id(0) == 0)
    def _():
        for g in range(8):
            rows_ref[:, 128 * g : 128 * g + 128] = o_ref[g].reshape(128, 128)
        uppers = (u0_ref, u1_ref, u2_ref, u3_ref)
        lowers = (l0_ref, l1_ref, l2_ref, l3_ref)
        for r in range(4):
            at = place(part_ref, r, 256)
            mid_ref[:, at] = (
                x_ref[:, at].astype(F32)
                + mm(rows_ref[:, 0:512], uppers[r][...])
                + mm(rows_ref[:, 512:1024], lowers[r][...])
            )
        mid = mid_ref[...]
        scale = lax.rsqrt(jnp.mean(mid * mid, axis=-1, keepdims=True) + EPSILON)
        hidden_ref[...] = (mid * scale * gains_ref[1:2]).astype(BF)

    for c in range(4):
        at = slice(256 * c, 256 * c + 256)
        rows = mm(pick_ref[...], hidden_ref[:, at]).astype(BF)
        slots_ref[:, :, at] = rows.reshape(16, 64, 256)


def kernel_experts_ready(
    part_ref,
    dy_ref,
    parts_ref,
    w0_ref,
    w1_ref,
    w2_ref,
    w3_ref,
    dys_ref,
    dact_ref,
    v_ref,
    gu_ref,
    rank_ref,
    gate_ref,
):
    step = pl.program_id(0)

    @pl.when(step == 0)
    def _():
        for r, w_ref in enumerate((w0_ref, w1_ref, w2_ref, w3_ref)):
            gu_ref[place(part_ref, r, 256), :] = w_ref[0:256, :]
            v_ref[place(part_ref, r, 128), :] = w_ref[256:384, :]
        before = jnp.where(row((128, 128)) < lane((128, 128)), 1.0, 0.0).astype(BF)
        parts = [parts_ref[:, k, :].astype(F32) for k in range(6)]
        even = parts[0] + parts[2] + parts[4]
        odd = parts[1] + parts[3] + parts[5]
        gate_ref[...] = jnp.where(lane((32, 128)) < 64, pltpu.roll(even, 64, 1), odd)
        chosen = gate_ref[...] > 0.0
        rank = mm(jnp.where(chosen, 1.0, 0.0).astype(BF), before)
        rank_ref[...] = jnp.where(chosen, rank, -1.0)

    slot = lax.broadcasted_iota(jnp.int32, (64, 128), 0).astype(F32)
    grads = []
    for j in range(4):
        source = 4 * step + j
        pick = slot == rank_ref[pl.ds(source, 1), :]
        weight = jnp.sum(
            jnp.where(pick, gate_ref[pl.ds(source, 1), :], 0.0), axis=1, keepdims=True
        )
        rows = mm(jnp.where(pick, 1.0, 0.0).astype(BF), dy_ref[0, j, 0])
        grads.append((rows * weight).astype(BF))
    dys = jnp.concatenate(grads, axis=0)
    dys_ref[...] = dys.reshape(4, 64, WIDTH)
    dact_ref[...] = mm(dys, v_ref[...], NT)


def kernel_experts(h_ref, gu_ref, dact_ref, act_ref, dboth_ref, dxs_ref):
    both = mm(h_ref[...].reshape(512, WIDTH), gu_ref[...])
    gate_h, up_h = both[:, :512], both[:, 512:]
    sig = jax.nn.sigmoid(gate_h)
    swished = gate_h * sig
    act_ref[...] = (swished * up_h).astype(BF)
    dact = dact_ref[...]
    dgate = (dact * up_h * sig * (1.0 + gate_h * (1.0 - sig))).astype(BF)
    dup = (dact * swished).astype(BF)
    dboth = jnp.concatenate([dgate, dup], axis=1)
    dboth_ref[...] = dboth
    dxs_ref[...] = mm(dboth, gu_ref[...], NT).astype(BF).reshape(8, 64, WIDTH)


def kernel_experts_after(
    h_ref, act_ref, dys_ref, dboth_ref, v_ref, ys_ref, grad_ref, ggu_ref, gv_ref
):
    step = pl.program_id(0)

    @pl.when(step == 0)
    def _():
        ggu_ref[...] = jnp.zeros_like(ggu_ref)
        gv_ref[...] = jnp.zeros_like(gv_ref)

    act = act_ref[...]
    ys_ref[...] = mm(act, v_ref[...]).astype(BF).reshape(4, 64, WIDTH)
    h = h_ref[...].reshape(256, WIDTH)

    @pl.loop(0, 4)
    def _(c):
        at = pl.ds(pl.multiple_of(256 * c, 256), 256)
        ggu_ref[:, at] += mm(h, dboth_ref[:, at], TN)

    gv_ref[...] += mm(act, dys_ref[...].reshape(256, WIDTH), TN)

    @pl.when(step == 7)
    def _():
        for f in range(4):
            grad_ref[f, 0:256, :] = ggu_ref[256 * f : 256 * f + 256, :].astype(BF)
            grad_ref[f, 256:384, :] = gv_ref[128 * f : 128 * f + 128, :].astype(BF)


def kernel_middle_back(
    part_ref,
    dxs_ref,
    pick_ref,
    mid_ref,
    cot_ref,
    gains_ref,
    u0_ref,
    u1_ref,
    u2_ref,
    u3_ref,
    l0_ref,
    l1_ref,
    l2_ref,
    l3_ref,
    dmid_ref,
    parts_ref,
    msg_ref,
    ggain_ref,
    sum_ref,
    low_ref,
):
    step = pl.program_id(0)
    part = mm(pick_ref[...], dxs_ref[...].reshape(1024, WIDTH))

    @pl.when(step == 0)
    def _():
        sum_ref[...] = part

    @pl.when(step > 0)
    def _():
        sum_ref[...] += part

    @pl.when(step == 1)
    def _():
        mid = mid_ref[...]
        scale = lax.rsqrt(jnp.mean(mid * mid, axis=-1, keepdims=True) + EPSILON)
        dh = sum_ref[...]
        ggain_ref[...] = jnp.broadcast_to(
            jnp.sum(dh * (mid * scale), axis=0, keepdims=True), (8, WIDTH)
        )
        dn = dh * gains_ref[1:2]
        dmid = (
            cot_ref[...].astype(F32)
            + scale * dn
            - mid * (scale * scale * scale) * jnp.mean(dn * mid, axis=-1, keepdims=True)
        )
        dmid_ref[...] = dmid
        low_ref[...] = dmid.astype(BF)
        uppers = (u0_ref, u1_ref, u2_ref, u3_ref)
        lowers = (l0_ref, l1_ref, l2_ref, l3_ref)
        for r in range(4):
            parts_ref[r] = low_ref[:, place(part_ref, r, 256)]
        for h, w_refs in enumerate((uppers, lowers)):
            grad = mm(parts_ref[0], w_refs[0][...], NT)
            for r in range(1, 4):
                grad = grad + mm(parts_ref[r], w_refs[r][...], NT)
            grad = grad.astype(BF)
            for g in range(4):
                msg_ref[4 * h + g] = grad[:, 128 * g : 128 * g + 128].reshape(2, 64, 128)


def kernel_out_weight(
    o0_ref, o1_ref, o2_ref, o3_ref, da0_ref, da1_ref, da2_ref, da3_ref, gain_ref, grad_ref
):
    which = lax.broadcasted_iota(jnp.int32, (128, WIDTH), 0)
    grad_ref[:, 0:128] = jnp.transpose(jnp.where(which == 1, gain_ref[0:1], 0.0)).astype(BF)
    pairs = ((o0_ref, da0_ref), (o1_ref, da1_ref), (o2_ref, da2_ref), (o3_ref, da3_ref))

    @pl.loop(0, 8)
    def _(g):
        part = jnp.zeros((128, 256), F32)
        for o_ref, da_ref in pairs:
            part = part + mm(o_ref[g].reshape(128, 128), da_ref[...], TN)
        grad_ref[pl.ds(pl.multiple_of(128 * g, 128), 128), 128:384] = part.astype(BF)


def kernel_slices_back(
    d0_ref, d1_ref, d2_ref, d3_ref, dq_ref, cos_ref, sin_ref, table_ref, msg_ref
):
    def unrotate(w, cos, sin):
        partner = jnp.where(
            lane(w.shape) % 64 < 32, pltpu.roll(w, 96, 1), pltpu.roll(w, 32, 1)
        )
        return (w * cos - partner * sin).astype(BF)

    parts = []
    for half in range(2):
        at = slice(512 * half, 512 * half + 512)
        dkv = d0_ref[half].reshape(512, 128).astype(F32)
        for d_ref in (d1_ref, d2_ref, d3_ref):
            dkv = dkv + d_ref[half].reshape(512, 128).astype(F32)
        parts.append(unrotate(dkv, cos_ref[at, :], sin_ref[at, :]))
    for half in range(2):
        at = slice(512 * half, 512 * half + 512)
        for head in range(2):
            parts.append(
                unrotate(dq_ref[half, :, head].reshape(512, 128), cos_ref[at, :], sin_ref[at, :])
            )
    whole = jnp.concatenate(parts, axis=1)
    for f in range(4):
        msg_ref[:, f] = mm(whole, table_ref[f], NT).astype(BF).reshape(8, 64, 128)


def kernel_hidden_grad(part_ref, d_ref, w_ref, h0_ref, h1_ref, h2_ref, h3_ref):
    for r, h_ref in enumerate((h0_ref, h1_ref, h2_ref, h3_ref)):
        h_ref[...] = mm(d_ref[place(part_ref, r, 128), :], w_ref[:, 0:512], NT).astype(BF)


def kernel_grads(msg_ref, hidden_ref, w_ref, rest_ref, grads_ref, d_ref):
    low = lane((64, 128)) < 64
    for s in range(4):
        for p in range(4):
            even = msg_ref[8 * p + s].astype(F32)
            odd = msg_ref[8 * p + 4 + s].astype(F32)
            d_ref[128 * s : 128 * s + 64, 128 * p : 128 * p + 128] = jnp.where(
                low, even, pltpu.roll(odd, 64, 1)
            ).astype(BF)
            d_ref[128 * s + 64 : 128 * s + 128, 128 * p : 128 * p + 128] = jnp.where(
                low, pltpu.roll(even, 64, 1), odd
            ).astype(BF)
    total = mm(hidden_ref[...], d_ref[...], TN)
    grads_ref[:, 0:512] = total.astype(BF)
    gain = jnp.sum(total * w_ref[:, 0:512].astype(F32), axis=1, keepdims=True)
    gain = gain / w_ref[:, 512:640].astype(F32)[:, 0:1]
    rest = rest_ref[:, 0:128]
    grads_ref[:, 512:640] = jnp.where(lane((WIDTH, 128)) == 0, gain.astype(BF), rest)
    grads_ref[:, 640:896] = rest_ref[:, 128:384]


def kernel_input_grad(d0_ref, d1_ref, d2_ref, d3_ref, x_ref, dmid_ref, gains_ref, out_ref):
    dh = d0_ref[...].astype(F32)
    for d_ref in (d1_ref, d2_ref, d3_ref):
        dh = dh + d_ref[...].astype(F32)
    x = x_ref[...].astype(F32)
    scale = lax.rsqrt(jnp.mean(x * x, axis=-1, keepdims=True) + EPSILON)
    dn = dh * gains_ref[0:1]
    out_ref[...] = (
        dmid_ref[...]
        + scale * dn
        - x * (scale * scale * scale) * jnp.mean(dn * x, axis=-1, keepdims=True)
    )


def kernel_total(parts_ref, table_ref, qkv_ref, out_ref, gains_ref, sum_ref):
    total = parts_ref[0].astype(F32)
    for c in range(1, 32):
        total = total + parts_ref[c].astype(F32)
    sum_ref[...] = total
    rows = []
    for p in range(4):
        rows.append(
            jnp.concatenate([sum_ref[f, :, 128 * p : 128 * p + 128] for f in range(4)], axis=1)
        )
    rest = jnp.concatenate(rows, axis=0)
    parts = []
    for _ in range(3):
        part = rest.astype(BF)
        rest = rest - part.astype(F32)
        parts.append(part)
    whole = mm(jnp.concatenate(parts, axis=0), table_ref[...], NT)
    whole = whole[0:32] + whole[32:64] + whole[64:96]
    for p in range(4):
        piece = whole[8 * p : 8 * p + 8]
        qkv_ref[:, 256 * p : 256 * p + 256] = piece[:, 0:256]
        qkv_ref[:, 1024 + 128 * p : 1152 + 128 * p] = piece[:, 256:384]
        qkv_ref[:, 1536 + 128 * p : 1664 + 128 * p] = piece[:, 384:512]
    for f in range(4):
        out_ref[:, 256 * f : 256 * f + 256] = sum_ref[f, :, 640:896]
    gains_ref[...] = (
        sum_ref[0, :, 512:640]
        + sum_ref[1, :, 512:640]
        + sum_ref[2, :, 512:640]
        + sum_ref[3, :, 512:640]
    )


def kernel_output(ys_ref, high_ref, rest_ref, mid_ref, out_ref, sum_ref):
    step = pl.program_id(0)

    @pl.when(step == 0)
    def _():
        sum_ref[...] = mid_ref[...]

    ys = ys_ref[...].reshape(512, WIDTH)
    sum_ref[...] += mm(high_ref[...], ys) + mm(rest_ref[...], ys)

    @pl.when(step == 3)
    def _():
        out_ref[...] = sum_ref[...].astype(BF)


def angles(positions, features):
    frequency = ROPE_BASE ** (-(features.astype(F32) * 2.0 / 64))
    return positions.astype(F32)[:, None] * frequency[None, :]


def whole(shape):
    return pl.BlockSpec(shape, lambda t: (0,) * len(shape))


def exchange(value, axes):
    return lax.all_to_all(value, axes, split_axis=0, concat_axis=0, tiled=True)


def gather(value, axes):
    return lax.all_gather(value, axes, axis=0, tiled=True)


def after(value, marker):
    return lax.optimization_barrier((value, marker))[0]


def swap(value, axis):
    return lax.ppermute(value, axis, [(0, 1), (1, 0)])


def neighbours(value):
    return value, swap(value, "core"), swap(value, "zl")


def cross(parts, axes=FSDP):
    here = [parts[0]]
    for r in range(1, 4):
        here.append(lax.ppermute(parts[r], axes, [(i, i ^ r) for i in range(4)]))
    return here


def on_device(
    layer_input,
    routes,
    gates,
    cotangent,
    norm_attn,
    query_key_value_weight,
    output_weight,
    norm_ffn,
    exp_gate,
    exp_up,
    exp_down,
):
    mine = lax.axis_index("y")
    ctx_index = lax.axis_index(CTX)
    part_index = lax.axis_index(FSDP)
    mine_ref = mine.astype(jnp.int32).reshape(1)
    part_ref = part_index.astype(jnp.int32).reshape(1)
    x = layer_input.reshape(128, WIDTH)
    cot = cotangent.reshape(128, WIDTH)
    slice_table = jnp.asarray(slice_matrix(), BF)
    head_table = jnp.asarray(head_matrix(), BF)

    x_all = neighbours(x)
    rank, gate = call(
        kernel_route,
        (sds((32, 128), F32), sds((32, 128), F32)),
        (1e6, 1e5),
        in_specs=[VM, VM],
        out_specs=(VM, VM),
    )(routes.reshape(128, 8).T, gates.reshape(128, 8).T)
    which = lax.broadcasted_iota(jnp.int32, (8, 128), 1)
    gain_rows = jnp.where(
        which == 0, norm_attn[:, None], jnp.where(which == 1, norm_ffn[:, None], 0.0)
    )
    slices = call(
        kernel_slices,
        sds((32, 4, 8, 896), BF),
        (2e7, 3e6),
        in_specs=[VM] * 5,
        out_specs=VM,
    )(query_key_value_weight, gain_rows, slice_table, gate, output_weight)
    slices, rank, gate, x_all = lax.optimization_barrier((slices, rank, gate, x_all))
    x_all = x_all + (swap(x_all[2], "core"),)
    offset = jnp.arange(64, dtype=jnp.int32)
    token_pos = jnp.concatenate([ctx_index * 64 + offset, (63 - ctx_index) * 64 + offset])
    column = jnp.arange(512, dtype=jnp.int32)
    angle = angles(token_pos, 8 * part_index + column % 8)
    is_value = (column // 16) % 4 == 3
    sign = jnp.where((column // 8) % 2 == 0, -1.0, 1.0)
    cos_slice = jnp.where(is_value, 1.0, jnp.cos(angle))
    sin_slice = jnp.where(is_value, 0.0, jnp.sin(angle) * sign)
    w_slice = exchange(slices.reshape(128, 8, 896), ALL)
    w_slice, cos_slice, sin_slice = lax.optimization_barrier((w_slice, cos_slice, sin_slice))
    gate_parts = lax.dynamic_slice(
        w_slice.reshape(32, 4, 8, 896), (0, part_index, 0, 512), (32, 1, 8, 128)
    ).reshape(32, 8, 128)
    w_slice = w_slice.reshape(WIDTH, 896)
    picks, picks_turned, picks_high, picks_rest = call(
        kernel_picks,
        (sds((2048, 128), BF),) + (sds((128, 2048), BF),) * 3,
        (2e9, 4e6),
        in_specs=[VM, VM],
        out_specs=(VM,) * 4,
    )(rank, gate)

    msg, hidden, gains = call(
        kernel_project,
        (sds((32, 64, 128), BF), sds((512, WIDTH), BF), sds((8, WIDTH), F32)),
        (6e8, 4e6),
        in_specs=[SM] + [VM] * 7,
        out_specs=(VM, VM, VM),
    )(part_ref, *x_all, w_slice, cos_slice, sin_slice)
    across = swap(after(cot, w_slice), "zh")
    first = lax.axis_index("zh") == 0
    cot_pair = jnp.concatenate(
        [jnp.where(first, cot, across), jnp.where(first, across, cot)], axis=0
    )
    out_upper = neighbours(w_slice[0:512, 640:896])
    msg = exchange(msg, HEAD_AXES + FSDP)

    kv_copies, queries = call(
        kernel_heads,
        (sds((4, 1024, 128), BF), sds((2, 8, 2, 64, 128), BF)),
        (4e8, 3e6),
        in_specs=[VM, VM],
        out_specs=(VM, VM),
    )(msg.reshape(8, 4, 64, 128), head_table)
    queries = queries.reshape(2048, 128)
    kv_copies, out_upper = lax.optimization_barrier((kv_copies, out_upper))
    out_lower = neighbours(after(w_slice[512:1024, 640:896], msg))
    kv = exchange(kv_copies, ("y",)).reshape(4, 2, 8, 64, 128)
    expert_weights = jnp.concatenate(
        [jnp.concatenate([exp_gate[0], exp_up[0]], axis=1), exp_down[0]], axis=0
    ).astype(BF)
    block = 4 * jnp.arange(8, dtype=jnp.int32)[:, None] + mine
    quarter_pos = jnp.concatenate(
        [
            (block * 64 + offset[None, :]).reshape(-1),
            ((63 - block) * 64 + offset[None, :]).reshape(-1),
        ]
    )
    column = jnp.arange(128, dtype=jnp.int32)
    angle = angles(quarter_pos, column % 32)
    sign = jnp.where(column % 64 < 32, -1.0, 1.0)
    cos_heads = jnp.where(column >= 64, 1.0, jnp.cos(angle))
    sin_heads = jnp.where(column >= 64, 0.0, jnp.sin(angle) * sign)
    kv, out_lower, cos_heads, sin_heads = lax.optimization_barrier(
        (kv, out_lower, cos_heads, sin_heads)
    )
    experts_all = neighbours(after(expert_weights, msg))
    cot_all = gather(after(cot_pair, kv_copies), ("x", "y")).reshape(4, 4, 2, 128, WIDTH)
    out_upper = out_upper + (swap(after(out_upper[2], kv), "core"),)
    out_lower = out_lower + (swap(out_lower[2], "core"),)
    w_out = (*out_upper, *out_lower)
    msg_spec = pl.BlockSpec((2, 1, 64, 128), lambda t: (t % 4, t // 4, 0, 0))
    row_spec = pl.BlockSpec((256, 128), lambda t: (t, 0))
    log_spec = pl.BlockSpec((1, 8, 256), lambda t: (t, 0, 0))
    o_msg, log_total, o_rows, keys, turned = call(
        kernel_attend,
        (
            sds((8, 2, 64, 128), BF),
            sds((8, 8, 256), F32),
            sds((2048, 128), F32),
            sds((4096, 128), BF),
            sds((128, 4096), BF),
        ),
        (1e10, 5e6),
        grid=(8,),
        in_specs=[SM, whole((4, 2, 8, 64, 128)), row_spec],
        out_specs=(msg_spec, log_spec, row_spec, whole((4096, 128)), whole((128, 4096))),
        scratch_shapes=[
            pltpu.VMEM((8, 256), F32),
            pltpu.VMEM((8, 256), F32),
            pltpu.VMEM((64, 256), F32),
        ],
    )(mine_ref, kv, queries)
    o_msg, w_out, experts_all = lax.optimization_barrier((o_msg, w_out, experts_all))
    experts_all = experts_all + (swap(experts_all[2], "core"),)
    o_heads = exchange(o_msg, HEAD_AXES)

    slot_spec = pl.BlockSpec((4, 64, WIDTH), lambda t: (t, 0, 0))
    out_specs = [whole((512, 256))] * 8
    slots, mid = call(
        kernel_middle,
        (sds((32, 64, WIDTH), BF), sds((128, WIDTH), F32)),
        (9e8, 8e6),
        grid=(2,),
        in_specs=[SM, whole((8, 2, 64, 128))]
        + out_specs
        + [
            whole((128, WIDTH)),
            whole((8, WIDTH)),
            pl.BlockSpec((1024, 128), lambda t: (t, 0)),
        ],
        out_specs=(pl.BlockSpec((16, 64, WIDTH), lambda t: (t, 0, 0)), whole((128, WIDTH))),
        scratch_shapes=[pltpu.VMEM((128, WIDTH), BF), pltpu.VMEM((128, WIDTH), BF)],
    )(part_ref, o_heads, *w_out, x, gains, picks)
    cot_all = after(cot_all, mid)
    slots, experts_all = lax.optimization_barrier((slots, experts_all))
    o_all = neighbours(after(o_heads, mid))
    slots = exchange(slots, CTX)
    dys, dact, down, gate_up = call(
        kernel_experts_ready,
        (
            sds((32, 64, WIDTH), BF),
            sds((2048, 512), F32),
            sds((512, WIDTH), BF),
            sds((WIDTH, WIDTH), BF),
        ),
        (6e9, 2e7),
        grid=(8,),
        in_specs=[
            SM,
            pl.BlockSpec((1, 4, 1, 128, WIDTH), lambda t: (t // 2, 0, t % 2, 0, 0)),
            whole((32, 8, 128)),
        ]
        + [whole((384, WIDTH))] * 4,
        out_specs=(
            slot_spec,
            pl.BlockSpec((256, 512), lambda t: (t, 0)),
            whole((512, WIDTH)),
            whole((WIDTH, WIDTH)),
        ),
        scratch_shapes=[pltpu.VMEM((32, 128), F32), pltpu.VMEM((32, 128), F32)],
    )(part_ref, cot_all, gate_parts, *experts_all)
    act_spec = pl.BlockSpec((256, 512), lambda t: (t, 0))
    both_spec = pl.BlockSpec((256, WIDTH), lambda t: (t, 0))
    act, dboth, dxs = call(
        kernel_experts,
        (sds((2048, 512), BF), sds((2048, WIDTH), BF), sds((32, 64, WIDTH), BF)),
        (9e9, 2e7),
        grid=(4,),
        in_specs=[
            pl.BlockSpec((8, 64, WIDTH), lambda t: (t, 0, 0)),
            whole((WIDTH, WIDTH)),
            pl.BlockSpec((512, 512), lambda t: (t, 0)),
        ],
        out_specs=(
            pl.BlockSpec((512, 512), lambda t: (t, 0)),
            pl.BlockSpec((512, WIDTH), lambda t: (t, 0)),
            pl.BlockSpec((8, 64, WIDTH), lambda t: (t, 0, 0)),
        ),
    )(slots, gate_up, dact)
    ys, expert_grads = call(
        kernel_experts_after,
        (sds((32, 64, WIDTH), BF), sds((4, 384, WIDTH), BF)),
        (9e9, 2e7),
        grid=(8,),
        in_specs=[slot_spec, act_spec, slot_spec, both_spec, whole((512, WIDTH))],
        out_specs=(slot_spec, whole((4, 384, WIDTH))),
        scratch_shapes=[pltpu.VMEM((WIDTH, WIDTH), F32), pltpu.VMEM((512, WIDTH), F32)],
    )(slots, act, dys, dboth, down)
    dxs, o_all = lax.optimization_barrier((dxs, o_all))
    o_all = o_all + (swap(o_all[2], "core"),)
    dxs = exchange(dxs, CTX)
    expert_own = lax.psum_scatter(
        expert_grads.reshape(4 * 384, WIDTH), FSDP, scatter_dimension=0, tiled=True
    ).astype(F32)
    dxs, ys, o_all = lax.optimization_barrier((dxs, ys, o_all))

    dmid, da_parts, grad_msg, gain_ffn_part = call(
        kernel_middle_back,
        (
            sds((128, WIDTH), F32),
            sds((4, 128, 256), BF),
            sds((8, 2, 64, 128), BF),
            sds((8, WIDTH), F32),
        ),
        (9e8, 8e6),
        grid=(2,),
        in_specs=[
            SM,
            pl.BlockSpec((16, 64, WIDTH), lambda t: (t, 0, 0)),
            pl.BlockSpec((128, 1024), lambda t: (0, t)),
            whole((128, WIDTH)),
            whole((128, WIDTH)),
            whole((8, WIDTH)),
        ]
        + out_specs,
        out_specs=(
            whole((128, WIDTH)),
            whole((4, 128, 256)),
            whole((8, 2, 64, 128)),
            whole((8, WIDTH)),
        ),
        scratch_shapes=[pltpu.VMEM((128, WIDTH), F32), pltpu.VMEM((128, WIDTH), BF)],
    )(part_ref, dxs, picks_turned, mid, cot, gains, *w_out)
    grad_heads = exchange(grad_msg, HEAD_AXES)
    ys, grad_heads = lax.optimization_barrier((ys, grad_heads))
    ys = exchange(ys, CTX)
    dq, *dkv = call(
        kernel_attend_back,
        (sds((2048, 128), F32),) + (sds((2, 8, 64, 128), BF),) * 4,
        (2e10, 7e6),
        grid=(8,),
        in_specs=[
            SM,
            whole((4096, 128)),
            whole((128, 4096)),
            row_spec,
            msg_spec,
            log_spec,
            row_spec,
        ],
        out_specs=(row_spec,) + (whole((2, 8, 64, 128)),) * 4,
        scratch_shapes=[pltpu.VMEM((4096, 128), F32)],
    )(mine_ref, keys, turned, queries, grad_heads, log_total, o_rows)
    da_here = cross(da_parts)
    dkv = cross(dkv, ("y",))
    dkv, ys, da_here = lax.optimization_barrier((dkv, ys, da_here))
    rest_part = call(
        kernel_out_weight,
        sds((WIDTH, 384), BF),
        (3e8, 2e6),
        in_specs=[VM] * 9,
        out_specs=VM,
    )(*o_all, *da_here, gain_ffn_part)
    layer_output = call(
        kernel_output,
        sds((128, WIDTH), BF),
        (1e9, 5e6),
        grid=(4,),
        in_specs=[
            pl.BlockSpec((8, 64, WIDTH), lambda t: (t, 0, 0)),
            pl.BlockSpec((128, 512), lambda t: (0, t)),
            pl.BlockSpec((128, 512), lambda t: (0, t)),
            whole((128, WIDTH)),
        ],
        out_specs=whole((128, WIDTH)),
        scratch_shapes=[pltpu.VMEM((128, WIDTH), F32)],
    )(ys, picks_high, picks_rest, mid)

    back = call(
        kernel_slices_back,
        sds((8, 4, 64, 128), BF),
        (4e8, 5e6),
        in_specs=[VM] * 8,
        out_specs=VM,
    )(*dkv, dq.reshape(2, 8, 2, 64, 128), cos_heads, sin_heads, head_table)
    back = exchange(back.reshape(32, 64, 128), HEAD_AXES + FSDP)

    grads, d_all = call(
        kernel_grads,
        (sds((WIDTH, 896), BF), sds((512, 512), BF)),
        (6e8, 5e6),
        in_specs=[VM] * 4,
        out_specs=(VM, VM),
    )(back, hidden, w_slice, rest_part)
    dh_parts = call(
        kernel_hidden_grad,
        (sds((128, WIDTH), BF),) * 4,
        (6e8, 5e6),
        in_specs=[SM, VM, VM],
        out_specs=(VM,) * 4,
    )(part_ref, d_all, w_slice)
    grads = exchange(grads.reshape(128, 8, 896), ALL)
    grad_qkv, grad_out, grad_gains = call(
        kernel_total,
        (sds((8, 2048), F32), sds((8, WIDTH), F32), sds((8, 128), F32)),
        (1e8, 4e6),
        in_specs=[VM, VM],
        out_specs=(VM, VM, VM),
        scratch_shapes=[pltpu.VMEM((4, 8, 896), F32)],
    )(grads.reshape(32, 4, 8, 896), slice_table)
    dh_here = cross(dh_parts)
    input_grad = call(
        kernel_input_grad,
        sds((128, WIDTH), F32),
        (1e6, 2e6),
        in_specs=[VM] * 7,
        out_specs=VM,
    )(*after(dh_here, grad_qkv), x, dmid, gains)
    return (
        layer_output.reshape(layer_input.shape),
        input_grad.reshape(layer_input.shape),
        grad_gains[:, 0],
        grad_qkv,
        grad_out,
        grad_gains[:, 1],
        expert_own[0:256, 0:512][None],
        expert_own[0:256, 512:1024][None],
        expert_own[256:384][None],
    )


def solution(mesh):
    parts = Mesh(mesh.devices.reshape(4, 2, 4, 2, 2), ALL)
    tokens = P(FSDP, CTX, None, None, None, None)
    experts = P(CTX, FSDP, None)
    in_specs = (
        tokens,
        tokens,
        tokens,
        tokens,
        P(ALL),
        P(ALL, None),
        P(ALL, None),
        P(ALL),
        experts,
        experts,
        experts,
    )
    out_specs = (
        tokens,
        tokens,
        P(ALL),
        P(ALL, None),
        P(ALL, None),
        P(ALL),
        experts,
        experts,
        experts,
    )
    return jax.shard_map(
        on_device, mesh=parts, in_specs=in_specs, out_specs=out_specs, check_vma=False
    )
```

```python
import functools

import jax
import jax.numpy as jnp
import numpy as np
from jax import lax
from jax.experimental import pallas as pl
from jax.experimental.pallas import tpu as pltpu
from jax.sharding import Mesh
from jax.sharding import PartitionSpec as P

WIDTH = 1024
EPSILON = 1e-06
ROPE_BASE = 10000.0
MASKED = -1e30
BF = jnp.bfloat16
F32 = jnp.float32
CTX = ("x", "zh", "y")
HEAD_AXES = ("x", "zh")
FSDP = ("zl", "core")
ALL = CTX + FSDP
VMEM_LIMIT = 56 * 1024 * 1024

NT = (((1,), (1,)), ((), ()))
TN = (((0,), (0,)), ((), ()))


def mm(a, b, dims=None):
    if dims is None:
        return jnp.dot(a, b, preferred_element_type=F32)
    return lax.dot_general(a, b, dims, preferred_element_type=F32)


def lane(shape):
    return lax.broadcasted_iota(jnp.int32, shape, len(shape) - 1)


def row(shape):
    return lax.broadcasted_iota(jnp.int32, shape, len(shape) - 2)


def call(kernel, out_shape, cost, **kw):
    flops, bytes_accessed = cost
    return pl.pallas_call(
        kernel,
        out_shape=out_shape,
        compiler_params=pltpu.CompilerParams(vmem_limit_bytes=VMEM_LIMIT),
        cost_estimate=pl.CostEstimate(
            flops=int(flops), bytes_accessed=int(bytes_accessed), transcendentals=0
        ),
        **kw,
    )


def sds(shape, dtype):
    return jax.ShapeDtypeStruct(shape, dtype)


VM = pl.BlockSpec(memory_space=pltpu.VMEM)
SM = pl.BlockSpec(memory_space=pltpu.SMEM)


def slice_matrix():
    table = np.zeros((512, 512), np.float32)
    for k in range(512):
        section, place = k // 128, k % 128
        if section < 2:
            pair, part = section, place // 64
        else:
            pair, part = place // 64, section
        feat = place % 64
        f = (feat % 32) // 8
        column = pair * 64 + part * 16 + (feat // 32) * 8 + feat % 8
        table[k, f * 128 + column] = 1.0
    return table


def head_matrix():
    table = np.zeros((4, 128, 768), np.float32)
    for f in range(4):
        for block in range(2):
            for part in range(4):
                for j in range(16):
                    feat = (j // 8) * 32 + 8 * f + j % 8
                    source = block * 64 + part * 16 + j
                    if part == 2:
                        target = block * 128 + feat
                    elif part == 3:
                        target = block * 128 + 64 + feat
                    else:
                        target = 256 + block * 256 + part * 128 + feat
                    table[f, source, target] = 1.0
    return table


def place(part_ref, r, size):
    return pl.ds(pl.multiple_of(lax.bitwise_xor(part_ref[0], r) * size, size), size)


def kernel_route(picks_ref, gates_ref, rank_ref, gate_ref):
    experts = row((32, 128))
    gate = jnp.zeros((32, 128), F32)
    chosen = jnp.zeros((32, 128), F32)
    for k in range(8):
        hit = picks_ref[k : k + 1, :] == experts
        gate = gate + jnp.where(hit, gates_ref[k : k + 1, :], 0.0)
        chosen = chosen + jnp.where(hit, 1.0, 0.0)
    before = jnp.where(row((128, 128)) < lane((128, 128)), 1.0, 0.0).astype(BF)
    rank = mm(chosen.astype(BF), before)
    rank_ref[...] = jnp.where(chosen > 0.5, rank, -1.0)
    gate_ref[...] = gate


def kernel_slices(w_ref, gains_ref, table_ref, gate_ref, out_weight_ref, out_ref):
    w = w_ref[...].astype(BF).astype(F32)
    parts = []
    for p in range(4):
        parts.append(
            jnp.concatenate(
                [
                    w[:, 256 * p : 256 * p + 256],
                    w[:, 1024 + 128 * p : 1152 + 128 * p],
                    w[:, 1536 + 128 * p : 1664 + 128 * p],
                ],
                axis=1,
            )
        )
    stacked = jnp.concatenate(parts, axis=0).astype(BF)
    cut = mm(stacked, table_ref[...])
    columns = []
    for f in range(4):
        columns.append(
            jnp.concatenate(
                [cut[8 * p : 8 * p + 8, 128 * f : 128 * f + 128] for p in range(4)], axis=1
            ).astype(BF)
        )
    gains = gains_ref[...]
    left = lane((8, 128)) < 64
    sub = row((8, 128))
    for c in range(32):
        gate = gate_ref[c : c + 1, :]
        high = gate.astype(BF).astype(F32)
        middle = (gate - high).astype(BF).astype(F32)
        rest = gate - high - middle
        parts = jnp.where(
            sub < 2, high, jnp.where(sub < 4, middle, jnp.where(sub < 6, rest, 0.0))
        )
        parts = jnp.where(sub % 2 == 0, pltpu.roll(parts, 64, 1), parts)
        last = jnp.where(left, gains, parts).astype(BF)
        for f in range(4):
            out_ref[c, f, :, 0:512] = columns[f]
            out_ref[c, f, :, 512:640] = last
            out_ref[c, f, :, 640:896] = out_weight_ref[:, 256 * f : 256 * f + 256].astype(BF)


def kernel_picks(rank_ref, gate_ref, pick_ref, turned_ref, high_ref, rest_ref):
    slot = lax.broadcasted_iota(jnp.int32, (64, 128), 0).astype(F32)

    @pl.loop(0, 16)
    def _(p):
        picks, weights = [], []
        for e in (2 * p, 2 * p + 1):
            hit = slot == rank_ref[pl.ds(e, 1), :]
            picks.append(jnp.where(hit, 1.0, 0.0))
            weights.append(jnp.where(hit, gate_ref[pl.ds(e, 1), :], 0.0))
        picks = jnp.concatenate(picks, axis=0)
        weights = jnp.transpose(jnp.concatenate(weights, axis=0))
        at = pl.ds(pl.multiple_of(128 * p, 128), 128)
        pick_ref[at, :] = picks.astype(BF)
        turned_ref[:, at] = jnp.transpose(picks).astype(BF)
        high = weights.astype(BF)
        high_ref[:, at] = high
        rest_ref[:, at] = (weights - high.astype(F32)).astype(BF)


def kernel_project(
    part_ref, x0_ref, x1_ref, x2_ref, x3_ref, w_ref, cos_ref, sin_ref, msg_ref, hidden_ref, gains_ref
):
    gains = jnp.transpose(w_ref[:, 512:640].astype(F32))
    gains_ref[...] = gains[:8]
    for r, x_ref in enumerate((x0_ref, x1_ref, x2_ref, x3_ref)):
        x = x_ref[...].astype(F32)
        scale = lax.rsqrt(jnp.mean(x * x, axis=-1, keepdims=True) + EPSILON)
        hidden_ref[place(part_ref, r, 128), :] = (x * scale * gains[0:1]).astype(BF)
    proj = mm(hidden_ref[...], w_ref[:, 0:512])
    ahead = pltpu.roll(proj, 512 - 8, 1)
    behind = pltpu.roll(proj, 8, 1)
    partner = jnp.where((lane((512, 512)) // 8) % 2 == 0, ahead, behind)
    cos = jnp.concatenate([cos_ref[...]] * 4, axis=0)
    sin = jnp.concatenate([sin_ref[...]] * 4, axis=0)
    turned = proj * cos + partner * sin
    low = lane((64, 128)) < 64
    for s in range(4):
        for p in range(4):
            front = turned[128 * s : 128 * s + 64, 128 * p : 128 * p + 128]
            back = turned[128 * s + 64 : 128 * s + 128, 128 * p : 128 * p + 128]
            msg_ref[8 * p + s] = jnp.where(low, front, pltpu.roll(back, 64, 1)).astype(BF)
            msg_ref[8 * p + 4 + s] = jnp.where(low, pltpu.roll(front, 64, 1), back).astype(BF)


def kernel_heads(msg_ref, table_ref, kv_ref, q_ref):
    out = jnp.zeros((512, 768), F32)
    for f in range(4):
        out = out + mm(msg_ref[:, f].reshape(512, 128), table_ref[f])
    pairs = out[:, 0:256].astype(BF)
    for half in range(2):
        block = pairs[:, 128 * half : 128 * half + 128]
        for y in range(4):
            kv_ref[y, 512 * half : 512 * half + 512, :] = block
    queries = (out[:, 256:768] * 0.125).astype(BF)
    for half in range(2):
        for head in range(2):
            at = 256 * half + 128 * head
            q_ref[half, :, head] = queries[:, at : at + 128].reshape(8, 64, 128)


def tile_positions(tile, mine):
    front = tile < 4
    i = jnp.where(front, tile, tile - 4)
    q = lane((1, 256))
    k = lax.broadcasted_iota(jnp.int32, (512, 1), 0)
    q_front = (8 * i + 4 * (q // 128) + mine) * 64 + q % 64
    q_back = (63 - 8 * i - 4 * (q // 128) - mine) * 64 + q % 64
    k_front = 512 * i + k
    k_back = (59 - 8 * i + 4 * (k // 256) - (k % 256) // 64) * 64 + k % 64
    return jnp.where(front, q_front, q_back), jnp.where(front, k_front, k_back)


def kernel_attend(
    mine_ref,
    kv_ref,
    q_ref,
    msg_ref,
    log_ref,
    out_ref,
    keys_ref,
    turned_ref,
    peak_ref,
    total_ref,
    mixed_ref,
):
    tile = pl.program_id(0)

    @pl.when(tile == 0)
    def _():
        for group in range(16):
            half, place = (0, group) if group < 8 else (1, 15 - group)
            for y in range(4):
                at = 256 * group + 64 * y
                keys_ref[at : at + 64, :] = kv_ref[y, half, place]
        for c in range(8):
            turned_ref[:, 512 * c : 512 * c + 512] = jnp.transpose(
                keys_ref[512 * c : 512 * c + 512, :].astype(F32)
            ).astype(BF)

    q = q_ref[...]
    q_pos, k_pos = tile_positions(tile, mine_ref[0])

    def run(first, count, last):
        def keys(c):
            return pl.ds(pl.multiple_of(first + 512 * c, 512), 512)

        peak = peak_ref[0:1]
        total = total_ref[0:1]
        mixed = mixed_ref[...]
        later = mm(keys_ref[keys(0), :], q, NT)
        for c in range(count):
            scores = later
            if c + 1 < count:
                later = mm(keys_ref[keys(c + 1), :], q, NT)
            elif last:
                scores = jnp.where(k_pos <= q_pos, scores, MASKED)
            higher = jnp.maximum(peak, jnp.max(scores, axis=0, keepdims=True))
            weights = jnp.exp(scores - higher)
            fade = jnp.exp(peak - higher)
            total = total * fade + jnp.sum(weights, axis=0, keepdims=True)
            mixed = mixed * fade + mm(turned_ref[64:128, keys(c)], weights.astype(BF))
            peak = higher
        peak_ref[...] = jnp.broadcast_to(peak, (8, 256))
        total_ref[...] = jnp.broadcast_to(total, (8, 256))
        mixed_ref[...] = mixed

    peak_ref[...] = jnp.full((8, 256), MASKED, F32)
    total_ref[...] = jnp.zeros((8, 256), F32)
    mixed_ref[...] = jnp.zeros((64, 256), F32)

    @pl.when(tile >= 4)
    def _():
        run(0, 4, False)

    first = jnp.where(tile >= 4, 2048, 0)
    rest = jnp.where(tile >= 4, 8 - tile, tile + 1)
    for count in range(1, 5):
        pl.when(rest == count)(functools.partial(run, first, count, True))

    total = total_ref[0:1]
    log_ref[0] = jnp.broadcast_to(peak_ref[0:1] + jnp.log(total), (8, 256))
    mixed = mixed_ref[...] / total
    out = jnp.transpose(jnp.concatenate([jnp.zeros((64, 256), F32), mixed], axis=0))
    out_ref[...] = out
    low = lane((64, 128)) < 64
    for a in range(2):
        one = out[128 * a : 128 * a + 64]
        two = out[128 * a + 64 : 128 * a + 128]
        msg_ref[a, 0] = jnp.where(low, pltpu.roll(one, 64, 1), two).astype(BF)


def kernel_attend_back(
    mine_ref, keys_ref, turned_ref, q_ref, grad_ref, log_ref, out_ref, dq_ref, d0_ref, d1_ref, d2_ref, d3_ref, sum_ref
):
    tile = pl.program_id(0)

    @pl.when(tile == 0)
    def _():
        sum_ref[...] = jnp.zeros_like(sum_ref)

    q = q_ref[...]
    low = lane((64, 128)) < 64
    pieces = []
    for a in range(2):
        both = grad_ref[a, 0].astype(F32)
        pieces.append(jnp.where(low, 0.0, pltpu.roll(both, 64, 1)))
        pieces.append(jnp.where(low, 0.0, both))
    grad = jnp.concatenate(pieces, axis=0)
    delta = jnp.sum(jnp.transpose(grad * out_ref[...]), axis=0, keepdims=True)
    grad = grad.astype(BF)
    q_pos, k_pos = tile_positions(tile, mine_ref[0])
    log_total = log_ref[0][0:1]

    def step(c, dq, last):
        at = pl.ds(pl.multiple_of(c * 512, 512), 512)
        keys = keys_ref[at, :]
        scores = mm(keys, q, NT)
        if last:
            scores = jnp.where(k_pos <= q_pos, scores, MASKED)
        weights = jnp.exp(scores - log_total)
        slope = (weights * (mm(keys, grad, NT) - delta)).astype(BF)
        sum_ref[at, :] += mm(slope, q) + mm(weights.astype(BF), grad)
        return dq + mm(turned_ref[0:64, at], slope)

    count = jnp.where(tile < 4, tile + 1, 12 - tile)
    dq = lax.fori_loop(0, count - 1, lambda c, v: step(c, v, False), jnp.zeros((64, 256), F32))
    dq = step(count - 1, dq, True)
    dq_ref[...] = jnp.transpose(jnp.concatenate([dq * 0.125, jnp.zeros((64, 256), F32)], axis=0))

    @pl.when(tile == 7)
    def _():
        for group in range(16):
            half, place = (0, group) if group < 8 else (1, 15 - group)
            for r, dkv_ref in enumerate((d0_ref, d1_ref, d2_ref, d3_ref)):
                at = 256 * group + 64 * lax.bitwise_xor(mine_ref[0], r)
                part = sum_ref[pl.ds(pl.multiple_of(at, 64), 64), :]
                dkv_ref[half, place] = part.astype(BF)


def kernel_middle(
    part_ref,
    o_ref,
    u0_ref,
    u1_ref,
    u2_ref,
    u3_ref,
    l0_ref,
    l1_ref,
    l2_ref,
    l3_ref,
    x_ref,
    gains_ref,
    pick_ref,
    slots_ref,
    mid_ref,
    rows_ref,
    hidden_ref,
):
    @pl.when(pl.program_id(0) == 0)
    def _():
        for g in range(8):
            rows_ref[:, 128 * g : 128 * g + 128] = o_ref[g].reshape(128, 128)
        uppers = (u0_ref, u1_ref, u2_ref, u3_ref)
        lowers = (l0_ref, l1_ref, l2_ref, l3_ref)
        for r in range(4):
            at = place(part_ref, r, 256)
            mid_ref[:, at] = (
                x_ref[:, at].astype(F32)
                + mm(rows_ref[:, 0:512], uppers[r][...])
                + mm(rows_ref[:, 512:1024], lowers[r][...])
            )
        mid = mid_ref[...]
        scale = lax.rsqrt(jnp.mean(mid * mid, axis=-1, keepdims=True) + EPSILON)
        hidden_ref[...] = (mid * scale * gains_ref[1:2]).astype(BF)

    for c in range(4):
        at = slice(256 * c, 256 * c + 256)
        rows = mm(pick_ref[...], hidden_ref[:, at]).astype(BF)
        slots_ref[:, :, at] = rows.reshape(16, 64, 256)


def kernel_experts_ready(
    part_ref,
    dy_ref,
    parts_ref,
    w0_ref,
    w1_ref,
    w2_ref,
    w3_ref,
    dys_ref,
    dact_ref,
    v_ref,
    gu_ref,
    rank_ref,
    gate_ref,
):
    step = pl.program_id(0)

    @pl.when(step == 0)
    def _():
        for r, w_ref in enumerate((w0_ref, w1_ref, w2_ref, w3_ref)):
            gu_ref[place(part_ref, r, 256), :] = w_ref[0:256, :]
            v_ref[place(part_ref, r, 128), :] = w_ref[256:384, :]
        before = jnp.where(row((128, 128)) < lane((128, 128)), 1.0, 0.0).astype(BF)
        parts = [parts_ref[:, k, :].astype(F32) for k in range(6)]
        even = parts[0] + parts[2] + parts[4]
        odd = parts[1] + parts[3] + parts[5]
        gate_ref[...] = jnp.where(lane((32, 128)) < 64, pltpu.roll(even, 64, 1), odd)
        chosen = gate_ref[...] > 0.0
        rank = mm(jnp.where(chosen, 1.0, 0.0).astype(BF), before)
        rank_ref[...] = jnp.where(chosen, rank, -1.0)

    slot = lax.broadcasted_iota(jnp.int32, (64, 128), 0).astype(F32)
    grads = []
    for j in range(4):
        source = 4 * step + j
        pick = slot == rank_ref[pl.ds(source, 1), :]
        weight = jnp.sum(
            jnp.where(pick, gate_ref[pl.ds(source, 1), :], 0.0), axis=1, keepdims=True
        )
        rows = mm(jnp.where(pick, 1.0, 0.0).astype(BF), dy_ref[0, j, 0])
        grads.append((rows * weight).astype(BF))
    dys = jnp.concatenate(grads, axis=0)
    dys_ref[...] = dys.reshape(4, 64, WIDTH)
    dact_ref[...] = mm(dys, v_ref[...], NT)


def kernel_experts(h_ref, gu_ref, dact_ref, act_ref, dboth_ref, dxs_ref):
    def project(part):
        return mm(h_ref[4 * part : 4 * part + 4].reshape(256, WIDTH), gu_ref[...])

    later = project(0)
    for part in range(2):
        both = later
        if part == 0:
            later = project(1)
        at = slice(256 * part, 256 * part + 256)
        gate_h, up_h = both[:, :512], both[:, 512:]
        sig = 0.5 * jnp.tanh(0.5 * gate_h) + 0.5
        swished = gate_h * sig
        act_ref[at, :] = (swished * up_h).astype(BF)
        dact = dact_ref[at, :]
        dgate = (dact * up_h * (sig + swished * (1.0 - sig))).astype(BF)
        dup = (dact * swished).astype(BF)
        dboth = jnp.concatenate([dgate, dup], axis=1)
        dboth_ref[at, :] = dboth
        dxs = mm(dboth, gu_ref[...], NT).astype(BF)
        dxs_ref[4 * part : 4 * part + 4] = dxs.reshape(4, 64, WIDTH)


def kernel_experts_after(
    h_ref, act_ref, dys_ref, dboth_ref, v_ref, ys_ref, grad_ref, ggu_ref, gv_ref
):
    step = pl.program_id(0)

    @pl.when(step == 0)
    def _():
        ggu_ref[...] = jnp.zeros_like(ggu_ref)
        gv_ref[...] = jnp.zeros_like(gv_ref)

    act = act_ref[...]
    ys_ref[...] = mm(act, v_ref[...]).astype(BF).reshape(4, 64, WIDTH)
    h = h_ref[...].reshape(256, WIDTH)

    @pl.loop(0, 4)
    def _(c):
        at = pl.ds(pl.multiple_of(256 * c, 256), 256)
        ggu_ref[:, at] += mm(h, dboth_ref[:, at], TN)

    gv_ref[...] += mm(act, dys_ref[...].reshape(256, WIDTH), TN)

    @pl.when(step == 7)
    def _():
        for f in range(4):
            grad_ref[f, 0:256, :] = ggu_ref[256 * f : 256 * f + 256, :].astype(BF)
            grad_ref[f, 256:384, :] = gv_ref[128 * f : 128 * f + 128, :].astype(BF)


def kernel_middle_back(
    part_ref,
    dxs_ref,
    pick_ref,
    mid_ref,
    cot_ref,
    gains_ref,
    u0_ref,
    u1_ref,
    u2_ref,
    u3_ref,
    l0_ref,
    l1_ref,
    l2_ref,
    l3_ref,
    dmid_ref,
    parts_ref,
    msg_ref,
    ggain_ref,
    sum_ref,
    low_ref,
):
    step = pl.program_id(0)
    part = mm(pick_ref[...], dxs_ref[...].reshape(1024, WIDTH))

    @pl.when(step == 0)
    def _():
        sum_ref[...] = part

    @pl.when(step > 0)
    def _():
        sum_ref[...] += part

    @pl.when(step == 1)
    def _():
        mid = mid_ref[...]
        scale = lax.rsqrt(jnp.mean(mid * mid, axis=-1, keepdims=True) + EPSILON)
        dh = sum_ref[...]
        ggain_ref[...] = jnp.broadcast_to(
            jnp.sum(dh * (mid * scale), axis=0, keepdims=True), (8, WIDTH)
        )
        dn = dh * gains_ref[1:2]
        dmid = (
            cot_ref[...].astype(F32)
            + scale * dn
            - mid * (scale * scale * scale) * jnp.mean(dn * mid, axis=-1, keepdims=True)
        )
        dmid_ref[...] = dmid
        low_ref[...] = dmid.astype(BF)
        uppers = (u0_ref, u1_ref, u2_ref, u3_ref)
        lowers = (l0_ref, l1_ref, l2_ref, l3_ref)
        for r in range(4):
            parts_ref[r] = low_ref[:, place(part_ref, r, 256)]
        for h, w_refs in enumerate((uppers, lowers)):
            grad = mm(parts_ref[0], w_refs[0][...], NT)
            for r in range(1, 4):
                grad = grad + mm(parts_ref[r], w_refs[r][...], NT)
            grad = grad.astype(BF)
            for g in range(4):
                msg_ref[4 * h + g] = grad[:, 128 * g : 128 * g + 128].reshape(2, 64, 128)


def kernel_out_weight(
    o0_ref, o1_ref, o2_ref, o3_ref, da0_ref, da1_ref, da2_ref, da3_ref, gain_ref, grad_ref
):
    which = lax.broadcasted_iota(jnp.int32, (128, WIDTH), 0)
    grad_ref[:, 0:128] = jnp.transpose(jnp.where(which == 1, gain_ref[0:1], 0.0)).astype(BF)
    pairs = ((o0_ref, da0_ref), (o1_ref, da1_ref), (o2_ref, da2_ref), (o3_ref, da3_ref))

    @pl.loop(0, 8)
    def _(g):
        part = jnp.zeros((128, 256), F32)
        for o_ref, da_ref in pairs:
            part = part + mm(o_ref[g].reshape(128, 128), da_ref[...], TN)
        grad_ref[pl.ds(pl.multiple_of(128 * g, 128), 128), 128:384] = part.astype(BF)


def unrotate(w, cos, sin):
    partner = jnp.where(lane(w.shape) % 64 < 32, pltpu.roll(w, 96, 1), pltpu.roll(w, 32, 1))
    return (w * cos - partner * sin).astype(BF)


def kernel_queries_back(
    dq_ref, cos_ref, sin_ref, table_ref, hidden_ref, msg_ref, hidden_turned_ref
):
    for s in range(4):
        at = slice(128 * s, 128 * s + 128)
        hidden_turned_ref[:, at] = jnp.transpose(hidden_ref[at, :].astype(F32)).astype(BF)
    parts = []
    for half in range(2):
        at = slice(512 * half, 512 * half + 512)
        for head in range(2):
            dq = dq_ref[half, :, head].reshape(512, 128)
            parts.append(unrotate(dq, cos_ref[at, :], sin_ref[at, :]))
    whole = jnp.concatenate(parts, axis=1)
    for f in range(4):
        rows = mm(whole, table_ref[f, :, 256:768], NT)
        msg_ref[:, f] = rows.astype(BF).reshape(8, 64, 128)


def kernel_slices_back(
    d0_ref, d1_ref, d2_ref, d3_ref, queries_ref, cos_ref, sin_ref, table_ref, msg_ref
):
    parts = []
    for half in range(2):
        at = slice(512 * half, 512 * half + 512)
        dkv = d0_ref[half].reshape(512, 128).astype(F32)
        for d_ref in (d1_ref, d2_ref, d3_ref):
            dkv = dkv + d_ref[half].reshape(512, 128).astype(F32)
        parts.append(unrotate(dkv, cos_ref[at, :], sin_ref[at, :]))
    whole = jnp.concatenate(parts, axis=1)
    for f in range(4):
        rows = mm(whole, table_ref[f, :, 0:256], NT) + queries_ref[:, f].reshape(512, 128)
        msg_ref[:, f] = rows.astype(BF).reshape(8, 64, 128)


def kernel_hidden_grad(part_ref, d_ref, w_ref, h0_ref, h1_ref, h2_ref, h3_ref):
    for r, h_ref in enumerate((h0_ref, h1_ref, h2_ref, h3_ref)):
        h_ref[...] = mm(d_ref[place(part_ref, r, 128), :], w_ref[:, 0:512], NT).astype(BF)


def kernel_grads(msg_ref, hidden_ref, w_ref, rest_ref, grads_ref, d_ref):
    low = lane((64, 128)) < 64
    for s in range(4):
        for p in range(4):
            even = msg_ref[8 * p + s].astype(F32)
            odd = msg_ref[8 * p + 4 + s].astype(F32)
            d_ref[128 * s : 128 * s + 64, 128 * p : 128 * p + 128] = jnp.where(
                low, even, pltpu.roll(odd, 64, 1)
            ).astype(BF)
            d_ref[128 * s + 64 : 128 * s + 128, 128 * p : 128 * p + 128] = jnp.where(
                low, pltpu.roll(even, 64, 1), odd
            ).astype(BF)
    total = mm(hidden_ref[...], d_ref[...])
    grads_ref[:, 0:512] = total.astype(BF)
    gain = jnp.sum(total * w_ref[:, 0:512].astype(F32), axis=1, keepdims=True)
    gain = gain / w_ref[:, 512:640].astype(F32)[:, 0:1]
    rest = rest_ref[:, 0:128]
    grads_ref[:, 512:640] = jnp.where(lane((WIDTH, 128)) == 0, gain.astype(BF), rest)
    grads_ref[:, 640:896] = rest_ref[:, 128:384]


def kernel_input_grad(d0_ref, d1_ref, d2_ref, d3_ref, x_ref, dmid_ref, gains_ref, out_ref):
    dh = d0_ref[...].astype(F32)
    for d_ref in (d1_ref, d2_ref, d3_ref):
        dh = dh + d_ref[...].astype(F32)
    x = x_ref[...].astype(F32)
    scale = lax.rsqrt(jnp.mean(x * x, axis=-1, keepdims=True) + EPSILON)
    dn = dh * gains_ref[0:1]
    out_ref[...] = (
        dmid_ref[...]
        + scale * dn
        - x * (scale * scale * scale) * jnp.mean(dn * x, axis=-1, keepdims=True)
    )


def kernel_total(parts_ref, table_ref, qkv_ref, out_ref, gains_ref, sum_ref):
    total = parts_ref[0].astype(F32)
    for c in range(1, 32):
        total = total + parts_ref[c].astype(F32)
    sum_ref[...] = total
    rows = []
    for p in range(4):
        rows.append(
            jnp.concatenate([sum_ref[f, :, 128 * p : 128 * p + 128] for f in range(4)], axis=1)
        )
    rest = jnp.concatenate(rows, axis=0)
    parts = []
    for _ in range(3):
        part = rest.astype(BF)
        rest = rest - part.astype(F32)
        parts.append(part)
    whole = mm(jnp.concatenate(parts, axis=0), table_ref[...], NT)
    whole = whole[0:32] + whole[32:64] + whole[64:96]
    for p in range(4):
        piece = whole[8 * p : 8 * p + 8]
        qkv_ref[:, 256 * p : 256 * p + 256] = piece[:, 0:256]
        qkv_ref[:, 1024 + 128 * p : 1152 + 128 * p] = piece[:, 256:384]
        qkv_ref[:, 1536 + 128 * p : 1664 + 128 * p] = piece[:, 384:512]
    for f in range(4):
        out_ref[:, 256 * f : 256 * f + 256] = sum_ref[f, :, 640:896]
    gains_ref[...] = (
        sum_ref[0, :, 512:640]
        + sum_ref[1, :, 512:640]
        + sum_ref[2, :, 512:640]
        + sum_ref[3, :, 512:640]
    )


def kernel_output(ys_ref, high_ref, rest_ref, mid_ref, out_ref, sum_ref):
    step = pl.program_id(0)

    @pl.when(step == 0)
    def _():
        sum_ref[...] = mid_ref[...]

    ys = ys_ref[...].reshape(512, WIDTH)
    sum_ref[...] += mm(high_ref[...], ys) + mm(rest_ref[...], ys)

    @pl.when(step == 3)
    def _():
        out_ref[...] = sum_ref[...].astype(BF)


def angles(positions, features):
    frequency = ROPE_BASE ** (-(features.astype(F32) * 2.0 / 64))
    return positions.astype(F32)[:, None] * frequency[None, :]


def whole(shape):
    return pl.BlockSpec(shape, lambda t: (0,) * len(shape))


def exchange(value, axes):
    return lax.all_to_all(value, axes, split_axis=0, concat_axis=0, tiled=True)


def gather(value, axes):
    return lax.all_gather(value, axes, axis=0, tiled=True)


def after(value, marker):
    return lax.optimization_barrier((value, marker))[0]


def swap(value, axis):
    return lax.ppermute(value, axis, [(0, 1), (1, 0)])


def neighbours(value):
    return value, swap(value, "core"), swap(value, "zl")


def cross(parts, axes=FSDP):
    here = [parts[0]]
    for r in range(1, 4):
        here.append(lax.ppermute(parts[r], axes, [(i, i ^ r) for i in range(4)]))
    return here


def on_device(
    layer_input,
    routes,
    gates,
    cotangent,
    norm_attn,
    query_key_value_weight,
    output_weight,
    norm_ffn,
    exp_gate,
    exp_up,
    exp_down,
):
    mine = lax.axis_index("y")
    ctx_index = lax.axis_index(CTX)
    part_index = lax.axis_index(FSDP)
    mine_ref = mine.astype(jnp.int32).reshape(1)
    part_ref = part_index.astype(jnp.int32).reshape(1)
    x = layer_input.reshape(128, WIDTH)
    cot = cotangent.reshape(128, WIDTH)
    slice_table = jnp.asarray(slice_matrix(), BF)
    head_table = jnp.asarray(head_matrix(), BF)

    x_all = neighbours(x)
    rank, gate = call(
        kernel_route,
        (sds((32, 128), F32), sds((32, 128), F32)),
        (1e6, 1e5),
        in_specs=[VM, VM],
        out_specs=(VM, VM),
    )(routes.reshape(128, 8).T, gates.reshape(128, 8).T)
    which = lax.broadcasted_iota(jnp.int32, (8, 128), 1)
    gain_rows = jnp.where(
        which == 0, norm_attn[:, None], jnp.where(which == 1, norm_ffn[:, None], 0.0)
    )
    slices = call(
        kernel_slices,
        sds((32, 4, 8, 896), BF),
        (2e7, 3e6),
        in_specs=[VM] * 5,
        out_specs=VM,
    )(query_key_value_weight, gain_rows, slice_table, gate, output_weight)
    slices, rank, gate, x_all = lax.optimization_barrier((slices, rank, gate, x_all))
    x_all = x_all + (swap(x_all[2], "core"),)
    offset = jnp.arange(64, dtype=jnp.int32)
    token_pos = jnp.concatenate([ctx_index * 64 + offset, (63 - ctx_index) * 64 + offset])
    column = jnp.arange(512, dtype=jnp.int32)
    angle = angles(token_pos, 8 * part_index + column % 8)
    is_value = (column // 16) % 4 == 3
    sign = jnp.where((column // 8) % 2 == 0, -1.0, 1.0)
    cos_slice = jnp.where(is_value, 1.0, jnp.cos(angle))
    sin_slice = jnp.where(is_value, 0.0, jnp.sin(angle) * sign)
    w_slice = exchange(slices.reshape(128, 8, 896), ALL)
    w_slice, cos_slice, sin_slice = lax.optimization_barrier((w_slice, cos_slice, sin_slice))
    gate_parts = lax.dynamic_slice(
        w_slice.reshape(32, 4, 8, 896), (0, part_index, 0, 512), (32, 1, 8, 128)
    ).reshape(32, 8, 128)
    w_slice = w_slice.reshape(WIDTH, 896)
    picks, picks_turned, picks_high, picks_rest = call(
        kernel_picks,
        (sds((2048, 128), BF),) + (sds((128, 2048), BF),) * 3,
        (2e9, 4e6),
        in_specs=[VM, VM],
        out_specs=(VM,) * 4,
    )(rank, gate)

    msg, hidden, gains = call(
        kernel_project,
        (sds((32, 64, 128), BF), sds((512, WIDTH), BF), sds((8, WIDTH), F32)),
        (6e8, 4e6),
        in_specs=[SM] + [VM] * 7,
        out_specs=(VM, VM, VM),
    )(part_ref, *x_all, w_slice, cos_slice, sin_slice)
    across = swap(after(cot, w_slice), "zh")
    first = lax.axis_index("zh") == 0
    cot_pair = jnp.concatenate(
        [jnp.where(first, cot, across), jnp.where(first, across, cot)], axis=0
    )
    out_upper = neighbours(w_slice[0:512, 640:896])
    msg = exchange(msg, HEAD_AXES + FSDP)

    kv_copies, queries = call(
        kernel_heads,
        (sds((4, 1024, 128), BF), sds((2, 8, 2, 64, 128), BF)),
        (4e8, 3e6),
        in_specs=[VM, VM],
        out_specs=(VM, VM),
    )(msg.reshape(8, 4, 64, 128), head_table)
    queries = queries.reshape(2048, 128)
    kv_copies, out_upper = lax.optimization_barrier((kv_copies, out_upper))
    out_lower = neighbours(after(w_slice[512:1024, 640:896], msg))
    kv = exchange(kv_copies, ("y",)).reshape(4, 2, 8, 64, 128)
    expert_weights = jnp.concatenate(
        [jnp.concatenate([exp_gate[0], exp_up[0]], axis=1), exp_down[0]], axis=0
    ).astype(BF)
    block = 4 * jnp.arange(8, dtype=jnp.int32)[:, None] + mine
    quarter_pos = jnp.concatenate(
        [
            (block * 64 + offset[None, :]).reshape(-1),
            ((63 - block) * 64 + offset[None, :]).reshape(-1),
        ]
    )
    column = jnp.arange(128, dtype=jnp.int32)
    angle = angles(quarter_pos, column % 32)
    sign = jnp.where(column % 64 < 32, -1.0, 1.0)
    cos_heads = jnp.where(column >= 64, 1.0, jnp.cos(angle))
    sin_heads = jnp.where(column >= 64, 0.0, jnp.sin(angle) * sign)
    kv, out_lower, cos_heads, sin_heads = lax.optimization_barrier(
        (kv, out_lower, cos_heads, sin_heads)
    )
    experts_all = neighbours(after(expert_weights, msg))
    cot_all = gather(after(cot_pair, kv_copies), ("x", "y")).reshape(4, 4, 2, 128, WIDTH)
    out_upper = out_upper + (swap(after(out_upper[2], kv), "core"),)
    out_lower = out_lower + (swap(out_lower[2], "core"),)
    w_out = (*out_upper, *out_lower)
    msg_spec = pl.BlockSpec((2, 1, 64, 128), lambda t: (t % 4, t // 4, 0, 0))
    row_spec = pl.BlockSpec((256, 128), lambda t: (t, 0))
    log_spec = pl.BlockSpec((1, 8, 256), lambda t: (t, 0, 0))
    o_msg, log_total, o_rows, keys, turned = call(
        kernel_attend,
        (
            sds((8, 2, 64, 128), BF),
            sds((8, 8, 256), F32),
            sds((2048, 128), F32),
            sds((4096, 128), BF),
            sds((128, 4096), BF),
        ),
        (1e10, 5e6),
        grid=(8,),
        in_specs=[SM, whole((4, 2, 8, 64, 128)), row_spec],
        out_specs=(msg_spec, log_spec, row_spec, whole((4096, 128)), whole((128, 4096))),
        scratch_shapes=[
            pltpu.VMEM((8, 256), F32),
            pltpu.VMEM((8, 256), F32),
            pltpu.VMEM((64, 256), F32),
        ],
    )(mine_ref, kv, queries)
    o_msg, w_out, experts_all = lax.optimization_barrier((o_msg, w_out, experts_all))
    experts_all = experts_all + (swap(experts_all[2], "core"),)
    o_heads = exchange(o_msg, HEAD_AXES)

    slot_spec = pl.BlockSpec((4, 64, WIDTH), lambda t: (t, 0, 0))
    out_specs = [whole((512, 256))] * 8
    slots, mid = call(
        kernel_middle,
        (sds((32, 64, WIDTH), BF), sds((128, WIDTH), F32)),
        (9e8, 8e6),
        grid=(2,),
        in_specs=[SM, whole((8, 2, 64, 128))]
        + out_specs
        + [
            whole((128, WIDTH)),
            whole((8, WIDTH)),
            pl.BlockSpec((1024, 128), lambda t: (t, 0)),
        ],
        out_specs=(pl.BlockSpec((16, 64, WIDTH), lambda t: (t, 0, 0)), whole((128, WIDTH))),
        scratch_shapes=[pltpu.VMEM((128, WIDTH), BF), pltpu.VMEM((128, WIDTH), BF)],
    )(part_ref, o_heads, *w_out, x, gains, picks)
    cot_all = after(cot_all, mid)
    slots, experts_all = lax.optimization_barrier((slots, experts_all))
    slots = exchange(slots, CTX)
    dys, dact, down, gate_up = call(
        kernel_experts_ready,
        (
            sds((32, 64, WIDTH), BF),
            sds((2048, 512), F32),
            sds((512, WIDTH), BF),
            sds((WIDTH, WIDTH), BF),
        ),
        (6e9, 2e7),
        grid=(8,),
        in_specs=[
            SM,
            pl.BlockSpec((1, 4, 1, 128, WIDTH), lambda t: (t // 2, 0, t % 2, 0, 0)),
            whole((32, 8, 128)),
        ]
        + [whole((384, WIDTH))] * 4,
        out_specs=(
            slot_spec,
            pl.BlockSpec((256, 512), lambda t: (t, 0)),
            whole((512, WIDTH)),
            whole((WIDTH, WIDTH)),
        ),
        scratch_shapes=[pltpu.VMEM((32, 128), F32), pltpu.VMEM((32, 128), F32)],
    )(part_ref, cot_all, gate_parts, *experts_all)
    act_spec = pl.BlockSpec((256, 512), lambda t: (t, 0))
    both_spec = pl.BlockSpec((256, WIDTH), lambda t: (t, 0))
    act, dboth, dxs = call(
        kernel_experts,
        (sds((2048, 512), BF), sds((2048, WIDTH), BF), sds((32, 64, WIDTH), BF)),
        (9e9, 2e7),
        grid=(4,),
        in_specs=[
            pl.BlockSpec((8, 64, WIDTH), lambda t: (t, 0, 0)),
            whole((WIDTH, WIDTH)),
            pl.BlockSpec((512, 512), lambda t: (t, 0)),
        ],
        out_specs=(
            pl.BlockSpec((512, 512), lambda t: (t, 0)),
            pl.BlockSpec((512, WIDTH), lambda t: (t, 0)),
            pl.BlockSpec((8, 64, WIDTH), lambda t: (t, 0, 0)),
        ),
    )(slots, gate_up, dact)
    ys, expert_grads = call(
        kernel_experts_after,
        (sds((32, 64, WIDTH), BF), sds((4, 384, WIDTH), BF)),
        (9e9, 2e7),
        grid=(8,),
        in_specs=[slot_spec, act_spec, slot_spec, both_spec, whole((512, WIDTH))],
        out_specs=(slot_spec, whole((4, 384, WIDTH))),
        scratch_shapes=[pltpu.VMEM((WIDTH, WIDTH), F32), pltpu.VMEM((512, WIDTH), F32)],
    )(slots, act, dys, dboth, down)
    o_all = neighbours(after(o_heads, dxs))
    dxs = exchange(dxs, CTX)
    expert_own = lax.psum_scatter(
        expert_grads.reshape(4 * 384, WIDTH), FSDP, scatter_dimension=0, tiled=True
    ).astype(F32)
    dxs, ys = lax.optimization_barrier((dxs, ys))

    dmid, da_parts, grad_msg, gain_ffn_part = call(
        kernel_middle_back,
        (
            sds((128, WIDTH), F32),
            sds((4, 128, 256), BF),
            sds((8, 2, 64, 128), BF),
            sds((8, WIDTH), F32),
        ),
        (9e8, 8e6),
        grid=(2,),
        in_specs=[
            SM,
            pl.BlockSpec((16, 64, WIDTH), lambda t: (t, 0, 0)),
            pl.BlockSpec((128, 1024), lambda t: (0, t)),
            whole((128, WIDTH)),
            whole((128, WIDTH)),
            whole((8, WIDTH)),
        ]
        + out_specs,
        out_specs=(
            whole((128, WIDTH)),
            whole((4, 128, 256)),
            whole((8, 2, 64, 128)),
            whole((8, WIDTH)),
        ),
        scratch_shapes=[pltpu.VMEM((128, WIDTH), F32), pltpu.VMEM((128, WIDTH), BF)],
    )(part_ref, dxs, picks_turned, mid, cot, gains, *w_out)
    grad_heads = exchange(grad_msg, HEAD_AXES)
    ys, grad_heads, o_all = lax.optimization_barrier((ys, grad_heads, o_all))
    o_all = o_all + (swap(o_all[2], "core"),)
    ys = exchange(ys, CTX)
    dq, *dkv = call(
        kernel_attend_back,
        (sds((2048, 128), F32),) + (sds((2, 8, 64, 128), BF),) * 4,
        (2e10, 7e6),
        grid=(8,),
        in_specs=[
            SM,
            whole((4096, 128)),
            whole((128, 4096)),
            row_spec,
            msg_spec,
            log_spec,
            row_spec,
        ],
        out_specs=(row_spec,) + (whole((2, 8, 64, 128)),) * 4,
        scratch_shapes=[pltpu.VMEM((4096, 128), F32)],
    )(mine_ref, keys, turned, queries, grad_heads, log_total, o_rows)
    da_here = cross(da_parts)
    dkv = cross(dkv, ("y",))
    queries_back, hidden_turned = call(
        kernel_queries_back,
        (sds((8, 4, 64, 128), BF), sds((WIDTH, 512), BF)),
        (3e8, 4e6),
        in_specs=[VM] * 5,
        out_specs=(VM, VM),
    )(dq.reshape(2, 8, 2, 64, 128), cos_heads, sin_heads, head_table, hidden)
    dkv, ys, da_here, queries_back = lax.optimization_barrier((dkv, ys, da_here, queries_back))
    rest_part = call(
        kernel_out_weight,
        sds((WIDTH, 384), BF),
        (3e8, 2e6),
        in_specs=[VM] * 9,
        out_specs=VM,
    )(*o_all, *da_here, gain_ffn_part)
    layer_output = call(
        kernel_output,
        sds((128, WIDTH), BF),
        (1e9, 5e6),
        grid=(4,),
        in_specs=[
            pl.BlockSpec((8, 64, WIDTH), lambda t: (t, 0, 0)),
            pl.BlockSpec((128, 512), lambda t: (0, t)),
            pl.BlockSpec((128, 512), lambda t: (0, t)),
            whole((128, WIDTH)),
        ],
        out_specs=whole((128, WIDTH)),
        scratch_shapes=[pltpu.VMEM((128, WIDTH), F32)],
    )(ys, picks_high, picks_rest, mid)

    back = call(
        kernel_slices_back,
        sds((8, 4, 64, 128), BF),
        (2e8, 3e6),
        in_specs=[VM] * 8,
        out_specs=VM,
    )(*dkv, queries_back, cos_heads, sin_heads, head_table)
    back = exchange(back.reshape(32, 64, 128), HEAD_AXES + FSDP)

    grads, d_all = call(
        kernel_grads,
        (sds((WIDTH, 896), BF), sds((512, 512), BF)),
        (6e8, 5e6),
        in_specs=[VM] * 4,
        out_specs=(VM, VM),
    )(back, hidden_turned, w_slice, rest_part)
    dh_parts = call(
        kernel_hidden_grad,
        (sds((128, WIDTH), BF),) * 4,
        (6e8, 5e6),
        in_specs=[SM, VM, VM],
        out_specs=(VM,) * 4,
    )(part_ref, d_all, w_slice)
    grads = exchange(grads.reshape(128, 8, 896), ALL)
    grad_qkv, grad_out, grad_gains = call(
        kernel_total,
        (sds((8, 2048), F32), sds((8, WIDTH), F32), sds((8, 128), F32)),
        (1e8, 4e6),
        in_specs=[VM, VM],
        out_specs=(VM, VM, VM),
        scratch_shapes=[pltpu.VMEM((4, 8, 896), F32)],
    )(grads.reshape(32, 4, 8, 896), slice_table)
    dh_here = cross(dh_parts)
    input_grad = call(
        kernel_input_grad,
        sds((128, WIDTH), F32),
        (1e6, 2e6),
        in_specs=[VM] * 7,
        out_specs=VM,
    )(*after(dh_here, grad_qkv), x, dmid, gains)
    return (
        layer_output.reshape(layer_input.shape),
        input_grad.reshape(layer_input.shape),
        grad_gains[:, 0],
        grad_qkv,
        grad_out,
        grad_gains[:, 1],
        expert_own[0:256, 0:512][None],
        expert_own[0:256, 512:1024][None],
        expert_own[256:384][None],
    )


def solution(mesh):
    parts = Mesh(mesh.devices.reshape(4, 2, 4, 2, 2), ALL)
    tokens = P(FSDP, CTX, None, None, None, None)
    experts = P(CTX, FSDP, None)
    in_specs = (
        tokens,
        tokens,
        tokens,
        tokens,
        P(ALL),
        P(ALL, None),
        P(ALL, None),
        P(ALL),
        experts,
        experts,
        experts,
    )
    out_specs = (
        tokens,
        tokens,
        P(ALL),
        P(ALL, None),
        P(ALL, None),
        P(ALL),
        experts,
        experts,
        experts,
    )
    return jax.shard_map(
        on_device, mesh=parts, in_specs=in_specs, out_specs=out_specs, check_vma=False
    )
```

```python
import functools

import jax
import jax.numpy as jnp
import numpy as np
from jax import lax
from jax.experimental import pallas as pl
from jax.experimental.pallas import tpu as pltpu
from jax.sharding import Mesh
from jax.sharding import PartitionSpec as P

WIDTH = 1024
EPSILON = 1e-06
ROPE_BASE = 10000.0
MASKED = -1e30
BF = jnp.bfloat16
F32 = jnp.float32
CTX = ("x", "zh", "y")
HEAD_AXES = ("x", "zh")
FSDP = ("zl", "core")
ALL = CTX + FSDP
VMEM_LIMIT = 56 * 1024 * 1024

NT = (((1,), (1,)), ((), ()))
TN = (((0,), (0,)), ((), ()))


def mm(a, b, dims=None):
    if dims is None:
        return jnp.dot(a, b, preferred_element_type=F32)
    return lax.dot_general(a, b, dims, preferred_element_type=F32)


def lane(shape):
    return lax.broadcasted_iota(jnp.int32, shape, len(shape) - 1)


def row(shape):
    return lax.broadcasted_iota(jnp.int32, shape, len(shape) - 2)


def call(kernel, out_shape, cost, **kw):
    flops, bytes_accessed = cost
    return pl.pallas_call(
        kernel,
        out_shape=out_shape,
        compiler_params=pltpu.CompilerParams(vmem_limit_bytes=VMEM_LIMIT),
        cost_estimate=pl.CostEstimate(
            flops=int(flops), bytes_accessed=int(bytes_accessed), transcendentals=0
        ),
        **kw,
    )


def sds(shape, dtype):
    return jax.ShapeDtypeStruct(shape, dtype)


VM = pl.BlockSpec(memory_space=pltpu.VMEM)
SM = pl.BlockSpec(memory_space=pltpu.SMEM)


def slice_matrix():
    table = np.zeros((512, 512), np.float32)
    for k in range(512):
        section, place = k // 128, k % 128
        if section < 2:
            pair, part = section, place // 64
        else:
            pair, part = place // 64, section
        feat = place % 64
        f = (feat % 32) // 8
        column = pair * 64 + part * 16 + (feat // 32) * 8 + feat % 8
        table[k, f * 128 + column] = 1.0
    return table


def head_matrix():
    table = np.zeros((4, 128, 768), np.float32)
    for f in range(4):
        for block in range(2):
            for part in range(4):
                for j in range(16):
                    feat = (j // 8) * 32 + 8 * f + j % 8
                    source = block * 64 + part * 16 + j
                    if part == 2:
                        target = block * 128 + feat
                    elif part == 3:
                        target = block * 128 + 64 + feat
                    else:
                        target = 256 + block * 256 + part * 128 + feat
                    table[f, source, target] = 1.0
    return table


def place(part_ref, r, size):
    return pl.ds(pl.multiple_of(lax.bitwise_xor(part_ref[0], r) * size, size), size)


def kernel_route(picks_ref, gates_ref, rank_ref, gate_ref):
    experts = row((32, 128))
    gate = jnp.zeros((32, 128), F32)
    chosen = jnp.zeros((32, 128), F32)
    for k in range(8):
        hit = picks_ref[k : k + 1, :] == experts
        gate = gate + jnp.where(hit, gates_ref[k : k + 1, :], 0.0)
        chosen = chosen + jnp.where(hit, 1.0, 0.0)
    before = jnp.where(row((128, 128)) < lane((128, 128)), 1.0, 0.0).astype(BF)
    rank = mm(chosen.astype(BF), before)
    rank_ref[...] = jnp.where(chosen > 0.5, rank, -1.0)
    gate_ref[...] = gate


def kernel_slices(w_ref, gains_ref, table_ref, gate_ref, out_weight_ref, out_ref):
    w = w_ref[...].astype(BF).astype(F32)
    parts = []
    for p in range(4):
        parts.append(
            jnp.concatenate(
                [
                    w[:, 256 * p : 256 * p + 256],
                    w[:, 1024 + 128 * p : 1152 + 128 * p],
                    w[:, 1536 + 128 * p : 1664 + 128 * p],
                ],
                axis=1,
            )
        )
    stacked = jnp.concatenate(parts, axis=0).astype(BF)
    cut = mm(stacked, table_ref[...])
    columns = []
    for f in range(4):
        columns.append(
            jnp.concatenate(
                [cut[8 * p : 8 * p + 8, 128 * f : 128 * f + 128] for p in range(4)], axis=1
            ).astype(BF)
        )
    gains = gains_ref[...]
    left = lane((8, 128)) < 64
    sub = row((8, 128))
    for c in range(32):
        gate = gate_ref[c : c + 1, :]
        high = gate.astype(BF).astype(F32)
        middle = (gate - high).astype(BF).astype(F32)
        rest = gate - high - middle
        parts = jnp.where(
            sub < 2, high, jnp.where(sub < 4, middle, jnp.where(sub < 6, rest, 0.0))
        )
        parts = jnp.where(sub % 2 == 0, pltpu.roll(parts, 64, 1), parts)
        last = jnp.where(left, gains, parts).astype(BF)
        for f in range(4):
            out_ref[c, f, :, 0:512] = columns[f]
            out_ref[c, f, :, 512:640] = last
            out_ref[c, f, :, 640:896] = out_weight_ref[:, 256 * f : 256 * f + 256].astype(BF)


def kernel_picks(rank_ref, gate_ref, pick_ref, turned_ref, high_ref, rest_ref):
    slot = lax.broadcasted_iota(jnp.int32, (64, 128), 0).astype(F32)

    @pl.loop(0, 16)
    def _(p):
        picks, weights = [], []
        for e in (2 * p, 2 * p + 1):
            hit = slot == rank_ref[pl.ds(e, 1), :]
            picks.append(jnp.where(hit, 1.0, 0.0))
            weights.append(jnp.where(hit, gate_ref[pl.ds(e, 1), :], 0.0))
        picks = jnp.concatenate(picks, axis=0)
        weights = jnp.transpose(jnp.concatenate(weights, axis=0))
        at = pl.ds(pl.multiple_of(128 * p, 128), 128)
        pick_ref[at, :] = picks.astype(BF)
        turned_ref[:, at] = jnp.transpose(picks).astype(BF)
        high = weights.astype(BF)
        high_ref[:, at] = high
        rest_ref[:, at] = (weights - high.astype(F32)).astype(BF)


def kernel_project(
    part_ref, x0_ref, x1_ref, x2_ref, x3_ref, w_ref, cos_ref, sin_ref, msg_ref, hidden_ref, gains_ref
):
    gains = jnp.transpose(w_ref[:, 512:640].astype(F32))
    gains_ref[...] = gains[:8]
    for r, x_ref in enumerate((x0_ref, x1_ref, x2_ref, x3_ref)):
        x = x_ref[...].astype(F32)
        scale = lax.rsqrt(jnp.mean(x * x, axis=-1, keepdims=True) + EPSILON)
        hidden_ref[place(part_ref, r, 128), :] = (x * scale * gains[0:1]).astype(BF)
    proj = mm(hidden_ref[...], w_ref[:, 0:512])
    ahead = pltpu.roll(proj, 512 - 8, 1)
    behind = pltpu.roll(proj, 8, 1)
    partner = jnp.where((lane((512, 512)) // 8) % 2 == 0, ahead, behind)
    cos = jnp.concatenate([cos_ref[...]] * 4, axis=0)
    sin = jnp.concatenate([sin_ref[...]] * 4, axis=0)
    turned = proj * cos + partner * sin
    low = lane((64, 128)) < 64
    for s in range(4):
        for p in range(4):
            front = turned[128 * s : 128 * s + 64, 128 * p : 128 * p + 128]
            back = turned[128 * s + 64 : 128 * s + 128, 128 * p : 128 * p + 128]
            msg_ref[8 * p + s] = jnp.where(low, front, pltpu.roll(back, 64, 1)).astype(BF)
            msg_ref[8 * p + 4 + s] = jnp.where(low, pltpu.roll(front, 64, 1), back).astype(BF)


def kernel_heads(msg_ref, table_ref, kv_ref, q_ref):
    out = jnp.zeros((512, 768), F32)
    for f in range(4):
        out = out + mm(msg_ref[:, f].reshape(512, 128), table_ref[f])
    pairs = out[:, 0:256].astype(BF)
    for half in range(2):
        block = pairs[:, 128 * half : 128 * half + 128]
        for y in range(4):
            kv_ref[y, 512 * half : 512 * half + 512, :] = block
    queries = (out[:, 256:768] * 0.125).astype(BF)
    for half in range(2):
        for head in range(2):
            at = 256 * half + 128 * head
            q_ref[half, :, head] = queries[:, at : at + 128].reshape(8, 64, 128)


def tile_positions(tile, mine):
    front = tile < 4
    i = jnp.where(front, tile, tile - 4)
    q = lane((1, 256))
    k = lax.broadcasted_iota(jnp.int32, (512, 1), 0)
    q_front = (8 * i + 4 * (q // 128) + mine) * 64 + q % 64
    q_back = (63 - 8 * i - 4 * (q // 128) - mine) * 64 + q % 64
    k_front = 512 * i + k
    k_back = (59 - 8 * i + 4 * (k // 256) - (k % 256) // 64) * 64 + k % 64
    return jnp.where(front, q_front, q_back), jnp.where(front, k_front, k_back)


def kernel_attend(
    mine_ref,
    kv_ref,
    q_ref,
    msg_ref,
    log_ref,
    out_ref,
    keys_ref,
    turned_ref,
    peak_ref,
    total_ref,
    mixed_ref,
):
    tile = pl.program_id(0)

    @pl.when(tile == 0)
    def _():
        for group in range(16):
            half, place = (0, group) if group < 8 else (1, 15 - group)
            for y in range(4):
                at = 256 * group + 64 * y
                keys_ref[at : at + 64, :] = kv_ref[y, half, place]
        for c in range(8):
            turned_ref[:, 512 * c : 512 * c + 512] = jnp.transpose(
                keys_ref[512 * c : 512 * c + 512, :].astype(F32)
            ).astype(BF)

    q = q_ref[...]
    q_pos, k_pos = tile_positions(tile, mine_ref[0])

    def run(first, count, last):
        def keys(c):
            return pl.ds(pl.multiple_of(first + 512 * c, 512), 512)

        peak = peak_ref[0:1]
        total = total_ref[0:1]
        mixed = mixed_ref[...]
        later = mm(keys_ref[keys(0), :], q, NT)
        for c in range(count):
            scores = later
            if c + 1 < count:
                later = mm(keys_ref[keys(c + 1), :], q, NT)
            elif last:
                scores = jnp.where(k_pos <= q_pos, scores, MASKED)
            higher = jnp.maximum(peak, jnp.max(scores, axis=0, keepdims=True))
            weights = jnp.exp(scores - higher)
            fade = jnp.exp(peak - higher)
            total = total * fade + jnp.sum(weights, axis=0, keepdims=True)
            mixed = mixed * fade + mm(turned_ref[64:128, keys(c)], weights.astype(BF))
            peak = higher
        peak_ref[...] = jnp.broadcast_to(peak, (8, 256))
        total_ref[...] = jnp.broadcast_to(total, (8, 256))
        mixed_ref[...] = mixed

    peak_ref[...] = jnp.full((8, 256), MASKED, F32)
    total_ref[...] = jnp.zeros((8, 256), F32)
    mixed_ref[...] = jnp.zeros((64, 256), F32)

    @pl.when(tile >= 4)
    def _():
        run(0, 4, False)

    first = jnp.where(tile >= 4, 2048, 0)
    rest = jnp.where(tile >= 4, 8 - tile, tile + 1)
    for count in range(1, 5):
        pl.when(rest == count)(functools.partial(run, first, count, True))

    total = total_ref[0:1]
    log_ref[0] = jnp.broadcast_to(peak_ref[0:1] + jnp.log(total), (8, 256))
    mixed = mixed_ref[...] / total
    out = jnp.transpose(jnp.concatenate([jnp.zeros((64, 256), F32), mixed], axis=0))
    out_ref[...] = out
    low = lane((64, 128)) < 64
    for a in range(2):
        one = out[128 * a : 128 * a + 64]
        two = out[128 * a + 64 : 128 * a + 128]
        msg_ref[a, 0] = jnp.where(low, pltpu.roll(one, 64, 1), two).astype(BF)


def kernel_attend_back(
    mine_ref, keys_ref, turned_ref, q_ref, grad_ref, log_ref, out_ref, dq_ref, d0_ref, d1_ref, d2_ref, d3_ref, sum_ref
):
    tile = pl.program_id(0)

    @pl.when(tile == 0)
    def _():
        sum_ref[...] = jnp.zeros_like(sum_ref)

    q = q_ref[...]
    low = lane((64, 128)) < 64
    pieces = []
    for a in range(2):
        both = grad_ref[a, 0].astype(F32)
        pieces.append(jnp.where(low, 0.0, pltpu.roll(both, 64, 1)))
        pieces.append(jnp.where(low, 0.0, both))
    grad = jnp.concatenate(pieces, axis=0)
    delta = jnp.sum(jnp.transpose(grad * out_ref[...]), axis=0, keepdims=True)
    grad = grad.astype(BF)
    q_pos, k_pos = tile_positions(tile, mine_ref[0])
    log_total = log_ref[0][0:1]

    def step(c, dq, last):
        at = pl.ds(pl.multiple_of(c * 512, 512), 512)
        keys = keys_ref[at, :]
        scores = mm(keys, q, NT)
        if last:
            scores = jnp.where(k_pos <= q_pos, scores, MASKED)
        weights = jnp.exp(scores - log_total)
        slope = (weights * (mm(keys, grad, NT) - delta)).astype(BF)
        sum_ref[at, :] += mm(slope, q) + mm(weights.astype(BF), grad)
        return dq + mm(turned_ref[0:64, at], slope)

    count = jnp.where(tile < 4, tile + 1, 12 - tile)
    dq = lax.fori_loop(0, count - 1, lambda c, v: step(c, v, False), jnp.zeros((64, 256), F32))
    dq = step(count - 1, dq, True)
    dq_ref[...] = jnp.transpose(jnp.concatenate([dq * 0.125, jnp.zeros((64, 256), F32)], axis=0))

    @pl.when(tile == 7)
    def _():
        for group in range(16):
            half, place = (0, group) if group < 8 else (1, 15 - group)
            for r, dkv_ref in enumerate((d0_ref, d1_ref, d2_ref, d3_ref)):
                at = 256 * group + 64 * lax.bitwise_xor(mine_ref[0], r)
                part = sum_ref[pl.ds(pl.multiple_of(at, 64), 64), :]
                dkv_ref[half, place] = part.astype(BF)


def kernel_middle(
    part_ref,
    o_ref,
    u0_ref,
    u1_ref,
    u2_ref,
    u3_ref,
    l0_ref,
    l1_ref,
    l2_ref,
    l3_ref,
    x_ref,
    gains_ref,
    pick_ref,
    slots_ref,
    mid_ref,
    rows_ref,
    hidden_ref,
):
    @pl.when(pl.program_id(0) == 0)
    def _():
        for g in range(8):
            rows_ref[:, 128 * g : 128 * g + 128] = o_ref[g].reshape(128, 128)
        uppers = (u0_ref, u1_ref, u2_ref, u3_ref)
        lowers = (l0_ref, l1_ref, l2_ref, l3_ref)
        for r in range(4):
            at = place(part_ref, r, 256)
            mid_ref[:, at] = (
                x_ref[:, at].astype(F32)
                + mm(rows_ref[:, 0:512], uppers[r][...])
                + mm(rows_ref[:, 512:1024], lowers[r][...])
            )
        mid = mid_ref[...]
        scale = lax.rsqrt(jnp.mean(mid * mid, axis=-1, keepdims=True) + EPSILON)
        hidden_ref[...] = (mid * scale * gains_ref[1:2]).astype(BF)

    for c in range(4):
        at = slice(256 * c, 256 * c + 256)
        rows = mm(pick_ref[...], hidden_ref[:, at]).astype(BF)
        slots_ref[:, :, at] = rows.reshape(16, 64, 256)


def kernel_experts_ready(
    part_ref,
    dy_ref,
    parts_ref,
    w0_ref,
    w1_ref,
    w2_ref,
    w3_ref,
    dys_ref,
    dact_ref,
    v_ref,
    gu_ref,
    rank_ref,
    gate_ref,
):
    step = pl.program_id(0)

    @pl.when(step == 0)
    def _():
        for r, w_ref in enumerate((w0_ref, w1_ref, w2_ref, w3_ref)):
            gu_ref[place(part_ref, r, 256), :] = w_ref[0:256, :]
            v_ref[place(part_ref, r, 128), :] = w_ref[256:384, :]
        before = jnp.where(row((128, 128)) < lane((128, 128)), 1.0, 0.0).astype(BF)
        parts = [parts_ref[:, k, :].astype(F32) for k in range(6)]
        even = parts[0] + parts[2] + parts[4]
        odd = parts[1] + parts[3] + parts[5]
        gate_ref[...] = jnp.where(lane((32, 128)) < 64, pltpu.roll(even, 64, 1), odd)
        chosen = gate_ref[...] > 0.0
        rank = mm(jnp.where(chosen, 1.0, 0.0).astype(BF), before)
        rank_ref[...] = jnp.where(chosen, rank, -1.0)

    slot = lax.broadcasted_iota(jnp.int32, (64, 128), 0).astype(F32)
    grads = []
    for j in range(4):
        source = 4 * step + j
        pick = slot == rank_ref[pl.ds(source, 1), :]
        weight = jnp.sum(
            jnp.where(pick, gate_ref[pl.ds(source, 1), :], 0.0), axis=1, keepdims=True
        )
        rows = mm(jnp.where(pick, 1.0, 0.0).astype(BF), dy_ref[0, j, 0])
        grads.append((rows * weight).astype(BF))
    dys = jnp.concatenate(grads, axis=0)
    dys_ref[...] = dys.reshape(4, 64, WIDTH)
    dact_ref[...] = mm(dys, v_ref[...], NT)


def kernel_experts(h_ref, gu_ref, dact_ref, act_ref, dboth_ref, dxs_ref):
    def project(part):
        return mm(h_ref[4 * part : 4 * part + 4].reshape(256, WIDTH), gu_ref[...])

    later = project(0)
    for part in range(2):
        both = later
        if part == 0:
            later = project(1)
        at = slice(256 * part, 256 * part + 256)
        gate_h, up_h = both[:, :512], both[:, 512:]
        sig = 0.5 * jnp.tanh(0.5 * gate_h) + 0.5
        swished = gate_h * sig
        act_ref[at, :] = (swished * up_h).astype(BF)
        dact = dact_ref[at, :]
        dgate = (dact * up_h * (sig + swished * (1.0 - sig))).astype(BF)
        dup = (dact * swished).astype(BF)
        dboth = jnp.concatenate([dgate, dup], axis=1)
        dboth_ref[at, :] = dboth
        dxs = mm(dboth, gu_ref[...], NT).astype(BF)
        dxs_ref[4 * part : 4 * part + 4] = dxs.reshape(4, 64, WIDTH)


def kernel_experts_after(
    h_ref, act_ref, dys_ref, dboth_ref, v_ref, ys_ref, grad_ref, ggu_ref, gv_ref
):
    step = pl.program_id(0)

    @pl.when(step == 0)
    def _():
        ggu_ref[...] = jnp.zeros_like(ggu_ref)
        gv_ref[...] = jnp.zeros_like(gv_ref)

    act = act_ref[...]
    ys_ref[...] = mm(act, v_ref[...]).astype(BF).reshape(4, 64, WIDTH)
    h = h_ref[...].reshape(256, WIDTH)

    @pl.loop(0, 4)
    def _(c):
        at = pl.ds(pl.multiple_of(256 * c, 256), 256)
        ggu_ref[:, at] += mm(h, dboth_ref[:, at], TN)

    gv_ref[...] += mm(act, dys_ref[...].reshape(256, WIDTH), TN)

    @pl.when(step == 7)
    def _():
        for f in range(4):
            grad_ref[f, 0:256, :] = ggu_ref[256 * f : 256 * f + 256, :].astype(BF)
            grad_ref[f, 256:384, :] = gv_ref[128 * f : 128 * f + 128, :].astype(BF)


def kernel_middle_back(
    part_ref,
    dxs_ref,
    pick_ref,
    mid_ref,
    cot_ref,
    gains_ref,
    u0_ref,
    u1_ref,
    u2_ref,
    u3_ref,
    l0_ref,
    l1_ref,
    l2_ref,
    l3_ref,
    dmid_ref,
    parts_ref,
    msg_ref,
    ggain_ref,
    sum_ref,
    low_ref,
):
    step = pl.program_id(0)
    part = mm(pick_ref[...], dxs_ref[...].reshape(1024, WIDTH))

    @pl.when(step == 0)
    def _():
        sum_ref[...] = part

    @pl.when(step > 0)
    def _():
        sum_ref[...] += part

    @pl.when(step == 1)
    def _():
        mid = mid_ref[...]
        scale = lax.rsqrt(jnp.mean(mid * mid, axis=-1, keepdims=True) + EPSILON)
        dh = sum_ref[...]
        ggain_ref[...] = jnp.broadcast_to(
            jnp.sum(dh * (mid * scale), axis=0, keepdims=True), (8, WIDTH)
        )
        dn = dh * gains_ref[1:2]
        dmid = (
            cot_ref[...].astype(F32)
            + scale * dn
            - mid * (scale * scale * scale) * jnp.mean(dn * mid, axis=-1, keepdims=True)
        )
        dmid_ref[...] = dmid
        low_ref[...] = dmid.astype(BF)
        uppers = (u0_ref, u1_ref, u2_ref, u3_ref)
        lowers = (l0_ref, l1_ref, l2_ref, l3_ref)
        for r in range(4):
            parts_ref[r] = low_ref[:, place(part_ref, r, 256)]
        for h, w_refs in enumerate((uppers, lowers)):
            grad = mm(parts_ref[0], w_refs[0][...], NT)
            for r in range(1, 4):
                grad = grad + mm(parts_ref[r], w_refs[r][...], NT)
            grad = grad.astype(BF)
            for g in range(4):
                msg_ref[4 * h + g] = grad[:, 128 * g : 128 * g + 128].reshape(2, 64, 128)


def kernel_out_weight(
    o0_ref, o1_ref, o2_ref, o3_ref, da0_ref, da1_ref, da2_ref, da3_ref, gain_ref, grad_ref
):
    which = lax.broadcasted_iota(jnp.int32, (128, WIDTH), 0)
    grad_ref[:, 0:128] = jnp.transpose(jnp.where(which == 1, gain_ref[0:1], 0.0)).astype(BF)
    pairs = ((o0_ref, da0_ref), (o1_ref, da1_ref), (o2_ref, da2_ref), (o3_ref, da3_ref))

    @pl.loop(0, 8)
    def _(g):
        part = jnp.zeros((128, 256), F32)
        for o_ref, da_ref in pairs:
            part = part + mm(o_ref[g].reshape(128, 128), da_ref[...], TN)
        grad_ref[pl.ds(pl.multiple_of(128 * g, 128), 128), 128:384] = part.astype(BF)


def unrotate(w, cos, sin):
    partner = jnp.where(lane(w.shape) % 64 < 32, pltpu.roll(w, 96, 1), pltpu.roll(w, 32, 1))
    return (w * cos - partner * sin).astype(BF)


def kernel_queries_back(
    dq_ref, cos_ref, sin_ref, table_ref, hidden_ref, msg_ref, hidden_turned_ref
):
    for s in range(4):
        at = slice(128 * s, 128 * s + 128)
        hidden_turned_ref[:, at] = jnp.transpose(hidden_ref[at, :].astype(F32)).astype(BF)
    parts = []
    for half in range(2):
        at = slice(512 * half, 512 * half + 512)
        for head in range(2):
            dq = dq_ref[half, :, head].reshape(512, 128)
            parts.append(unrotate(dq, cos_ref[at, :], sin_ref[at, :]))
    whole = jnp.concatenate(parts, axis=1)
    for f in range(4):
        rows = mm(whole, table_ref[f, :, 256:768], NT)
        msg_ref[:, f] = rows.astype(BF).reshape(8, 64, 128)


def kernel_slices_back(
    d0_ref, d1_ref, d2_ref, d3_ref, queries_ref, cos_ref, sin_ref, table_ref, msg_ref
):
    parts = []
    for half in range(2):
        at = slice(512 * half, 512 * half + 512)
        dkv = d0_ref[half].reshape(512, 128).astype(F32)
        for d_ref in (d1_ref, d2_ref, d3_ref):
            dkv = dkv + d_ref[half].reshape(512, 128).astype(F32)
        parts.append(unrotate(dkv, cos_ref[at, :], sin_ref[at, :]))
    whole = jnp.concatenate(parts, axis=1)
    for f in range(4):
        rows = mm(whole, table_ref[f, :, 0:256], NT) + queries_ref[:, f].reshape(512, 128)
        msg_ref[:, f] = rows.astype(BF).reshape(8, 64, 128)


def kernel_hidden_grad(part_ref, d_ref, w_ref, h0_ref, h1_ref, h2_ref, h3_ref):
    for r, h_ref in enumerate((h0_ref, h1_ref, h2_ref, h3_ref)):
        h_ref[...] = mm(d_ref[place(part_ref, r, 128), :], w_ref[:, 0:512], NT).astype(BF)


def kernel_grads(msg_ref, hidden_ref, rest_ref, grads_ref, d_ref):
    low = lane((64, 128)) < 64
    for s in range(4):
        for p in range(4):
            even = msg_ref[8 * p + s].astype(F32)
            odd = msg_ref[8 * p + 4 + s].astype(F32)
            d_ref[128 * s : 128 * s + 64, 128 * p : 128 * p + 128] = jnp.where(
                low, even, pltpu.roll(odd, 64, 1)
            ).astype(BF)
            d_ref[128 * s + 64 : 128 * s + 128, 128 * p : 128 * p + 128] = jnp.where(
                low, pltpu.roll(even, 64, 1), odd
            ).astype(BF)
    total = mm(hidden_ref[...], d_ref[...])
    grads_ref[:, 0:512] = total.astype(BF)
    grads_ref[:, 512:896] = rest_ref[...]


def kernel_input_grad(d0_ref, d1_ref, d2_ref, d3_ref, x_ref, dmid_ref, gains_ref, out_ref):
    dh = d0_ref[...].astype(F32)
    for d_ref in (d1_ref, d2_ref, d3_ref):
        dh = dh + d_ref[...].astype(F32)
    x = x_ref[...].astype(F32)
    scale = lax.rsqrt(jnp.mean(x * x, axis=-1, keepdims=True) + EPSILON)
    dn = dh * gains_ref[0:1]
    out_ref[...] = (
        dmid_ref[...]
        + scale * dn
        - x * (scale * scale * scale) * jnp.mean(dn * x, axis=-1, keepdims=True)
    )


def kernel_total(parts_ref, table_ref, w_ref, rows_ref, qkv_ref, out_ref, gains_ref, sum_ref):
    total = parts_ref[0].astype(F32)
    for c in range(1, 32):
        total = total + parts_ref[c].astype(F32)
    sum_ref[...] = total
    rows = []
    for p in range(4):
        rows.append(
            jnp.concatenate([sum_ref[f, :, 128 * p : 128 * p + 128] for f in range(4)], axis=1)
        )
    rest = jnp.concatenate(rows, axis=0)
    parts = []
    for _ in range(3):
        part = rest.astype(BF)
        rest = rest - part.astype(F32)
        parts.append(part)
    whole = mm(jnp.concatenate(parts, axis=0), table_ref[...], NT)
    whole = whole[0:32] + whole[32:64] + whole[64:96]
    for p in range(4):
        piece = whole[8 * p : 8 * p + 8]
        qkv_ref[:, 256 * p : 256 * p + 256] = piece[:, 0:256]
        qkv_ref[:, 1024 + 128 * p : 1152 + 128 * p] = piece[:, 256:384]
        qkv_ref[:, 1536 + 128 * p : 1664 + 128 * p] = piece[:, 384:512]
    for f in range(4):
        out_ref[:, 256 * f : 256 * f + 256] = sum_ref[f, :, 640:896]
    gains = (
        sum_ref[0, :, 512:640]
        + sum_ref[1, :, 512:640]
        + sum_ref[2, :, 512:640]
        + sum_ref[3, :, 512:640]
    )
    w = w_ref[...].astype(BF).astype(F32)
    first = jnp.sum(w * qkv_ref[...], axis=1, keepdims=True)
    first = first / rows_ref[:, 0:1].astype(BF).astype(F32)
    gains_ref[...] = jnp.where(lane((8, 128)) == 0, first, gains)


def kernel_output(ys_ref, high_ref, rest_ref, mid_ref, out_ref, sum_ref):
    step = pl.program_id(0)

    @pl.when(step == 0)
    def _():
        sum_ref[...] = mid_ref[...]

    ys = ys_ref[...].reshape(512, WIDTH)
    sum_ref[...] += mm(high_ref[...], ys) + mm(rest_ref[...], ys)

    @pl.when(step == 3)
    def _():
        out_ref[...] = sum_ref[...].astype(BF)


def angles(positions, features):
    frequency = ROPE_BASE ** (-(features.astype(F32) * 2.0 / 64))
    return positions.astype(F32)[:, None] * frequency[None, :]


def whole(shape):
    return pl.BlockSpec(shape, lambda t: (0,) * len(shape))


def exchange(value, axes):
    return lax.all_to_all(value, axes, split_axis=0, concat_axis=0, tiled=True)


def gather(value, axes):
    return lax.all_gather(value, axes, axis=0, tiled=True)


def after(value, marker):
    return lax.optimization_barrier((value, marker))[0]


def swap(value, axis):
    return lax.ppermute(value, axis, [(0, 1), (1, 0)])


def neighbours(value):
    return value, swap(value, "core"), swap(value, "zl")


def cross(parts, axes=FSDP):
    here = [parts[0]]
    for r in range(1, 4):
        here.append(lax.ppermute(parts[r], axes, [(i, i ^ r) for i in range(4)]))
    return here


def on_device(
    layer_input,
    routes,
    gates,
    cotangent,
    norm_attn,
    query_key_value_weight,
    output_weight,
    norm_ffn,
    exp_gate,
    exp_up,
    exp_down,
):
    mine = lax.axis_index("y")
    ctx_index = lax.axis_index(CTX)
    part_index = lax.axis_index(FSDP)
    mine_ref = mine.astype(jnp.int32).reshape(1)
    part_ref = part_index.astype(jnp.int32).reshape(1)
    x = layer_input.reshape(128, WIDTH)
    cot = cotangent.reshape(128, WIDTH)
    slice_table = jnp.asarray(slice_matrix(), BF)
    head_table = jnp.asarray(head_matrix(), BF)

    x_all = neighbours(x)
    rank, gate = call(
        kernel_route,
        (sds((32, 128), F32), sds((32, 128), F32)),
        (1e6, 1e5),
        in_specs=[VM, VM],
        out_specs=(VM, VM),
    )(routes.reshape(128, 8).T, gates.reshape(128, 8).T)
    which = lax.broadcasted_iota(jnp.int32, (8, 128), 1)
    gain_rows = jnp.where(
        which == 0, norm_attn[:, None], jnp.where(which == 1, norm_ffn[:, None], 0.0)
    )
    slices = call(
        kernel_slices,
        sds((32, 4, 8, 896), BF),
        (2e7, 3e6),
        in_specs=[VM] * 5,
        out_specs=VM,
    )(query_key_value_weight, gain_rows, slice_table, gate, output_weight)
    slices, rank, gate, x_all = lax.optimization_barrier((slices, rank, gate, x_all))
    x_all = x_all + (swap(x_all[2], "core"),)
    offset = jnp.arange(64, dtype=jnp.int32)
    token_pos = jnp.concatenate([ctx_index * 64 + offset, (63 - ctx_index) * 64 + offset])
    column = jnp.arange(512, dtype=jnp.int32)
    angle = angles(token_pos, 8 * part_index + column % 8)
    is_value = (column // 16) % 4 == 3
    sign = jnp.where((column // 8) % 2 == 0, -1.0, 1.0)
    cos_slice = jnp.where(is_value, 1.0, jnp.cos(angle))
    sin_slice = jnp.where(is_value, 0.0, jnp.sin(angle) * sign)
    w_slice = exchange(slices.reshape(128, 8, 896), ALL)
    w_slice, cos_slice, sin_slice = lax.optimization_barrier((w_slice, cos_slice, sin_slice))
    gate_parts = lax.dynamic_slice(
        w_slice.reshape(32, 4, 8, 896), (0, part_index, 0, 512), (32, 1, 8, 128)
    ).reshape(32, 8, 128)
    w_slice = w_slice.reshape(WIDTH, 896)
    picks, picks_turned, picks_high, picks_rest = call(
        kernel_picks,
        (sds((2048, 128), BF),) + (sds((128, 2048), BF),) * 3,
        (2e9, 4e6),
        in_specs=[VM, VM],
        out_specs=(VM,) * 4,
    )(rank, gate)

    msg, hidden, gains = call(
        kernel_project,
        (sds((32, 64, 128), BF), sds((512, WIDTH), BF), sds((8, WIDTH), F32)),
        (6e8, 4e6),
        in_specs=[SM] + [VM] * 7,
        out_specs=(VM, VM, VM),
    )(part_ref, *x_all, w_slice, cos_slice, sin_slice)
    across = swap(after(cot, w_slice), "zh")
    first = lax.axis_index("zh") == 0
    cot_pair = jnp.concatenate(
        [jnp.where(first, cot, across), jnp.where(first, across, cot)], axis=0
    )
    out_upper = neighbours(w_slice[0:512, 640:896])
    msg = exchange(msg, HEAD_AXES + FSDP)

    kv_copies, queries = call(
        kernel_heads,
        (sds((4, 1024, 128), BF), sds((2, 8, 2, 64, 128), BF)),
        (4e8, 3e6),
        in_specs=[VM, VM],
        out_specs=(VM, VM),
    )(msg.reshape(8, 4, 64, 128), head_table)
    queries = queries.reshape(2048, 128)
    kv_copies, out_upper = lax.optimization_barrier((kv_copies, out_upper))
    out_lower = neighbours(after(w_slice[512:1024, 640:896], msg))
    kv = exchange(kv_copies, ("y",)).reshape(4, 2, 8, 64, 128)
    expert_weights = jnp.concatenate(
        [jnp.concatenate([exp_gate[0], exp_up[0]], axis=1), exp_down[0]], axis=0
    ).astype(BF)
    block = 4 * jnp.arange(8, dtype=jnp.int32)[:, None] + mine
    quarter_pos = jnp.concatenate(
        [
            (block * 64 + offset[None, :]).reshape(-1),
            ((63 - block) * 64 + offset[None, :]).reshape(-1),
        ]
    )
    column = jnp.arange(128, dtype=jnp.int32)
    angle = angles(quarter_pos, column % 32)
    sign = jnp.where(column % 64 < 32, -1.0, 1.0)
    cos_heads = jnp.where(column >= 64, 1.0, jnp.cos(angle))
    sin_heads = jnp.where(column >= 64, 0.0, jnp.sin(angle) * sign)
    kv, out_lower, cos_heads, sin_heads = lax.optimization_barrier(
        (kv, out_lower, cos_heads, sin_heads)
    )
    experts_all = neighbours(after(expert_weights, msg))
    cot_all = gather(after(cot_pair, kv_copies), ("x", "y")).reshape(4, 4, 2, 128, WIDTH)
    out_upper = out_upper + (swap(after(out_upper[2], kv), "core"),)
    out_lower = out_lower + (swap(out_lower[2], "core"),)
    w_out = (*out_upper, *out_lower)
    msg_spec = pl.BlockSpec((2, 1, 64, 128), lambda t: (t % 4, t // 4, 0, 0))
    row_spec = pl.BlockSpec((256, 128), lambda t: (t, 0))
    log_spec = pl.BlockSpec((1, 8, 256), lambda t: (t, 0, 0))
    o_msg, log_total, o_rows, keys, turned = call(
        kernel_attend,
        (
            sds((8, 2, 64, 128), BF),
            sds((8, 8, 256), F32),
            sds((2048, 128), F32),
            sds((4096, 128), BF),
            sds((128, 4096), BF),
        ),
        (1e10, 5e6),
        grid=(8,),
        in_specs=[SM, whole((4, 2, 8, 64, 128)), row_spec],
        out_specs=(msg_spec, log_spec, row_spec, whole((4096, 128)), whole((128, 4096))),
        scratch_shapes=[
            pltpu.VMEM((8, 256), F32),
            pltpu.VMEM((8, 256), F32),
            pltpu.VMEM((64, 256), F32),
        ],
    )(mine_ref, kv, queries)
    o_msg, w_out, experts_all = lax.optimization_barrier((o_msg, w_out, experts_all))
    experts_all = experts_all + (swap(experts_all[2], "core"),)
    o_heads = exchange(o_msg, HEAD_AXES)

    slot_spec = pl.BlockSpec((4, 64, WIDTH), lambda t: (t, 0, 0))
    out_specs = [whole((512, 256))] * 8
    slots, mid = call(
        kernel_middle,
        (sds((32, 64, WIDTH), BF), sds((128, WIDTH), F32)),
        (9e8, 8e6),
        grid=(2,),
        in_specs=[SM, whole((8, 2, 64, 128))]
        + out_specs
        + [
            whole((128, WIDTH)),
            whole((8, WIDTH)),
            pl.BlockSpec((1024, 128), lambda t: (t, 0)),
        ],
        out_specs=(pl.BlockSpec((16, 64, WIDTH), lambda t: (t, 0, 0)), whole((128, WIDTH))),
        scratch_shapes=[pltpu.VMEM((128, WIDTH), BF), pltpu.VMEM((128, WIDTH), BF)],
    )(part_ref, o_heads, *w_out, x, gains, picks)
    cot_all = after(cot_all, mid)
    slots, experts_all = lax.optimization_barrier((slots, experts_all))
    slots = exchange(slots, CTX)
    dys, dact, down, gate_up = call(
        kernel_experts_ready,
        (
            sds((32, 64, WIDTH), BF),
            sds((2048, 512), F32),
            sds((512, WIDTH), BF),
            sds((WIDTH, WIDTH), BF),
        ),
        (6e9, 2e7),
        grid=(8,),
        in_specs=[
            SM,
            pl.BlockSpec((1, 4, 1, 128, WIDTH), lambda t: (t // 2, 0, t % 2, 0, 0)),
            whole((32, 8, 128)),
        ]
        + [whole((384, WIDTH))] * 4,
        out_specs=(
            slot_spec,
            pl.BlockSpec((256, 512), lambda t: (t, 0)),
            whole((512, WIDTH)),
            whole((WIDTH, WIDTH)),
        ),
        scratch_shapes=[pltpu.VMEM((32, 128), F32), pltpu.VMEM((32, 128), F32)],
    )(part_ref, cot_all, gate_parts, *experts_all)
    act_spec = pl.BlockSpec((256, 512), lambda t: (t, 0))
    both_spec = pl.BlockSpec((256, WIDTH), lambda t: (t, 0))
    act, dboth, dxs = call(
        kernel_experts,
        (sds((2048, 512), BF), sds((2048, WIDTH), BF), sds((32, 64, WIDTH), BF)),
        (9e9, 2e7),
        grid=(4,),
        in_specs=[
            pl.BlockSpec((8, 64, WIDTH), lambda t: (t, 0, 0)),
            whole((WIDTH, WIDTH)),
            pl.BlockSpec((512, 512), lambda t: (t, 0)),
        ],
        out_specs=(
            pl.BlockSpec((512, 512), lambda t: (t, 0)),
            pl.BlockSpec((512, WIDTH), lambda t: (t, 0)),
            pl.BlockSpec((8, 64, WIDTH), lambda t: (t, 0, 0)),
        ),
    )(slots, gate_up, dact)
    ys, expert_grads = call(
        kernel_experts_after,
        (sds((32, 64, WIDTH), BF), sds((4, 384, WIDTH), BF)),
        (9e9, 2e7),
        grid=(8,),
        in_specs=[slot_spec, act_spec, slot_spec, both_spec, whole((512, WIDTH))],
        out_specs=(slot_spec, whole((4, 384, WIDTH))),
        scratch_shapes=[pltpu.VMEM((WIDTH, WIDTH), F32), pltpu.VMEM((512, WIDTH), F32)],
    )(slots, act, dys, dboth, down)
    o_all = neighbours(after(o_heads, dxs))
    dxs = exchange(dxs, CTX)
    expert_own = lax.psum_scatter(
        expert_grads.reshape(4 * 384, WIDTH), FSDP, scatter_dimension=0, tiled=True
    ).astype(F32)
    dxs, ys = lax.optimization_barrier((dxs, ys))

    dmid, da_parts, grad_msg, gain_ffn_part = call(
        kernel_middle_back,
        (
            sds((128, WIDTH), F32),
            sds((4, 128, 256), BF),
            sds((8, 2, 64, 128), BF),
            sds((8, WIDTH), F32),
        ),
        (9e8, 8e6),
        grid=(2,),
        in_specs=[
            SM,
            pl.BlockSpec((16, 64, WIDTH), lambda t: (t, 0, 0)),
            pl.BlockSpec((128, 1024), lambda t: (0, t)),
            whole((128, WIDTH)),
            whole((128, WIDTH)),
            whole((8, WIDTH)),
        ]
        + out_specs,
        out_specs=(
            whole((128, WIDTH)),
            whole((4, 128, 256)),
            whole((8, 2, 64, 128)),
            whole((8, WIDTH)),
        ),
        scratch_shapes=[pltpu.VMEM((128, WIDTH), F32), pltpu.VMEM((128, WIDTH), BF)],
    )(part_ref, dxs, picks_turned, mid, cot, gains, *w_out)
    grad_heads = exchange(grad_msg, HEAD_AXES)
    ys, grad_heads, o_all = lax.optimization_barrier((ys, grad_heads, o_all))
    o_all = o_all + (swap(o_all[2], "core"),)
    ys = exchange(ys, CTX)
    dq, *dkv = call(
        kernel_attend_back,
        (sds((2048, 128), F32),) + (sds((2, 8, 64, 128), BF),) * 4,
        (2e10, 7e6),
        grid=(8,),
        in_specs=[
            SM,
            whole((4096, 128)),
            whole((128, 4096)),
            row_spec,
            msg_spec,
            log_spec,
            row_spec,
        ],
        out_specs=(row_spec,) + (whole((2, 8, 64, 128)),) * 4,
        scratch_shapes=[pltpu.VMEM((4096, 128), F32)],
    )(mine_ref, keys, turned, queries, grad_heads, log_total, o_rows)
    da_here = cross(da_parts)
    dkv = cross(dkv, ("y",))
    queries_back, hidden_turned = call(
        kernel_queries_back,
        (sds((8, 4, 64, 128), BF), sds((WIDTH, 512), BF)),
        (3e8, 4e6),
        in_specs=[VM] * 5,
        out_specs=(VM, VM),
    )(dq.reshape(2, 8, 2, 64, 128), cos_heads, sin_heads, head_table, hidden)
    dkv, ys, da_here, queries_back = lax.optimization_barrier((dkv, ys, da_here, queries_back))
    rest_part = call(
        kernel_out_weight,
        sds((WIDTH, 384), BF),
        (3e8, 2e6),
        in_specs=[VM] * 9,
        out_specs=VM,
    )(*o_all, *da_here, gain_ffn_part)
    layer_output = call(
        kernel_output,
        sds((128, WIDTH), BF),
        (1e9, 5e6),
        grid=(4,),
        in_specs=[
            pl.BlockSpec((8, 64, WIDTH), lambda t: (t, 0, 0)),
            pl.BlockSpec((128, 512), lambda t: (0, t)),
            pl.BlockSpec((128, 512), lambda t: (0, t)),
            whole((128, WIDTH)),
        ],
        out_specs=whole((128, WIDTH)),
        scratch_shapes=[pltpu.VMEM((128, WIDTH), F32)],
    )(ys, picks_high, picks_rest, mid)

    back = call(
        kernel_slices_back,
        sds((8, 4, 64, 128), BF),
        (2e8, 3e6),
        in_specs=[VM] * 8,
        out_specs=VM,
    )(*dkv, queries_back, cos_heads, sin_heads, head_table)
    back = exchange(back.reshape(32, 64, 128), HEAD_AXES + FSDP)

    grads, d_all = call(
        kernel_grads,
        (sds((WIDTH, 896), BF), sds((512, 512), BF)),
        (6e8, 5e6),
        in_specs=[VM] * 3,
        out_specs=(VM, VM),
    )(back, hidden_turned, rest_part)
    dh_parts = call(
        kernel_hidden_grad,
        (sds((128, WIDTH), BF),) * 4,
        (6e8, 5e6),
        in_specs=[SM, VM, VM],
        out_specs=(VM,) * 4,
    )(part_ref, d_all, w_slice)
    grads = exchange(grads.reshape(128, 8, 896), ALL)
    grad_qkv, grad_out, grad_gains = call(
        kernel_total,
        (sds((8, 2048), F32), sds((8, WIDTH), F32), sds((8, 128), F32)),
        (1e8, 4e6),
        in_specs=[VM] * 4,
        out_specs=(VM, VM, VM),
        scratch_shapes=[pltpu.VMEM((4, 8, 896), F32)],
    )(grads.reshape(32, 4, 8, 896), slice_table, query_key_value_weight, gain_rows)
    dh_here = cross(dh_parts)
    input_grad = call(
        kernel_input_grad,
        sds((128, WIDTH), F32),
        (1e6, 2e6),
        in_specs=[VM] * 7,
        out_specs=VM,
    )(*after(dh_here, grad_qkv), x, dmid, gains)
    return (
        layer_output.reshape(layer_input.shape),
        input_grad.reshape(layer_input.shape),
        grad_gains[:, 0],
        grad_qkv,
        grad_out,
        grad_gains[:, 1],
        expert_own[0:256, 0:512][None],
        expert_own[0:256, 512:1024][None],
        expert_own[256:384][None],
    )


def solution(mesh):
    parts = Mesh(mesh.devices.reshape(4, 2, 4, 2, 2), ALL)
    tokens = P(FSDP, CTX, None, None, None, None)
    experts = P(CTX, FSDP, None)
    in_specs = (
        tokens,
        tokens,
        tokens,
        tokens,
        P(ALL),
        P(ALL, None),
        P(ALL, None),
        P(ALL),
        experts,
        experts,
        experts,
    )
    out_specs = (
        tokens,
        tokens,
        P(ALL),
        P(ALL, None),
        P(ALL, None),
        P(ALL),
        experts,
        experts,
        experts,
    )
    return jax.shard_map(
        on_device, mesh=parts, in_specs=in_specs, out_specs=out_specs, check_vma=False
    )
```

```python
import functools

import jax
import jax.numpy as jnp
import numpy as np
from jax import lax
from jax.experimental import pallas as pl
from jax.experimental.pallas import tpu as pltpu
from jax.sharding import Mesh
from jax.sharding import PartitionSpec as P

WIDTH = 1024
EPSILON = 1e-06
ROPE_BASE = 10000.0
MASKED = -1e30
BF = jnp.bfloat16
F32 = jnp.float32
CTX = ("x", "zh", "y")
HEAD_AXES = ("x", "zh")
FSDP = ("zl", "core")
ALL = CTX + FSDP
VMEM_LIMIT = 56 * 1024 * 1024

NT = (((1,), (1,)), ((), ()))
TN = (((0,), (0,)), ((), ()))


def mm(a, b, dims=None):
    if dims is None:
        return jnp.dot(a, b, preferred_element_type=F32)
    return lax.dot_general(a, b, dims, preferred_element_type=F32)


def lane(shape):
    return lax.broadcasted_iota(jnp.int32, shape, len(shape) - 1)


def row(shape):
    return lax.broadcasted_iota(jnp.int32, shape, len(shape) - 2)


def call(kernel, out_shape, cost, **kw):
    flops, bytes_accessed = cost
    return pl.pallas_call(
        kernel,
        out_shape=out_shape,
        compiler_params=pltpu.CompilerParams(vmem_limit_bytes=VMEM_LIMIT),
        cost_estimate=pl.CostEstimate(
            flops=int(flops), bytes_accessed=int(bytes_accessed), transcendentals=0
        ),
        **kw,
    )


def sds(shape, dtype):
    return jax.ShapeDtypeStruct(shape, dtype)


VM = pl.BlockSpec(memory_space=pltpu.VMEM)
SM = pl.BlockSpec(memory_space=pltpu.SMEM)


def slice_matrix():
    table = np.zeros((512, 512), np.float32)
    for k in range(512):
        section, place = k // 128, k % 128
        if section < 2:
            pair, part = section, place // 64
        else:
            pair, part = place // 64, section
        feat = place % 64
        f = (feat % 32) // 8
        column = pair * 64 + part * 16 + (feat // 32) * 8 + feat % 8
        table[k, f * 128 + column] = 1.0
    return table


def head_matrix():
    table = np.zeros((4, 128, 768), np.float32)
    for f in range(4):
        for block in range(2):
            for part in range(4):
                for j in range(16):
                    feat = (j // 8) * 32 + 8 * f + j % 8
                    source = block * 64 + part * 16 + j
                    if part == 2:
                        target = block * 128 + feat
                    elif part == 3:
                        target = block * 128 + 64 + feat
                    else:
                        target = 256 + block * 256 + part * 128 + feat
                    table[f, source, target] = 1.0
    return table


def place(part_ref, r, size):
    return pl.ds(pl.multiple_of(lax.bitwise_xor(part_ref[0], r) * size, size), size)


def kernel_route(picks_ref, gates_ref, rank_ref, gate_ref):
    experts = row((32, 128))
    gate = jnp.zeros((32, 128), F32)
    chosen = jnp.zeros((32, 128), F32)
    for k in range(8):
        hit = picks_ref[k : k + 1, :] == experts
        gate = gate + jnp.where(hit, gates_ref[k : k + 1, :], 0.0)
        chosen = chosen + jnp.where(hit, 1.0, 0.0)
    before = jnp.where(row((128, 128)) < lane((128, 128)), 1.0, 0.0).astype(BF)
    rank = mm(chosen.astype(BF), before)
    rank_ref[...] = jnp.where(chosen > 0.5, rank, -1.0)
    gate_ref[...] = gate


def kernel_slices(w_ref, gains_ref, table_ref, gate_ref, out_weight_ref, out_ref):
    w = w_ref[...].astype(BF).astype(F32)
    parts = []
    for p in range(4):
        parts.append(
            jnp.concatenate(
                [
                    w[:, 256 * p : 256 * p + 256],
                    w[:, 1024 + 128 * p : 1152 + 128 * p],
                    w[:, 1536 + 128 * p : 1664 + 128 * p],
                ],
                axis=1,
            )
        )
    stacked = jnp.concatenate(parts, axis=0).astype(BF)
    cut = mm(stacked, table_ref[...])
    columns = []
    for f in range(4):
        columns.append(
            jnp.concatenate(
                [cut[8 * p : 8 * p + 8, 128 * f : 128 * f + 128] for p in range(4)], axis=1
            ).astype(BF)
        )
    gains = gains_ref[...]
    left = lane((8, 128)) < 64
    sub = row((8, 128))
    for c in range(32):
        gate = gate_ref[c : c + 1, :]
        high = gate.astype(BF).astype(F32)
        middle = (gate - high).astype(BF).astype(F32)
        rest = gate - high - middle
        parts = jnp.where(
            sub < 2, high, jnp.where(sub < 4, middle, jnp.where(sub < 6, rest, 0.0))
        )
        parts = jnp.where(sub % 2 == 0, pltpu.roll(parts, 64, 1), parts)
        last = jnp.where(left, gains, parts).astype(BF)
        for f in range(4):
            out_ref[c, f, :, 0:512] = columns[f]
            out_ref[c, f, :, 512:640] = last
            out_ref[c, f, :, 640:896] = out_weight_ref[:, 256 * f : 256 * f + 256].astype(BF)


def kernel_picks(rank_ref, gate_ref, pick_ref, turned_ref, high_ref, rest_ref):
    slot = lax.broadcasted_iota(jnp.int32, (64, 128), 0).astype(F32)

    @pl.loop(0, 16)
    def _(p):
        picks, weights = [], []
        for e in (2 * p, 2 * p + 1):
            hit = slot == rank_ref[pl.ds(e, 1), :]
            picks.append(jnp.where(hit, 1.0, 0.0))
            weights.append(jnp.where(hit, gate_ref[pl.ds(e, 1), :], 0.0))
        picks = jnp.concatenate(picks, axis=0)
        weights = jnp.transpose(jnp.concatenate(weights, axis=0))
        at = pl.ds(pl.multiple_of(128 * p, 128), 128)
        pick_ref[at, :] = picks.astype(BF)
        turned_ref[:, at] = jnp.transpose(picks).astype(BF)
        high = weights.astype(BF)
        high_ref[:, at] = high
        rest_ref[:, at] = (weights - high.astype(F32)).astype(BF)


def kernel_project(
    part_ref, x0_ref, x1_ref, x2_ref, x3_ref, w_ref, cos_ref, sin_ref, msg_ref, hidden_ref, gains_ref
):
    gains = jnp.transpose(w_ref[:, 512:640].astype(F32))
    gains_ref[...] = gains[:8]
    for r, x_ref in enumerate((x0_ref, x1_ref, x2_ref, x3_ref)):
        x = x_ref[...].astype(F32)
        scale = lax.rsqrt(jnp.mean(x * x, axis=-1, keepdims=True) + EPSILON)
        hidden_ref[place(part_ref, r, 128), :] = (x * scale * gains[0:1]).astype(BF)
    proj = mm(hidden_ref[...], w_ref[:, 0:512])
    ahead = pltpu.roll(proj, 512 - 8, 1)
    behind = pltpu.roll(proj, 8, 1)
    partner = jnp.where((lane((512, 512)) // 8) % 2 == 0, ahead, behind)
    cos = jnp.concatenate([cos_ref[...]] * 4, axis=0)
    sin = jnp.concatenate([sin_ref[...]] * 4, axis=0)
    turned = proj * cos + partner * sin
    low = lane((64, 128)) < 64
    for s in range(4):
        for p in range(4):
            front = turned[128 * s : 128 * s + 64, 128 * p : 128 * p + 128]
            back = turned[128 * s + 64 : 128 * s + 128, 128 * p : 128 * p + 128]
            msg_ref[8 * p + s] = jnp.where(low, front, pltpu.roll(back, 64, 1)).astype(BF)
            msg_ref[8 * p + 4 + s] = jnp.where(low, pltpu.roll(front, 64, 1), back).astype(BF)


def kernel_heads(msg_ref, table_ref, kv_ref, q_ref):
    rows = jnp.concatenate([msg_ref[:, f].reshape(512, 128) for f in range(4)], axis=1)
    out = mm(rows, table_ref[...].reshape(512, 768))
    pairs = out[:, 0:256].astype(BF)
    for half in range(2):
        block = pairs[:, 128 * half : 128 * half + 128]
        for y in range(4):
            kv_ref[y, 512 * half : 512 * half + 512, :] = block
    queries = (out[:, 256:768] * 0.125).astype(BF)
    for half in range(2):
        for head in range(2):
            at = 256 * half + 128 * head
            q_ref[half, :, head] = queries[:, at : at + 128].reshape(8, 64, 128)


def tile_positions(tile, mine):
    front = tile < 4
    i = jnp.where(front, tile, tile - 4)
    q = lane((1, 256))
    k = lax.broadcasted_iota(jnp.int32, (512, 1), 0)
    q_front = (8 * i + 4 * (q // 128) + mine) * 64 + q % 64
    q_back = (63 - 8 * i - 4 * (q // 128) - mine) * 64 + q % 64
    k_front = 512 * i + k
    k_back = (59 - 8 * i + 4 * (k // 256) - (k % 256) // 64) * 64 + k % 64
    return jnp.where(front, q_front, q_back), jnp.where(front, k_front, k_back)


def kernel_attend(
    mine_ref,
    kv_ref,
    q_ref,
    msg_ref,
    log_ref,
    out_ref,
    keys_ref,
    turned_ref,
    peak_ref,
    total_ref,
    mixed_ref,
):
    tile = pl.program_id(0)

    @pl.when(tile == 0)
    def _():
        for group in range(16):
            half, place = (0, group) if group < 8 else (1, 15 - group)
            for y in range(4):
                at = 256 * group + 64 * y
                keys_ref[at : at + 64, :] = kv_ref[y, half, place]
        for c in range(8):
            turned_ref[:, 512 * c : 512 * c + 512] = jnp.transpose(
                keys_ref[512 * c : 512 * c + 512, :].astype(F32)
            ).astype(BF)

    q = q_ref[...]
    q_pos, k_pos = tile_positions(tile, mine_ref[0])

    def run(first, count, last):
        def keys(c):
            return pl.ds(pl.multiple_of(first + 512 * c, 512), 512)

        peak = peak_ref[0:1]
        total = total_ref[0:1]
        mixed = mixed_ref[...]
        later = mm(keys_ref[keys(0), :], q, NT)
        for c in range(count):
            scores = later
            if c + 1 < count:
                later = mm(keys_ref[keys(c + 1), :], q, NT)
            elif last:
                scores = jnp.where(k_pos <= q_pos, scores, MASKED)
            higher = jnp.maximum(peak, jnp.max(scores, axis=0, keepdims=True))
            weights = jnp.exp(scores - higher)
            fade = jnp.exp(peak - higher)
            total = total * fade + jnp.sum(weights, axis=0, keepdims=True)
            mixed = mixed * fade + mm(turned_ref[64:128, keys(c)], weights.astype(BF))
            peak = higher
        peak_ref[...] = jnp.broadcast_to(peak, (8, 256))
        total_ref[...] = jnp.broadcast_to(total, (8, 256))
        mixed_ref[...] = mixed

    peak_ref[...] = jnp.full((8, 256), MASKED, F32)
    total_ref[...] = jnp.zeros((8, 256), F32)
    mixed_ref[...] = jnp.zeros((64, 256), F32)

    @pl.when(tile >= 4)
    def _():
        run(0, 4, False)

    first = jnp.where(tile >= 4, 2048, 0)
    rest = jnp.where(tile >= 4, 8 - tile, tile + 1)
    for count in range(1, 5):
        pl.when(rest == count)(functools.partial(run, first, count, True))

    total = total_ref[0:1]
    log_ref[0] = jnp.broadcast_to(peak_ref[0:1] + jnp.log(total), (8, 256))
    mixed = mixed_ref[...] / total
    out = jnp.transpose(jnp.concatenate([jnp.zeros((64, 256), F32), mixed], axis=0))
    out_ref[...] = out
    low = lane((64, 128)) < 64
    for a in range(2):
        one = out[128 * a : 128 * a + 64]
        two = out[128 * a + 64 : 128 * a + 128]
        msg_ref[a, 0] = jnp.where(low, pltpu.roll(one, 64, 1), two).astype(BF)


def kernel_attend_back(
    mine_ref, keys_ref, turned_ref, q_ref, grad_ref, log_ref, out_ref, dq_ref, d0_ref, d1_ref, d2_ref, d3_ref, sum_ref
):
    tile = pl.program_id(0)

    @pl.when(tile == 0)
    def _():
        sum_ref[...] = jnp.zeros_like(sum_ref)

    q = q_ref[...]
    low = lane((64, 128)) < 64
    pieces = []
    for a in range(2):
        both = grad_ref[a, 0].astype(F32)
        pieces.append(jnp.where(low, 0.0, pltpu.roll(both, 64, 1)))
        pieces.append(jnp.where(low, 0.0, both))
    grad = jnp.concatenate(pieces, axis=0)
    delta = jnp.sum(jnp.transpose(grad * out_ref[...]), axis=0, keepdims=True)
    grad = grad.astype(BF)
    q_pos, k_pos = tile_positions(tile, mine_ref[0])
    log_total = log_ref[0][0:1]

    def step(c, dq, last):
        at = pl.ds(pl.multiple_of(c * 512, 512), 512)
        keys = keys_ref[at, :]
        scores = mm(keys, q, NT)
        if last:
            scores = jnp.where(k_pos <= q_pos, scores, MASKED)
        weights = jnp.exp(scores - log_total)
        slope = (weights * (mm(keys, grad, NT) - delta)).astype(BF)
        sum_ref[at, :] += mm(slope, q) + mm(weights.astype(BF), grad)
        return dq + mm(turned_ref[0:64, at], slope)

    count = jnp.where(tile < 4, tile + 1, 12 - tile)
    dq = lax.fori_loop(0, count - 1, lambda c, v: step(c, v, False), jnp.zeros((64, 256), F32))
    dq = step(count - 1, dq, True)
    dq_ref[...] = jnp.transpose(jnp.concatenate([dq * 0.125, jnp.zeros((64, 256), F32)], axis=0))

    @pl.when(tile == 7)
    def _():
        for group in range(16):
            half, place = (0, group) if group < 8 else (1, 15 - group)
            for r, dkv_ref in enumerate((d0_ref, d1_ref, d2_ref, d3_ref)):
                at = 256 * group + 64 * lax.bitwise_xor(mine_ref[0], r)
                part = sum_ref[pl.ds(pl.multiple_of(at, 64), 64), :]
                dkv_ref[half, place] = part.astype(BF)


def kernel_middle(
    part_ref,
    o_ref,
    u0_ref,
    u1_ref,
    u2_ref,
    u3_ref,
    l0_ref,
    l1_ref,
    l2_ref,
    l3_ref,
    x_ref,
    gains_ref,
    pick_ref,
    slots_ref,
    mid_ref,
    rows_ref,
    hidden_ref,
):
    @pl.when(pl.program_id(0) == 0)
    def _():
        for g in range(8):
            rows_ref[:, 128 * g : 128 * g + 128] = o_ref[g].reshape(128, 128)
        uppers = (u0_ref, u1_ref, u2_ref, u3_ref)
        lowers = (l0_ref, l1_ref, l2_ref, l3_ref)
        for r in range(4):
            at = place(part_ref, r, 256)
            mid_ref[:, at] = (
                x_ref[:, at].astype(F32)
                + mm(rows_ref[:, 0:512], uppers[r][...])
                + mm(rows_ref[:, 512:1024], lowers[r][...])
            )
        mid = mid_ref[...]
        scale = lax.rsqrt(jnp.mean(mid * mid, axis=-1, keepdims=True) + EPSILON)
        hidden_ref[...] = (mid * scale * gains_ref[1:2]).astype(BF)

    for c in range(4):
        at = slice(256 * c, 256 * c + 256)
        rows = mm(pick_ref[...], hidden_ref[:, at]).astype(BF)
        slots_ref[:, :, at] = rows.reshape(16, 64, 256)


def kernel_experts_ready(
    part_ref,
    dy_ref,
    parts_ref,
    w0_ref,
    w1_ref,
    w2_ref,
    w3_ref,
    dys_ref,
    dact_ref,
    v_ref,
    gu_ref,
    rank_ref,
    gate_ref,
):
    step = pl.program_id(0)

    @pl.when(step == 0)
    def _():
        for r, w_ref in enumerate((w0_ref, w1_ref, w2_ref, w3_ref)):
            gu_ref[place(part_ref, r, 256), :] = w_ref[0:256, :]
            v_ref[place(part_ref, r, 128), :] = w_ref[256:384, :]
        before = jnp.where(row((128, 128)) < lane((128, 128)), 1.0, 0.0).astype(BF)
        parts = [parts_ref[:, k, :].astype(F32) for k in range(6)]
        even = parts[0] + parts[2] + parts[4]
        odd = parts[1] + parts[3] + parts[5]
        gate_ref[...] = jnp.where(lane((32, 128)) < 64, pltpu.roll(even, 64, 1), odd)
        chosen = gate_ref[...] > 0.0
        rank = mm(jnp.where(chosen, 1.0, 0.0).astype(BF), before)
        rank_ref[...] = jnp.where(chosen, rank, -1.0)

    slot = lax.broadcasted_iota(jnp.int32, (64, 128), 0).astype(F32)
    grads = []
    for j in range(4):
        source = 4 * step + j
        pick = slot == rank_ref[pl.ds(source, 1), :]
        weight = jnp.sum(
            jnp.where(pick, gate_ref[pl.ds(source, 1), :], 0.0), axis=1, keepdims=True
        )
        rows = mm(jnp.where(pick, 1.0, 0.0).astype(BF), dy_ref[0, j, 0])
        grads.append((rows * weight).astype(BF))
    dys = jnp.concatenate(grads, axis=0)
    dys_ref[...] = dys.reshape(4, 64, WIDTH)
    dact_ref[...] = mm(dys, v_ref[...], NT)


def kernel_experts(h_ref, gu_ref, dact_ref, act_ref, dboth_ref, dxs_ref):
    def project(part):
        return mm(h_ref[4 * part : 4 * part + 4].reshape(256, WIDTH), gu_ref[...])

    later = project(0)
    for part in range(2):
        both = later
        if part == 0:
            later = project(1)
        at = slice(256 * part, 256 * part + 256)
        gate_h, up_h = both[:, :512], both[:, 512:]
        sig = 0.5 * jnp.tanh(0.5 * gate_h) + 0.5
        swished = gate_h * sig
        act_ref[at, :] = (swished * up_h).astype(BF)
        dact = dact_ref[at, :]
        dgate = (dact * up_h * (sig + swished * (1.0 - sig))).astype(BF)
        dup = (dact * swished).astype(BF)
        dboth = jnp.concatenate([dgate, dup], axis=1)
        dboth_ref[at, :] = dboth
        dxs = mm(dboth, gu_ref[...], NT).astype(BF)
        dxs_ref[4 * part : 4 * part + 4] = dxs.reshape(4, 64, WIDTH)


def kernel_experts_after(
    h_ref, act_ref, dys_ref, dboth_ref, v_ref, ys_ref, grad_ref, ggu_ref, gv_ref
):
    step = pl.program_id(0)

    @pl.when(step == 0)
    def _():
        ggu_ref[...] = jnp.zeros_like(ggu_ref)
        gv_ref[...] = jnp.zeros_like(gv_ref)

    act = act_ref[...]
    ys_ref[...] = mm(act, v_ref[...]).astype(BF).reshape(4, 64, WIDTH)
    h = h_ref[...].reshape(256, WIDTH)

    @pl.loop(0, 4)
    def _(c):
        at = pl.ds(pl.multiple_of(256 * c, 256), 256)
        ggu_ref[:, at] += mm(h, dboth_ref[:, at], TN)

    gv_ref[...] += mm(act, dys_ref[...].reshape(256, WIDTH), TN)

    @pl.when(step == 7)
    def _():
        for f in range(4):
            grad_ref[f, 0:256, :] = ggu_ref[256 * f : 256 * f + 256, :].astype(BF)
            grad_ref[f, 256:384, :] = gv_ref[128 * f : 128 * f + 128, :].astype(BF)


def kernel_middle_back(
    part_ref,
    dxs_ref,
    pick_ref,
    mid_ref,
    cot_ref,
    gains_ref,
    u0_ref,
    u1_ref,
    u2_ref,
    u3_ref,
    l0_ref,
    l1_ref,
    l2_ref,
    l3_ref,
    dmid_ref,
    parts_ref,
    msg_ref,
    ggain_ref,
    sum_ref,
    low_ref,
):
    step = pl.program_id(0)
    part = mm(pick_ref[...], dxs_ref[...].reshape(1024, WIDTH))

    @pl.when(step == 0)
    def _():
        sum_ref[...] = part

    @pl.when(step > 0)
    def _():
        sum_ref[...] += part

    @pl.when(step == 1)
    def _():
        mid = mid_ref[...]
        scale = lax.rsqrt(jnp.mean(mid * mid, axis=-1, keepdims=True) + EPSILON)
        dh = sum_ref[...]
        ggain_ref[...] = jnp.broadcast_to(
            jnp.sum(dh * (mid * scale), axis=0, keepdims=True), (8, WIDTH)
        )
        dn = dh * gains_ref[1:2]
        dmid = (
            cot_ref[...].astype(F32)
            + scale * dn
            - mid * (scale * scale * scale) * jnp.mean(dn * mid, axis=-1, keepdims=True)
        )
        dmid_ref[...] = dmid
        low_ref[...] = dmid.astype(BF)
        uppers = (u0_ref, u1_ref, u2_ref, u3_ref)
        lowers = (l0_ref, l1_ref, l2_ref, l3_ref)
        for r in range(4):
            parts_ref[r] = low_ref[:, place(part_ref, r, 256)]
        for h, w_refs in enumerate((uppers, lowers)):
            grad = mm(parts_ref[0], w_refs[0][...], NT)
            for r in range(1, 4):
                grad = grad + mm(parts_ref[r], w_refs[r][...], NT)
            grad = grad.astype(BF)
            for g in range(4):
                msg_ref[4 * h + g] = grad[:, 128 * g : 128 * g + 128].reshape(2, 64, 128)


def kernel_out_weight(
    o0_ref, o1_ref, o2_ref, o3_ref, da0_ref, da1_ref, da2_ref, da3_ref, gain_ref, grad_ref
):
    which = lax.broadcasted_iota(jnp.int32, (128, WIDTH), 0)
    grad_ref[:, 0:128] = jnp.transpose(jnp.where(which == 1, gain_ref[0:1], 0.0)).astype(BF)
    pairs = ((o0_ref, da0_ref), (o1_ref, da1_ref), (o2_ref, da2_ref), (o3_ref, da3_ref))

    @pl.loop(0, 8)
    def _(g):
        part = jnp.zeros((128, 256), F32)
        for o_ref, da_ref in pairs:
            part = part + mm(o_ref[g].reshape(128, 128), da_ref[...], TN)
        grad_ref[pl.ds(pl.multiple_of(128 * g, 128), 128), 128:384] = part.astype(BF)


def unrotate(w, cos, sin):
    partner = jnp.where(lane(w.shape) % 64 < 32, pltpu.roll(w, 96, 1), pltpu.roll(w, 32, 1))
    return (w * cos - partner * sin).astype(BF)


def kernel_queries_back(
    dq_ref, cos_ref, sin_ref, table_ref, hidden_ref, msg_ref, hidden_turned_ref
):
    for s in range(4):
        at = slice(128 * s, 128 * s + 128)
        hidden_turned_ref[:, at] = jnp.transpose(hidden_ref[at, :].astype(F32)).astype(BF)
    parts = []
    for half in range(2):
        at = slice(512 * half, 512 * half + 512)
        for head in range(2):
            dq = dq_ref[half, :, head].reshape(512, 128)
            parts.append(unrotate(dq, cos_ref[at, :], sin_ref[at, :]))
    whole = jnp.concatenate(parts, axis=1)
    for f in range(4):
        rows = mm(whole, table_ref[f, :, 256:768], NT)
        msg_ref[:, f] = rows.astype(BF).reshape(8, 64, 128)


def kernel_slices_back(
    d0_ref, d1_ref, d2_ref, d3_ref, queries_ref, cos_ref, sin_ref, table_ref, msg_ref
):
    parts = []
    for half in range(2):
        at = slice(512 * half, 512 * half + 512)
        dkv = d0_ref[half].reshape(512, 128).astype(F32)
        for d_ref in (d1_ref, d2_ref, d3_ref):
            dkv = dkv + d_ref[half].reshape(512, 128).astype(F32)
        parts.append(unrotate(dkv, cos_ref[at, :], sin_ref[at, :]))
    whole = jnp.concatenate(parts, axis=1)
    cut = mm(whole, table_ref[:, :, 0:256].reshape(512, 256), NT)
    for f in range(4):
        rows = cut[:, 128 * f : 128 * f + 128] + queries_ref[:, f].reshape(512, 128)
        msg_ref[:, f] = rows.astype(BF).reshape(8, 64, 128)


def kernel_hidden_grad(part_ref, d_ref, w_ref, h0_ref, h1_ref, h2_ref, h3_ref):
    for r, h_ref in enumerate((h0_ref, h1_ref, h2_ref, h3_ref)):
        h_ref[...] = mm(d_ref[place(part_ref, r, 128), :], w_ref[:, 0:512], NT).astype(BF)


def kernel_grads(msg_ref, hidden_ref, rest_ref, grads_ref, d_ref):
    low = lane((64, 128)) < 64
    for s in range(4):
        for p in range(4):
            even = msg_ref[8 * p + s].astype(F32)
            odd = msg_ref[8 * p + 4 + s].astype(F32)
            d_ref[128 * s : 128 * s + 64, 128 * p : 128 * p + 128] = jnp.where(
                low, even, pltpu.roll(odd, 64, 1)
            ).astype(BF)
            d_ref[128 * s + 64 : 128 * s + 128, 128 * p : 128 * p + 128] = jnp.where(
                low, pltpu.roll(even, 64, 1), odd
            ).astype(BF)
    total = mm(hidden_ref[...], d_ref[...])
    grads_ref[:, 0:512] = total.astype(BF)
    grads_ref[:, 512:896] = rest_ref[...]


def kernel_input_grad(d0_ref, d1_ref, d2_ref, d3_ref, x_ref, dmid_ref, gains_ref, out_ref):
    dh = d0_ref[...].astype(F32)
    for d_ref in (d1_ref, d2_ref, d3_ref):
        dh = dh + d_ref[...].astype(F32)
    x = x_ref[...].astype(F32)
    scale = lax.rsqrt(jnp.mean(x * x, axis=-1, keepdims=True) + EPSILON)
    dn = dh * gains_ref[0:1]
    out_ref[...] = (
        dmid_ref[...]
        + scale * dn
        - x * (scale * scale * scale) * jnp.mean(dn * x, axis=-1, keepdims=True)
    )


def kernel_total(parts_ref, table_ref, w_ref, rows_ref, qkv_ref, out_ref, gains_ref, sum_ref):
    total = parts_ref[0].astype(F32)
    for c in range(1, 32):
        total = total + parts_ref[c].astype(F32)
    sum_ref[...] = total
    rows = []
    for p in range(4):
        rows.append(
            jnp.concatenate([sum_ref[f, :, 128 * p : 128 * p + 128] for f in range(4)], axis=1)
        )
    rest = jnp.concatenate(rows, axis=0)
    parts = []
    for _ in range(3):
        part = rest.astype(BF)
        rest = rest - part.astype(F32)
        parts.append(part)
    whole = mm(jnp.concatenate(parts, axis=0), table_ref[...], NT)
    whole = whole[0:32] + whole[32:64] + whole[64:96]
    for p in range(4):
        piece = whole[8 * p : 8 * p + 8]
        qkv_ref[:, 256 * p : 256 * p + 256] = piece[:, 0:256]
        qkv_ref[:, 1024 + 128 * p : 1152 + 128 * p] = piece[:, 256:384]
        qkv_ref[:, 1536 + 128 * p : 1664 + 128 * p] = piece[:, 384:512]
    for f in range(4):
        out_ref[:, 256 * f : 256 * f + 256] = sum_ref[f, :, 640:896]
    gains = (
        sum_ref[0, :, 512:640]
        + sum_ref[1, :, 512:640]
        + sum_ref[2, :, 512:640]
        + sum_ref[3, :, 512:640]
    )
    w = w_ref[...].astype(BF).astype(F32)
    first = jnp.sum(w * qkv_ref[...], axis=1, keepdims=True)
    first = first / rows_ref[:, 0:1].astype(BF).astype(F32)
    gains_ref[...] = jnp.where(lane((8, 128)) == 0, first, gains)


def kernel_output(ys_ref, high_ref, rest_ref, mid_ref, out_ref, sum_ref):
    step = pl.program_id(0)

    @pl.when(step == 0)
    def _():
        sum_ref[...] = mid_ref[...]

    ys = ys_ref[...].reshape(512, WIDTH)
    sum_ref[...] += mm(high_ref[...], ys) + mm(rest_ref[...], ys)

    @pl.when(step == 3)
    def _():
        out_ref[...] = sum_ref[...].astype(BF)


def angles(positions, features):
    frequency = ROPE_BASE ** (-(features.astype(F32) * 2.0 / 64))
    return positions.astype(F32)[:, None] * frequency[None, :]


def whole(shape):
    return pl.BlockSpec(shape, lambda t: (0,) * len(shape))


def exchange(value, axes):
    return lax.all_to_all(value, axes, split_axis=0, concat_axis=0, tiled=True)


def gather(value, axes):
    return lax.all_gather(value, axes, axis=0, tiled=True)


def after(value, marker):
    return lax.optimization_barrier((value, marker))[0]


def swap(value, axis):
    return lax.ppermute(value, axis, [(0, 1), (1, 0)])


def neighbours(value):
    return value, swap(value, "core"), swap(value, "zl")


def cross(parts, axes=FSDP):
    here = [parts[0]]
    for r in range(1, 4):
        here.append(lax.ppermute(parts[r], axes, [(i, i ^ r) for i in range(4)]))
    return here


def on_device(
    layer_input,
    routes,
    gates,
    cotangent,
    norm_attn,
    query_key_value_weight,
    output_weight,
    norm_ffn,
    exp_gate,
    exp_up,
    exp_down,
):
    mine = lax.axis_index("y")
    ctx_index = lax.axis_index(CTX)
    part_index = lax.axis_index(FSDP)
    mine_ref = mine.astype(jnp.int32).reshape(1)
    part_ref = part_index.astype(jnp.int32).reshape(1)
    x = layer_input.reshape(128, WIDTH)
    cot = cotangent.reshape(128, WIDTH)
    slice_table = jnp.asarray(slice_matrix(), BF)
    head_table = jnp.asarray(head_matrix(), BF)

    x_all = neighbours(x)
    rank, gate = call(
        kernel_route,
        (sds((32, 128), F32), sds((32, 128), F32)),
        (1e6, 1e5),
        in_specs=[VM, VM],
        out_specs=(VM, VM),
    )(routes.reshape(128, 8).T, gates.reshape(128, 8).T)
    which = lax.broadcasted_iota(jnp.int32, (8, 128), 1)
    gain_rows = jnp.where(
        which == 0, norm_attn[:, None], jnp.where(which == 1, norm_ffn[:, None], 0.0)
    )
    slices = call(
        kernel_slices,
        sds((32, 4, 8, 896), BF),
        (2e7, 3e6),
        in_specs=[VM] * 5,
        out_specs=VM,
    )(query_key_value_weight, gain_rows, slice_table, gate, output_weight)
    slices, rank, gate, x_all = lax.optimization_barrier((slices, rank, gate, x_all))
    x_all = x_all + (swap(x_all[2], "core"),)
    offset = jnp.arange(64, dtype=jnp.int32)
    token_pos = jnp.concatenate([ctx_index * 64 + offset, (63 - ctx_index) * 64 + offset])
    column = jnp.arange(512, dtype=jnp.int32)
    angle = angles(token_pos, 8 * part_index + column % 8)
    is_value = (column // 16) % 4 == 3
    sign = jnp.where((column // 8) % 2 == 0, -1.0, 1.0)
    cos_slice = jnp.where(is_value, 1.0, jnp.cos(angle))
    sin_slice = jnp.where(is_value, 0.0, jnp.sin(angle) * sign)
    w_slice = exchange(slices.reshape(128, 8, 896), ALL)
    w_slice, cos_slice, sin_slice = lax.optimization_barrier((w_slice, cos_slice, sin_slice))
    gate_parts = lax.dynamic_slice(
        w_slice.reshape(32, 4, 8, 896), (0, part_index, 0, 512), (32, 1, 8, 128)
    ).reshape(32, 8, 128)
    w_slice = w_slice.reshape(WIDTH, 896)
    picks, picks_turned, picks_high, picks_rest = call(
        kernel_picks,
        (sds((2048, 128), BF),) + (sds((128, 2048), BF),) * 3,
        (2e9, 4e6),
        in_specs=[VM, VM],
        out_specs=(VM,) * 4,
    )(rank, gate)

    msg, hidden, gains = call(
        kernel_project,
        (sds((32, 64, 128), BF), sds((512, WIDTH), BF), sds((8, WIDTH), F32)),
        (6e8, 4e6),
        in_specs=[SM] + [VM] * 7,
        out_specs=(VM, VM, VM),
    )(part_ref, *x_all, w_slice, cos_slice, sin_slice)
    across = swap(after(cot, w_slice), "zh")
    first = lax.axis_index("zh") == 0
    cot_pair = jnp.concatenate(
        [jnp.where(first, cot, across), jnp.where(first, across, cot)], axis=0
    )
    out_upper = neighbours(w_slice[0:512, 640:896])
    msg = exchange(msg, HEAD_AXES + FSDP)

    kv_copies, queries = call(
        kernel_heads,
        (sds((4, 1024, 128), BF), sds((2, 8, 2, 64, 128), BF)),
        (4e8, 3e6),
        in_specs=[VM, VM],
        out_specs=(VM, VM),
    )(msg.reshape(8, 4, 64, 128), head_table)
    queries = queries.reshape(2048, 128)
    kv_copies, out_upper = lax.optimization_barrier((kv_copies, out_upper))
    out_lower = neighbours(after(w_slice[512:1024, 640:896], msg))
    kv = exchange(kv_copies, ("y",)).reshape(4, 2, 8, 64, 128)
    expert_weights = jnp.concatenate(
        [jnp.concatenate([exp_gate[0], exp_up[0]], axis=1), exp_down[0]], axis=0
    ).astype(BF)
    block = 4 * jnp.arange(8, dtype=jnp.int32)[:, None] + mine
    quarter_pos = jnp.concatenate(
        [
            (block * 64 + offset[None, :]).reshape(-1),
            ((63 - block) * 64 + offset[None, :]).reshape(-1),
        ]
    )
    column = jnp.arange(128, dtype=jnp.int32)
    angle = angles(quarter_pos, column % 32)
    sign = jnp.where(column % 64 < 32, -1.0, 1.0)
    cos_heads = jnp.where(column >= 64, 1.0, jnp.cos(angle))
    sin_heads = jnp.where(column >= 64, 0.0, jnp.sin(angle) * sign)
    kv, out_lower, cos_heads, sin_heads = lax.optimization_barrier(
        (kv, out_lower, cos_heads, sin_heads)
    )
    experts_all = neighbours(after(expert_weights, msg))
    cot_all = gather(after(cot_pair, kv_copies), ("x", "y")).reshape(4, 4, 2, 128, WIDTH)
    out_upper = out_upper + (swap(after(out_upper[2], kv), "core"),)
    out_lower = out_lower + (swap(out_lower[2], "core"),)
    w_out = (*out_upper, *out_lower)
    msg_spec = pl.BlockSpec((2, 1, 64, 128), lambda t: (t % 4, t // 4, 0, 0))
    row_spec = pl.BlockSpec((256, 128), lambda t: (t, 0))
    log_spec = pl.BlockSpec((1, 8, 256), lambda t: (t, 0, 0))
    o_msg, log_total, o_rows, keys, turned = call(
        kernel_attend,
        (
            sds((8, 2, 64, 128), BF),
            sds((8, 8, 256), F32),
            sds((2048, 128), F32),
            sds((4096, 128), BF),
            sds((128, 4096), BF),
        ),
        (1e10, 5e6),
        grid=(8,),
        in_specs=[SM, whole((4, 2, 8, 64, 128)), row_spec],
        out_specs=(msg_spec, log_spec, row_spec, whole((4096, 128)), whole((128, 4096))),
        scratch_shapes=[
            pltpu.VMEM((8, 256), F32),
            pltpu.VMEM((8, 256), F32),
            pltpu.VMEM((64, 256), F32),
        ],
    )(mine_ref, kv, queries)
    o_msg, w_out, experts_all = lax.optimization_barrier((o_msg, w_out, experts_all))
    experts_all = experts_all + (swap(experts_all[2], "core"),)
    o_heads = exchange(o_msg, HEAD_AXES)

    slot_spec = pl.BlockSpec((4, 64, WIDTH), lambda t: (t, 0, 0))
    out_specs = [whole((512, 256))] * 8
    slots, mid = call(
        kernel_middle,
        (sds((32, 64, WIDTH), BF), sds((128, WIDTH), F32)),
        (9e8, 8e6),
        grid=(2,),
        in_specs=[SM, whole((8, 2, 64, 128))]
        + out_specs
        + [
            whole((128, WIDTH)),
            whole((8, WIDTH)),
            pl.BlockSpec((1024, 128), lambda t: (t, 0)),
        ],
        out_specs=(pl.BlockSpec((16, 64, WIDTH), lambda t: (t, 0, 0)), whole((128, WIDTH))),
        scratch_shapes=[pltpu.VMEM((128, WIDTH), BF), pltpu.VMEM((128, WIDTH), BF)],
    )(part_ref, o_heads, *w_out, x, gains, picks)
    cot_all = after(cot_all, mid)
    slots, experts_all = lax.optimization_barrier((slots, experts_all))
    slots = exchange(slots, CTX)
    dys, dact, down, gate_up = call(
        kernel_experts_ready,
        (
            sds((32, 64, WIDTH), BF),
            sds((2048, 512), F32),
            sds((512, WIDTH), BF),
            sds((WIDTH, WIDTH), BF),
        ),
        (6e9, 2e7),
        grid=(8,),
        in_specs=[
            SM,
            pl.BlockSpec((1, 4, 1, 128, WIDTH), lambda t: (t // 2, 0, t % 2, 0, 0)),
            whole((32, 8, 128)),
        ]
        + [whole((384, WIDTH))] * 4,
        out_specs=(
            slot_spec,
            pl.BlockSpec((256, 512), lambda t: (t, 0)),
            whole((512, WIDTH)),
            whole((WIDTH, WIDTH)),
        ),
        scratch_shapes=[pltpu.VMEM((32, 128), F32), pltpu.VMEM((32, 128), F32)],
    )(part_ref, cot_all, gate_parts, *experts_all)
    act_spec = pl.BlockSpec((256, 512), lambda t: (t, 0))
    both_spec = pl.BlockSpec((256, WIDTH), lambda t: (t, 0))
    act, dboth, dxs = call(
        kernel_experts,
        (sds((2048, 512), BF), sds((2048, WIDTH), BF), sds((32, 64, WIDTH), BF)),
        (9e9, 2e7),
        grid=(4,),
        in_specs=[
            pl.BlockSpec((8, 64, WIDTH), lambda t: (t, 0, 0)),
            whole((WIDTH, WIDTH)),
            pl.BlockSpec((512, 512), lambda t: (t, 0)),
        ],
        out_specs=(
            pl.BlockSpec((512, 512), lambda t: (t, 0)),
            pl.BlockSpec((512, WIDTH), lambda t: (t, 0)),
            pl.BlockSpec((8, 64, WIDTH), lambda t: (t, 0, 0)),
        ),
    )(slots, gate_up, dact)
    ys, expert_grads = call(
        kernel_experts_after,
        (sds((32, 64, WIDTH), BF), sds((4, 384, WIDTH), BF)),
        (9e9, 2e7),
        grid=(8,),
        in_specs=[slot_spec, act_spec, slot_spec, both_spec, whole((512, WIDTH))],
        out_specs=(slot_spec, whole((4, 384, WIDTH))),
        scratch_shapes=[pltpu.VMEM((WIDTH, WIDTH), F32), pltpu.VMEM((512, WIDTH), F32)],
    )(slots, act, dys, dboth, down)
    o_all = neighbours(after(o_heads, dxs))
    dxs = exchange(dxs, CTX)
    expert_own = lax.psum_scatter(
        expert_grads.reshape(4 * 384, WIDTH), FSDP, scatter_dimension=0, tiled=True
    ).astype(F32)
    dxs, ys = lax.optimization_barrier((dxs, ys))

    dmid, da_parts, grad_msg, gain_ffn_part = call(
        kernel_middle_back,
        (
            sds((128, WIDTH), F32),
            sds((4, 128, 256), BF),
            sds((8, 2, 64, 128), BF),
            sds((8, WIDTH), F32),
        ),
        (9e8, 8e6),
        grid=(2,),
        in_specs=[
            SM,
            pl.BlockSpec((16, 64, WIDTH), lambda t: (t, 0, 0)),
            pl.BlockSpec((128, 1024), lambda t: (0, t)),
            whole((128, WIDTH)),
            whole((128, WIDTH)),
            whole((8, WIDTH)),
        ]
        + out_specs,
        out_specs=(
            whole((128, WIDTH)),
            whole((4, 128, 256)),
            whole((8, 2, 64, 128)),
            whole((8, WIDTH)),
        ),
        scratch_shapes=[pltpu.VMEM((128, WIDTH), F32), pltpu.VMEM((128, WIDTH), BF)],
    )(part_ref, dxs, picks_turned, mid, cot, gains, *w_out)
    grad_heads = exchange(grad_msg, HEAD_AXES)
    ys, grad_heads, o_all = lax.optimization_barrier((ys, grad_heads, o_all))
    o_all = o_all + (swap(o_all[2], "core"),)
    ys = exchange(ys, CTX)
    dq, *dkv = call(
        kernel_attend_back,
        (sds((2048, 128), F32),) + (sds((2, 8, 64, 128), BF),) * 4,
        (2e10, 7e6),
        grid=(8,),
        in_specs=[
            SM,
            whole((4096, 128)),
            whole((128, 4096)),
            row_spec,
            msg_spec,
            log_spec,
            row_spec,
        ],
        out_specs=(row_spec,) + (whole((2, 8, 64, 128)),) * 4,
        scratch_shapes=[pltpu.VMEM((4096, 128), F32)],
    )(mine_ref, keys, turned, queries, grad_heads, log_total, o_rows)
    da_here = cross(da_parts)
    dkv = cross(dkv, ("y",))
    queries_back, hidden_turned = call(
        kernel_queries_back,
        (sds((8, 4, 64, 128), BF), sds((WIDTH, 512), BF)),
        (3e8, 4e6),
        in_specs=[VM] * 5,
        out_specs=(VM, VM),
    )(dq.reshape(2, 8, 2, 64, 128), cos_heads, sin_heads, head_table, hidden)
    dkv, ys, da_here, queries_back = lax.optimization_barrier((dkv, ys, da_here, queries_back))
    rest_part = call(
        kernel_out_weight,
        sds((WIDTH, 384), BF),
        (3e8, 2e6),
        in_specs=[VM] * 9,
        out_specs=VM,
    )(*o_all, *da_here, gain_ffn_part)
    layer_output = call(
        kernel_output,
        sds((128, WIDTH), BF),
        (1e9, 5e6),
        grid=(4,),
        in_specs=[
            pl.BlockSpec((8, 64, WIDTH), lambda t: (t, 0, 0)),
            pl.BlockSpec((128, 512), lambda t: (0, t)),
            pl.BlockSpec((128, 512), lambda t: (0, t)),
            whole((128, WIDTH)),
        ],
        out_specs=whole((128, WIDTH)),
        scratch_shapes=[pltpu.VMEM((128, WIDTH), F32)],
    )(ys, picks_high, picks_rest, mid)

    back = call(
        kernel_slices_back,
        sds((8, 4, 64, 128), BF),
        (2e8, 3e6),
        in_specs=[VM] * 8,
        out_specs=VM,
    )(*dkv, queries_back, cos_heads, sin_heads, head_table)
    back = exchange(back.reshape(32, 64, 128), HEAD_AXES + FSDP)

    grads, d_all = call(
        kernel_grads,
        (sds((WIDTH, 896), BF), sds((512, 512), BF)),
        (6e8, 5e6),
        in_specs=[VM] * 3,
        out_specs=(VM, VM),
    )(back, hidden_turned, rest_part)
    dh_parts = call(
        kernel_hidden_grad,
        (sds((128, WIDTH), BF),) * 4,
        (6e8, 5e6),
        in_specs=[SM, VM, VM],
        out_specs=(VM,) * 4,
    )(part_ref, d_all, w_slice)
    grads = exchange(grads.reshape(128, 8, 896), ALL)
    grad_qkv, grad_out, grad_gains = call(
        kernel_total,
        (sds((8, 2048), F32), sds((8, WIDTH), F32), sds((8, 128), F32)),
        (1e8, 4e6),
        in_specs=[VM] * 4,
        out_specs=(VM, VM, VM),
        scratch_shapes=[pltpu.VMEM((4, 8, 896), F32)],
    )(grads.reshape(32, 4, 8, 896), slice_table, query_key_value_weight, gain_rows)
    dh_here = cross(dh_parts)
    input_grad = call(
        kernel_input_grad,
        sds((128, WIDTH), F32),
        (1e6, 2e6),
        in_specs=[VM] * 7,
        out_specs=VM,
    )(*after(dh_here, grad_qkv), x, dmid, gains)
    return (
        layer_output.reshape(layer_input.shape),
        input_grad.reshape(layer_input.shape),
        grad_gains[:, 0],
        grad_qkv,
        grad_out,
        grad_gains[:, 1],
        expert_own[0:256, 0:512][None],
        expert_own[0:256, 512:1024][None],
        expert_own[256:384][None],
    )


def solution(mesh):
    parts = Mesh(mesh.devices.reshape(4, 2, 4, 2, 2), ALL)
    tokens = P(FSDP, CTX, None, None, None, None)
    experts = P(CTX, FSDP, None)
    in_specs = (
        tokens,
        tokens,
        tokens,
        tokens,
        P(ALL),
        P(ALL, None),
        P(ALL, None),
        P(ALL),
        experts,
        experts,
        experts,
    )
    out_specs = (
        tokens,
        tokens,
        P(ALL),
        P(ALL, None),
        P(ALL, None),
        P(ALL),
        experts,
        experts,
        experts,
    )
    return jax.shard_map(
        on_device, mesh=parts, in_specs=in_specs, out_specs=out_specs, check_vma=False
    )
```
